32 devices in a mesh: pp: 4 (over z), ep: 8 (over y, x, core).
Axes of the slice: x: 2, y: 2, z: 4, core: 2. Of those that a mesh axis runs over, the one named last changes fastest.
Arguments:
- fwd_act: bfloat16 [2048, 3584], P(('pp', 'ep')), may hold values from -6 to 6
- fwd_ids: int32 [2048, 1], P(('pp', 'ep')), may hold values from 0 to 3; in each aligned block of 64 rows (0 to 63, 64 to 127, ...) at most 17 rows name the same one
- bwd_act: bfloat16 [2048, 3584], P(('pp', 'ep')), may hold values from -6 to 6
- bwd_ids: int32 [2048, 1], P(('pp', 'ep')), may hold values from 0 to 3; in each aligned block of 64 rows (0 to 63, 64 to 127, ...) at most 17 rows name the same one
- bwd_grad: bfloat16 [2048, 3584], P(('pp', 'ep')), may hold values from -6 to 6
- norm_gain: bfloat16 [4, 3584], P('pp'), may hold values from 0.099609375 to 1.8984375
- router: bfloat16 [4, 3584, 4], P('pp'), may hold values from -0.09375 to 0.09375
- w_gate: bfloat16 [32, 3584, 512], P(('pp', 'ep')), may hold values from -0.09375 to 0.09375
- w_down: bfloat16 [32, 512, 3584], P(('pp', 'ep')), may hold values from -0.1875 to 0.1875
- saved_gate: bfloat16 [4, 8, 136, 512], P('pp', 'ep'), may hold values from -6 to 6
Outputs:
- fwd_next: bfloat16 [2048, 3584], P(('pp', 'ep'))
- bwd_next: bfloat16 [2048, 3584], P(('pp', 'ep'))
The draws below stay inside these ranges and needn't reach their ends.
Inputs may be any that keep to these rules, and one draw needn't show every extreme that they name: `fwd_ids`: each row names one held expert. Among the rows of one device no expert is named by more than 17 rows; some device names some expert exactly 17 times. `bwd_ids`: as for fwd_ids.
All inputs are finite; a program needn't handle non-finite values.
Results may differ from the reference program's by a relative error of at most 0.015.
Values may be sent and summed in bfloat16 or wider, within the bound.
No kernel may reach another device: no remote copies, remote signals or barrier semaphores. Data moves between devices by JAX's collectives and lax.ppermute only.
A program may use at most 128 MiB of HBM per device.

```python
import math
import jax
import jax.numpy as jnp
import numpy as np
from jax import lax

D = 3584
HID = 1024
EXPERTS = 4
TOPK = 1
TOK_DEV = 64
HSPLIT = 2
HSLICE = 512
CAP = 17
TOKENS = 512
N_PP = 4
N_EP = 8


def shard_levels(rng, extent, cuts, least, high):
    gain = 1.0
    for position, shards_of in cuts:
        steps = jax.random.uniform(jax.random.fold_in(jax.random.fold_in(rng, 6), position), (shards_of,), jnp.float32, least / len(cuts), high / len(cuts))
        gain = gain * jnp.repeat(jnp.exp(steps), extent[position] // shards_of).reshape((-1,) + (1,) * (len(extent) - 1 - position))
    return gain


def routed_block(stream_key, own, number, rows, number_of, top, most, skew):
    ranking = jax.random.permutation(stream_key, number_of)
    packed, usual = shares(number_of, rows * top, most, skew, True), shares(number_of, rows * top, most, skew, False)
    places = jnp.arange(number_of)

    def named(tallies, rotation):
        used = int((tallies > 0).sum())
        fixed = max(1, used // 4)
        passed = fixed + (places - fixed + rotation * (used - fixed)) % max(1, number_of - fixed)
        return jnp.zeros((number_of,), jnp.int32).at[ranking[jnp.where(places < fixed, places, passed)]].set(jnp.asarray(tallies, jnp.int32))

    tallies = jnp.where(number % 4 == 0, named(packed, number // 4), named(usual, number - number // 4 - 1))
    mixed = jax.random.permutation(jax.random.fold_in(own, 3), number_of)
    donor, taker = mixed[0:number_of // 2 * 2:2], mixed[1:number_of // 2 * 2:2]
    margin = jnp.minimum(tallies[donor] - 1, most - tallies[taker]) // 2
    margin = jnp.where((donor == ranking[0]) | (taker == ranking[0]) | (tallies[taker] == 0), 0, jnp.maximum(margin, 0))
    passed = jax.random.randint(jax.random.fold_in(own, 4), (number_of // 2,), 0, 1 << 20) % (margin + 1)
    tallies = tallies.at[donor].add(-passed).at[taker].add(passed)
    items = jnp.searchsorted(jnp.cumsum(tallies), jnp.arange(rows * top), side="right").astype(jnp.int32)
    listing = items.reshape(top, rows).T
    listing = listing[jax.random.permutation(jax.random.fold_in(own, 1), rows)]
    rotation = jax.random.randint(jax.random.fold_in(own, 2), (rows, 1), 0, top)
    return jnp.take_along_axis(listing, (jnp.arange(top)[None, :] + rotation) % top, axis=1)


def shares(number_of, total, limit, skew, full):
    loads = [(1 << 20) // math.isqrt(standing ** skew) + 1 for standing in range(1, number_of + 1)]
    largest = limit if full else min(limit, max(-(-total // number_of), total * loads[0] // sum(loads)))
    least = 1 if total - largest >= number_of - 1 else 0
    counts, spare = [largest] + [least] * (number_of - 1), total - largest - least * (number_of - 1)
    while spare > 0:
        movable = [i for i in range(1, number_of) if counts[i] < largest] or [i for i in range(1, number_of) if counts[i] < limit]
        whole, left = sum([loads[i] for i in movable]), spare
        for i in movable:
            more = min(limit - counts[i], max(1, left * loads[i] // whole), spare)
            counts[i] = counts[i] + more
            spare = spare - more
    return np.array(counts)


def centred(stream_key, shape, deviation, reach, cuts=(), kind=jnp.bfloat16):
    drawn = deviation * jax.random.normal(stream_key, shape, jnp.float32)
    if cuts:
        drawn = drawn * shard_levels(stream_key, shape, cuts, -0.22, 0.18)
    return jnp.clip(drawn, -reach, reach).astype(kind)


def setup_inputs(seed: int = 0) -> dict:
    splits = jax.random.split(jax.random.key(seed), 11)
    fwd_act = centred(splits[0], (N_PP * TOKENS, D), 1.0, 6.0, ((0, 32),))
    fwd_ids_keys = jax.random.split(jax.random.fold_in(splits[1], 1), (N_PP * TOKENS) // TOK_DEV)
    fwd_ids_turns = jax.random.permutation(jax.random.fold_in(splits[1], 3), (N_PP * TOKENS) // TOK_DEV)
    fwd_ids = jax.vmap(lambda own, number: routed_block(jax.random.fold_in(splits[1], 2), own, number, TOK_DEV, EXPERTS, TOPK, CAP, 2))(fwd_ids_keys, fwd_ids_turns).reshape((N_PP * TOKENS, TOPK))
    bwd_act = centred(splits[2], (N_PP * TOKENS, D), 1.0, 6.0, ((0, 32),))
    bwd_ids_keys = jax.random.split(jax.random.fold_in(splits[3], 1), (N_PP * TOKENS) // TOK_DEV)
    bwd_ids_turns = jax.random.permutation(jax.random.fold_in(splits[3], 3), (N_PP * TOKENS) // TOK_DEV)
    bwd_ids = jax.vmap(lambda own, number: routed_block(jax.random.fold_in(splits[3], 2), own, number, TOK_DEV, EXPERTS, TOPK, CAP, 2))(bwd_ids_keys, bwd_ids_turns).reshape((N_PP * TOKENS, TOPK))
    bwd_grad = centred(splits[4], (N_PP * TOKENS, D), 1.0, 6.0, ((0, 32),))
    norm_gain = jnp.clip(1.0 + 0.18 * jax.random.normal(splits[5], (N_PP, D), jnp.float32), 0.099609375, 1.8984375).astype(jnp.bfloat16)
    router = centred(splits[6], (N_PP, D, EXPERTS), D ** -0.5, 0.09375, ((0, 4),))
    w_gate = centred(splits[7], (N_PP * N_EP, D, HSLICE), D ** -0.5, 0.09375, ((0, 32),))
    w_down = centred(splits[8], (N_PP * N_EP, HSLICE, D), HID ** -0.5, 0.1875, ((0, 32),))
    saved_gate = centred(splits[9], (N_PP, N_EP, N_EP * CAP, HSLICE), 1.0, 6.0, ((0, 4), (1, 8)))
    return {"fwd_act": fwd_act, "fwd_ids": fwd_ids, "bwd_act": bwd_act, "bwd_ids": bwd_ids, "bwd_grad": bwd_grad, "norm_gain": norm_gain, "router": router, "w_gate": w_gate, "w_down": w_down, "saved_gate": saved_gate}


epsilon = 1e-06
route_scale = 2.5

def normalize(act, gain_row):
    values = act.astype(jnp.float32)
    scaled = lax.rsqrt(lax.optimization_barrier(jnp.mean(values * values, axis=-1, keepdims=True)) + epsilon)
    return ((values * scaled * gain_row.astype(jnp.float32)).astype(jnp.bfloat16), scaled)

def gating(normed, router_table, ids):
    logits = jnp.dot(normed, router_table, preferred_element_type=jnp.float32)
    affinity = jax.nn.sigmoid(logits)
    selected = (ids[:, :, None] == jnp.arange(router_table.shape[1], dtype=jnp.int32)[None, None, :]).astype(jnp.float32)
    gates = lax.optimization_barrier(jnp.sum(selected * affinity[:, None, :], axis=-1))
    return (gates, affinity, selected)

def positions(flat_ids, experts):
    onehot = (flat_ids[..., None] == jnp.arange(experts, dtype=jnp.int32)).astype(jnp.int32)
    earlier = jnp.cumsum(onehot, axis=-2) - onehot
    return lax.optimization_barrier(jnp.sum(earlier * onehot, axis=-1))

def slot_table(ids):
    flat_ids = ids.reshape(N_EP, TOK_DEV * TOPK)
    place = positions(flat_ids, EXPERTS)
    source = jnp.arange(N_EP, dtype=jnp.int32)[:, None]
    token = source * TOK_DEV + jnp.arange(TOK_DEV * TOPK, dtype=jnp.int32)[None, :] // TOPK
    slot_index = flat_ids * (N_EP * CAP) + source * CAP + place
    owner = jnp.full((EXPERTS * N_EP * CAP,), TOKENS, jnp.int32).at[slot_index.reshape(-1)].set(token.reshape(-1))
    return (owner, slot_index.reshape(TOKENS, TOPK))

def collect(rows, owner):
    padded = jnp.concatenate([rows, jnp.zeros((1, D), rows.dtype)], axis=0)
    return padded[owner].reshape(EXPERTS, N_EP * CAP, D)

def experts_forward(slot_rows, gate_parts, down_parts):
    rows_wide = slot_rows.astype(jnp.float32)

    def add_slice(total, parts):
        gate_proj = jnp.einsum('erd,edh->erh', rows_wide, parts[0].astype(jnp.float32))
        hidden = jax.nn.silu(gate_proj).astype(jnp.bfloat16)
        output = jnp.einsum('erh,ehd->erd', hidden.astype(jnp.float32), parts[1].astype(jnp.float32)).astype(jnp.bfloat16)
        return (total + output.astype(jnp.float32), None)
    total, unused = lax.scan(add_slice, jnp.zeros(slot_rows.shape, jnp.float32), (gate_parts, down_parts))
    return total

def experts_backward(slot_grads, saved_parts, gate_parts, down_parts):
    grads_wide = slot_grads.astype(jnp.float32)

    def add_slice(totals, parts):
        gate_proj = parts[0].astype(jnp.float32)
        down_wide = parts[2].astype(jnp.float32)
        hidden = jax.nn.silu(gate_proj).astype(jnp.bfloat16)
        output = jnp.einsum('erh,ehd->erd', hidden.astype(jnp.float32), down_wide).astype(jnp.bfloat16)
        dot_part = lax.optimization_barrier(jnp.sum(grads_wide * output.astype(jnp.float32), axis=-1)).astype(jnp.bfloat16)
        grad_hidden = jnp.einsum('erd,ehd->erh', grads_wide, down_wide)
        sigmoid_gate = jax.nn.sigmoid(gate_proj)
        grad_gate = (grad_hidden * sigmoid_gate * (1.0 + gate_proj * (1.0 - sigmoid_gate))).astype(jnp.bfloat16)
        grad_part = jnp.einsum('erh,edh->erd', grad_gate.astype(jnp.float32), parts[1].astype(jnp.float32)).astype(jnp.bfloat16)
        return ((totals[0] + grad_part.astype(jnp.float32), totals[1] + dot_part.astype(jnp.float32)), None)
    start = (jnp.zeros(slot_grads.shape, jnp.float32), jnp.zeros(slot_grads.shape[:2], jnp.float32))
    totals, unused = lax.scan(add_slice, start, (saved_parts, gate_parts, down_parts))
    return totals

def finish_forward(act, gates, gathered):
    mixed = lax.optimization_barrier(jnp.sum(gates[:, :, None] * gathered, axis=1))
    return (act.astype(jnp.float32) + route_scale * mixed).astype(jnp.bfloat16)

def finish_backward(act, grad, scaled, gain_row, router_table, gates, affinity, selected, grad_rows, dot_terms):
    route_coef = route_scale * gates
    grad_normed = lax.optimization_barrier(jnp.sum(route_coef[:, :, None] * grad_rows, axis=1))
    grad_gates = route_scale * dot_terms
    grad_affinity = lax.optimization_barrier(jnp.sum(selected * grad_gates[:, :, None], axis=1))
    grad_logits = (grad_affinity * affinity * (1.0 - affinity)).astype(jnp.bfloat16)
    grad_normed = grad_normed + jnp.dot(grad_logits, router_table.T, preferred_element_type=jnp.float32)
    values = act.astype(jnp.float32)
    grad_pre = grad_normed * gain_row.astype(jnp.float32)
    grad_act = scaled * (grad_pre - values * scaled * scaled * lax.optimization_barrier(jnp.mean(grad_pre * values, axis=-1, keepdims=True)))
    return (grad.astype(jnp.float32) + grad_act).astype(jnp.bfloat16)

def section_step(pieces):
    fwd_act, fwd_ids, bwd_act, bwd_ids, bwd_grad, gain_row, router_table, gate_section, down_section, saved_section = pieces
    gate_parts = gate_section.reshape(EXPERTS, HSPLIT, D, HSLICE).transpose(1, 0, 2, 3)
    down_parts = down_section.reshape(EXPERTS, HSPLIT, HSLICE, D).transpose(1, 0, 2, 3)
    saved_parts = saved_section.reshape(EXPERTS, HSPLIT, N_EP * CAP, HSLICE).transpose(1, 0, 2, 3)
    fwd_normed, fwd_scaled = normalize(fwd_act, gain_row)
    fwd_gates, fwd_aff, fwd_sel = gating(fwd_normed, router_table, fwd_ids)
    fwd_owner, fwd_slot = slot_table(fwd_ids)
    fwd_y = experts_forward(collect(fwd_normed, fwd_owner), gate_parts, down_parts)
    fwd_gathered = fwd_y.reshape(-1, D)[fwd_slot]
    fwd_result = finish_forward(fwd_act, fwd_gates, fwd_gathered)
    bwd_normed, bwd_scaled = normalize(bwd_act, gain_row)
    bwd_gates, bwd_aff, bwd_sel = gating(bwd_normed, router_table, bwd_ids)
    bwd_owner, bwd_slot = slot_table(bwd_ids)
    grad_rows, dot_terms = experts_backward(collect(bwd_grad, bwd_owner), saved_parts, gate_parts, down_parts)
    bwd_rows = grad_rows.reshape(-1, D)[bwd_slot]
    bwd_dots = dot_terms.reshape(-1)[bwd_slot]
    bwd_result = finish_backward(bwd_act, bwd_grad, bwd_scaled, gain_row, router_table, bwd_gates, bwd_aff, bwd_sel, bwd_rows, bwd_dots)
    return (fwd_result, bwd_result)

def reference(fwd_act, fwd_ids, bwd_act, bwd_ids, bwd_grad, norm_gain, router, w_gate, w_down, saved_gate):

    def split(arr):
        return arr.reshape((N_PP, arr.shape[0] // N_PP) + arr.shape[1:])
    pieces = (split(fwd_act), split(fwd_ids), split(bwd_act), split(bwd_ids), split(bwd_grad), norm_gain, router, split(w_gate), split(w_down), saved_gate)
    fwd_result, bwd_result = lax.map(section_step, pieces)
    fwd_next = jnp.roll(fwd_result, 1, axis=0).reshape(N_PP * TOKENS, D)
    bwd_next = jnp.roll(bwd_result, -1, axis=0).reshape(N_PP * TOKENS, D)
    return (fwd_next, bwd_next)
```

```python
import jax
import jax.numpy as jnp
from jax import lax
from jax.experimental import pallas as pl
from jax.experimental.pallas import tpu as pltpu
from jax.sharding import PartitionSpec as P

epsilon = 1e-06
route_scale = 2.5
fold = 256
none = 255.0
f32 = jnp.float32
bf16 = jnp.bfloat16


def call(body, outs, scratch, flops, nbytes, name):
    return pl.pallas_call(
        body,
        out_shape=outs,
        scratch_shapes=scratch,
        compiler_params=pltpu.CompilerParams(vmem_limit_bytes=48 * 1024 * 1024),
        cost_estimate=pl.CostEstimate(flops=flops, bytes_accessed=nbytes, transcendentals=0),
        name=name,
    )


def shape(dims, kind=bf16):
    return jax.ShapeDtypeStruct(dims, kind)


class Sizes:
    def __init__(self, groups, experts, tokens, width):
        self.experts = experts
        self.split = groups // experts
        self.tokens = tokens
        self.width = width
        self.main = tokens // experts
        self.cap = self.main + 1
        self.pieces = width // fold
        self.wide = width + fold
        self.rows = tokens + 16
        self.extra = max(16, 8 * self.split)
        assert self.main == 16 and self.pieces <= 14 and width % fold == 0
        assert experts <= 8 and experts & (experts - 1) == 0 and self.split & (self.split - 1) == 0


def pack_last(row, tile):
    for i in range(row.shape[1] // fold):
        tile[i : i + 1, :] = row[:, i * fold : (i + 1) * fold]


def unpack_last(chunk, z, tile, target, at):
    tile[...] = chunk[:, z.width :].astype(f32)
    for i in range(z.pieces):
        target[at : at + 1, i * fold : (i + 1) * fold] = tile[i : i + 1, :]


def slot_matrices(ids, block, z):
    tokens = z.tokens
    sub = lax.broadcasted_iota(jnp.int32, (tokens, tokens), 0)
    lane = lax.broadcasted_iota(jnp.int32, (tokens, tokens), 1)
    column = jnp.bitwise_xor(ids, block)
    row = jnp.sum(jnp.where(sub == lane, column, 0), axis=0, keepdims=True)
    same = column == row
    place_row = jnp.sum(jnp.where(same & (sub < lane), 1, 0), axis=0, keepdims=True)
    place_column = jnp.sum(jnp.where(same & (lane < sub), 1, 0), axis=1, keepdims=True)

    def slot(expert, place):
        return jnp.where(place < z.main, expert * z.main + place, tokens + expert)

    slot_row = slot(row, place_row)
    slot_column = slot(column, place_column)
    by_slot = lax.broadcasted_iota(jnp.int32, (z.rows, tokens), 0) == slot_row
    by_token = lax.broadcasted_iota(jnp.int32, (tokens, fold), 1) == slot_column
    token = lax.broadcasted_iota(jnp.int32, (tokens, fold), 0).astype(f32)
    token_row = jnp.sum(jnp.where(by_token, token - none, 0.0), axis=0, keepdims=True) + none
    return jnp.where(by_slot, 1.0, 0.0).astype(bf16), token_row


def write_chunks(z, selector, token_row, rows_ref, tile, chunks):
    last = jnp.dot(
        selector[z.tokens :, :], rows_ref[...], preferred_element_type=f32
    )
    step = z.width // 4
    for col in range(0, z.width, step):
        got = jnp.dot(
            selector[: z.tokens, :], rows_ref[:, col : col + step], preferred_element_type=f32
        ).astype(bf16)
        for k in range(z.experts):
            chunks[k][:, col : col + step] = got[k * z.main : (k + 1) * z.main]
    for k in range(z.experts):
        tile[...] = jnp.zeros_like(tile)
        pack_last(last[k : k + 1, :], tile)
        tile[z.pieces : z.pieces + 1, :] = token_row
        chunks[k][:, z.width :] = tile[...].astype(bf16)


def chunk_body(z, count, block, ids, *refs):
    sources, outs, tile = refs[:count], refs[count:-1], refs[-1]
    selector, token_row = slot_matrices(ids[...], block[0], z)
    for j in range(count):
        write_chunks(
            z, selector, token_row, sources[j], tile, outs[j * z.experts : (j + 1) * z.experts]
        )


def make_chunks(z, block, ids, sources, name):
    count = len(sources)

    def body(*refs):
        chunk_body(z, count, *refs)

    outs = call_with_scalar(
        body,
        [shape((z.main, z.wide))] * (z.experts * count),
        [pltpu.VMEM((16, fold), f32)],
        1 + count,
        2 * count * z.rows * z.tokens * z.width,
        4 * count * z.tokens * z.width,
        name,
    )(block, ids, *sources)
    return [outs[j * z.experts : (j + 1) * z.experts] for j in range(count)]


def call_with_scalar(body, outs, scratch, arrays, flops, nbytes, name):
    return pl.pallas_call(
        body,
        out_shape=outs,
        in_specs=[pl.BlockSpec(memory_space=pltpu.SMEM)]
        + [pl.BlockSpec(memory_space=pltpu.VMEM)] * arrays,
        scratch_shapes=scratch,
        compiler_params=pltpu.CompilerParams(vmem_limit_bytes=48 * 1024 * 1024),
        cost_estimate=pl.CostEstimate(flops=flops, bytes_accessed=nbytes, transcendentals=0),
        name=name,
    )


def collect_rows(z, chunks, held, last, tile):
    last[...] = jnp.zeros_like(last)
    for m in range(z.split):
        for k in range(z.experts):
            chunk = chunks[m * z.experts + k]
            at = m * z.tokens + k * z.main
            held[at : at + z.main, :] = chunk[:, : z.width]
            unpack_last(chunk, z, tile, last, m * 8 + k)
    held[z.split * z.tokens :, :] = last[...].astype(bf16)


def write_parts(z, values, outs, col):
    step = values.shape[1]
    for m in range(z.split):
        outs[m][: z.tokens, col : col + step] = values[
            m * z.tokens : (m + 1) * z.tokens
        ].astype(bf16)
        at = z.split * z.tokens + m * 8
        tail = values[at : at + 8]
        outs[m][z.tokens :, col : col + step] = jnp.concatenate(
            [tail, jnp.zeros((8, step), f32)], axis=0
        ).astype(bf16)


def norm_rows(h, gain):
    inv = lax.rsqrt(jnp.mean(h * h, axis=-1, keepdims=True) + epsilon)
    return (h * inv * gain).astype(bf16), inv


def forward_body(z, *refs):
    count = z.split * z.experts
    chunks = refs[:count]
    gain_ref, router_ref, gate_ref, down_ref = refs[count : count + 4]
    outs = refs[count + 4 : count + 4 + z.split]
    gates, held, last, tile = refs[count + 4 + z.split :]
    collect_rows(z, chunks, held, last, tile)
    gain = gain_ref[...].astype(f32)
    router = router_ref[...].astype(f32)
    total = held.shape[0]
    for at in range(0, total, 16):
        normed, _ = norm_rows(held[at : at + 16, :].astype(f32), gain)
        held[at : at + 16, :] = normed
        own = at if at < z.tokens else (z.tokens if at == z.split * z.tokens else None)
        if own is not None:
            logits = jnp.sum(normed.astype(f32) * router, axis=-1, keepdims=True)
            gates[own : own + 16, :] = jnp.broadcast_to(jax.nn.sigmoid(logits), (16, 128))
    gate_proj = jnp.dot(held[...], gate_ref[0], preferred_element_type=f32)
    hidden = jax.nn.silu(gate_proj).astype(bf16)
    step = 512
    for col in range(0, z.width, step):
        part = jnp.dot(hidden, down_ref[0, :, col : col + step], preferred_element_type=f32)
        write_parts(z, part, outs, col)


def experts_forward(z, chunks, gain, router_row, w_gate, w_down):
    total = z.split * z.tokens + z.extra

    def body(*refs):
        forward_body(z, *refs)

    outs = call(
        body,
        [shape((z.rows, z.width))] * z.split + [shape((z.rows, 128), f32)],
        [
            pltpu.VMEM((total, z.width), bf16),
            pltpu.VMEM((z.extra, z.width), f32),
            pltpu.VMEM((16, fold), f32),
        ],
        4 * total * w_gate.shape[1] * w_gate.shape[2],
        4 * w_gate.shape[1] * w_gate.shape[2],
        "experts_forward",
    )(*chunks, gain, router_row, w_gate, w_down)
    return outs[: z.split], outs[z.split]


def saved_selector(z, block, core, total, slots):
    row = lax.broadcasted_iota(jnp.int32, (total, slots), 0)
    slot = lax.broadcasted_iota(jnp.int32, (total, slots), 1)
    tail = row - z.split * z.tokens
    is_main = tail < 0
    m = jnp.where(is_main, row // z.tokens, tail // 8)
    k = jnp.where(is_main, row % z.tokens // z.main, tail % 8)
    p = jnp.where(is_main, row % z.main, z.main)
    source = jnp.bitwise_xor(k, block) * z.split + jnp.bitwise_xor(m, core)
    wanted = jnp.where((k < z.experts) & (m < z.split), source * z.cap + p, -1)
    return jnp.where(slot == wanted, 1.0, 0.0).astype(bf16)


nt = (((1,), (1,)), ((), ()))


def backward_body(z, where, *refs):
    count = z.split * z.experts
    chunks = refs[:count]
    saved_ref, gate_ref, down_ref = refs[count : count + 3]
    outs = refs[count + 3 : count + 3 + z.split]
    held, last, tile = refs[count + 3 + z.split :]
    total = held.shape[0]
    selector = saved_selector(z, where[0], where[1], total, saved_ref.shape[2])
    gate_proj = jnp.dot(selector, saved_ref[0, 0], preferred_element_type=f32)
    sg = jax.nn.sigmoid(gate_proj)
    hidden = (gate_proj * sg).astype(bf16).astype(f32)
    slope = sg * (1.0 + gate_proj * (1.0 - sg))
    collect_rows(z, chunks, held, last, tile)
    grad_hidden = lax.dot_general(held[...], down_ref[0], nt, preferred_element_type=f32)
    dots = jnp.sum(grad_hidden * hidden, axis=-1, keepdims=True)
    grad_gate = (grad_hidden * slope).astype(bf16)
    step = 512
    for col in range(0, z.width, step):
        part = lax.dot_general(
            grad_gate, gate_ref[0, col : col + step, :], nt, preferred_element_type=f32
        )
        write_parts(z, part, outs, col)
    write_parts(z, jnp.broadcast_to(dots, (total, 128)), outs, z.width)


def experts_backward(z, where, chunks, saved, w_gate, w_down):
    total = z.split * z.tokens + z.extra

    def body(*refs):
        backward_body(z, *refs)

    return call_with_scalar(
        body,
        [shape((z.rows, z.width + 128))] * z.split,
        [
            pltpu.VMEM((total, z.width), bf16),
            pltpu.VMEM((z.extra, z.width), f32),
            pltpu.VMEM((16, fold), f32),
        ],
        z.split * z.experts + 3,
        4 * total * w_gate.shape[1] * w_gate.shape[2],
        4 * w_gate.shape[1] * w_gate.shape[2],
        "experts_backward",
    )(where, *chunks, saved, w_gate, w_down)


def put_last(z, values, k, source_chunk, tile, out):
    tile[...] = jnp.zeros_like(tile)
    pack_last(values, tile)
    tokens = source_chunk[:, z.width :].astype(f32)
    tile[z.pieces : z.pieces + 1, :] = tokens[z.pieces : z.pieces + 1, :]
    out[:, z.width :] = tile[...].astype(bf16)


def finish_forward_body(z, *refs):
    e = z.experts
    chunks, parts = refs[:e], refs[e : e + z.split]
    gates = refs[e + z.split]
    outs = refs[e + z.split + 1 : 2 * e + z.split + 1]
    last, tile = refs[2 * e + z.split + 1 :]

    def mixed(at):
        y = parts[0][at : at + 16, :].astype(f32)
        for part in parts[1:]:
            y = y + part[at : at + 16, :].astype(f32)
        return route_scale * (gates[at : at + 16, 0:1] * y)

    last[...] = jnp.zeros_like(last)
    for k in range(e):
        h = chunks[k][:, : z.width].astype(f32)
        outs[k][:, : z.width] = (h + mixed(k * z.main)).astype(bf16)
        unpack_last(chunks[k], z, tile, last, k)
    last[...] = last[...] + mixed(z.tokens)
    for k in range(e):
        put_last(z, last[k : k + 1, :], k, chunks[k], tile, outs[k])


def finish_forward(z, chunks, parts, gates):
    def body(*refs):
        finish_forward_body(z, *refs)

    return call(
        body,
        [shape((z.main, z.wide))] * z.experts,
        [pltpu.VMEM((16, z.width), f32), pltpu.VMEM((16, fold), f32)],
        8 * z.rows * z.width,
        8 * z.rows * z.width,
        "finish_forward",
    )(*chunks, *parts, gates)


def finish_backward_body(z, *refs):
    e = z.experts
    acts, grads, parts = refs[:e], refs[e : 2 * e], refs[2 * e : 2 * e + z.split]
    gain_ref, router_ref = refs[2 * e + z.split : 2 * e + z.split + 2]
    outs = refs[2 * e + z.split + 2 : 3 * e + z.split + 2]
    last_act, last_grad, tile = refs[3 * e + z.split + 2 :]
    gain = gain_ref[...].astype(f32)
    router = router_ref[...].astype(f32)

    def finished(h, g, at):
        normed, inv = norm_rows(h, gain)
        logits = jnp.sum(normed.astype(f32) * router, axis=-1, keepdims=True)
        affinity = jax.nn.sigmoid(logits)
        rows = parts[0][at : at + 16, : z.width].astype(f32)
        dot = parts[0][at : at + 16, z.width :].astype(f32)
        for part in parts[1:]:
            rows = rows + part[at : at + 16, : z.width].astype(f32)
            dot = dot + part[at : at + 16, z.width :].astype(f32)
        dot = dot[:, 0:1]
        grad_logits = (route_scale * dot * affinity * (1.0 - affinity)).astype(bf16).astype(f32)
        grad_pre = (route_scale * affinity * rows + grad_logits * router) * gain
        centre = jnp.mean(grad_pre * h, axis=-1, keepdims=True)
        return g + inv * (grad_pre - h * (inv * inv * centre))

    last_act[...] = jnp.zeros_like(last_act)
    last_grad[...] = jnp.zeros_like(last_grad)
    for k in range(e):
        h = acts[k][:, : z.width].astype(f32)
        g = grads[k][:, : z.width].astype(f32)
        outs[k][:, : z.width] = finished(h, g, k * z.main).astype(bf16)
        unpack_last(acts[k], z, tile, last_act, k)
        unpack_last(grads[k], z, tile, last_grad, k)
    last_act[...] = finished(last_act[...], last_grad[...], z.tokens)
    for k in range(e):
        put_last(z, last_act[k : k + 1, :], k, grads[k], tile, outs[k])


def finish_backward(z, acts, grads, parts, gain, router_row):
    def body(*refs):
        finish_backward_body(z, *refs)

    return call(
        body,
        [shape((z.main, z.wide))] * z.experts,
        [
            pltpu.VMEM((16, z.width), f32),
            pltpu.VMEM((16, z.width), f32),
            pltpu.VMEM((16, fold), f32),
        ],
        30 * z.rows * z.width,
        10 * z.rows * z.width,
        "finish_backward",
    )(*acts, *grads, *parts, gain, router_row)


def order_body(z, *refs):
    chunks, out, held, last, tile = refs[: z.experts], *refs[z.experts :]
    last[...] = jnp.zeros_like(last)
    for k in range(z.experts):
        held[k * z.main : (k + 1) * z.main, :] = chunks[k][:, : z.width]
        unpack_last(chunks[k], z, tile, last, k)
    held[z.tokens :, :] = last[...].astype(bf16)
    token_row = chunks[0][:, z.width :].astype(f32)[z.pieces : z.pieces + 1, : z.rows]
    token = lax.broadcasted_iota(jnp.int32, (z.tokens, z.rows), 0).astype(f32)
    selector = jnp.where(token == token_row, 1.0, 0.0).astype(bf16)
    out[...] = jnp.dot(selector, held[...], preferred_element_type=f32).astype(bf16)


def order_rows(z, chunks, name):
    def body(*refs):
        order_body(z, *refs)

    return call(
        body,
        shape((z.tokens, z.width)),
        [
            pltpu.VMEM((z.rows, z.width), bf16),
            pltpu.VMEM((16, z.width), f32),
            pltpu.VMEM((16, fold), f32),
        ],
        2 * z.rows * z.tokens * z.width,
        4 * z.tokens * z.width,
        name,
    )(*chunks)


def dispatch(z, chunks):
    groups = z.experts * z.split
    got = [chunks[0]] + [None] * (z.experts - 1)
    for k in reversed(range(1, z.experts)):
        pairs = [(i, ((i // z.split) ^ k) * z.split + i % z.split) for i in range(groups)]
        got[k] = lax.ppermute(chunks[k], "ep", pairs)
    return got


def to_core(z, array, m):
    groups = z.experts * z.split
    pairs = [(i, i // z.split * z.split + ((i % z.split) ^ m)) for i in range(groups)]
    return lax.ppermute(array, "ep", pairs)


def to_section(z, chunks, by):
    groups = z.experts * z.split
    sections = lax.axis_size("pp")
    got = [None] * z.experts
    for k in reversed(range(z.experts)):
        pairs = [
            (s * groups + i, (s + by) % sections * groups + ((i // z.split) ^ k) * z.split + i % z.split)
            for s in range(sections)
            for i in range(groups)
        ]
        got[k] = lax.ppermute(chunks[k], ("pp", "ep"), pairs)
    return got


def on_device(
    fwd_act, fwd_ids, bwd_act, bwd_ids, bwd_grad, norm_gain, router, w_gate, w_down, saved_gate
):
    groups = lax.axis_size("ep")
    assert fwd_ids.shape[1] == 1
    z = Sizes(groups, router.shape[2], fwd_act.shape[0], fwd_act.shape[1])
    index = lax.axis_index("ep")
    block, core = index // z.split, index % z.split
    where = jnp.stack([block, core]).astype(jnp.int32)
    mine = jnp.arange(z.experts, dtype=jnp.int32) == block
    router_row = jnp.sum(jnp.where(mine, router[0].astype(f32), 0.0), axis=1)[None, :]

    (fwd_chunks,) = make_chunks(z, where, fwd_ids, [fwd_act], "forward_chunks")
    fwd_own = dispatch(z, fwd_chunks)
    grad_chunks, act_chunks = make_chunks(z, where, bwd_ids, [bwd_grad, bwd_act], "backward_chunks")
    grad_own = dispatch(z, grad_chunks)
    act_own = dispatch(z, act_chunks)

    fwd_all = list(fwd_own)
    for m in range(1, z.split):
        fwd_all += [to_core(z, chunk, m) for chunk in fwd_own]
    fwd_parts, fwd_gates = experts_forward(z, fwd_all, norm_gain, router_row, w_gate, w_down)
    fwd_parts = [fwd_parts[0]] + [to_core(z, fwd_parts[m], m) for m in range(1, z.split)]
    fwd_done = to_section(z, finish_forward(z, fwd_own, fwd_parts, fwd_gates), 1)

    grad_all = list(grad_own)
    for m in range(1, z.split):
        grad_all += [to_core(z, chunk, m) for chunk in grad_own]
    bwd_parts = experts_backward(z, where, grad_all, saved_gate, w_gate, w_down)
    bwd_parts = [bwd_parts[0]] + [to_core(z, bwd_parts[m], m) for m in range(1, z.split)]
    bwd_done = to_section(
        z, finish_backward(z, act_own, grad_own, bwd_parts, norm_gain, router_row), -1
    )
    return (order_rows(z, fwd_done, "forward_rows"), order_rows(z, bwd_done, "backward_rows"))


def solution(mesh):
    return jax.shard_map(
        on_device,
        mesh=mesh,
        in_specs=(
            P(("pp", "ep"), None),
            P(("pp", "ep"), None),
            P(("pp", "ep"), None),
            P(("pp", "ep"), None),
            P(("pp", "ep"), None),
            P("pp", None),
            P("pp", None, None),
            P(("pp", "ep"), None, None),
            P(("pp", "ep"), None, None),
            P("pp", "ep", None, None),
        ),
        out_specs=(P(("pp", "ep"), None), P(("pp", "ep"), None)),
        check_vma=False,
    )
```

```python
import jax
import jax.numpy as jnp
from jax import lax
from jax.experimental import pallas as pl
from jax.experimental.pallas import tpu as pltpu
from jax.sharding import PartitionSpec as P

epsilon = 1e-06
route_scale = 2.5
fold = 256
none = 255.0
f32 = jnp.float32
bf16 = jnp.bfloat16
nt = (((1,), (1,)), ((), ()))
spaces = {
    "s": pl.BlockSpec(memory_space=pltpu.SMEM),
    "v": pl.BlockSpec(memory_space=pltpu.VMEM),
    "a": pl.BlockSpec(memory_space=pl.ANY),
    "h": pl.BlockSpec(memory_space=pltpu.HBM),
}


def call(body, places, outs, scratch, megabytes, name):
    def run(*arrays):
        arrays = [
            pltpu.with_memory_space_constraint(array, pltpu.HBM) if place == "h" else array
            for array, place in zip(arrays, places, strict=True)
        ]
        return kernel(*arrays)

    kernel = pl.pallas_call(
        body,
        out_shape=outs,
        in_specs=[spaces[place] for place in places],
        scratch_shapes=scratch,
        compiler_params=pltpu.CompilerParams(vmem_limit_bytes=megabytes * 1024 * 1024),
        cost_estimate=pl.CostEstimate(flops=1000, bytes_accessed=1000, transcendentals=0),
        name=name,
    )
    return run


def shape(dims, kind=bf16):
    return jax.ShapeDtypeStruct(dims, kind)


class Sizes:
    def __init__(self, groups, experts, tokens, width):
        self.experts = experts
        self.split = groups // experts
        self.tokens = tokens
        self.width = width
        self.main = tokens // experts
        self.cap = self.main + 1
        self.pieces = width // fold
        self.wide = width + fold
        self.rows = tokens + 16
        assert self.main == 16 and self.pieces <= 14 and width % fold == 0
        assert experts <= 8 and experts & (experts - 1) == 0 and self.split & (self.split - 1) == 0


def pack_last(row, tile, first=0):
    for i in range(row.shape[1] // fold):
        tile[first + i : first + i + 1, :] = row[:, i * fold : (i + 1) * fold]


def unpack_last(chunk, z, tile, target, at):
    tile[...] = chunk[:, z.width :].astype(f32)
    for i in range(z.pieces):
        target[at : at + 1, i * fold : (i + 1) * fold] = tile[i : i + 1, :]


def slot_matrices(ids_row, block, z):
    tokens = z.tokens
    sub = lax.broadcasted_iota(jnp.int32, (tokens, tokens), 0)
    lane = lax.broadcasted_iota(jnp.int32, (tokens, tokens), 1)
    row = jnp.bitwise_xor(ids_row, block)
    column = jnp.sum(jnp.where(sub == lane, row, 0), axis=1, keepdims=True)
    same = column == row
    place_row = jnp.sum(jnp.where(same & (sub < lane), 1, 0), axis=0, keepdims=True)
    place_column = jnp.sum(jnp.where(same & (lane < sub), 1, 0), axis=1, keepdims=True)

    def slot(expert, place):
        return jnp.where(place < z.main, expert * z.main + place, tokens + expert)

    slot_row = slot(row, place_row)
    slot_column = slot(column, place_column)
    by_slot = lax.broadcasted_iota(jnp.int32, (z.rows, tokens), 0) == slot_row
    by_token = lax.broadcasted_iota(jnp.int32, (tokens, fold), 1) == slot_column
    token = lax.broadcasted_iota(jnp.int32, (tokens, fold), 0).astype(f32)
    token_row = jnp.sum(jnp.where(by_token, token - none, 0.0), axis=0, keepdims=True) + none
    return jnp.where(by_slot, 1.0, 0.0).astype(bf16), token_row


def write_chunks(z, selector, token_row, rows_ref, tiles, chunks):
    step = z.width // 2
    tiles[...] = jnp.zeros_like(tiles)
    for half in range(2):
        col = half * step
        got = jnp.dot(selector, rows_ref[:, col : col + step], preferred_element_type=f32)
        packed = got[: z.tokens].astype(bf16)
        for k in range(z.experts):
            chunks[k][:, col : col + step] = packed[k * z.main : (k + 1) * z.main]
            pack_last(got[z.tokens + k : z.tokens + k + 1], tiles.at[k], half * z.pieces // 2)
    for k in range(z.experts):
        tiles[k, z.pieces : z.pieces + 1, :] = token_row
        chunks[k][:, z.width :] = tiles[k].astype(bf16)


def make_chunks(z, where, ids, sources, after, name):
    count = len(sources)

    def body(where, ids_any, *refs):
        anys, outs = refs[:count], refs[count + len(after) : -4]
        ids, rows, tiles, sems = refs[-4:]
        copies = [pltpu.make_async_copy(ids_any, ids, sems.at[count])]
        copies += [pltpu.make_async_copy(anys[j], rows.at[j], sems.at[j]) for j in range(count)]
        for copy in copies:
            copy.start()
        copies[0].wait()
        selector, token_row = slot_matrices(ids[...], where[0], z)
        for j in range(count):
            copies[1 + j].wait()
            write_chunks(
                z, selector, token_row, rows.at[j], tiles, outs[j * z.experts : (j + 1) * z.experts]
            )

    outs = call(
        body,
        "sh" + "h" * count + "a" * len(after),
        [shape((z.main, z.wide))] * (z.experts * count),
        [
            pltpu.VMEM((1, z.tokens), jnp.int32),
            pltpu.VMEM((count, z.tokens, z.width), bf16),
            pltpu.VMEM((z.experts, 16, fold), f32),
            pltpu.SemaphoreType.DMA((count + 1,)),
        ],
        8,
        name,
    )(where, ids.reshape(1, z.tokens), *sources, *after)
    return [outs[j * z.experts : (j + 1) * z.experts] for j in range(count)]


def collect_rows(z, chunks, last, tile):
    last[...] = jnp.zeros_like(last)
    for k in range(z.experts):
        unpack_last(chunks[k], z, tile, last, k)


def norm_rows(h, gain):
    inv = lax.rsqrt(jnp.mean(h * h, axis=-1, keepdims=True) + epsilon)
    return (h * inv * gain).astype(bf16), inv


def normed_rows(z, chunks, vectors, after):
    def body(*refs):
        chunks, vectors = refs[: z.experts], refs[z.experts]
        normed_ref, gates_ref, last, tile = refs[z.experts + 1 + len(after) :]
        gain, router = vectors[0:1, :], vectors[1:2, :]
        collect_rows(z, chunks, last, tile)
        for k in range(z.experts + 1):
            h = last[...] if k == z.experts else chunks[k][:, : z.width].astype(f32)
            at = k * z.main
            normed, _ = norm_rows(h, gain)
            normed_ref[at : at + 16, :] = normed
            logits = jnp.sum(normed.astype(f32) * router, axis=-1, keepdims=True)
            gates_ref[at : at + 16, :] = jnp.broadcast_to(jax.nn.sigmoid(logits), (16, 128))

    return call(
        body,
        "v" * (z.experts + 1) + "a" * len(after),
        [shape((z.rows, z.width)), shape((z.rows, 128), f32)],
        [pltpu.VMEM((16, z.width), f32), pltpu.VMEM((16, fold), f32)],
        8,
        "normed_rows",
    )(*chunks, vectors, *after)


def grad_rows_of(z, chunks):
    def body(*refs):
        chunks, (rows, last, tile) = refs[: z.experts], refs[z.experts :]
        for k in range(z.experts):
            rows[k * z.main : (k + 1) * z.main, :] = chunks[k][:, : z.width]
        collect_rows(z, chunks, last, tile)
        rows[z.tokens :, :] = last[...].astype(bf16)

    return call(
        body,
        "v" * z.experts,
        shape((z.rows, z.width)),
        [pltpu.VMEM((16, z.width), f32), pltpu.VMEM((16, fold), f32)],
        8,
        "grad_rows",
    )(*chunks)


def write_parts(z, values, outs, col):
    values = values.astype(bf16)
    for m in range(z.split):
        outs[m][:, col : col + values.shape[1]] = values[m * z.rows : (m + 1) * z.rows]


def experts_forward(z, rows, w_gate, w_down):
    def body(*refs):
        rows, (gate_ref, down_ref), outs = (
            refs[: z.split],
            refs[z.split : z.split + 2],
            refs[z.split + 2 :],
        )
        held = jnp.concatenate([part[...] for part in rows], axis=0)
        gate_proj = jnp.dot(held, gate_ref[...], preferred_element_type=f32)
        hidden = jax.nn.silu(gate_proj).astype(bf16)
        step = 512
        for col in range(0, z.width, step):
            part = jnp.dot(hidden, down_ref[:, col : col + step], preferred_element_type=f32)
            write_parts(z, part, outs, col)

    return call(
        body,
        "v" * (z.split + 2),
        [shape((z.rows, z.width))] * z.split,
        [],
        16,
        "experts_forward",
    )(*rows, w_gate, w_down)


def load_section(z, where, gain, router, w_gate, w_down, saved, after):
    total, slots, width = z.split * z.rows, saved.shape[2], saved.shape[3]

    def body(where, gain_any, router_any, gate_any, down_any, saved_any, *refs):
        refs = refs[len(after) :]
        gate_ref, down_ref, vectors, hidden_ref, slope_ref = refs[:5]
        gain_ref, router_ref, saved_ref, sems = refs[5:]
        pairs = [(saved_any.at[0, 0], saved_ref), (gain_any, gain_ref), (router_any.at[0], router_ref)]
        for source, target in ((gate_any.at[0], gate_ref), (down_any.at[0], down_ref)):
            step = target.shape[0] // 4
            for at in range(0, target.shape[0], step):
                pairs.append((source.at[pl.ds(at, step)], target.at[pl.ds(at, step)]))
        copies = [
            pltpu.make_async_copy(source, target, sems.at[i])
            for i, (source, target) in enumerate(pairs)
        ]
        for copy in copies:
            copy.start()
        row = lax.broadcasted_iota(jnp.int32, (total, slots), 0)
        slot = lax.broadcasted_iota(jnp.int32, (total, slots), 1)
        m, at = row // z.rows, row % z.rows
        is_main = at < z.tokens
        k = jnp.where(is_main, at // z.main, at - z.tokens)
        p = jnp.where(is_main, at % z.main, z.main)
        source = jnp.bitwise_xor(k, where[0]) * z.split + jnp.bitwise_xor(m, where[1])
        wanted = jnp.where(k < z.experts, source * z.cap + p, -1)
        selector = jnp.where(slot == wanted, 1.0, 0.0).astype(bf16)
        copies[0].wait()
        gate_proj = jnp.dot(selector, saved_ref[...], preferred_element_type=f32)
        sg = jax.nn.sigmoid(gate_proj)
        hidden_ref[...] = (gate_proj * sg).astype(bf16)
        slope_ref[...] = sg * (1.0 + gate_proj * (1.0 - sg))
        copies[1].wait()
        copies[2].wait()
        vectors[...] = jnp.zeros_like(vectors)
        vectors[0:1, :] = gain_ref[...].astype(f32)
        table = router_ref[...].astype(f32)
        mine = lax.broadcasted_iota(jnp.int32, (z.experts, 1), 0) == where[0]
        vectors[1:2, :] = jnp.sum(jnp.where(mine, table, 0.0), axis=0, keepdims=True)
        for copy in copies[3:]:
            copy.wait()

    return call(
        body,
        "shhhhh" + "a" * len(after),
        [
            shape(w_gate.shape[1:]),
            shape(w_down.shape[1:]),
            shape((8, z.width), f32),
            shape((total, width)),
            shape((total, width), f32),
        ],
        [
            pltpu.VMEM((1, z.width), bf16),
            pltpu.VMEM((z.experts, z.width), bf16),
            pltpu.VMEM((slots, width), bf16),
            pltpu.SemaphoreType.DMA((11,)),
        ],
        24,
        "load_section",
    )(where, gain, router, w_gate, w_down, saved, *after)


def experts_backward(z, rows, hidden, slope, w_gate, w_down, after):
    def body(*refs):
        rows = refs[: z.split]
        hidden_ref, slope_ref, gate_ref, down_ref = refs[z.split : z.split + 4]
        outs = refs[z.split + 4 + len(after) :]
        held = jnp.concatenate([part[...] for part in rows], axis=0)
        grad_hidden = lax.dot_general(held, down_ref[...], nt, preferred_element_type=f32)
        dots = jnp.sum(grad_hidden * hidden_ref[...].astype(f32), axis=-1, keepdims=True)
        grad_gate = (grad_hidden * slope_ref[...]).astype(bf16)
        step = 512
        for col in range(0, z.width, step):
            part = lax.dot_general(
                grad_gate, gate_ref[col : col + step, :], nt, preferred_element_type=f32
            )
            write_parts(z, part, outs, col)
        write_parts(z, jnp.broadcast_to(dots, (dots.shape[0], 128)), outs, z.width)

    return call(
        body,
        "v" * (z.split + 4) + "a" * len(after),
        [shape((z.rows, z.width + 128))] * z.split,
        [],
        16,
        "experts_backward",
    )(*rows, hidden, slope, w_gate, w_down, *after)


def put_last(z, values, source_chunk, tile, out):
    tile[...] = jnp.zeros_like(tile)
    pack_last(values, tile)
    tokens = source_chunk[:, z.width :].astype(f32)
    tile[z.pieces : z.pieces + 1, :] = tokens[z.pieces : z.pieces + 1, :]
    out[:, z.width :] = tile[...].astype(bf16)


def finish_forward(z, chunks, parts, gates):
    def body(*refs):
        e = z.experts
        chunks, parts = refs[:e], refs[e : e + z.split]
        gates = refs[e + z.split]
        outs = refs[e + z.split + 1 : 2 * e + z.split + 1]
        last, tile = refs[2 * e + z.split + 1 :]

        def mixed(at):
            y = parts[0][at : at + 16, :].astype(f32)
            for part in parts[1:]:
                y = y + part[at : at + 16, :].astype(f32)
            return route_scale * (gates[at : at + 16, 0:1] * y)

        for k in range(e):
            h = chunks[k][:, : z.width].astype(f32)
            outs[k][:, : z.width] = (h + mixed(k * z.main)).astype(bf16)
        collect_rows(z, chunks, last, tile)
        last[...] = last[...] + mixed(z.tokens)
        for k in range(e):
            put_last(z, last[k : k + 1, :], chunks[k], tile, outs[k])

    return call(
        body,
        "v" * (z.experts + z.split + 1),
        [shape((z.main, z.wide))] * z.experts,
        [pltpu.VMEM((16, z.width), f32), pltpu.VMEM((16, fold), f32)],
        8,
        "finish_forward",
    )(*chunks, *parts, gates)


def finish_backward(z, acts, grads, parts, vectors):
    def body(*refs):
        e = z.experts
        acts, grads, parts = refs[:e], refs[e : 2 * e], refs[2 * e : 2 * e + z.split]
        vectors = refs[2 * e + z.split]
        outs = refs[2 * e + z.split + 1 : 3 * e + z.split + 1]
        last_act, last_grad, tile = refs[3 * e + z.split + 1 :]
        gain, router = vectors[0:1, :], vectors[1:2, :]

        def finished(h, g, at):
            normed, inv = norm_rows(h, gain)
            logits = jnp.sum(normed.astype(f32) * router, axis=-1, keepdims=True)
            affinity = jax.nn.sigmoid(logits)
            rows = parts[0][at : at + 16, : z.width].astype(f32)
            dot = parts[0][at : at + 16, z.width :].astype(f32)
            for part in parts[1:]:
                rows = rows + part[at : at + 16, : z.width].astype(f32)
                dot = dot + part[at : at + 16, z.width :].astype(f32)
            dot = dot[:, 0:1]
            grad_logits = (route_scale * dot * affinity * (1.0 - affinity)).astype(bf16).astype(f32)
            grad_pre = (route_scale * affinity * rows + grad_logits * router) * gain
            centre = jnp.mean(grad_pre * h, axis=-1, keepdims=True)
            return g + inv * (grad_pre - h * (inv * inv * centre))

        for k in range(e):
            h = acts[k][:, : z.width].astype(f32)
            g = grads[k][:, : z.width].astype(f32)
            outs[k][:, : z.width] = finished(h, g, k * z.main).astype(bf16)
        collect_rows(z, acts, last_act, tile)
        collect_rows(z, grads, last_grad, tile)
        last_act[...] = finished(last_act[...], last_grad[...], z.tokens)
        for k in range(e):
            put_last(z, last_act[k : k + 1, :], grads[k], tile, outs[k])

    return call(
        body,
        "v" * (2 * z.experts + z.split + 1),
        [shape((z.main, z.wide))] * z.experts,
        [
            pltpu.VMEM((16, z.width), f32),
            pltpu.VMEM((16, z.width), f32),
            pltpu.VMEM((16, fold), f32),
        ],
        8,
        "finish_backward",
    )(*acts, *grads, *parts, vectors)


def order_rows(z, chunks, name):
    def body(*refs):
        chunks, (out, held, last, tile) = refs[: z.experts], refs[z.experts :]
        for k in range(z.experts):
            held[k * z.main : (k + 1) * z.main, :] = chunks[k][:, : z.width]
        collect_rows(z, chunks, last, tile)
        held[z.tokens :, :] = last[...].astype(bf16)
        token_row = chunks[0][:, z.width :].astype(f32)[z.pieces : z.pieces + 1, : z.rows]
        token = lax.broadcasted_iota(jnp.int32, (z.tokens, z.rows), 0).astype(f32)
        selector = jnp.where(token == token_row, 1.0, 0.0).astype(bf16)
        out[...] = jnp.dot(selector, held[...], preferred_element_type=f32).astype(bf16)

    return call(
        body,
        "v" * z.experts,
        shape((z.tokens, z.width)),
        [
            pltpu.VMEM((z.rows, z.width), bf16),
            pltpu.VMEM((16, z.width), f32),
            pltpu.VMEM((16, fold), f32),
        ],
        8,
        name,
    )(*chunks)


def dispatch(z, chunks):
    groups = z.experts * z.split
    got = [chunks[0]] + [None] * (z.experts - 1)
    for k in reversed(range(1, z.experts)):
        pairs = [(i, ((i // z.split) ^ k) * z.split + i % z.split) for i in range(groups)]
        got[k] = lax.ppermute(chunks[k], "ep", pairs)
    return got


def to_core(z, array, m):
    groups = z.experts * z.split
    pairs = [(i, i // z.split * z.split + ((i % z.split) ^ m)) for i in range(groups)]
    return lax.ppermute(array, "ep", pairs)


def to_section(z, chunks, by):
    groups = z.experts * z.split
    sections = lax.axis_size("pp")
    got = [None] * z.experts
    for k in reversed(range(z.experts)):
        pairs = [
            (s * groups + i, (s + by) % sections * groups + ((i // z.split) ^ k) * z.split + i % z.split)
            for s in range(sections)
            for i in range(groups)
        ]
        got[k] = lax.ppermute(chunks[k], ("pp", "ep"), pairs)
    return got


def on_device(
    fwd_act, fwd_ids, bwd_act, bwd_ids, bwd_grad, norm_gain, router, w_gate, w_down, saved_gate
):
    groups = lax.axis_size("ep")
    assert fwd_ids.shape[1] == 1
    z = Sizes(groups, router.shape[2], fwd_act.shape[0], fwd_act.shape[1])
    index = lax.axis_index("ep")
    where = jnp.stack([index // z.split, index % z.split]).astype(jnp.int32)
    router = jnp.swapaxes(router, 1, 2)
    others = range(1, z.split)

    (fwd_chunks,) = make_chunks(z, where, fwd_ids, [fwd_act], [], "forward_chunks")
    fwd_own = dispatch(z, fwd_chunks)
    grad_chunks, act_chunks = make_chunks(
        z, where, bwd_ids, [bwd_grad, bwd_act], [fwd_chunks[0]], "backward_chunks"
    )
    grad_own = dispatch(z, grad_chunks)
    gate, down, vectors, hidden, slope = load_section(
        z, where, norm_gain, router, w_gate, w_down, saved_gate, [grad_chunks[0]]
    )

    normed, gates = normed_rows(z, fwd_own, vectors, [gate])
    fwd_all = [normed] + [to_core(z, normed, m) for m in others]
    fwd_parts = experts_forward(z, fwd_all, gate, down)
    fwd_parts = [fwd_parts[0]] + [to_core(z, fwd_parts[m], m) for m in others]
    fwd_out = finish_forward(z, fwd_own, fwd_parts, gates)
    fwd_done = to_section(z, fwd_out, 1)

    act_own = dispatch(z, act_chunks)
    grads = grad_rows_of(z, grad_own)
    grad_all = [grads] + [to_core(z, grads, m) for m in others]
    bwd_parts = experts_backward(
        z, grad_all, hidden, slope, gate, down, [*act_own[1:], fwd_out[0]]
    )
    bwd_parts = [bwd_parts[0]] + [to_core(z, bwd_parts[m], m) for m in others]
    bwd_done = to_section(z, finish_backward(z, act_own, grad_own, bwd_parts, vectors), -1)
    return (order_rows(z, fwd_done, "forward_rows"), order_rows(z, bwd_done, "backward_rows"))


def solution(mesh):
    return jax.shard_map(
        on_device,
        mesh=mesh,
        in_specs=(
            P(("pp", "ep"), None),
            P(("pp", "ep"), None),
            P(("pp", "ep"), None),
            P(("pp", "ep"), None),
            P(("pp", "ep"), None),
            P("pp", None),
            P("pp", None, None),
            P(("pp", "ep"), None, None),
            P(("pp", "ep"), None, None),
            P("pp", "ep", None, None),
        ),
        out_specs=(P(("pp", "ep"), None), P(("pp", "ep"), None)),
        check_vma=False,
    )
```

```python
import jax
import jax.numpy as jnp
from jax import lax
from jax.experimental import pallas as pl
from jax.experimental.pallas import tpu as pltpu
from jax.sharding import PartitionSpec as P

epsilon = 1e-06
route_scale = 2.5
fold = 256
none = 255.0
f32 = jnp.float32
bf16 = jnp.bfloat16
nt = (((1,), (1,)), ((), ()))
spaces = {
    "s": pl.BlockSpec(memory_space=pltpu.SMEM),
    "v": pl.BlockSpec(memory_space=pltpu.VMEM),
    "a": pl.BlockSpec(memory_space=pl.ANY),
    "h": pl.BlockSpec(memory_space=pltpu.HBM),
}


cost = {
    "backward_chunks": 10,
    "saved_rows": 40,
    "saved_terms": 40,
    "act_norms": 40,
    "act_gates": 40,
}


def call(body, places, outs, scratch, megabytes, name):
    def run(*arrays):
        arrays = [
            pltpu.with_memory_space_constraint(array, pltpu.HBM) if place == "h" else array
            for array, place in zip(arrays, places, strict=True)
        ]
        return kernel(*arrays)

    kernel = pl.pallas_call(
        body,
        out_shape=outs,
        in_specs=[spaces[place] for place in places],
        scratch_shapes=scratch,
        compiler_params=pltpu.CompilerParams(vmem_limit_bytes=megabytes * 1024 * 1024),
        cost_estimate=pl.CostEstimate(
            flops=int(cost.get(name, 0.1) * 1e9), bytes_accessed=1000, transcendentals=0
        ),
        name=name,
    )
    return run


def shape(dims, kind=bf16):
    return jax.ShapeDtypeStruct(dims, kind)


class Sizes:
    def __init__(self, groups, experts, tokens, width):
        self.experts = experts
        self.split = groups // experts
        self.tokens = tokens
        self.width = width
        self.main = tokens // experts
        self.cap = self.main + 1
        self.pieces = width // fold
        self.wide = width + fold
        self.rows = tokens + 16
        assert self.main == 16 and self.pieces <= 14 and width % fold == 0
        assert experts <= 8 and experts & (experts - 1) == 0 and self.split & (self.split - 1) == 0


def pack_last(row, tile, first=0):
    for i in range(row.shape[1] // fold):
        tile[first + i : first + i + 1, :] = row[:, i * fold : (i + 1) * fold]


def unpack_last(chunk, z, tile, target, at, base=0):
    tile[...] = chunk[base : base + 16, z.width :].astype(f32)
    for i in range(z.pieces):
        target[at : at + 1, i * fold : (i + 1) * fold] = tile[i : i + 1, :]


def slot_matrices(ids_row, block, z):
    tokens = z.tokens
    sub = lax.broadcasted_iota(jnp.int32, (tokens, tokens), 0)
    lane = lax.broadcasted_iota(jnp.int32, (tokens, tokens), 1)
    row = jnp.bitwise_xor(ids_row, block)
    column = jnp.sum(jnp.where(sub == lane, row, 0), axis=1, keepdims=True)
    same = column == row
    place_row = jnp.sum(jnp.where(same & (sub < lane), 1, 0), axis=0, keepdims=True)
    place_column = jnp.sum(jnp.where(same & (lane < sub), 1, 0), axis=1, keepdims=True)

    def slot(expert, place):
        return jnp.where(place < z.main, expert * z.main + place, tokens + expert)

    slot_row = slot(row, place_row)
    slot_column = slot(column, place_column)
    by_slot = lax.broadcasted_iota(jnp.int32, (z.rows, tokens), 0) == slot_row
    by_token = lax.broadcasted_iota(jnp.int32, (tokens, fold), 1) == slot_column
    token = lax.broadcasted_iota(jnp.int32, (tokens, fold), 0).astype(f32)
    token_row = jnp.sum(jnp.where(by_token, token - none, 0.0), axis=0, keepdims=True) + none
    return jnp.where(by_slot, 1.0, 0.0).astype(bf16), token_row


def write_chunks(z, selector, token_row, rows_ref, ready, tiles, chunks, base):
    step = z.width // 2
    tiles[...] = jnp.zeros_like(tiles)
    for half in range(2):
        ready[half].wait()
        col = half * step
        got = jnp.dot(selector, rows_ref[:, col : col + step], preferred_element_type=f32)
        packed = got[: z.tokens].astype(bf16)
        for k in range(z.experts):
            chunks[k][base : base + 16, col : col + step] = packed[k * z.main : (k + 1) * z.main]
            pack_last(got[z.tokens + k : z.tokens + k + 1], tiles.at[k], half * z.pieces // 2)
    for k in range(z.experts):
        tiles[k, z.pieces : z.pieces + 1, :] = token_row
        chunks[k][base : base + 16, z.width :] = tiles[k].astype(bf16)


def make_chunks(z, where, ids, sources, tables, after, name):
    count = len(sources)

    def body(where, ids_any, *refs):
        anys, tables_any = refs[:count], refs[count : count + len(tables)]
        outs, held = refs[count + len(tables) + len(after) :], ()
        if tables:
            *outs, gain_ref, router_ref, ids, rows, tiles, sems = outs
            *outs, vectors = outs
            held = (gain_ref, router_ref)
        else:
            *outs, ids, rows, tiles, sems = outs
        copies = [pltpu.make_async_copy(ids_any, ids, sems.at[2 * count])]
        step = z.width // 2
        for j in range(count):
            for half in range(2):
                cols = pl.ds(half * step, step)
                copies.append(
                    pltpu.make_async_copy(
                        anys[j].at[:, cols], rows.at[j, :, cols], sems.at[2 * j + half]
                    )
                )
        for i, (source, target) in enumerate(zip(tables_any, held)):
            copies.append(pltpu.make_async_copy(source, target, sems.at[2 * count + 1 + i]))
        for copy in copies:
            copy.start()
        copies[0].wait()
        selector, token_row = slot_matrices(ids[...], where[0], z)
        for j in range(count):
            ready = copies[1 + 2 * j : 3 + 2 * j]
            write_chunks(z, selector, token_row, rows.at[j], ready, tiles, outs, 16 * j)
        if tables:
            for copy in copies[1 + 2 * count :]:
                copy.wait()
            vectors[...] = jnp.zeros_like(vectors)
            vectors[0:1, :] = gain_ref[...].astype(f32)
            mine = lax.broadcasted_iota(jnp.int32, (z.experts, 1), 0) == where[0]
            table = jnp.where(mine, router_ref[0].astype(f32), 0.0)
            vectors[1:2, :] = jnp.sum(table, axis=0, keepdims=True)

    return call(
        body,
        "sh" + "h" * (count + len(tables)) + "a" * len(after),
        [shape((z.main * count, z.wide))] * z.experts
        + [shape((8, z.width), f32) for _ in tables[:1]],
        [pltpu.VMEM(table.shape, bf16) for table in tables]
        + [
            pltpu.VMEM((1, z.tokens), jnp.int32),
            pltpu.VMEM((count, z.tokens, z.width), bf16),
            pltpu.VMEM((z.experts, 16, fold), f32),
            pltpu.SemaphoreType.DMA((2 * count + 1 + len(tables),)),
        ],
        8,
        name,
    )(where, ids.reshape(1, z.tokens), *sources, *tables, *after)


def collect_rows(z, chunks, last, tile, base=0):
    last[...] = jnp.zeros_like(last)
    for k in range(z.experts):
        unpack_last(chunks[k], z, tile, last, k, base)


def norm_rows(h, gain):
    inv = lax.rsqrt(jnp.mean(h * h, axis=-1, keepdims=True) + epsilon)
    return (h * inv * gain).astype(bf16), inv


def normed_rows(z, chunks, vectors):
    def body(*refs):
        chunks, (vectors, normed_ref, gates_ref, last, tile) = refs[: z.experts], refs[z.experts :]
        gain, router = vectors[0:1, :], vectors[1:2, :]
        collect_rows(z, chunks, last, tile)
        for k in range(z.experts + 1):
            h = last[...] if k == z.experts else chunks[k][:, : z.width].astype(f32)
            at = k * z.main
            normed, _ = norm_rows(h, gain)
            normed_ref[at : at + 16, :] = normed
            logits = jnp.sum(normed.astype(f32) * router, axis=-1, keepdims=True)
            gates_ref[at : at + 16, :] = jnp.broadcast_to(jax.nn.sigmoid(logits), (16, 128))

    return call(
        body,
        "v" * (z.experts + 1),
        [shape((z.rows, z.width)), shape((z.rows, 128), f32), shape((16, z.width), f32)],
        [pltpu.VMEM((16, fold), f32)],
        8,
        "normed_rows",
    )(*chunks, vectors)


def grad_rows_of(z, chunks, after):
    def body(*refs):
        chunks, (rows, last, tile) = refs[: z.experts], refs[z.experts + len(after) :]
        for k in range(z.experts):
            rows[k * z.main : (k + 1) * z.main, :] = chunks[k][:16, : z.width]
        collect_rows(z, chunks, last, tile)
        rows[z.tokens :, :] = last[...].astype(bf16)

    return call(
        body,
        "v" * z.experts + "a" * len(after),
        [shape((z.rows, z.width)), shape((16, z.width), f32)],
        [pltpu.VMEM((16, fold), f32)],
        8,
        "grad_rows",
    )(*chunks, *after)


def act_norms(z, chunks, after):
    def body(*refs):
        chunks, (inv_ref, last, tile) = refs[: z.experts], refs[z.experts + len(after) :]
        collect_rows(z, chunks, last, tile, 16)
        for k in range(z.experts + 1):
            h = last[...] if k == z.experts else chunks[k][16:32, : z.width].astype(f32)
            at = k * z.main
            inv = lax.rsqrt(jnp.mean(h * h, axis=-1, keepdims=True) + epsilon)
            inv_ref[at : at + 16, :] = jnp.broadcast_to(inv, (16, 128))

    return call(
        body,
        "v" * z.experts + "a" * len(after),
        [shape((z.rows, 128), f32), shape((16, z.width), f32)],
        [pltpu.VMEM((16, fold), f32)],
        8,
        "act_norms",
    )(*chunks, *after)


def act_gates(z, chunks, last, inv, vectors, after):
    def body(*refs):
        chunks, (last, inv_ref, vectors) = refs[: z.experts], refs[z.experts : z.experts + 3]
        affinity_ref = refs[-1]
        gain, router = vectors[0:1, :], vectors[1:2, :]
        for k in range(z.experts + 1):
            h = last[...] if k == z.experts else chunks[k][16:32, : z.width].astype(f32)
            at = k * z.main
            normed = (h * inv_ref[at : at + 16, 0:1] * gain).astype(bf16).astype(f32)
            logits = jnp.sum(normed * router, axis=-1, keepdims=True)
            affinity_ref[at : at + 16, :] = jnp.broadcast_to(jax.nn.sigmoid(logits), (16, 128))

    return call(
        body,
        "v" * (z.experts + 3) + "a" * len(after),
        shape((z.rows, 128), f32),
        [],
        8,
        "act_gates",
    )(*chunks, last, inv, vectors, *after)


def write_parts(z, values, outs, col):
    values = values.astype(bf16)
    for m in range(z.split):
        outs[m][:, col : col + values.shape[1]] = values[m * z.rows : (m + 1) * z.rows]


def experts_forward(z, rows, w_gate, w_down, after):
    def body(*refs):
        rows, (gate_ref, down_ref), outs = (
            refs[: z.split],
            refs[z.split : z.split + 2],
            refs[z.split + 2 + len(after) :],
        )
        held = jnp.concatenate([part[...] for part in rows], axis=0)
        gate_proj = jnp.dot(held, gate_ref[0], preferred_element_type=f32)
        hidden = jax.nn.silu(gate_proj).astype(bf16)
        step = 512
        for col in range(0, z.width, step):
            part = jnp.dot(hidden, down_ref[0, :, col : col + step], preferred_element_type=f32)
            write_parts(z, part, outs, col)

    return call(
        body,
        "v" * (z.split + 2) + "a" * len(after),
        [shape((z.rows, z.width))] * z.split,
        [],
        16,
        "experts_forward",
    )(*rows, w_gate, w_down, *after)


def saved_rows(z, where, saved, weights, after):
    total, slots, width = z.split * z.rows, saved.shape[2], saved.shape[3]

    def body(where, saved_any, *refs):
        ordered_ref, saved_ref, sem = refs[len(weights) + len(after) :]
        copy = pltpu.make_async_copy(saved_any.at[0, 0], saved_ref, sem)
        copy.start()
        row = lax.broadcasted_iota(jnp.int32, (total, slots), 0)
        slot = lax.broadcasted_iota(jnp.int32, (total, slots), 1)
        m, at = row // z.rows, row % z.rows
        is_main = at < z.tokens
        k = jnp.where(is_main, at // z.main, at - z.tokens)
        p = jnp.where(is_main, at % z.main, z.main)
        source = jnp.bitwise_xor(k, where[0]) * z.split + jnp.bitwise_xor(m, where[1])
        wanted = jnp.where(k < z.experts, source * z.cap + p, -1)
        selector = jnp.where(slot == wanted, 1.0, 0.0).astype(bf16)
        copy.wait()
        ordered_ref[...] = jnp.dot(selector, saved_ref[...], preferred_element_type=f32)

    return call(
        body,
        "sh" + "v" * len(weights) + "a" * len(after),
        shape((total, width), f32),
        [pltpu.VMEM((slots, width), bf16), pltpu.SemaphoreType.DMA],
        8,
        "saved_rows",
    )(where, saved, *weights, *after)


def saved_terms(z, ordered, after):
    def body(ordered_ref, *refs):
        hidden_ref, slope_ref = refs[len(after) :]
        gate_proj = ordered_ref[...]
        sg = jax.nn.sigmoid(gate_proj)
        hidden_ref[...] = (gate_proj * sg).astype(bf16)
        slope_ref[...] = sg * (1.0 + gate_proj * (1.0 - sg))

    return call(
        body,
        "v" + "a" * len(after),
        [shape(ordered.shape), shape(ordered.shape, f32)],
        [],
        8,
        "saved_terms",
    )(ordered, *after)


def experts_backward(z, rows, hidden, slope, w_gate, w_down, after):
    def body(*refs):
        rows = refs[: z.split]
        hidden_ref, slope_ref, gate_ref, down_ref = refs[z.split : z.split + 4]
        outs = refs[z.split + 4 + len(after) :]
        held = jnp.concatenate([part[...] for part in rows], axis=0)
        grad_hidden = lax.dot_general(held, down_ref[0], nt, preferred_element_type=f32)
        dots = jnp.sum(grad_hidden * hidden_ref[...].astype(f32), axis=-1, keepdims=True)
        grad_gate = (grad_hidden * slope_ref[...]).astype(bf16)
        step = 512
        for col in range(0, z.width, step):
            part = lax.dot_general(
                grad_gate, gate_ref[0, col : col + step, :], nt, preferred_element_type=f32
            )
            write_parts(z, part, outs, col)
        write_parts(z, jnp.broadcast_to(dots, (dots.shape[0], 128)), outs, z.width)

    return call(
        body,
        "v" * (z.split + 4) + "a" * len(after),
        [shape((z.rows, z.width + 128))] * z.split,
        [],
        16,
        "experts_backward",
    )(*rows, hidden, slope, w_gate, w_down, *after)


def put_last(z, values, source_chunk, tile, out):
    tile[...] = jnp.zeros_like(tile)
    pack_last(values, tile)
    tokens = source_chunk[:16, z.width :].astype(f32)
    tile[z.pieces : z.pieces + 1, :] = tokens[z.pieces : z.pieces + 1, :]
    out[:, z.width :] = tile[...].astype(bf16)


def finish_forward(z, chunks, last, parts, gates, after):
    def body(*refs):
        e = z.experts
        chunks, last, parts = refs[:e], refs[e], refs[e + 1 : e + 1 + z.split]
        gates, outs, (tile,) = refs[e + 1 + z.split], refs[-1 - e : -1], refs[-1:]

        def mixed(at):
            y = parts[0][at : at + 16, :].astype(f32)
            for part in parts[1:]:
                y = y + part[at : at + 16, :].astype(f32)
            return route_scale * (gates[at : at + 16, 0:1] * y)

        tail = last[...] + mixed(z.tokens)
        for k in range(e):
            h = chunks[k][:, : z.width].astype(f32)
            outs[k][:, : z.width] = (h + mixed(k * z.main)).astype(bf16)
            put_last(z, tail[k : k + 1, :], chunks[k], tile, outs[k])

    return call(
        body,
        "v" * (z.experts + z.split + 2) + "a" * len(after),
        [shape((z.main, z.wide))] * z.experts,
        [pltpu.VMEM((16, fold), f32)],
        8,
        "finish_forward",
    )(*chunks, last, *parts, gates, *after)


def finish_backward(z, chunks, lasts, terms, parts, vectors):
    def body(*refs):
        e = z.experts
        chunks, (last_grad, last_act, inv_ref, affinity_ref) = refs[:e], refs[e : e + 4]
        parts, vectors = refs[e + 4 : e + 4 + z.split], refs[e + 4 + z.split]
        outs, (tile,) = refs[-1 - e : -1], refs[-1:]
        gain, router = vectors[0:1, :], vectors[1:2, :]

        def finished(h, g, at):
            inv, affinity = inv_ref[at : at + 16, 0:1], affinity_ref[at : at + 16, 0:1]
            rows = parts[0][at : at + 16, : z.width].astype(f32)
            dot = parts[0][at : at + 16, z.width :].astype(f32)
            for part in parts[1:]:
                rows = rows + part[at : at + 16, : z.width].astype(f32)
                dot = dot + part[at : at + 16, z.width :].astype(f32)
            dot = dot[:, 0:1]
            grad_logits = (route_scale * dot * affinity * (1.0 - affinity)).astype(bf16).astype(f32)
            grad_pre = (route_scale * affinity * rows + grad_logits * router) * gain
            centre = jnp.mean(grad_pre * h, axis=-1, keepdims=True)
            return g + inv * (grad_pre - h * (inv * inv * centre))

        tail = finished(last_act[...], last_grad[...], z.tokens)
        for k in range(e):
            g = chunks[k][:16, : z.width].astype(f32)
            h = chunks[k][16:32, : z.width].astype(f32)
            outs[k][:, : z.width] = finished(h, g, k * z.main).astype(bf16)
            put_last(z, tail[k : k + 1, :], chunks[k], tile, outs[k])

    return call(
        body,
        "v" * (z.experts + z.split + 5),
        [shape((z.main, z.wide))] * z.experts,
        [pltpu.VMEM((16, fold), f32)],
        8,
        "finish_backward",
    )(*chunks, *lasts, *terms, *parts, vectors)


def order_rows(z, chunks, name):
    def body(*refs):
        chunks, (out, held, last, tile) = refs[: z.experts], refs[z.experts :]
        for k in range(z.experts):
            held[k * z.main : (k + 1) * z.main, :] = chunks[k][:, : z.width]
        collect_rows(z, chunks, last, tile)
        held[z.tokens :, :] = last[...].astype(bf16)
        token_row = chunks[0][:, z.width :].astype(f32)[z.pieces : z.pieces + 1, : z.rows]
        token = lax.broadcasted_iota(jnp.int32, (z.tokens, z.rows), 0).astype(f32)
        selector = jnp.where(token == token_row, 1.0, 0.0).astype(bf16)
        out[...] = jnp.dot(selector, held[...], preferred_element_type=f32).astype(bf16)

    return call(
        body,
        "v" * z.experts,
        shape((z.tokens, z.width)),
        [
            pltpu.VMEM((z.rows, z.width), bf16),
            pltpu.VMEM((16, z.width), f32),
            pltpu.VMEM((16, fold), f32),
        ],
        8,
        name,
    )(*chunks)


def dispatch(z, chunks):
    groups = z.experts * z.split
    got = [chunks[0]] + [None] * (z.experts - 1)
    for k in reversed(range(1, z.experts)):
        pairs = [(i, ((i // z.split) ^ k) * z.split + i % z.split) for i in range(groups)]
        got[k] = lax.ppermute(chunks[k], "ep", pairs)
    return got


def to_core(z, array, m):
    groups = z.experts * z.split
    pairs = [(i, i // z.split * z.split + ((i % z.split) ^ m)) for i in range(groups)]
    return lax.ppermute(array, "ep", pairs)


def to_section(z, chunks, by):
    groups = z.experts * z.split
    sections = lax.axis_size("pp")
    got = [None] * z.experts
    for k in reversed(range(z.experts)):
        pairs = [
            (s * groups + i, (s + by) % sections * groups + ((i // z.split) ^ k) * z.split + i % z.split)
            for s in range(sections)
            for i in range(groups)
        ]
        got[k] = lax.ppermute(chunks[k], ("pp", "ep"), pairs)
    return got


def on_device(
    fwd_act, fwd_ids, bwd_act, bwd_ids, bwd_grad, norm_gain, router, w_gate, w_down, saved_gate
):
    groups = lax.axis_size("ep")
    assert fwd_ids.shape[1] == 1
    z = Sizes(groups, router.shape[2], fwd_act.shape[0], fwd_act.shape[1])
    index = lax.axis_index("ep")
    where = jnp.stack([index // z.split, index % z.split]).astype(jnp.int32)
    router = jnp.swapaxes(router, 1, 2)
    others = range(1, z.split)

    fwd_chunks = make_chunks(z, where, fwd_ids, [fwd_act], [], [], "forward_chunks")
    fwd_own = dispatch(z, fwd_chunks)
    *bwd_chunks, vectors = make_chunks(
        z,
        where,
        bwd_ids,
        [bwd_grad, bwd_act],
        [norm_gain, router],
        [fwd_chunks[0]],
        "backward_chunks",
    )
    bwd_own = dispatch(z, bwd_chunks)

    normed, gates, fwd_last = normed_rows(z, fwd_own, vectors)
    fwd_all = [normed] + [to_core(z, normed, m) for m in others]
    ordered = saved_rows(z, where, saved_gate, [w_gate, w_down], [gates])
    fwd_parts = experts_forward(z, fwd_all, w_gate, w_down, [ordered])
    hidden, slope = saved_terms(z, ordered, [fwd_parts[0]])
    fwd_parts = [fwd_parts[0]] + [to_core(z, fwd_parts[m], m) for m in others]
    fwd_out = finish_forward(z, fwd_own, fwd_last, fwd_parts, gates, [hidden])
    fwd_done = to_section(z, fwd_out, 1)

    grads, grad_last = grad_rows_of(z, bwd_own, [fwd_out[0]])
    grad_all = [grads] + [to_core(z, grads, m) for m in others]
    inv, act_last = act_norms(z, bwd_own, [grads])
    bwd_parts = experts_backward(z, grad_all, hidden, slope, w_gate, w_down, [inv])
    affinity = act_gates(z, bwd_own, act_last, inv, vectors, [bwd_parts[0]])
    bwd_parts = [bwd_parts[0]] + [to_core(z, bwd_parts[m], m) for m in others]
    bwd_out = finish_backward(
        z, bwd_own, [grad_last, act_last], [inv, affinity], bwd_parts, vectors
    )
    bwd_done = to_section(z, bwd_out, -1)
    return (order_rows(z, fwd_done, "forward_rows"), order_rows(z, bwd_done, "backward_rows"))


def solution(mesh):
    return jax.shard_map(
        on_device,
        mesh=mesh,
        in_specs=(
            P(("pp", "ep"), None),
            P(("pp", "ep"), None),
            P(("pp", "ep"), None),
            P(("pp", "ep"), None),
            P(("pp", "ep"), None),
            P("pp", None),
            P("pp", None, None),
            P(("pp", "ep"), None, None),
            P(("pp", "ep"), None, None),
            P("pp", "ep", None, None),
        ),
        out_specs=(P(("pp", "ep"), None), P(("pp", "ep"), None)),
        check_vma=False,
    )
```

```python
import jax
import jax.numpy as jnp
from jax import lax
from jax.experimental import pallas as pl
from jax.experimental.pallas import tpu as pltpu
from jax.sharding import PartitionSpec as P

epsilon = 1e-06
route_scale = 2.5
fold = 256
none = 255.0
f32 = jnp.float32
bf16 = jnp.bfloat16
nt = (((1,), (1,)), ((), ()))
spaces = {
    "s": pl.BlockSpec(memory_space=pltpu.SMEM),
    "v": pl.BlockSpec(memory_space=pltpu.VMEM),
    "a": pl.BlockSpec(memory_space=pl.ANY),
    "h": pl.BlockSpec(memory_space=pltpu.HBM),
}


cost = {
    "normed_rows": 5,
    "saved_terms": 40,
    "act_norms": 40,
    "act_gates": 40,
}


def call(body, places, outs, scratch, megabytes, name, out_specs=None):
    def run(*arrays):
        arrays = [
            pltpu.with_memory_space_constraint(array, pltpu.HBM) if place == "h" else array
            for array, place in zip(arrays, places, strict=True)
        ]
        return kernel(*arrays)

    where_to = {} if out_specs is None else {"out_specs": out_specs}
    kernel = pl.pallas_call(
        body,
        out_shape=outs,
        in_specs=[spaces[place] for place in places],
        **where_to,
        scratch_shapes=scratch,
        compiler_params=pltpu.CompilerParams(vmem_limit_bytes=megabytes * 1024 * 1024),
        cost_estimate=pl.CostEstimate(
            flops=int(cost.get(name, 0.1) * 1e9), bytes_accessed=1000, transcendentals=0
        ),
        name=name,
    )
    return run


def shape(dims, kind=bf16):
    return jax.ShapeDtypeStruct(dims, kind)


class Sizes:
    def __init__(self, groups, experts, tokens, width):
        self.experts = experts
        self.split = groups // experts
        self.tokens = tokens
        self.width = width
        self.main = tokens // experts
        self.cap = self.main + 1
        self.pieces = width // fold
        self.wide = width + fold
        self.rows = tokens + 16
        assert self.main == 16 and self.pieces <= 14 and width % fold == 0
        assert experts <= 8 and experts & (experts - 1) == 0 and self.split & (self.split - 1) == 0


def pack_last(row, tile, first=0):
    for i in range(row.shape[1] // fold):
        tile[first + i : first + i + 1, :] = row[:, i * fold : (i + 1) * fold]


def unpack_last(chunk, z, tile, target, at, base=0):
    tile[...] = chunk[base : base + 16, z.width :].astype(f32)
    for i in range(z.pieces):
        target[at : at + 1, i * fold : (i + 1) * fold] = tile[i : i + 1, :]


def slot_matrices(ids_row, block, z):
    tokens = z.tokens
    sub = lax.broadcasted_iota(jnp.int32, (tokens, tokens), 0)
    lane = lax.broadcasted_iota(jnp.int32, (tokens, tokens), 1)
    row = jnp.bitwise_xor(ids_row, block)
    column = jnp.sum(jnp.where(sub == lane, row, 0), axis=1, keepdims=True)
    same = column == row
    place_row = jnp.sum(jnp.where(same & (sub < lane), 1, 0), axis=0, keepdims=True)
    place_column = jnp.sum(jnp.where(same & (lane < sub), 1, 0), axis=1, keepdims=True)

    def slot(expert, place):
        return jnp.where(place < z.main, expert * z.main + place, tokens + expert)

    slot_row = slot(row, place_row)
    slot_column = slot(column, place_column)
    by_slot = lax.broadcasted_iota(jnp.int32, (z.rows, tokens), 0) == slot_row
    lane = lax.broadcasted_iota(jnp.int32, (tokens, fold), 1)
    by_token = jnp.where(lane < tokens, lane, tokens + (lane - tokens) // 16) == slot_column
    token = lax.broadcasted_iota(jnp.int32, (tokens, fold), 0).astype(f32)
    token_row = jnp.sum(jnp.where(by_token, token - none, 0.0), axis=0, keepdims=True) + none
    return jnp.where(by_slot, 1.0, 0.0).astype(bf16), token_row


def write_chunks(z, selector, token_row, rows_ref, ready, tiles, chunks, base):
    step = z.width // 2
    tiles[...] = jnp.zeros_like(tiles)
    for half in range(2):
        ready[half].wait()
        col = half * step
        got = jnp.dot(selector, rows_ref[:, col : col + step], preferred_element_type=f32)
        packed = got[: z.tokens].astype(bf16)
        for k in range(z.experts):
            chunks[k][base : base + 16, col : col + step] = packed[k * z.main : (k + 1) * z.main]
            pack_last(got[z.tokens + k : z.tokens + k + 1], tiles.at[k], half * z.pieces // 2)
    for k in range(z.experts):
        tiles[k, z.pieces : z.pieces + 1, :] = token_row
        chunks[k][base : base + 16, z.width :] = tiles[k].astype(bf16)


def make_chunks(z, where, ids, sources, tables, after, name):
    count = len(sources)

    def body(where, ids_any, *refs):
        anys, tables_any = refs[:count], refs[count : count + len(tables)]
        outs, held = refs[count + len(tables) + len(after) :], ()
        if tables:
            *outs, gain_ref, router_ref, ids, rows, tiles, sems = outs
            *outs, vectors = outs
            held = (gain_ref, router_ref)
        else:
            *outs, ids, rows, tiles, sems = outs
        copies = [pltpu.make_async_copy(ids_any, ids, sems.at[2 * count])]
        step = z.width // 2
        for j in range(count):
            for half in range(2):
                cols = pl.ds(half * step, step)
                copies.append(
                    pltpu.make_async_copy(
                        anys[j].at[:, cols], rows.at[j, :, cols], sems.at[2 * j + half]
                    )
                )
        for i, (source, target) in enumerate(zip(tables_any, held)):
            copies.append(pltpu.make_async_copy(source, target, sems.at[2 * count + 1 + i]))
        for copy in copies:
            copy.start()
        copies[0].wait()
        selector, token_row = slot_matrices(ids[...], where[0], z)
        for j in range(count):
            ready = copies[1 + 2 * j : 3 + 2 * j]
            write_chunks(z, selector, token_row, rows.at[j], ready, tiles, outs, 16 * j)
        if tables:
            for copy in copies[1 + 2 * count :]:
                copy.wait()
            vectors[...] = jnp.zeros_like(vectors)
            vectors[0:1, :] = gain_ref[...].astype(f32)
            mine = lax.broadcasted_iota(jnp.int32, (z.experts, 1), 0) == where[0]
            table = jnp.where(mine, router_ref[0].astype(f32), 0.0)
            vectors[1:2, :] = jnp.sum(table, axis=0, keepdims=True)

    return call(
        body,
        "sh" + "h" * (count + len(tables)) + "a" * len(after),
        [shape((z.main * count, z.wide))] * z.experts
        + [shape((8, z.width), f32) for _ in tables[:1]],
        [pltpu.VMEM(table.shape, bf16) for table in tables]
        + [
            pltpu.VMEM((1, z.tokens), jnp.int32),
            pltpu.VMEM((count, z.tokens, z.width), bf16),
            pltpu.VMEM((z.experts, 16, fold), f32),
            pltpu.SemaphoreType.DMA((2 * count + 1 + len(tables),)),
        ],
        8,
        name,
    )(where, ids.reshape(1, z.tokens), *sources, *tables, *after)


def collect_rows(z, chunks, last, tile, base=0):
    last[...] = jnp.zeros_like(last)
    for k in range(z.experts):
        unpack_last(chunks[k], z, tile, last, k, base)


def norm_rows(h, gain):
    inv = lax.rsqrt(jnp.mean(h * h, axis=-1, keepdims=True) + epsilon)
    return (h * inv * gain).astype(bf16), inv


def normed_rows(z, chunks, vectors):
    def body(*refs):
        chunks, (vectors, normed_ref, gates_ref, last, tile) = refs[: z.experts], refs[z.experts :]
        gain, router = vectors[0:1, :], vectors[1:2, :]
        collect_rows(z, chunks, last, tile)
        for k in range(z.experts + 1):
            h = last[...] if k == z.experts else chunks[k][:, : z.width].astype(f32)
            at = k * z.main
            normed, _ = norm_rows(h, gain)
            normed_ref[at : at + 16, :] = normed
            logits = jnp.sum(normed.astype(f32) * router, axis=-1, keepdims=True)
            gates_ref[at : at + 16, :] = jnp.broadcast_to(jax.nn.sigmoid(logits), (16, 128))

    return call(
        body,
        "v" * (z.experts + 1),
        [shape((z.rows, z.width)), shape((z.rows, 128), f32), shape((16, z.width), f32)],
        [pltpu.VMEM((16, fold), f32)],
        8,
        "normed_rows",
    )(*chunks, vectors)


def grad_rows_of(z, chunks, after):
    def body(*refs):
        chunks, (rows, last, tile) = refs[: z.experts], refs[z.experts + len(after) :]
        for k in range(z.experts):
            rows[k * z.main : (k + 1) * z.main, :] = chunks[k][:16, : z.width]
        collect_rows(z, chunks, last, tile)
        rows[z.tokens :, :] = last[...].astype(bf16)

    return call(
        body,
        "v" * z.experts + "a" * len(after),
        [shape((z.rows, z.width)), shape((16, z.width), f32)],
        [pltpu.VMEM((16, fold), f32)],
        8,
        "grad_rows",
    )(*chunks, *after)


def act_norms(z, chunks, after):
    def body(*refs):
        chunks, (inv_ref, last, tile) = refs[: z.experts], refs[z.experts + len(after) :]
        collect_rows(z, chunks, last, tile, 16)
        for k in range(z.experts + 1):
            h = last[...] if k == z.experts else chunks[k][16:32, : z.width].astype(f32)
            at = k * z.main
            inv = lax.rsqrt(jnp.mean(h * h, axis=-1, keepdims=True) + epsilon)
            inv_ref[at : at + 16, :] = jnp.broadcast_to(inv, (16, 128))

    return call(
        body,
        "v" * z.experts + "a" * len(after),
        [shape((z.rows, 128), f32), shape((16, z.width), f32)],
        [pltpu.VMEM((16, fold), f32)],
        8,
        "act_norms",
    )(*chunks, *after)


def act_gates(z, chunks, last, inv, vectors, after):
    def body(*refs):
        chunks, (last, inv_ref, vectors) = refs[: z.experts], refs[z.experts : z.experts + 3]
        affinity_ref = refs[-1]
        gain, router = vectors[0:1, :], vectors[1:2, :]
        for k in range(z.experts + 1):
            h = last[...] if k == z.experts else chunks[k][16:32, : z.width].astype(f32)
            at = k * z.main
            normed = (h * inv_ref[at : at + 16, 0:1] * gain).astype(bf16).astype(f32)
            logits = jnp.sum(normed * router, axis=-1, keepdims=True)
            affinity_ref[at : at + 16, :] = jnp.broadcast_to(jax.nn.sigmoid(logits), (16, 128))

    return call(
        body,
        "v" * (z.experts + 3) + "a" * len(after),
        shape((z.rows, 128), f32),
        [],
        8,
        "act_gates",
    )(*chunks, last, inv, vectors, *after)


def write_parts(z, values, outs, col):
    values = values.astype(bf16)
    for m in range(z.split):
        outs[m][:, col : col + values.shape[1]] = values[m * z.rows : (m + 1) * z.rows]


def experts_forward(z, rows, w_gate, w_down, after):
    def body(*refs):
        rows, (gate_ref, down_ref), outs = (
            refs[: z.split],
            refs[z.split : z.split + 2],
            refs[z.split + 2 + len(after) :],
        )
        held = jnp.concatenate([part[...] for part in rows], axis=0)
        gate_proj = jnp.dot(held, gate_ref[0], preferred_element_type=f32)
        hidden = jax.nn.silu(gate_proj).astype(bf16)
        step = 512
        for col in range(0, z.width, step):
            part = jnp.dot(hidden, down_ref[0, :, col : col + step], preferred_element_type=f32)
            write_parts(z, part, outs, col)

    return call(
        body,
        "v" * (z.split + 2) + "a" * len(after),
        [shape((z.rows, z.width))] * z.split,
        [],
        16,
        "experts_forward",
    )(*rows, w_gate, w_down, *after)


def saved_terms(z, where, saved, after):
    total, slots, width = z.split * z.rows, saved.shape[2], saved.shape[3]

    def body(where, saved_any, *refs):
        hidden_ref, slope_ref, saved_ref, sem = refs[len(after) :]
        copy = pltpu.make_async_copy(saved_any.at[0, 0], saved_ref, sem)
        copy.start()
        row = lax.broadcasted_iota(jnp.int32, (total, slots), 0)
        slot = lax.broadcasted_iota(jnp.int32, (total, slots), 1)
        m, at = row // z.rows, row % z.rows
        is_main = at < z.tokens
        k = jnp.where(is_main, at // z.main, at - z.tokens)
        p = jnp.where(is_main, at % z.main, z.main)
        source = jnp.bitwise_xor(k, where[0]) * z.split + jnp.bitwise_xor(m, where[1])
        wanted = jnp.where(k < z.experts, source * z.cap + p, -1)
        selector = jnp.where(slot == wanted, 1.0, 0.0).astype(bf16)
        copy.wait()
        gate_proj = jnp.dot(selector, saved_ref[...], preferred_element_type=f32)
        sg = jax.nn.sigmoid(gate_proj)
        hidden_ref[...] = (gate_proj * sg).astype(bf16)
        slope_ref[...] = sg * (1.0 + gate_proj * (1.0 - sg))

    return call(
        body,
        "sh" + "a" * len(after),
        [shape((total, width)), shape((total, width), f32)],
        [pltpu.VMEM((slots, width), bf16), pltpu.SemaphoreType.DMA],
        8,
        "saved_terms",
    )(where, saved, *after)


def experts_backward(z, rows, hidden, slope, w_gate, w_down, after):
    def body(*refs):
        rows = refs[: z.split]
        hidden_ref, slope_ref, gate_ref, down_ref = refs[z.split : z.split + 4]
        outs = refs[z.split + 4 + len(after) :]
        held = jnp.concatenate([part[...] for part in rows], axis=0)
        grad_hidden = lax.dot_general(held, down_ref[0], nt, preferred_element_type=f32)
        dots = jnp.sum(grad_hidden * hidden_ref[...].astype(f32), axis=-1, keepdims=True)
        grad_gate = (grad_hidden * slope_ref[...]).astype(bf16)
        step = 512
        for col in range(0, z.width, step):
            part = lax.dot_general(
                grad_gate, gate_ref[0, col : col + step, :], nt, preferred_element_type=f32
            )
            write_parts(z, part, outs, col)
        write_parts(z, jnp.broadcast_to(dots, (dots.shape[0], 128)), outs, z.width)

    return call(
        body,
        "v" * (z.split + 4) + "a" * len(after),
        [shape((z.rows, z.width + 128))] * z.split,
        [],
        16,
        "experts_backward",
    )(*rows, hidden, slope, w_gate, w_down, *after)


def put_last(z, values, source_chunk, tile, out):
    tile[...] = jnp.zeros_like(tile)
    pack_last(values, tile)
    tokens = source_chunk[:16, z.width :].astype(f32)
    tile[z.pieces : z.pieces + 1, :] = tokens[z.pieces : z.pieces + 1, :]
    out[:, z.width :] = tile[...].astype(bf16)


def finish_forward(z, ks, chunks, last, parts, gates, after):
    count = len(ks)

    def body(*refs):
        chunks, last, parts = refs[:count], refs[count], refs[count + 1 : count + 1 + z.split]
        gates, outs, tile = refs[count + 1 + z.split], refs[-1 - count : -1], refs[-1]

        def mixed(at):
            y = parts[0][at : at + 16, :].astype(f32)
            for part in parts[1:]:
                y = y + part[at : at + 16, :].astype(f32)
            return route_scale * (gates[at : at + 16, 0:1] * y)

        tail = last[...] + mixed(z.tokens)
        for k, chunk, out in zip(ks, chunks, outs):
            h = chunk[:, : z.width].astype(f32)
            out[:, : z.width] = (h + mixed(k * z.main)).astype(bf16)
            put_last(z, tail[k : k + 1, :], chunk, tile, out)

    return call(
        body,
        "v" * (count + z.split + 2) + "a" * len(after),
        [shape((z.main, z.wide))] * count,
        [pltpu.VMEM((16, fold), f32)],
        8,
        "finish_forward_" + "".join(map(str, ks)),
    )(*[chunks[k] for k in ks], last, *parts, gates, *after)


def finish_backward(z, order, chunks, lasts, terms, parts, vectors, after):
    def body(*refs):
        e = z.experts
        chunks, (last_grad, last_act, inv_ref, affinity_ref) = refs[:e], refs[e : e + 4]
        parts, vectors = refs[e + 4 : e + 4 + z.split], refs[e + 4 + z.split]
        outs, (tile,) = refs[-1 - e : -1], refs[-1:]
        outs = [outs[order.index(k)] for k in range(e)]
        gain, router = vectors[0:1, :], vectors[1:2, :]

        def finished(h, g, at):
            inv, affinity = inv_ref[at : at + 16, 0:1], affinity_ref[at : at + 16, 0:1]
            rows = parts[0][at : at + 16, : z.width].astype(f32)
            dot = parts[0][at : at + 16, z.width :].astype(f32)
            for part in parts[1:]:
                rows = rows + part[at : at + 16, : z.width].astype(f32)
                dot = dot + part[at : at + 16, z.width :].astype(f32)
            dot = dot[:, 0:1]
            grad_logits = (route_scale * dot * affinity * (1.0 - affinity)).astype(bf16).astype(f32)
            grad_pre = (route_scale * affinity * rows + grad_logits * router) * gain
            centre = jnp.mean(grad_pre * h, axis=-1, keepdims=True)
            return g + inv * (grad_pre - h * (inv * inv * centre))

        tail = finished(last_act[...], last_grad[...], z.tokens)
        for k in range(e):
            g = chunks[k][:16, : z.width].astype(f32)
            h = chunks[k][16:32, : z.width].astype(f32)
            outs[k][:, : z.width] = finished(h, g, k * z.main).astype(bf16)
            put_last(z, tail[k : k + 1, :], chunks[k], tile, outs[k])

    return call(
        body,
        "v" * (z.experts + z.split + 5) + "a" * len(after),
        [shape((z.main, z.wide))] * z.experts,
        [pltpu.VMEM((16, fold), f32)],
        8,
        "finish_backward",
    )(*chunks, *lasts, *terms, *parts, vectors, *after)


def order_rows(z, chunks, name):
    lanes = z.tokens + 16 * z.experts
    steps = 7 if z.pieces % 7 == 0 else z.pieces

    def body(*refs):
        chunks, (out_any, out, sems) = refs[: z.experts], refs[z.experts :]
        tiles = [chunk[:, z.width :] for chunk in chunks]
        token_row = tiles[0].astype(f32)[z.pieces : z.pieces + 1, :lanes]
        token = lax.broadcasted_iota(jnp.int32, (z.tokens, lanes), 0).astype(f32)
        lane = lax.broadcasted_iota(jnp.int32, (z.tokens, lanes), 1)
        piece = jnp.where(lane < z.tokens, -1, lane % 16)
        ours = token == token_row
        copies = []
        for i in range(z.pieces):
            cols = pl.ds(i * fold, fold)
            mine = ours & ((piece < 0) | (piece == i))
            selector = jnp.where(mine, 1.0, 0.0).astype(bf16)
            rows = jnp.concatenate([chunk[:, cols] for chunk in chunks] + tiles, axis=0)
            out[:, cols] = jnp.dot(selector, rows, preferred_element_type=f32).astype(bf16)
            if (i + 1) % (z.pieces // steps) == 0:
                done = pl.ds((i + 1) * fold - z.width // steps, z.width // steps)
                copy = pltpu.make_async_copy(out.at[:, done], out_any.at[:, done], sems.at[len(copies)])
                copy.start()
                copies.append(copy)
        for copy in copies:
            copy.wait()

    return call(
        body,
        "v" * z.experts,
        shape((z.tokens, z.width)),
        [pltpu.VMEM((z.tokens, z.width), bf16), pltpu.SemaphoreType.DMA((steps,))],
        8,
        name,
        spaces["a"],
    )(*chunks)


def dispatch(z, chunks):
    groups = z.experts * z.split
    got = [chunks[0]] + [None] * (z.experts - 1)
    for k in reversed(range(1, z.experts)):
        pairs = [(i, ((i // z.split) ^ k) * z.split + i % z.split) for i in range(groups)]
        got[k] = lax.ppermute(chunks[k], "ep", pairs)
    return got


def to_core(z, array, m):
    groups = z.experts * z.split
    pairs = [(i, i // z.split * z.split + ((i % z.split) ^ m)) for i in range(groups)]
    return lax.ppermute(array, "ep", pairs)


def to_section(z, chunk, k, by):
    groups = z.experts * z.split
    sections = lax.axis_size("pp")
    pairs = [
        (s * groups + i, (s + by) % sections * groups + ((i // z.split) ^ k) * z.split + i % z.split)
        for s in range(sections)
        for i in range(groups)
    ]
    return lax.ppermute(chunk, ("pp", "ep"), pairs)


def on_device(
    fwd_act, fwd_ids, bwd_act, bwd_ids, bwd_grad, norm_gain, router, w_gate, w_down, saved_gate
):
    groups = lax.axis_size("ep")
    assert fwd_ids.shape[1] == 1
    z = Sizes(groups, router.shape[2], fwd_act.shape[0], fwd_act.shape[1])
    index = lax.axis_index("ep")
    where = jnp.stack([index // z.split, index % z.split]).astype(jnp.int32)
    router = jnp.swapaxes(router, 1, 2)
    others = range(1, z.split)

    fwd_chunks = make_chunks(z, where, fwd_ids, [fwd_act], [], [], "forward_chunks")
    fwd_own = dispatch(z, fwd_chunks)
    *bwd_chunks, vectors = make_chunks(
        z,
        where,
        bwd_ids,
        [bwd_grad, bwd_act],
        [norm_gain, router],
        [fwd_chunks[0]],
        "backward_chunks",
    )
    bwd_own = dispatch(z, bwd_chunks)

    normed, gates, fwd_last = normed_rows(z, fwd_own, vectors)
    fwd_all = [normed] + [to_core(z, normed, m) for m in others]
    fwd_parts = experts_forward(z, fwd_all, w_gate, w_down, [])
    hidden, slope = saved_terms(z, where, saved_gate, [fwd_parts[0]])
    fwd_parts = [fwd_parts[0]] + [to_core(z, fwd_parts[m], m) for m in others]
    fwd_done = {}

    def finish(ks, after):
        outs = finish_forward(z, ks, [fwd_own[k] for k in range(z.experts)], fwd_last, fwd_parts, gates, after)
        for k, out in zip(ks, outs):
            fwd_done[k] = to_section(z, out, k, 1)
        return outs[0]

    order = [*range(z.experts - 1, 0, -1), 0]
    first = finish(order[:-1], [hidden])
    grads, grad_last = grad_rows_of(z, bwd_own, [first])
    grad_all = [grads] + [to_core(z, grads, m) for m in others]
    inv, act_last = act_norms(z, bwd_own, [grads])
    bwd_parts = experts_backward(z, grad_all, hidden, slope, w_gate, w_down, [inv])
    affinity = act_gates(z, bwd_own, act_last, inv, vectors, [bwd_parts[0]])
    third = finish(order[-1:], [affinity])
    bwd_parts = [bwd_parts[0]] + [to_core(z, bwd_parts[m], m) for m in others]
    bwd_out = finish_backward(
        z, order, bwd_own, [grad_last, act_last], [inv, affinity], bwd_parts, vectors, [third]
    )
    bwd_done = {k: to_section(z, out, k, -1) for k, out in zip(order, bwd_out)}
    bwd_done = [bwd_done[k] for k in range(z.experts)]
    fwd_done = [fwd_done[k] for k in range(z.experts)]
    return (order_rows(z, fwd_done, "forward_rows"), order_rows(z, bwd_done, "backward_rows"))


def solution(mesh):
    return jax.shard_map(
        on_device,
        mesh=mesh,
        in_specs=(
            P(("pp", "ep"), None),
            P(("pp", "ep"), None),
            P(("pp", "ep"), None),
            P(("pp", "ep"), None),
            P(("pp", "ep"), None),
            P("pp", None),
            P("pp", None, None),
            P(("pp", "ep"), None, None),
            P(("pp", "ep"), None, None),
            P("pp", "ep", None, None),
        ),
        out_specs=(P(("pp", "ep"), None), P(("pp", "ep"), None)),
        check_vma=False,
    )
```

```python
import jax
import jax.numpy as jnp
from jax import lax
from jax.experimental import pallas as pl
from jax.experimental.pallas import tpu as pltpu
from jax.sharding import PartitionSpec as P

epsilon = 1e-06
route_scale = 2.5
fold = 256
none = 255.0
f32 = jnp.float32
bf16 = jnp.bfloat16
nt = (((1,), (1,)), ((), ()))
spaces = {
    "s": pl.BlockSpec(memory_space=pltpu.SMEM),
    "v": pl.BlockSpec(memory_space=pltpu.VMEM),
    "a": pl.BlockSpec(memory_space=pl.ANY),
    "h": pl.BlockSpec(memory_space=pltpu.HBM),
}


cost = {
    "normed_rows": 5,
    "saved_terms": 40,
    "grad_rows": 40,
    "finish_forward_32": 4,
    "act_norms": 40,
}


def call(body, places, outs, scratch, megabytes, name, out_specs=None):
    def run(*arrays):
        arrays = [
            pltpu.with_memory_space_constraint(array, pltpu.HBM) if place == "h" else array
            for array, place in zip(arrays, places, strict=True)
        ]
        return kernel(*arrays)

    where_to = {} if out_specs is None else {"out_specs": out_specs}
    kernel = pl.pallas_call(
        body,
        out_shape=outs,
        in_specs=[spaces[place] for place in places],
        **where_to,
        scratch_shapes=scratch,
        compiler_params=pltpu.CompilerParams(vmem_limit_bytes=megabytes * 1024 * 1024),
        cost_estimate=pl.CostEstimate(
            flops=int(cost.get(name, 0.1) * 1e9), bytes_accessed=1000, transcendentals=0
        ),
        name=name,
    )
    return run


def shape(dims, kind=bf16):
    return jax.ShapeDtypeStruct(dims, kind)


class Sizes:
    def __init__(self, groups, experts, tokens, width):
        self.experts = experts
        self.split = groups // experts
        self.tokens = tokens
        self.width = width
        self.main = tokens // experts
        self.cap = self.main + 1
        self.pieces = width // fold
        self.wide = width + fold
        self.rows = tokens + 16
        assert self.main == 16 and self.pieces <= 14 and width % fold == 0
        assert experts <= 8 and experts & (experts - 1) == 0 and self.split & (self.split - 1) == 0


def pack_last(row, tile, first=0):
    for i in range(row.shape[1] // fold):
        tile[first + i : first + i + 1, :] = row[:, i * fold : (i + 1) * fold]


def unpack_last(chunk, z, tile, target, at, base=0):
    tile[...] = chunk[base : base + 16, z.width :].astype(f32)
    for i in range(z.pieces):
        target[at : at + 1, i * fold : (i + 1) * fold] = tile[i : i + 1, :]


def slot_matrices(ids_row, block, z):
    tokens = z.tokens
    sub = lax.broadcasted_iota(jnp.int32, (tokens, tokens), 0)
    lane = lax.broadcasted_iota(jnp.int32, (tokens, tokens), 1)
    row = jnp.bitwise_xor(ids_row, block)
    column = jnp.sum(jnp.where(sub == lane, row, 0), axis=1, keepdims=True)
    same = column == row
    place_row = jnp.sum(jnp.where(same & (sub < lane), 1, 0), axis=0, keepdims=True)
    place_column = jnp.sum(jnp.where(same & (lane < sub), 1, 0), axis=1, keepdims=True)

    def slot(expert, place):
        return jnp.where(place < z.main, expert * z.main + place, tokens + expert)

    slot_row = slot(row, place_row)
    slot_column = slot(column, place_column)
    by_slot = lax.broadcasted_iota(jnp.int32, (z.rows, tokens), 0) == slot_row
    lane = lax.broadcasted_iota(jnp.int32, (tokens, fold), 1)
    by_token = jnp.where(lane < tokens, lane, tokens + (lane - tokens) // 16) == slot_column
    token = lax.broadcasted_iota(jnp.int32, (tokens, fold), 0).astype(f32)
    token_row = jnp.sum(jnp.where(by_token, token - none, 0.0), axis=0, keepdims=True) + none
    return jnp.where(by_slot, 1.0, 0.0).astype(bf16), column, slot_column, token_row


def write_chunks(z, selector, rows_ref, ready, tiles, chunks):
    step = z.width // 2
    for half in range(2):
        ready[half].wait()
        col = half * step
        got = jnp.dot(selector, rows_ref[:, col : col + step], preferred_element_type=f32)
        packed = got[: z.tokens].astype(bf16)
        for k in range(z.experts):
            chunks[k][:, col : col + step] = packed[k * z.main : (k + 1) * z.main]
            pack_last(got[z.tokens + k : z.tokens + k + 1], tiles.at[k], half * z.pieces // 2)


def halves(z, source, target, sems, at):
    step = z.width // 2
    return [
        pltpu.make_async_copy(
            source.at[:, pl.ds(i * step, step)], target.at[:, pl.ds(i * step, step)], sems.at[at + i]
        )
        for i in range(2)
    ]


def forward_chunks(z, where, ids, act, held):
    def body(where, ids_any, act_any, held_any, *refs):
        *chunks, held, ids, rows, tiles, sems = refs
        first = pltpu.make_async_copy(ids_any, ids, sems.at[2])
        ready = halves(z, act_any, rows, sems, 0)
        extra = pltpu.make_async_copy(held_any, held, sems.at[3])
        for copy in [first, *ready, extra]:
            copy.start()
        tiles[...] = jnp.zeros_like(tiles)
        first.wait()
        selector, _, _, token_row = slot_matrices(ids[...], where[0], z)
        write_chunks(z, selector, rows, ready, tiles, chunks)
        for k in range(z.experts):
            tiles[k, z.pieces : z.pieces + 1, :] = token_row
            chunks[k][:, z.width :] = tiles[k].astype(bf16)
        extra.wait()

    *chunks, held = call(
        body,
        "shhh",
        [shape((z.main, z.wide))] * z.experts + [shape(held.shape)],
        [
            pltpu.VMEM((1, z.tokens), jnp.int32),
            pltpu.VMEM((z.tokens, z.width), bf16),
            pltpu.VMEM((z.experts, 16, fold), f32),
            pltpu.SemaphoreType.DMA((4,)),
        ],
        8,
        "forward_chunks",
    )(where, ids.reshape(1, z.tokens), act, held)
    return chunks, held


def two_parts(value):
    high = value.astype(bf16).astype(f32)
    return [high, (value - high).astype(bf16).astype(f32)]


def backward_chunks(z, where, ids, grad, act, gain, router):
    def body(where, ids_any, grad_any, act_ref, gain_any, router_any, *refs):
        *chunks, vectors, ids, rows, tiles, gain_ref, router_ref, sems = refs
        first = pltpu.make_async_copy(ids_any, ids, sems.at[2])
        ready = halves(z, grad_any, rows, sems, 0)
        tables = [
            pltpu.make_async_copy(gain_any, gain_ref, sems.at[3]),
            pltpu.make_async_copy(router_any.at[0], router_ref, sems.at[4]),
        ]
        for copy in [first, *tables, *ready]:
            copy.start()
        tiles[...] = jnp.zeros_like(tiles)
        first.wait()
        selector, column, slot_column, token_row = slot_matrices(ids[...], where[0], z)
        for copy in tables:
            copy.wait()
        gain = gain_ref[...].astype(f32)
        h = act_ref[...].astype(f32)
        normed, inv = norm_rows(h, gain)
        logits = lax.dot_general(normed, router_ref[...], nt, preferred_element_type=f32)
        expert = lax.broadcasted_iota(jnp.int32, logits.shape, 1)
        named = jnp.bitwise_xor(column, where[0])
        logit = jnp.sum(jnp.where(expert == named, logits, 0.0), axis=-1, keepdims=True)
        write_chunks(z, selector, rows, ready, tiles, chunks)
        centre = jnp.mean(rows[...].astype(f32) * h, axis=-1, keepdims=True)
        parts = two_parts(inv) + two_parts(jax.nn.sigmoid(logit)) + two_parts(centre)
        lane = lax.broadcasted_iota(jnp.int32, (z.tokens, fold), 1)
        token = lax.broadcasted_iota(jnp.int32, (z.tokens, fold), 0).astype(f32)
        values = jnp.zeros((z.tokens, fold), f32)
        for i, part in enumerate(parts):
            values = jnp.where(lane // 32 == i, part, values)
        place = lane % 32
        for k in range(z.experts):
            slot = jnp.where(place < z.main, k * z.main + place, z.tokens + k)
            mine = (slot == slot_column) & (place <= z.main)
            own_tokens = jnp.sum(jnp.where(mine, token - none, 0.0), axis=0, keepdims=True) + none
            scalars = jnp.sum(jnp.where(mine, values, 0.0), axis=0, keepdims=True)
            both = jnp.where(lane[0:1] < 128, token_row, own_tokens)
            tiles[k, z.pieces : z.pieces + 1, :] = both
            tiles[k, z.pieces + 1 : z.pieces + 2, :] = scalars
            chunks[k][:, z.width :] = tiles[k].astype(bf16)
        vectors[...] = jnp.zeros_like(vectors)
        vectors[0:1, :] = gain
        mine = lax.broadcasted_iota(jnp.int32, (z.experts, 1), 0) == where[0]
        table = jnp.where(mine, router_ref[...].astype(f32), 0.0)
        vectors[1:2, :] = jnp.sum(table, axis=0, keepdims=True)

    *chunks, vectors = call(
        body,
        "shhvhh",
        [shape((z.main, z.wide))] * z.experts + [shape((8, z.width), f32)],
        [
            pltpu.VMEM((1, z.tokens), jnp.int32),
            pltpu.VMEM((z.tokens, z.width), bf16),
            pltpu.VMEM((z.experts, 16, fold), f32),
            pltpu.VMEM((1, z.width), bf16),
            pltpu.VMEM((z.experts, z.width), bf16),
            pltpu.SemaphoreType.DMA((5,)),
        ],
        12,
        "backward_chunks",
    )(where, ids.reshape(1, z.tokens), grad, act, gain, router)
    return chunks, vectors


def collect_rows(z, chunks, last, tile, base=0):
    last[...] = jnp.zeros_like(last)
    for k in range(z.experts):
        unpack_last(chunks[k], z, tile, last, k, base)


def norm_rows(h, gain):
    inv = lax.rsqrt(jnp.mean(h * h, axis=-1, keepdims=True) + epsilon)
    return (h * inv * gain).astype(bf16), inv


def normed_rows(z, chunks, vectors):
    def body(*refs):
        chunks, (vectors, normed_ref, gates_ref, last, tile) = refs[: z.experts], refs[z.experts :]
        gain, router = vectors[0:1, :], vectors[1:2, :]
        collect_rows(z, chunks, last, tile)
        for k in range(z.experts + 1):
            h = last[...] if k == z.experts else chunks[k][:, : z.width].astype(f32)
            at = k * z.main
            normed, _ = norm_rows(h, gain)
            normed_ref[at : at + 16, :] = normed
            logits = jnp.sum(normed.astype(f32) * router, axis=-1, keepdims=True)
            gates_ref[at : at + 16, :] = jnp.broadcast_to(jax.nn.sigmoid(logits), (16, 128))

    return call(
        body,
        "v" * (z.experts + 1),
        [shape((z.rows, z.width)), shape((z.rows, 128), f32), shape((16, z.width), f32)],
        [pltpu.VMEM((16, fold), f32)],
        8,
        "normed_rows",
    )(*chunks, vectors)


def grad_rows_of(z, chunks, after):
    def body(*refs):
        chunks, (rows, last, inv_ref, affinity_ref, tile) = (
            refs[: z.experts],
            refs[z.experts + len(after) :],
        )
        for k in range(z.experts):
            rows[k * z.main : (k + 1) * z.main, :] = chunks[k][:, : z.width]
        collect_rows(z, chunks, last, tile)
        rows[z.tokens :, :] = last[...].astype(bf16)
        sub = lax.broadcasted_iota(jnp.int32, (16, fold), 0)
        lane = lax.broadcasted_iota(jnp.int32, (16, fold), 1)
        scalars = [
            chunk[:, z.width :].astype(f32)[z.pieces + 1 : z.pieces + 2, :] for chunk in chunks
        ]
        for first, out in ((0, inv_ref), (64, affinity_ref)):
            place = lane - first
            tail = jnp.zeros((16, fold), f32)
            for k in range(z.experts):
                mine = (place == sub) | (place == sub + 32)
                column = jnp.sum(jnp.where(mine, scalars[k], 0.0), axis=-1, keepdims=True)
                out[k * z.main : (k + 1) * z.main, :] = jnp.broadcast_to(column, (16, 128))
                mine = ((place == z.main) | (place == z.main + 32)) & (sub == k)
                tail = tail + jnp.where(mine, scalars[k], 0.0)
            column = jnp.sum(tail, axis=-1, keepdims=True)
            out[z.tokens :, :] = jnp.broadcast_to(column, (16, 128))

    return call(
        body,
        "v" * z.experts + "a" * len(after),
        [shape((z.rows, z.width)), shape((16, z.width), f32)] + [shape((z.rows, 128), f32)] * 2,
        [pltpu.VMEM((16, fold), f32)],
        8,
        "grad_rows",
    )(*chunks, *after)


def act_norms(z, act, after):
    def body(act_ref, *refs):
        h = act_ref[...].astype(f32)
        square = 1.0 / (jnp.mean(h * h, axis=-1, keepdims=True) + epsilon)
        refs[-1][...] = jnp.broadcast_to(square, (z.tokens, 128))

    return call(
        body,
        "v" + "a" * len(after),
        shape((z.tokens, 128), f32),
        [],
        8,
        "act_norms",
    )(act, *after)


def write_parts(z, values, outs, col):
    values = values.astype(bf16)
    for m in range(z.split):
        outs[m][:, col : col + values.shape[1]] = values[m * z.rows : (m + 1) * z.rows]


def experts_forward(z, rows, w_gate, w_down, after):
    def body(*refs):
        rows, (gate_ref, down_ref), outs = (
            refs[: z.split],
            refs[z.split : z.split + 2],
            refs[z.split + 2 + len(after) :],
        )
        held = jnp.concatenate([part[...] for part in rows], axis=0)
        gate_proj = jnp.dot(held, gate_ref[0], preferred_element_type=f32)
        hidden = jax.nn.silu(gate_proj).astype(bf16)
        step = 512
        for col in range(0, z.width, step):
            part = jnp.dot(hidden, down_ref[0, :, col : col + step], preferred_element_type=f32)
            write_parts(z, part, outs, col)

    return call(
        body,
        "v" * (z.split + 2) + "a" * len(after),
        [shape((z.rows, z.width))] * z.split,
        [],
        16,
        "experts_forward",
    )(*rows, w_gate, w_down, *after)


def saved_terms(z, where, saved, after):
    total, slots, width = z.split * z.rows, saved.shape[2], saved.shape[3]

    def body(where, saved_any, *refs):
        hidden_ref, slope_ref, saved_ref, sem = refs[len(after) :]
        copy = pltpu.make_async_copy(saved_any.at[0, 0], saved_ref, sem)
        copy.start()
        row = lax.broadcasted_iota(jnp.int32, (total, slots), 0)
        slot = lax.broadcasted_iota(jnp.int32, (total, slots), 1)
        m, at = row // z.rows, row % z.rows
        is_main = at < z.tokens
        k = jnp.where(is_main, at // z.main, at - z.tokens)
        p = jnp.where(is_main, at % z.main, z.main)
        source = jnp.bitwise_xor(k, where[0]) * z.split + jnp.bitwise_xor(m, where[1])
        wanted = jnp.where(k < z.experts, source * z.cap + p, -1)
        selector = jnp.where(slot == wanted, 1.0, 0.0).astype(bf16)
        copy.wait()
        gate_proj = jnp.dot(selector, saved_ref[...], preferred_element_type=f32)
        sg = jax.nn.sigmoid(gate_proj)
        hidden_ref[...] = (gate_proj * sg).astype(bf16)
        slope_ref[...] = sg * (1.0 + gate_proj * (1.0 - sg))

    return call(
        body,
        "sh" + "a" * len(after),
        [shape((total, width)), shape((total, width), f32)],
        [pltpu.VMEM((slots, width), bf16), pltpu.SemaphoreType.DMA],
        8,
        "saved_terms",
    )(where, saved, *after)


def experts_backward(z, rows, hidden, slope, w_gate, w_down, after):
    def body(*refs):
        rows = refs[: z.split]
        hidden_ref, slope_ref, gate_ref, down_ref = refs[z.split : z.split + 4]
        outs = refs[z.split + 4 + len(after) :]
        held = jnp.concatenate([part[...] for part in rows], axis=0)
        grad_hidden = lax.dot_general(held, down_ref[0], nt, preferred_element_type=f32)
        dots = jnp.sum(grad_hidden * hidden_ref[...].astype(f32), axis=-1, keepdims=True)
        grad_gate = (grad_hidden * slope_ref[...]).astype(bf16)
        step = 512
        for col in range(0, z.width, step):
            part = lax.dot_general(
                grad_gate, gate_ref[0, col : col + step, :], nt, preferred_element_type=f32
            )
            write_parts(z, part, outs, col)
        write_parts(z, jnp.broadcast_to(dots, (dots.shape[0], 128)), outs, z.width)

    return call(
        body,
        "v" * (z.split + 4) + "a" * len(after),
        [shape((z.rows, z.width + 128))] * z.split,
        [],
        16,
        "experts_backward",
    )(*rows, hidden, slope, w_gate, w_down, *after)


def put_last(z, values, source_chunk, tile, out):
    tile[...] = source_chunk[:, z.width :].astype(f32)
    pack_last(values, tile)
    out[:, z.width :] = tile[...].astype(bf16)


def finish_forward(z, ks, chunks, last, parts, gates, after):
    count = len(ks)

    def body(*refs):
        chunks, last, parts = refs[:count], refs[count], refs[count + 1 : count + 1 + z.split]
        gates, outs, tile = refs[count + 1 + z.split], refs[-1 - count : -1], refs[-1]

        def mixed(at):
            y = parts[0][at : at + 16, :].astype(f32)
            for part in parts[1:]:
                y = y + part[at : at + 16, :].astype(f32)
            return route_scale * (gates[at : at + 16, 0:1] * y)

        tail = last[...] + mixed(z.tokens)
        for k, chunk, out in zip(ks, chunks, outs):
            h = chunk[:, : z.width].astype(f32)
            out[:, : z.width] = (h + mixed(k * z.main)).astype(bf16)
            put_last(z, tail[k : k + 1, :], chunk, tile, out)

    return call(
        body,
        "v" * (count + z.split + 2) + "a" * len(after),
        [shape((z.main, z.wide))] * count,
        [pltpu.VMEM((16, fold), f32)],
        8,
        "finish_forward_" + "".join(map(str, ks)),
    )(*[chunks[k] for k in ks], last, *parts, gates, *after)


def finish_backward(z, order, chunks, last, terms, parts, vectors, after):
    def body(*refs):
        e = z.experts
        chunks, (last, inv_ref, affinity_ref) = refs[:e], refs[e : e + 3]
        parts, vectors = refs[e + 3 : e + 3 + z.split], refs[e + 3 + z.split]
        outs, (tile,) = refs[-1 - e : -1], refs[-1:]
        gain, router = vectors[0:1, :], vectors[1:2, :]
        gain_router = gain * router

        def finished(g, at):
            inv, affinity = inv_ref[at : at + 16, 0:1], affinity_ref[at : at + 16, 0:1]
            rows = parts[0][at : at + 16, : z.width].astype(f32)
            dot = parts[0][at : at + 16, z.width :].astype(f32)
            for part in parts[1:]:
                rows = rows + part[at : at + 16, : z.width].astype(f32)
                dot = dot + part[at : at + 16, z.width :].astype(f32)
            dot = dot[:, 0:1]
            grad_logits = (route_scale * dot * affinity * (1.0 - affinity)).astype(bf16).astype(f32)
            rows = rows * gain * (inv * route_scale * affinity)
            return g + (rows + gain_router * (inv * grad_logits))

        tail = finished(last[...], z.tokens)
        for k, out in zip(order, outs):
            g = chunks[k][:, : z.width].astype(f32)
            out[:, : z.width] = finished(g, k * z.main).astype(bf16)
            put_last(z, tail[k : k + 1, :], chunks[k], tile, out)

    return call(
        body,
        "v" * (z.experts + z.split + 4) + "a" * len(after),
        [shape((z.main, z.wide))] * z.experts,
        [pltpu.VMEM((16, fold), f32)],
        8,
        "finish_backward",
    )(*chunks, last, *terms, *parts, vectors, *after)


def order_matrices(z, chunks):
    lanes = z.tokens + 16 * z.experts
    tiles = [chunk[:, z.width :] for chunk in chunks]
    token_row = tiles[0].astype(f32)[z.pieces : z.pieces + 1, :lanes]
    token = lax.broadcasted_iota(jnp.int32, (z.tokens, lanes), 0).astype(f32)
    lane = lax.broadcasted_iota(jnp.int32, (z.tokens, lanes), 1)
    piece = jnp.where(lane < z.tokens, -1, lane % 16)
    ours = token == token_row
    for i in range(z.pieces):
        cols = pl.ds(i * fold, fold)
        selector = jnp.where(ours & ((piece < 0) | (piece == i)), 1.0, 0.0).astype(bf16)
        rows = jnp.concatenate([chunk[:, cols] for chunk in chunks] + tiles, axis=0)
        yield cols, jnp.dot(selector, rows, preferred_element_type=f32)


def write_out(z, out, out_any, sems, steps):
    width = z.width // steps
    copies = []

    def next_copy():
        cols = pl.ds(len(copies) * width, width)
        copy = pltpu.make_async_copy(out.at[:, cols], out_any.at[:, cols], sems.at[len(copies)])
        copy.start()
        copies.append(copy)

    return copies, next_copy


def order_forward(z, chunks):
    steps = 7 if z.pieces % 7 == 0 else z.pieces

    def body(*refs):
        chunks, (out_any, out, sems) = refs[: z.experts], refs[z.experts :]
        copies, next_copy = write_out(z, out, out_any, sems, steps)
        for i, (cols, rows) in enumerate(order_matrices(z, chunks)):
            out[:, cols] = rows.astype(bf16)
            if (i + 1) % (z.pieces // steps) == 0:
                next_copy()
        for copy in copies:
            copy.wait()

    return call(
        body,
        "v" * z.experts,
        shape((z.tokens, z.width)),
        [pltpu.VMEM((z.tokens, z.width), bf16), pltpu.SemaphoreType.DMA((steps,))],
        8,
        "forward_rows",
        spaces["a"],
    )(*chunks)


def order_backward(z, chunks, act, squares):
    steps = 7 if z.pieces % 7 == 0 else z.pieces

    def body(*refs):
        chunks = refs[: z.experts]
        act, squares, out_any, out, held, sems = refs[z.experts :]
        copies, next_copy = write_out(z, out, out_any, sems, steps)
        total = jnp.zeros((z.tokens, fold), f32)
        for cols, rows in order_matrices(z, chunks):
            held[:, cols] = rows
            total = total + rows * act[:, cols].astype(f32)
        lanes = pl.ds(z.width + 128, 128)
        token = lax.broadcasted_iota(jnp.int32, (z.tokens, 128), 0).astype(f32)
        lane = lax.broadcasted_iota(jnp.int32, (z.tokens, 128), 1)
        centre = jnp.zeros((z.tokens, 128), f32)
        for chunk in chunks:
            tile = chunk[:, lanes].astype(f32)
            mine = (tile[z.pieces : z.pieces + 1, :] == token) & (lane < 64)
            centre = centre + jnp.where(mine, tile[z.pieces + 1 : z.pieces + 2, :], 0.0)
        mean = jnp.sum(total, axis=-1, keepdims=True) * (1.0 / z.width)
        scale = squares[:, 0:1] * (mean - jnp.sum(centre, axis=-1, keepdims=True))
        width = z.width // steps
        for i in range(steps):
            cols = pl.ds(i * width, width)
            out[:, cols] = (held[:, cols] - act[:, cols].astype(f32) * scale).astype(bf16)
            next_copy()
        for copy in copies:
            copy.wait()

    return call(
        body,
        "v" * (z.experts + 2),
        shape((z.tokens, z.width)),
        [
            pltpu.VMEM((z.tokens, z.width), bf16),
            pltpu.VMEM((z.tokens, z.width), f32),
            pltpu.SemaphoreType.DMA((steps,)),
        ],
        8,
        "backward_rows",
        spaces["a"],
    )(*chunks, act, squares)


def dispatch(z, chunks):
    groups = z.experts * z.split
    got = [chunks[0]] + [None] * (z.experts - 1)
    for k in reversed(range(1, z.experts)):
        pairs = [(i, ((i // z.split) ^ k) * z.split + i % z.split) for i in range(groups)]
        got[k] = lax.ppermute(chunks[k], "ep", pairs)
    return got


def to_core(z, array, m):
    groups = z.experts * z.split
    pairs = [(i, i // z.split * z.split + ((i % z.split) ^ m)) for i in range(groups)]
    return lax.ppermute(array, "ep", pairs)


def to_section(z, chunk, k, by):
    groups = z.experts * z.split
    sections = lax.axis_size("pp")
    pairs = [
        (s * groups + i, (s + by) % sections * groups + ((i // z.split) ^ k) * z.split + i % z.split)
        for s in range(sections)
        for i in range(groups)
    ]
    return lax.ppermute(chunk, ("pp", "ep"), pairs)


def on_device(
    fwd_act, fwd_ids, bwd_act, bwd_ids, bwd_grad, norm_gain, router, w_gate, w_down, saved_gate
):
    groups = lax.axis_size("ep")
    assert fwd_ids.shape[1] == 1
    z = Sizes(groups, router.shape[2], fwd_act.shape[0], fwd_act.shape[1])
    index = lax.axis_index("ep")
    where = jnp.stack([index // z.split, index % z.split]).astype(jnp.int32)
    router = jnp.swapaxes(router, 1, 2)
    others = range(1, z.split)

    fwd_chunks, held = forward_chunks(z, where, fwd_ids, fwd_act, bwd_act)
    fwd_own = dispatch(z, fwd_chunks)
    next_act = to_section(z, held, 0, -1)
    bwd_chunks, vectors = backward_chunks(z, where, bwd_ids, bwd_grad, held, norm_gain, router)
    bwd_own = dispatch(z, bwd_chunks)

    normed, gates, fwd_last = normed_rows(z, fwd_own, vectors)
    fwd_all = [normed] + [to_core(z, normed, m) for m in others]
    hidden, slope = saved_terms(z, where, saved_gate, [gates])
    fwd_parts = experts_forward(z, fwd_all, w_gate, w_down, [hidden])
    grads, grad_last, inv, affinity = grad_rows_of(z, bwd_own, [fwd_parts[0]])
    grad_all = [grads] + [to_core(z, grads, m) for m in others]
    fwd_parts = [fwd_parts[0]] + [to_core(z, fwd_parts[m], m) for m in others]
    fwd_done = {}

    def finish(ks, after):
        outs = finish_forward(z, ks, fwd_own, fwd_last, fwd_parts, gates, after)
        for k, out in zip(ks, outs):
            fwd_done[k] = to_section(z, out, k, 1)
        return outs[0]

    order = [*range(z.experts - 1, 0, -1), 0]
    first = finish(order[:2], [grads, next_act])
    bwd_parts = experts_backward(z, grad_all, hidden, slope, w_gate, w_down, [first])
    squares = act_norms(z, next_act, [bwd_parts[0], *fwd_done.values()])
    second = finish(order[2:], [squares])
    bwd_parts = [bwd_parts[0]] + [to_core(z, bwd_parts[m], m) for m in others]
    bwd_out = finish_backward(
        z, order, bwd_own, grad_last, [inv, affinity], bwd_parts, vectors, [second]
    )
    bwd_done = {k: to_section(z, out, k, -1) for k, out in zip(order, bwd_out)}
    return (
        order_forward(z, [fwd_done[k] for k in range(z.experts)]),
        order_backward(z, [bwd_done[k] for k in range(z.experts)], next_act, squares),
    )


def solution(mesh):
    return jax.shard_map(
        on_device,
        mesh=mesh,
        in_specs=(
            P(("pp", "ep"), None),
            P(("pp", "ep"), None),
            P(("pp", "ep"), None),
            P(("pp", "ep"), None),
            P(("pp", "ep"), None),
            P("pp", None),
            P("pp", None, None),
            P(("pp", "ep"), None, None),
            P(("pp", "ep"), None, None),
            P("pp", "ep", None, None),
        ),
        out_specs=(P(("pp", "ep"), None), P(("pp", "ep"), None)),
        check_vma=False,
    )
```

```python
import jax
import jax.numpy as jnp
from jax import lax
from jax.experimental import pallas as pl
from jax.experimental.pallas import tpu as pltpu
from jax.sharding import PartitionSpec as P

epsilon = 1e-06
route_scale = 2.5
fold = 256
none = 255.0
f32 = jnp.float32
bf16 = jnp.bfloat16
nt = (((1,), (1,)), ((), ()))
spaces = {
    "s": pl.BlockSpec(memory_space=pltpu.SMEM),
    "v": pl.BlockSpec(memory_space=pltpu.VMEM),
    "a": pl.BlockSpec(memory_space=pl.ANY),
    "h": pl.BlockSpec(memory_space=pltpu.HBM),
}


cost = {
    "backward_chunks": 10,
    "later": 15,
    "saved_terms": 15,
    "act_norms": 15,
    "act_gates": 15,
}


def call(body, places, outs, scratch, megabytes, name, out_specs=None):
    def run(*arrays):
        arrays = [
            pltpu.with_memory_space_constraint(array, pltpu.HBM) if place == "h" else array
            for array, place in zip(arrays, places, strict=True)
        ]
        return kernel(*arrays)

    where_to = {} if out_specs is None else {"out_specs": out_specs}
    kernel = pl.pallas_call(
        body,
        out_shape=outs,
        in_specs=[spaces[place] for place in places],
        **where_to,
        scratch_shapes=scratch,
        compiler_params=pltpu.CompilerParams(vmem_limit_bytes=megabytes * 1024 * 1024),
        cost_estimate=pl.CostEstimate(
            flops=int(cost.get(name, 0.1) * 1e9), bytes_accessed=1000, transcendentals=0
        ),
        name=name,
    )
    return run


def shape(dims, kind=bf16):
    return jax.ShapeDtypeStruct(dims, kind)


class Sizes:
    def __init__(self, groups, experts, tokens, width):
        self.experts = experts
        self.split = groups // experts
        self.tokens = tokens
        self.width = width
        self.main = tokens // experts
        self.cap = self.main + 1
        self.pieces = width // fold
        self.wide = width + fold
        self.rows = tokens + 16
        self.order = [experts - 1, *range(1, experts - 1), 0]
        assert self.main == 16 and self.pieces <= 14 and width % fold == 0
        assert experts <= 8 and experts & (experts - 1) == 0 and self.split & (self.split - 1) == 0


def pack_last(row, tile, first=0):
    for i in range(row.shape[1] // fold):
        tile[first + i : first + i + 1, :] = row[:, i * fold : (i + 1) * fold]


def unpack_last(chunk, z, tile, target, at, base=0):
    tile[...] = chunk[base : base + 16, z.width :].astype(f32)
    for i in range(z.pieces):
        target[at : at + 1, i * fold : (i + 1) * fold] = tile[i : i + 1, :]


def slot_matrices(ids_row, block, z):
    tokens = z.tokens
    sub = lax.broadcasted_iota(jnp.int32, (tokens, tokens), 0)
    lane = lax.broadcasted_iota(jnp.int32, (tokens, tokens), 1)
    row = jnp.bitwise_xor(ids_row, block)
    column = jnp.sum(jnp.where(sub == lane, row, 0), axis=1, keepdims=True)
    same = column == row
    place_row = jnp.sum(jnp.where(same & (sub < lane), 1, 0), axis=0, keepdims=True)
    place_column = jnp.sum(jnp.where(same & (lane < sub), 1, 0), axis=1, keepdims=True)

    def slot(expert, place):
        return jnp.where(place < z.main, expert * z.main + place, tokens + expert)

    slot_row = slot(row, place_row)
    slot_column = slot(column, place_column)
    by_slot = lax.broadcasted_iota(jnp.int32, (z.rows, tokens), 0) == slot_row
    lane = lax.broadcasted_iota(jnp.int32, (tokens, fold), 1)
    by_token = jnp.where(lane < tokens, lane, tokens + (lane - tokens) // 16) == slot_column
    token = lax.broadcasted_iota(jnp.int32, (tokens, fold), 0).astype(f32)
    token_row = jnp.sum(jnp.where(by_token, token - none, 0.0), axis=0, keepdims=True) + none
    return jnp.where(by_slot, 1.0, 0.0).astype(bf16), token_row


def write_chunks(z, selector, token_row, rows_ref, ready, tiles, chunks, base):
    step = z.width // 2
    tiles[...] = jnp.zeros_like(tiles)
    for half in range(2):
        ready[half].wait()
        col = half * step
        got = jnp.dot(selector, rows_ref[:, col : col + step], preferred_element_type=f32)
        packed = got[: z.tokens].astype(bf16)
        for k in range(z.experts):
            chunks[k][base : base + 16, col : col + step] = packed[k * z.main : (k + 1) * z.main]
            pack_last(got[z.tokens + k : z.tokens + k + 1], tiles.at[k], half * z.pieces // 2)
    for k in range(z.experts):
        tiles[k, z.pieces : z.pieces + 1, :] = token_row
        chunks[k][base : base + 16, z.width :] = tiles[k].astype(bf16)


def make_chunks(z, where, ids, sources, tables, after, name):
    count = len(sources)

    def body(where, ids_any, *refs):
        anys, tables_any = refs[:count], refs[count : count + len(tables)]
        outs, held = refs[count + len(tables) + len(after) :], ()
        if tables:
            *outs, gain_ref, router_ref, ids, rows, tiles, sems = outs
            *outs, vectors = outs
            held = (gain_ref, router_ref)
        else:
            *outs, ids, rows, tiles, sems = outs
        copies = [pltpu.make_async_copy(ids_any, ids, sems.at[2 * count])]
        step = z.width // 2
        for j in range(count):
            for half in range(2):
                cols = pl.ds(half * step, step)
                copies.append(
                    pltpu.make_async_copy(
                        anys[j].at[:, cols], rows.at[j, :, cols], sems.at[2 * j + half]
                    )
                )
        for i, (source, target) in enumerate(zip(tables_any, held)):
            copies.append(pltpu.make_async_copy(source, target, sems.at[2 * count + 1 + i]))
        for copy in copies:
            copy.start()
        copies[0].wait()
        selector, token_row = slot_matrices(ids[...], where[0], z)
        for j in range(count):
            ready = copies[1 + 2 * j : 3 + 2 * j]
            write_chunks(z, selector, token_row, rows.at[j], ready, tiles, outs, 16 * j)
        if tables:
            for copy in copies[1 + 2 * count :]:
                copy.wait()
            vectors[...] = jnp.zeros_like(vectors)
            vectors[0:1, :] = gain_ref[...].astype(f32)
            mine = lax.broadcasted_iota(jnp.int32, (z.experts, 1), 0) == where[0]
            table = jnp.where(mine, router_ref[0].astype(f32), 0.0)
            vectors[1:2, :] = jnp.sum(table, axis=0, keepdims=True)

    return call(
        body,
        "sh" + "h" * (count + len(tables)) + "a" * len(after),
        [shape((z.main * count, z.wide))] * z.experts
        + [shape((8, z.width), f32) for _ in tables[:1]],
        [pltpu.VMEM(table.shape, bf16) for table in tables]
        + [
            pltpu.VMEM((1, z.tokens), jnp.int32),
            pltpu.VMEM((count, z.tokens, z.width), bf16),
            pltpu.VMEM((z.experts, 16, fold), f32),
            pltpu.SemaphoreType.DMA((2 * count + 1 + len(tables),)),
        ],
        8,
        name,
    )(where, ids.reshape(1, z.tokens), *sources, *tables, *after)


def later(chunk, weights, after):
    def body(chunk, *refs):
        refs[-1][...] = chunk[...]

    places = "v" + "v" * len(weights) + "a" * len(after)
    return call(body, places, shape(chunk.shape), [], 8, "later")(chunk, *weights, *after)


def collect_rows(z, chunks, last, tile, base=0):
    last[...] = jnp.zeros_like(last)
    for k in range(z.experts):
        unpack_last(chunks[k], z, tile, last, k, base)


def norm_rows(h, gain):
    inv = lax.rsqrt(jnp.mean(h * h, axis=-1, keepdims=True) + epsilon)
    return (h * inv * gain).astype(bf16), inv


def normed_rows(z, chunks, vectors):
    order = z.order

    def body(*refs):
        chunks, (vectors, normed_ref, gates_ref, last, tile) = refs[: z.experts], refs[z.experts :]
        chunks = [chunks[order.index(k)] for k in range(z.experts)]
        gain, router = vectors[0:1, :], vectors[1:2, :]
        collect_rows(z, chunks, last, tile)
        for k in range(z.experts + 1):
            h = last[...] if k == z.experts else chunks[k][:, : z.width].astype(f32)
            at = k * z.main
            normed, _ = norm_rows(h, gain)
            normed_ref[at : at + 16, :] = normed
            logits = jnp.sum(normed.astype(f32) * router, axis=-1, keepdims=True)
            gates_ref[at : at + 16, :] = jnp.broadcast_to(jax.nn.sigmoid(logits), (16, 128))

    return call(
        body,
        "v" * (z.experts + 1),
        [shape((z.rows, z.width)), shape((z.rows, 128), f32), shape((16, z.width), f32)],
        [pltpu.VMEM((16, fold), f32)],
        8,
        "normed_rows",
    )(*[chunks[k] for k in order], vectors)


def grad_rows_of(z, chunks, after):
    def body(*refs):
        chunks, (rows, last, tile) = refs[: z.experts], refs[z.experts + len(after) :]
        for k in range(z.experts):
            rows[k * z.main : (k + 1) * z.main, :] = chunks[k][:16, : z.width]
        collect_rows(z, chunks, last, tile)
        rows[z.tokens :, :] = last[...].astype(bf16)

    return call(
        body,
        "v" * z.experts + "a" * len(after),
        [shape((z.rows, z.width)), shape((16, z.width), f32)],
        [pltpu.VMEM((16, fold), f32)],
        8,
        "grad_rows",
    )(*chunks, *after)


def act_norms(z, chunks, after):
    def body(*refs):
        chunks, (inv_ref, last, tile) = refs[: z.experts], refs[z.experts + len(after) :]
        collect_rows(z, chunks, last, tile, 16)
        for k in range(z.experts + 1):
            h = last[...] if k == z.experts else chunks[k][16:32, : z.width].astype(f32)
            at = k * z.main
            inv = lax.rsqrt(jnp.mean(h * h, axis=-1, keepdims=True) + epsilon)
            inv_ref[at : at + 16, :] = jnp.broadcast_to(inv, (16, 128))

    return call(
        body,
        "v" * z.experts + "a" * len(after),
        [shape((z.rows, 128), f32), shape((16, z.width), f32)],
        [pltpu.VMEM((16, fold), f32)],
        8,
        "act_norms",
    )(*chunks, *after)


def act_gates(z, chunks, last, inv, vectors, after):
    def body(*refs):
        chunks, (last, inv_ref, vectors) = refs[: z.experts], refs[z.experts : z.experts + 3]
        affinity_ref = refs[-1]
        gain, router = vectors[0:1, :], vectors[1:2, :]
        for k in range(z.experts + 1):
            h = last[...] if k == z.experts else chunks[k][16:32, : z.width].astype(f32)
            at = k * z.main
            normed = (h * inv_ref[at : at + 16, 0:1] * gain).astype(bf16).astype(f32)
            logits = jnp.sum(normed * router, axis=-1, keepdims=True)
            affinity_ref[at : at + 16, :] = jnp.broadcast_to(jax.nn.sigmoid(logits), (16, 128))

    return call(
        body,
        "v" * (z.experts + 3) + "a" * len(after),
        shape((z.rows, 128), f32),
        [],
        8,
        "act_gates",
    )(*chunks, last, inv, vectors, *after)


def write_parts(z, values, outs, col):
    values = values.astype(bf16)
    for m in range(z.split):
        outs[m][:, col : col + values.shape[1]] = values[m * z.rows : (m + 1) * z.rows]


def experts_forward(z, rows, w_gate, w_down, after):
    def body(*refs):
        rows, (gate_ref, down_ref), outs = (
            refs[: z.split],
            refs[z.split : z.split + 2],
            refs[z.split + 2 + len(after) :],
        )
        held = jnp.concatenate([part[...] for part in rows], axis=0)
        gate_proj = jnp.dot(held, gate_ref[0], preferred_element_type=f32)
        hidden = jax.nn.silu(gate_proj).astype(bf16)
        step = 512
        for col in range(0, z.width, step):
            part = jnp.dot(hidden, down_ref[0, :, col : col + step], preferred_element_type=f32)
            write_parts(z, part, outs, col)

    return call(
        body,
        "v" * (z.split + 2) + "a" * len(after),
        [shape((z.rows, z.width))] * z.split,
        [],
        16,
        "experts_forward",
    )(*rows, w_gate, w_down, *after)


def saved_terms(z, where, saved, after):
    total, slots, width = z.split * z.rows, saved.shape[2], saved.shape[3]

    def body(where, saved_any, *refs):
        hidden_ref, slope_ref, saved_ref, sem = refs[len(after) :]
        copy = pltpu.make_async_copy(saved_any.at[0, 0], saved_ref, sem)
        copy.start()
        row = lax.broadcasted_iota(jnp.int32, (total, slots), 0)
        slot = lax.broadcasted_iota(jnp.int32, (total, slots), 1)
        m, at = row // z.rows, row % z.rows
        is_main = at < z.tokens
        k = jnp.where(is_main, at // z.main, at - z.tokens)
        p = jnp.where(is_main, at % z.main, z.main)
        source = jnp.bitwise_xor(k, where[0]) * z.split + jnp.bitwise_xor(m, where[1])
        wanted = jnp.where(k < z.experts, source * z.cap + p, -1)
        selector = jnp.where(slot == wanted, 1.0, 0.0).astype(bf16)
        copy.wait()
        gate_proj = jnp.dot(selector, saved_ref[...], preferred_element_type=f32)
        sg = jax.nn.sigmoid(gate_proj)
        hidden_ref[...] = (gate_proj * sg).astype(bf16)
        slope_ref[...] = sg * (1.0 + gate_proj * (1.0 - sg))

    return call(
        body,
        "sh" + "a" * len(after),
        [shape((total, width)), shape((total, width), f32)],
        [pltpu.VMEM((slots, width), bf16), pltpu.SemaphoreType.DMA],
        8,
        "saved_terms",
    )(where, saved, *after)


def experts_backward(z, rows, hidden, slope, w_gate, w_down, after):
    def body(*refs):
        rows = refs[: z.split]
        hidden_ref, slope_ref, gate_ref, down_ref = refs[z.split : z.split + 4]
        outs = refs[z.split + 4 + len(after) :]
        held = jnp.concatenate([part[...] for part in rows], axis=0)
        grad_hidden = lax.dot_general(held, down_ref[0], nt, preferred_element_type=f32)
        dots = jnp.sum(grad_hidden * hidden_ref[...].astype(f32), axis=-1, keepdims=True)
        grad_gate = (grad_hidden * slope_ref[...]).astype(bf16)
        step = 512
        for col in range(0, z.width, step):
            part = lax.dot_general(
                grad_gate, gate_ref[0, col : col + step, :], nt, preferred_element_type=f32
            )
            write_parts(z, part, outs, col)
        write_parts(z, jnp.broadcast_to(dots, (dots.shape[0], 128)), outs, z.width)

    return call(
        body,
        "v" * (z.split + 4) + "a" * len(after),
        [shape((z.rows, z.width + 128))] * z.split,
        [],
        16,
        "experts_backward",
    )(*rows, hidden, slope, w_gate, w_down, *after)


def put_last(z, values, source_chunk, tile, out):
    tile[...] = jnp.zeros_like(tile)
    pack_last(values, tile)
    tokens = source_chunk[:16, z.width :].astype(f32)
    tile[z.pieces : z.pieces + 1, :] = tokens[z.pieces : z.pieces + 1, :]
    out[:, z.width :] = tile[...].astype(bf16)


def finish_forward(z, ks, chunks, last, parts, gates, after):
    count = len(ks)

    def body(*refs):
        chunks, last, parts = refs[:count], refs[count], refs[count + 1 : count + 1 + z.split]
        gates, outs, tile = refs[count + 1 + z.split], refs[-1 - count : -1], refs[-1]

        def mixed(at):
            y = parts[0][at : at + 16, :].astype(f32)
            for part in parts[1:]:
                y = y + part[at : at + 16, :].astype(f32)
            return route_scale * (gates[at : at + 16, 0:1] * y)

        tail = last[...] + mixed(z.tokens)
        for k, chunk, out in zip(ks, chunks, outs):
            h = chunk[:, : z.width].astype(f32)
            out[:, : z.width] = (h + mixed(k * z.main)).astype(bf16)
            put_last(z, tail[k : k + 1, :], chunk, tile, out)

    return call(
        body,
        "v" * (count + z.split + 2) + "a" * len(after),
        [shape((z.main, z.wide))] * count,
        [pltpu.VMEM((16, fold), f32)],
        8,
        "finish_forward_" + "".join(map(str, ks)),
    )(*[chunks[k] for k in ks], last, *parts, gates, *after)


def finish_backward(z, order, chunks, lasts, terms, parts, vectors, after):
    def body(*refs):
        e = z.experts
        chunks, (last_grad, last_act, inv_ref, affinity_ref) = refs[:e], refs[e : e + 4]
        parts, vectors = refs[e + 4 : e + 4 + z.split], refs[e + 4 + z.split]
        outs, (tile,) = refs[-1 - e : -1], refs[-1:]
        outs = [outs[order.index(k)] for k in range(e)]
        gain, router = vectors[0:1, :], vectors[1:2, :]

        def finished(h, g, at):
            inv, affinity = inv_ref[at : at + 16, 0:1], affinity_ref[at : at + 16, 0:1]
            rows = parts[0][at : at + 16, : z.width].astype(f32)
            dot = parts[0][at : at + 16, z.width :].astype(f32)
            for part in parts[1:]:
                rows = rows + part[at : at + 16, : z.width].astype(f32)
                dot = dot + part[at : at + 16, z.width :].astype(f32)
            dot = dot[:, 0:1]
            grad_logits = (route_scale * dot * affinity * (1.0 - affinity)).astype(bf16).astype(f32)
            grad_pre = (route_scale * affinity * rows + grad_logits * router) * gain
            centre = jnp.mean(grad_pre * h, axis=-1, keepdims=True)
            return g + inv * (grad_pre - h * (inv * inv * centre))

        tail = finished(last_act[...], last_grad[...], z.tokens)
        for k in range(e):
            g = chunks[k][:16, : z.width].astype(f32)
            h = chunks[k][16:32, : z.width].astype(f32)
            outs[k][:, : z.width] = finished(h, g, k * z.main).astype(bf16)
            put_last(z, tail[k : k + 1, :], chunks[k], tile, outs[k])

    return call(
        body,
        "v" * (z.experts + z.split + 5) + "a" * len(after),
        [shape((z.main, z.wide))] * z.experts,
        [pltpu.VMEM((16, fold), f32)],
        8,
        "finish_backward",
    )(*chunks, *lasts, *terms, *parts, vectors, *after)


def order_rows(z, chunks, name):
    order = z.order
    lanes = z.tokens + 16 * z.experts
    steps = 7 if z.pieces % 7 == 0 else z.pieces

    def body(*refs):
        chunks, (out_any, out, sems) = refs[: z.experts], refs[z.experts :]
        chunks = [chunks[order.index(k)] for k in range(z.experts)]
        tiles = [chunk[:, z.width :] for chunk in chunks]
        token_row = tiles[0].astype(f32)[z.pieces : z.pieces + 1, :lanes]
        token = lax.broadcasted_iota(jnp.int32, (z.tokens, lanes), 0).astype(f32)
        lane = lax.broadcasted_iota(jnp.int32, (z.tokens, lanes), 1)
        piece = jnp.where(lane < z.tokens, -1, lane % 16)
        ours = token == token_row
        copies = []
        for i in range(z.pieces):
            cols = pl.ds(i * fold, fold)
            mine = ours & ((piece < 0) | (piece == i))
            selector = jnp.where(mine, 1.0, 0.0).astype(bf16)
            rows = jnp.concatenate([chunk[:, cols] for chunk in chunks] + tiles, axis=0)
            out[:, cols] = jnp.dot(selector, rows, preferred_element_type=f32).astype(bf16)
            if (i + 1) % (z.pieces // steps) == 0:
                done = pl.ds((i + 1) * fold - z.width // steps, z.width // steps)
                copy = pltpu.make_async_copy(out.at[:, done], out_any.at[:, done], sems.at[len(copies)])
                copy.start()
                copies.append(copy)
        for copy in copies:
            copy.wait()

    return call(
        body,
        "v" * z.experts,
        shape((z.tokens, z.width)),
        [pltpu.VMEM((z.tokens, z.width), bf16), pltpu.SemaphoreType.DMA((steps,))],
        8,
        name,
        spaces["a"],
    )(*[chunks[k] for k in order])


def dispatch(z, chunks):
    groups = z.experts * z.split
    got = [chunks[0]] + [None] * (z.experts - 1)
    for k in reversed(range(1, z.experts)):
        pairs = [(i, ((i // z.split) ^ k) * z.split + i % z.split) for i in range(groups)]
        got[k] = lax.ppermute(chunks[k], "ep", pairs)
    return got


def to_core(z, array, m):
    groups = z.experts * z.split
    pairs = [(i, i // z.split * z.split + ((i % z.split) ^ m)) for i in range(groups)]
    return lax.ppermute(array, "ep", pairs)


def to_section(z, chunk, k, by):
    groups = z.experts * z.split
    sections = lax.axis_size("pp")
    pairs = [
        (s * groups + i, (s + by) % sections * groups + ((i // z.split) ^ k) * z.split + i % z.split)
        for s in range(sections)
        for i in range(groups)
    ]
    return lax.ppermute(chunk, ("pp", "ep"), pairs)


def on_device(
    fwd_act, fwd_ids, bwd_act, bwd_ids, bwd_grad, norm_gain, router, w_gate, w_down, saved_gate
):
    groups = lax.axis_size("ep")
    assert fwd_ids.shape[1] == 1
    z = Sizes(groups, router.shape[2], fwd_act.shape[0], fwd_act.shape[1])
    index = lax.axis_index("ep")
    where = jnp.stack([index // z.split, index % z.split]).astype(jnp.int32)
    router = jnp.swapaxes(router, 1, 2)
    others = range(1, z.split)

    fwd_chunks = make_chunks(z, where, fwd_ids, [fwd_act], [], [], "forward_chunks")
    fwd_own = dispatch(z, fwd_chunks)
    *bwd_chunks, vectors = make_chunks(
        z,
        where,
        bwd_ids,
        [bwd_grad, bwd_act],
        [norm_gain, router],
        [fwd_chunks[0]],
        "backward_chunks",
    )
    normed, gates, fwd_last = normed_rows(z, fwd_own, vectors)
    bwd_chunks[z.experts // 2] = later(bwd_chunks[z.experts // 2], [w_gate, w_down], [gates])
    bwd_own = dispatch(z, bwd_chunks)
    fwd_all = [normed] + [to_core(z, normed, m) for m in others]
    fwd_parts = experts_forward(z, fwd_all, w_gate, w_down, [])
    hidden, slope = saved_terms(z, where, saved_gate, [fwd_parts[0]])
    fwd_parts = [fwd_parts[0]] + [to_core(z, fwd_parts[m], m) for m in others]
    fwd_done = {}

    def finish(ks, after):
        outs = finish_forward(z, ks, fwd_own, fwd_last, fwd_parts, gates, after)
        for k, out in zip(ks, outs):
            fwd_done[k] = to_section(z, out, k, 1)
        return outs[0]

    order = z.order
    first = finish(order[:2], [hidden])
    grads, grad_last = grad_rows_of(z, bwd_own, [first])
    grad_all = [grads] + [to_core(z, grads, m) for m in others]
    inv, act_last = act_norms(z, bwd_own, [grads])
    bwd_parts = experts_backward(z, grad_all, hidden, slope, w_gate, w_down, [inv])
    affinity = act_gates(
        z, bwd_own, act_last, inv, vectors, [bwd_parts[0], *fwd_done.values()]
    )
    second = finish(order[2:], [affinity])
    bwd_parts = [bwd_parts[0]] + [to_core(z, bwd_parts[m], m) for m in others]
    bwd_out = finish_backward(
        z, order, bwd_own, [grad_last, act_last], [inv, affinity], bwd_parts, vectors, [second]
    )
    bwd_done = {k: to_section(z, out, k, -1) for k, out in zip(order, bwd_out)}
    fwd_done = [fwd_done[k] for k in range(z.experts)]
    bwd_done = [bwd_done[k] for k in range(z.experts)]
    return (order_rows(z, fwd_done, "forward_rows"), order_rows(z, bwd_done, "backward_rows"))


def solution(mesh):
    return jax.shard_map(
        on_device,
        mesh=mesh,
        in_specs=(
            P(("pp", "ep"), None),
            P(("pp", "ep"), None),
            P(("pp", "ep"), None),
            P(("pp", "ep"), None),
            P(("pp", "ep"), None),
            P("pp", None),
            P("pp", None, None),
            P(("pp", "ep"), None, None),
            P(("pp", "ep"), None, None),
            P("pp", "ep", None, None),
        ),
        out_specs=(P(("pp", "ep"), None), P(("pp", "ep"), None)),
        check_vma=False,
    )
```

```python
import jax
import jax.numpy as jnp
from jax import lax
from jax.experimental import pallas as pl
from jax.experimental.pallas import tpu as pltpu
from jax.sharding import PartitionSpec as P

epsilon = 1e-06
route_scale = 2.5
fold = 256
none = 255.0
f32 = jnp.float32
bf16 = jnp.bfloat16
nt = (((1,), (1,)), ((), ()))
spaces = {
    "s": pl.BlockSpec(memory_space=pltpu.SMEM),
    "v": pl.BlockSpec(memory_space=pltpu.VMEM),
    "a": pl.BlockSpec(memory_space=pl.ANY),
    "h": pl.BlockSpec(memory_space=pltpu.HBM),
}


cost = {
    "backward_chunks": 10,
    "saved_rows": 15,
    "saved_terms": 15,
    "act_norms": 15,
    "act_gates": 15,
}


def call(body, places, outs, scratch, megabytes, name, out_specs=None):
    def run(*arrays):
        arrays = [
            pltpu.with_memory_space_constraint(array, pltpu.HBM) if place == "h" else array
            for array, place in zip(arrays, places, strict=True)
        ]
        return kernel(*arrays)

    where_to = {} if out_specs is None else {"out_specs": out_specs}
    kernel = pl.pallas_call(
        body,
        out_shape=outs,
        in_specs=[spaces[place] for place in places],
        **where_to,
        scratch_shapes=scratch,
        compiler_params=pltpu.CompilerParams(vmem_limit_bytes=megabytes * 1024 * 1024),
        cost_estimate=pl.CostEstimate(
            flops=int(cost.get(name, 0.1) * 1e9), bytes_accessed=1000, transcendentals=0
        ),
        name=name,
    )
    return run


def shape(dims, kind=bf16):
    return jax.ShapeDtypeStruct(dims, kind)


class Sizes:
    def __init__(self, groups, experts, tokens, width):
        self.experts = experts
        self.split = groups // experts
        self.tokens = tokens
        self.width = width
        self.main = tokens // experts
        self.cap = self.main + 1
        self.pieces = width // fold
        self.wide = width + fold
        self.rows = tokens + 16
        self.order = [experts - 1, *range(1, experts - 1), 0]
        assert self.main == 16 and self.pieces <= 14 and width % fold == 0
        assert experts <= 8 and experts & (experts - 1) == 0 and self.split & (self.split - 1) == 0


def pack_last(row, tile, first=0):
    for i in range(row.shape[1] // fold):
        tile[first + i : first + i + 1, :] = row[:, i * fold : (i + 1) * fold]


def unpack_last(chunk, z, tile, target, at, base=0):
    tile[...] = chunk[base : base + 16, z.width :].astype(f32)
    for i in range(z.pieces):
        target[at : at + 1, i * fold : (i + 1) * fold] = tile[i : i + 1, :]


def slot_matrices(ids_row, block, z):
    tokens = z.tokens
    sub = lax.broadcasted_iota(jnp.int32, (tokens, tokens), 0)
    lane = lax.broadcasted_iota(jnp.int32, (tokens, tokens), 1)
    row = jnp.bitwise_xor(ids_row, block)
    column = jnp.sum(jnp.where(sub == lane, row, 0), axis=1, keepdims=True)
    same = column == row
    place_row = jnp.sum(jnp.where(same & (sub < lane), 1, 0), axis=0, keepdims=True)
    place_column = jnp.sum(jnp.where(same & (lane < sub), 1, 0), axis=1, keepdims=True)

    def slot(expert, place):
        return jnp.where(place < z.main, expert * z.main + place, tokens + expert)

    slot_row = slot(row, place_row)
    slot_column = slot(column, place_column)
    by_slot = lax.broadcasted_iota(jnp.int32, (z.rows, tokens), 0) == slot_row
    lane = lax.broadcasted_iota(jnp.int32, (tokens, fold), 1)
    by_token = jnp.where(lane < tokens, lane, tokens + (lane - tokens) // 16) == slot_column
    token = lax.broadcasted_iota(jnp.int32, (tokens, fold), 0).astype(f32)
    token_row = jnp.sum(jnp.where(by_token, token - none, 0.0), axis=0, keepdims=True) + none
    return jnp.where(by_slot, 1.0, 0.0).astype(bf16), token_row


def write_chunks(z, selector, token_row, rows_ref, ready, tiles, chunks, base):
    step = z.width // 2
    tiles[...] = jnp.zeros_like(tiles)
    for half in range(2):
        ready[half].wait()
        col = half * step
        got = jnp.dot(selector, rows_ref[:, col : col + step], preferred_element_type=f32)
        packed = got[: z.tokens].astype(bf16)
        for k in range(z.experts):
            chunks[k][base : base + 16, col : col + step] = packed[k * z.main : (k + 1) * z.main]
            pack_last(got[z.tokens + k : z.tokens + k + 1], tiles.at[k], half * z.pieces // 2)
    for k in range(z.experts):
        tiles[k, z.pieces : z.pieces + 1, :] = token_row
        chunks[k][base : base + 16, z.width :] = tiles[k].astype(bf16)


def make_chunks(z, where, ids, sources, tables, after, name):
    count = len(sources)

    def body(where, ids_any, *refs):
        anys, tables_any = refs[:count], refs[count : count + len(tables)]
        outs, held = refs[count + len(tables) + len(after) :], ()
        if tables:
            *outs, gain_ref, router_ref, ids, rows, tiles, sems = outs
            *outs, vectors = outs
            held = (gain_ref, router_ref)
        else:
            *outs, ids, rows, tiles, sems = outs
        copies = [pltpu.make_async_copy(ids_any, ids, sems.at[2 * count])]
        step = z.width // 2
        for j in range(count):
            for half in range(2):
                cols = pl.ds(half * step, step)
                copies.append(
                    pltpu.make_async_copy(
                        anys[j].at[:, cols], rows.at[j, :, cols], sems.at[2 * j + half]
                    )
                )
        for i, (source, target) in enumerate(zip(tables_any, held)):
            copies.append(pltpu.make_async_copy(source, target, sems.at[2 * count + 1 + i]))
        for copy in copies:
            copy.start()
        copies[0].wait()
        selector, token_row = slot_matrices(ids[...], where[0], z)
        for j in range(count):
            ready = copies[1 + 2 * j : 3 + 2 * j]
            write_chunks(z, selector, token_row, rows.at[j], ready, tiles, outs, 16 * j)
        if tables:
            for copy in copies[1 + 2 * count :]:
                copy.wait()
            vectors[...] = jnp.zeros_like(vectors)
            vectors[0:1, :] = gain_ref[...].astype(f32)
            mine = lax.broadcasted_iota(jnp.int32, (z.experts, 1), 0) == where[0]
            table = jnp.where(mine, router_ref[0].astype(f32), 0.0)
            vectors[1:2, :] = jnp.sum(table, axis=0, keepdims=True)

    return call(
        body,
        "sh" + "h" * (count + len(tables)) + "a" * len(after),
        [shape((z.main * count, z.wide))] * z.experts
        + [shape((8, z.width), f32) for _ in tables[:1]],
        [pltpu.VMEM(table.shape, bf16) for table in tables]
        + [
            pltpu.VMEM((1, z.tokens), jnp.int32),
            pltpu.VMEM((count, z.tokens, z.width), bf16),
            pltpu.VMEM((z.experts, 16, fold), f32),
            pltpu.SemaphoreType.DMA((2 * count + 1 + len(tables),)),
        ],
        8,
        name,
    )(where, ids.reshape(1, z.tokens), *sources, *tables, *after)


def collect_rows(z, chunks, last, tile, base=0):
    last[...] = jnp.zeros_like(last)
    for k in range(z.experts):
        unpack_last(chunks[k], z, tile, last, k, base)


def norm_rows(h, gain):
    inv = lax.rsqrt(jnp.mean(h * h, axis=-1, keepdims=True) + epsilon)
    return (h * inv * gain).astype(bf16), inv


def normed_rows(z, chunks, vectors):
    order = z.order

    def body(*refs):
        chunks, (vectors, normed_ref, gates_ref, last, tile) = refs[: z.experts], refs[z.experts :]
        chunks = [chunks[order.index(k)] for k in range(z.experts)]
        gain, router = vectors[0:1, :], vectors[1:2, :]
        collect_rows(z, chunks, last, tile)
        for k in range(z.experts + 1):
            h = last[...] if k == z.experts else chunks[k][:, : z.width].astype(f32)
            at = k * z.main
            normed, _ = norm_rows(h, gain)
            normed_ref[at : at + 16, :] = normed
            logits = jnp.sum(normed.astype(f32) * router, axis=-1, keepdims=True)
            gates_ref[at : at + 16, :] = jnp.broadcast_to(jax.nn.sigmoid(logits), (16, 128))

    return call(
        body,
        "v" * (z.experts + 1),
        [shape((z.rows, z.width)), shape((z.rows, 128), f32), shape((16, z.width), f32)],
        [pltpu.VMEM((16, fold), f32)],
        8,
        "normed_rows",
    )(*[chunks[k] for k in order], vectors)


def grad_rows_of(z, chunks, after):
    def body(*refs):
        chunks, (rows, last, tile) = refs[: z.experts], refs[z.experts + len(after) :]
        for k in range(z.experts):
            rows[k * z.main : (k + 1) * z.main, :] = chunks[k][:16, : z.width]
        collect_rows(z, chunks, last, tile)
        rows[z.tokens :, :] = last[...].astype(bf16)

    return call(
        body,
        "v" * z.experts + "a" * len(after),
        [shape((z.rows, z.width)), shape((16, z.width), f32)],
        [pltpu.VMEM((16, fold), f32)],
        8,
        "grad_rows",
    )(*chunks, *after)


def act_norms(z, chunks, after):
    def body(*refs):
        chunks, (inv_ref, last, tile) = refs[: z.experts], refs[z.experts + len(after) :]
        collect_rows(z, chunks, last, tile, 16)
        for k in range(z.experts + 1):
            h = last[...] if k == z.experts else chunks[k][16:32, : z.width].astype(f32)
            at = k * z.main
            inv = lax.rsqrt(jnp.mean(h * h, axis=-1, keepdims=True) + epsilon)
            inv_ref[at : at + 16, :] = jnp.broadcast_to(inv, (16, 128))

    return call(
        body,
        "v" * z.experts + "a" * len(after),
        [shape((z.rows, 128), f32), shape((16, z.width), f32)],
        [pltpu.VMEM((16, fold), f32)],
        8,
        "act_norms",
    )(*chunks, *after)


def act_gates(z, chunks, last, inv, vectors, after):
    def body(*refs):
        chunks, (last, inv_ref, vectors) = refs[: z.experts], refs[z.experts : z.experts + 3]
        affinity_ref = refs[-1]
        gain, router = vectors[0:1, :], vectors[1:2, :]
        for k in range(z.experts + 1):
            h = last[...] if k == z.experts else chunks[k][16:32, : z.width].astype(f32)
            at = k * z.main
            normed = (h * inv_ref[at : at + 16, 0:1] * gain).astype(bf16).astype(f32)
            logits = jnp.sum(normed * router, axis=-1, keepdims=True)
            affinity_ref[at : at + 16, :] = jnp.broadcast_to(jax.nn.sigmoid(logits), (16, 128))

    return call(
        body,
        "v" * (z.experts + 3) + "a" * len(after),
        shape((z.rows, 128), f32),
        [],
        8,
        "act_gates",
    )(*chunks, last, inv, vectors, *after)


def write_parts(z, values, outs, col):
    values = values.astype(bf16)
    for m in range(z.split):
        outs[m][:, col : col + values.shape[1]] = values[m * z.rows : (m + 1) * z.rows]


def experts_forward(z, rows, w_gate, w_down, after):
    def body(*refs):
        rows, (gate_ref, down_ref), outs = (
            refs[: z.split],
            refs[z.split : z.split + 2],
            refs[z.split + 2 + len(after) :],
        )
        held = jnp.concatenate([part[...] for part in rows], axis=0)
        gate_proj = jnp.dot(held, gate_ref[0], preferred_element_type=f32)
        hidden = jax.nn.silu(gate_proj).astype(bf16)
        step = 512
        for col in range(0, z.width, step):
            part = jnp.dot(hidden, down_ref[0, :, col : col + step], preferred_element_type=f32)
            write_parts(z, part, outs, col)

    return call(
        body,
        "v" * (z.split + 2) + "a" * len(after),
        [shape((z.rows, z.width))] * z.split,
        [],
        16,
        "experts_forward",
    )(*rows, w_gate, w_down, *after)


def saved_rows(z, where, saved, weights, after):
    total, slots, width = z.split * z.rows, saved.shape[2], saved.shape[3]

    def body(where, saved_any, *refs):
        ordered_ref, saved_ref, sem = refs[len(weights) + len(after) :]
        copy = pltpu.make_async_copy(saved_any.at[0, 0], saved_ref, sem)
        copy.start()
        row = lax.broadcasted_iota(jnp.int32, (total, slots), 0)
        slot = lax.broadcasted_iota(jnp.int32, (total, slots), 1)
        m, at = row // z.rows, row % z.rows
        is_main = at < z.tokens
        k = jnp.where(is_main, at // z.main, at - z.tokens)
        p = jnp.where(is_main, at % z.main, z.main)
        source = jnp.bitwise_xor(k, where[0]) * z.split + jnp.bitwise_xor(m, where[1])
        wanted = jnp.where(k < z.experts, source * z.cap + p, -1)
        selector = jnp.where(slot == wanted, 1.0, 0.0).astype(bf16)
        copy.wait()
        ordered_ref[...] = jnp.dot(selector, saved_ref[...], preferred_element_type=f32)

    return call(
        body,
        "sh" + "v" * len(weights) + "a" * len(after),
        shape((total, width), f32),
        [pltpu.VMEM((slots, width), bf16), pltpu.SemaphoreType.DMA],
        8,
        "saved_rows",
    )(where, saved, *weights, *after)


def saved_terms(z, ordered, after):
    def body(ordered_ref, *refs):
        hidden_ref, slope_ref = refs[len(after) :]
        gate_proj = ordered_ref[...]
        sg = jax.nn.sigmoid(gate_proj)
        hidden_ref[...] = (gate_proj * sg).astype(bf16)
        slope_ref[...] = sg * (1.0 + gate_proj * (1.0 - sg))

    return call(
        body,
        "v" + "a" * len(after),
        [shape(ordered.shape), shape(ordered.shape, f32)],
        [],
        8,
        "saved_terms",
    )(ordered, *after)


def experts_backward(z, rows, hidden, slope, w_gate, w_down, after):
    def body(*refs):
        rows = refs[: z.split]
        hidden_ref, slope_ref, gate_ref, down_ref = refs[z.split : z.split + 4]
        outs = refs[z.split + 4 + len(after) :]
        held = jnp.concatenate([part[...] for part in rows], axis=0)
        grad_hidden = lax.dot_general(held, down_ref[0], nt, preferred_element_type=f32)
        dots = jnp.sum(grad_hidden * hidden_ref[...].astype(f32), axis=-1, keepdims=True)
        grad_gate = (grad_hidden * slope_ref[...]).astype(bf16)
        step = 512
        for col in range(0, z.width, step):
            part = lax.dot_general(
                grad_gate, gate_ref[0, col : col + step, :], nt, preferred_element_type=f32
            )
            write_parts(z, part, outs, col)
        write_parts(z, jnp.broadcast_to(dots, (dots.shape[0], 128)), outs, z.width)

    return call(
        body,
        "v" * (z.split + 4) + "a" * len(after),
        [shape((z.rows, z.width + 128))] * z.split,
        [],
        16,
        "experts_backward",
    )(*rows, hidden, slope, w_gate, w_down, *after)


def put_last(z, values, source_chunk, tile, out):
    tile[...] = jnp.zeros_like(tile)
    pack_last(values, tile)
    tokens = source_chunk[:16, z.width :].astype(f32)
    tile[z.pieces : z.pieces + 1, :] = tokens[z.pieces : z.pieces + 1, :]
    out[:, z.width :] = tile[...].astype(bf16)


def finish_forward(z, ks, chunks, last, parts, gates, after):
    count = len(ks)

    def body(*refs):
        chunks, last, parts = refs[:count], refs[count], refs[count + 1 : count + 1 + z.split]
        gates, out, tile = refs[count + 1 + z.split], refs[-2], refs[-1]

        def mixed(at):
            y = parts[0][at : at + 16, :].astype(f32)
            for part in parts[1:]:
                y = y + part[at : at + 16, :].astype(f32)
            return route_scale * (gates[at : at + 16, 0:1] * y)

        tail = last[...] + mixed(z.tokens)
        for i, (k, chunk) in enumerate(zip(ks, chunks)):
            h = chunk[:, : z.width].astype(f32)
            rows = out.at[pl.ds(i * 16, 16)]
            rows[:, : z.width] = (h + mixed(k * z.main)).astype(bf16)
            put_last(z, tail[k : k + 1, :], chunk, tile, rows)

    return call(
        body,
        "v" * (count + z.split + 2) + "a" * len(after),
        shape((count * z.main, z.wide)),
        [pltpu.VMEM((16, fold), f32)],
        8,
        "finish_forward_" + "".join(map(str, ks)),
    )(*[chunks[k] for k in ks], last, *parts, gates, *after)


def lower_chunk(z, double, after):
    def body(double, *refs):
        refs[-1][...] = double[16:32, :]

    places = "v" + "a" * len(after)
    return call(body, places, shape((16, z.wide)), [], 8, "lower_chunk")(double, *after)


def finish_backward(z, order, chunks, lasts, terms, parts, vectors, after):
    def body(*refs):
        e = z.experts
        chunks, (last_grad, last_act, inv_ref, affinity_ref) = refs[:e], refs[e : e + 4]
        parts, vectors = refs[e + 4 : e + 4 + z.split], refs[e + 4 + z.split]
        outs, (tile,) = refs[-1 - e : -1], refs[-1:]
        outs = [outs[order.index(k)] for k in range(e)]
        gain, router = vectors[0:1, :], vectors[1:2, :]

        def finished(h, g, at):
            inv, affinity = inv_ref[at : at + 16, 0:1], affinity_ref[at : at + 16, 0:1]
            rows = parts[0][at : at + 16, : z.width].astype(f32)
            dot = parts[0][at : at + 16, z.width :].astype(f32)
            for part in parts[1:]:
                rows = rows + part[at : at + 16, : z.width].astype(f32)
                dot = dot + part[at : at + 16, z.width :].astype(f32)
            dot = dot[:, 0:1]
            grad_logits = (route_scale * dot * affinity * (1.0 - affinity)).astype(bf16).astype(f32)
            grad_pre = (route_scale * affinity * rows + grad_logits * router) * gain
            centre = jnp.mean(grad_pre * h, axis=-1, keepdims=True)
            return g + inv * (grad_pre - h * (inv * inv * centre))

        tail = finished(last_act[...], last_grad[...], z.tokens)
        for k in range(e):
            g = chunks[k][:16, : z.width].astype(f32)
            h = chunks[k][16:32, : z.width].astype(f32)
            outs[k][:, : z.width] = finished(h, g, k * z.main).astype(bf16)
            put_last(z, tail[k : k + 1, :], chunks[k], tile, outs[k])

    return call(
        body,
        "v" * (z.experts + z.split + 5) + "a" * len(after),
        [shape((z.main, z.wide))] * z.experts,
        [pltpu.VMEM((16, fold), f32)],
        8,
        "finish_backward",
    )(*chunks, *lasts, *terms, *parts, vectors, *after)


def order_rows(z, arrays, places, after, name):
    count = len(arrays)
    lanes = z.tokens + 16 * z.experts
    steps = 7 if z.pieces % 7 == 0 else z.pieces

    def body(*refs):
        arrays, (out_any, out, sems) = refs[:count], refs[count + len(after) :]
        chunks = [arrays[i].at[pl.ds(at, 16)] for i, at in places]
        tiles = [chunk[:, z.width :] for chunk in chunks]
        token_row = tiles[0].astype(f32)[z.pieces : z.pieces + 1, :lanes]
        token = lax.broadcasted_iota(jnp.int32, (z.tokens, lanes), 0).astype(f32)
        lane = lax.broadcasted_iota(jnp.int32, (z.tokens, lanes), 1)
        piece = jnp.where(lane < z.tokens, -1, lane % 16)
        ours = token == token_row
        copies = []
        for i in range(z.pieces):
            cols = pl.ds(i * fold, fold)
            mine = ours & ((piece < 0) | (piece == i))
            selector = jnp.where(mine, 1.0, 0.0).astype(bf16)
            rows = jnp.concatenate([chunk[:, cols] for chunk in chunks] + tiles, axis=0)
            out[:, cols] = jnp.dot(selector, rows, preferred_element_type=f32).astype(bf16)
            if (i + 1) % (z.pieces // steps) == 0:
                done = pl.ds((i + 1) * fold - z.width // steps, z.width // steps)
                copy = pltpu.make_async_copy(out.at[:, done], out_any.at[:, done], sems.at[len(copies)])
                copy.start()
                copies.append(copy)
        for copy in copies:
            copy.wait()

    return call(
        body,
        "v" * count + "a" * len(after),
        shape((z.tokens, z.width)),
        [pltpu.VMEM((z.tokens, z.width), bf16), pltpu.SemaphoreType.DMA((steps,))],
        8,
        name,
        spaces["a"],
    )(*arrays, *after)


def permute_blocks(z, arrays, k):
    groups = z.experts * z.split
    pairs = [(i, ((i // z.split) ^ k) * z.split + i % z.split) for i in range(groups)]
    return [lax.ppermute(array, "ep", pairs) for array in arrays]


def dispatch(z, chunks):
    return [chunks[0]] + [permute_blocks(z, [chunks[k]], k)[0] for k in range(1, z.experts)]


def to_core(z, array, m):
    groups = z.experts * z.split
    pairs = [(i, i // z.split * z.split + ((i % z.split) ^ m)) for i in range(groups)]
    return lax.ppermute(array, "ep", pairs)


def to_section(z, chunk, k, by):
    groups = z.experts * z.split
    sections = lax.axis_size("pp")
    pairs = [
        (s * groups + i, (s + by) % sections * groups + ((i // z.split) ^ k) * z.split + i % z.split)
        for s in range(sections)
        for i in range(groups)
    ]
    return lax.ppermute(chunk, ("pp", "ep"), pairs)


def on_device(
    fwd_act, fwd_ids, bwd_act, bwd_ids, bwd_grad, norm_gain, router, w_gate, w_down, saved_gate
):
    groups = lax.axis_size("ep")
    assert fwd_ids.shape[1] == 1
    z = Sizes(groups, router.shape[2], fwd_act.shape[0], fwd_act.shape[1])
    index = lax.axis_index("ep")
    where = jnp.stack([index // z.split, index % z.split]).astype(jnp.int32)
    router = jnp.swapaxes(router, 1, 2)
    others = range(1, z.split)

    fwd_chunks = make_chunks(z, where, fwd_ids, [fwd_act], [], [], "forward_chunks")
    fwd_own = dispatch(z, fwd_chunks)
    *bwd_chunks, vectors = make_chunks(
        z,
        where,
        bwd_ids,
        [bwd_grad, bwd_act],
        [norm_gain, router],
        [fwd_chunks[0]],
        "backward_chunks",
    )
    bwd_own = dispatch(z, bwd_chunks)

    normed, gates, fwd_last = normed_rows(z, fwd_own, vectors)
    fwd_all = [normed] + [to_core(z, normed, m) for m in others]
    ordered = saved_rows(z, where, saved_gate, [w_gate, w_down], [gates])
    fwd_parts = experts_forward(z, fwd_all, w_gate, w_down, [ordered])
    hidden, slope = saved_terms(z, ordered, [fwd_parts[0]])
    fwd_parts = [fwd_parts[0]] + [to_core(z, fwd_parts[m], m) for m in others]

    def finish(ks, after):
        return finish_forward(z, ks, fwd_own, fwd_last, fwd_parts, gates, after)

    half = max(3, z.experts // 2 + 1)
    double = finish([0, 1], [hidden])
    got = to_section(z, double, 0, 1)
    grads, grad_last = grad_rows_of(z, bwd_own, [double])
    grad_all = [grads] + [to_core(z, grads, m) for m in others]
    inv, act_last = act_norms(z, bwd_own, [grads])
    fwd_done = [to_section(z, finish([k], [inv]), k, 1) for k in range(2, half)]
    bwd_parts = experts_backward(z, grad_all, hidden, slope, w_gate, w_down, [inv])
    affinity = act_gates(z, bwd_own, act_last, inv, vectors, [bwd_parts[0], got])
    (relayed,) = permute_blocks(z, [lower_chunk(z, got, [affinity])], 1)
    third = [finish([k], [affinity]) for k in range(half, z.experts)]
    fwd_done += [to_section(z, out, k, 1) for k, out in zip(range(half, z.experts), third)]
    bwd_parts = [bwd_parts[0]] + [to_core(z, bwd_parts[m], m) for m in others]
    bwd_out = finish_backward(
        z, z.order, bwd_own, [grad_last, act_last], [inv, affinity], bwd_parts, vectors, third
    )
    bwd_done = {k: to_section(z, out, k, -1) for k, out in zip(z.order, bwd_out)}

    places = [(k, 0) for k in range(z.experts)]
    fwd_next = order_rows(z, [got, relayed, *fwd_done], places, [], "forward_rows")
    places = [(z.order.index(k), 0) for k in range(z.experts)]
    bwd_next = order_rows(z, [bwd_done[k] for k in z.order], places, [], "backward_rows")
    return (fwd_next, bwd_next)


def solution(mesh):
    return jax.shard_map(
        on_device,
        mesh=mesh,
        in_specs=(
            P(("pp", "ep"), None),
            P(("pp", "ep"), None),
            P(("pp", "ep"), None),
            P(("pp", "ep"), None),
            P(("pp", "ep"), None),
            P("pp", None),
            P("pp", None, None),
            P(("pp", "ep"), None, None),
            P(("pp", "ep"), None, None),
            P("pp", "ep", None, None),
        ),
        out_specs=(P(("pp", "ep"), None), P(("pp", "ep"), None)),
        check_vma=False,
    )
```

```python
import jax
import jax.numpy as jnp
from jax import lax
from jax.experimental import pallas as pl
from jax.experimental.pallas import tpu as pltpu
from jax.sharding import PartitionSpec as P

epsilon = 1e-06
route_scale = 2.5
fold = 256
none = 255.0
f32 = jnp.float32
bf16 = jnp.bfloat16
nt = (((1,), (1,)), ((), ()))
spaces = {
    "s": pl.BlockSpec(memory_space=pltpu.SMEM),
    "v": pl.BlockSpec(memory_space=pltpu.VMEM),
    "a": pl.BlockSpec(memory_space=pl.ANY),
    "h": pl.BlockSpec(memory_space=pltpu.HBM),
}


cost = {
    "backward_chunks": 10,
    "saved_rows": 15,
    "saved_terms": 15,
    "act_norms": 15,
    "act_gates": 15,
}


def call(body, places, outs, scratch, megabytes, name, out_specs=None):
    def run(*arrays):
        arrays = [
            pltpu.with_memory_space_constraint(array, pltpu.HBM) if place == "h" else array
            for array, place in zip(arrays, places, strict=True)
        ]
        return kernel(*arrays)

    where_to = {} if out_specs is None else {"out_specs": out_specs}
    kernel = pl.pallas_call(
        body,
        out_shape=outs,
        in_specs=[spaces[place] for place in places],
        **where_to,
        scratch_shapes=scratch,
        compiler_params=pltpu.CompilerParams(vmem_limit_bytes=megabytes * 1024 * 1024),
        cost_estimate=pl.CostEstimate(
            flops=int(cost.get(name, 0.1) * 1e9), bytes_accessed=1000, transcendentals=0
        ),
        name=name,
    )
    return run


def shape(dims, kind=bf16):
    return jax.ShapeDtypeStruct(dims, kind)


class Sizes:
    def __init__(self, groups, experts, tokens, width):
        self.experts = experts
        self.split = groups // experts
        self.tokens = tokens
        self.width = width
        self.main = tokens // experts
        self.cap = self.main + 1
        self.pieces = width // fold
        self.wide = width + fold
        self.rows = tokens + 16
        self.order = [experts - 1, *range(1, experts - 1), 0]
        assert self.main == 16 and self.pieces <= 14 and width % fold == 0
        assert experts <= 8 and experts & (experts - 1) == 0 and self.split & (self.split - 1) == 0


def pack_last(row, tile, first=0):
    for i in range(row.shape[1] // fold):
        tile[first + i : first + i + 1, :] = row[:, i * fold : (i + 1) * fold]


def unpack_last(chunk, z, tile, target, at, base=0):
    tile[...] = chunk[base : base + 16, z.width :].astype(f32)
    for i in range(z.pieces):
        target[at : at + 1, i * fold : (i + 1) * fold] = tile[i : i + 1, :]


def slot_matrices(ids_row, block, z):
    tokens = z.tokens
    sub = lax.broadcasted_iota(jnp.int32, (tokens, tokens), 0)
    lane = lax.broadcasted_iota(jnp.int32, (tokens, tokens), 1)
    row = jnp.bitwise_xor(ids_row, block)
    column = jnp.sum(jnp.where(sub == lane, row, 0), axis=1, keepdims=True)
    same = column == row
    place_row = jnp.sum(jnp.where(same & (sub < lane), 1, 0), axis=0, keepdims=True)
    place_column = jnp.sum(jnp.where(same & (lane < sub), 1, 0), axis=1, keepdims=True)

    def slot(expert, place):
        return jnp.where(place < z.main, expert * z.main + place, tokens + expert)

    slot_row = slot(row, place_row)
    slot_column = slot(column, place_column)
    by_slot = lax.broadcasted_iota(jnp.int32, (z.rows, tokens), 0) == slot_row
    lane = lax.broadcasted_iota(jnp.int32, (tokens, fold), 1)
    by_token = jnp.where(lane < tokens, lane, tokens + (lane - tokens) // 16) == slot_column
    token = lax.broadcasted_iota(jnp.int32, (tokens, fold), 0).astype(f32)
    token_row = jnp.sum(jnp.where(by_token, token - none, 0.0), axis=0, keepdims=True) + none
    return jnp.where(by_slot, 1.0, 0.0).astype(bf16), token_row


def write_chunks(z, selector, token_row, rows_ref, ready, tiles, chunks, base):
    step = z.width // 2
    tiles[...] = jnp.zeros_like(tiles)
    for half in range(2):
        ready[half].wait()
        col = half * step
        got = jnp.dot(selector, rows_ref[:, col : col + step], preferred_element_type=f32)
        packed = got[: z.tokens].astype(bf16)
        for k in range(z.experts):
            chunks[k][base : base + 16, col : col + step] = packed[k * z.main : (k + 1) * z.main]
            pack_last(got[z.tokens + k : z.tokens + k + 1], tiles.at[k], half * z.pieces // 2)
    for k in range(z.experts):
        tiles[k, z.pieces : z.pieces + 1, :] = token_row
        chunks[k][base : base + 16, z.width :] = tiles[k].astype(bf16)


def make_chunks(z, where, ids, sources, tables, after, name):
    count = len(sources)

    def body(where, ids_any, *refs):
        anys, tables_any = refs[:count], refs[count : count + len(tables)]
        outs, held = refs[count + len(tables) + len(after) :], ()
        if tables:
            *outs, gain_ref, router_ref, ids, rows, tiles, sems = outs
            *outs, vectors = outs
            held = (gain_ref, router_ref)
        else:
            *outs, ids, rows, tiles, sems = outs
        copies = [pltpu.make_async_copy(ids_any, ids, sems.at[2 * count])]
        step = z.width // 2
        for j in range(count):
            for half in range(2):
                cols = pl.ds(half * step, step)
                copies.append(
                    pltpu.make_async_copy(
                        anys[j].at[:, cols], rows.at[j, :, cols], sems.at[2 * j + half]
                    )
                )
        for i, (source, target) in enumerate(zip(tables_any, held)):
            copies.append(pltpu.make_async_copy(source, target, sems.at[2 * count + 1 + i]))
        for copy in copies:
            copy.start()
        copies[0].wait()
        selector, token_row = slot_matrices(ids[...], where[0], z)
        for j in range(count):
            ready = copies[1 + 2 * j : 3 + 2 * j]
            write_chunks(z, selector, token_row, rows.at[j], ready, tiles, outs, 16 * j)
        if tables:
            for copy in copies[1 + 2 * count :]:
                copy.wait()
            vectors[...] = jnp.zeros_like(vectors)
            vectors[0:1, :] = gain_ref[...].astype(f32)
            mine = lax.broadcasted_iota(jnp.int32, (z.experts, 1), 0) == where[0]
            table = jnp.where(mine, router_ref[0].astype(f32), 0.0)
            vectors[1:2, :] = jnp.sum(table, axis=0, keepdims=True)

    return call(
        body,
        "sh" + "h" * (count + len(tables)) + "a" * len(after),
        [shape((z.main * count, z.wide))] * z.experts
        + [shape((8, z.width), f32) for _ in tables[:1]],
        [pltpu.VMEM(table.shape, bf16) for table in tables]
        + [
            pltpu.VMEM((1, z.tokens), jnp.int32),
            pltpu.VMEM((count, z.tokens, z.width), bf16),
            pltpu.VMEM((z.experts, 16, fold), f32),
            pltpu.SemaphoreType.DMA((2 * count + 1 + len(tables),)),
        ],
        8,
        name,
    )(where, ids.reshape(1, z.tokens), *sources, *tables, *after)


def collect_rows(z, chunks, last, tile, base=0):
    last[...] = jnp.zeros_like(last)
    for k in range(z.experts):
        unpack_last(chunks[k], z, tile, last, k, base)


def norm_rows(h, gain):
    inv = lax.rsqrt(jnp.mean(h * h, axis=-1, keepdims=True) + epsilon)
    return (h * inv * gain).astype(bf16), inv


def normed_rows(z, chunks, vectors):
    def body(*refs):
        chunks, (vectors, normed_ref, gates_ref, last, tile) = refs[: z.experts], refs[z.experts :]
        gain, router = vectors[0:1, :], vectors[1:2, :]
        collect_rows(z, chunks, last, tile)
        for k in range(z.experts + 1):
            h = last[...] if k == z.experts else chunks[k][:, : z.width].astype(f32)
            at = k * z.main
            normed, _ = norm_rows(h, gain)
            normed_ref[at : at + 16, :] = normed
            logits = jnp.sum(normed.astype(f32) * router, axis=-1, keepdims=True)
            gates_ref[at : at + 16, :] = jnp.broadcast_to(jax.nn.sigmoid(logits), (16, 128))

    return call(
        body,
        "v" * (z.experts + 1),
        [shape((z.rows, z.width)), shape((z.rows, 128), f32), shape((16, z.width), f32)],
        [pltpu.VMEM((16, fold), f32)],
        8,
        "normed_rows",
    )(*chunks, vectors)


def grad_rows_of(z, chunks, after):
    def body(*refs):
        chunks, (rows, last, tile) = refs[: z.experts], refs[z.experts + len(after) :]
        for k in range(z.experts):
            rows[k * z.main : (k + 1) * z.main, :] = chunks[k][:16, : z.width]
        collect_rows(z, chunks, last, tile)
        rows[z.tokens :, :] = last[...].astype(bf16)

    return call(
        body,
        "v" * z.experts + "a" * len(after),
        [shape((z.rows, z.width)), shape((16, z.width), f32)],
        [pltpu.VMEM((16, fold), f32)],
        8,
        "grad_rows",
    )(*chunks, *after)


def act_norms(z, chunks, after):
    def body(*refs):
        chunks, (inv_ref, last, tile) = refs[: z.experts], refs[z.experts + len(after) :]
        collect_rows(z, chunks, last, tile, 16)
        for k in range(z.experts + 1):
            h = last[...] if k == z.experts else chunks[k][16:32, : z.width].astype(f32)
            at = k * z.main
            inv = lax.rsqrt(jnp.mean(h * h, axis=-1, keepdims=True) + epsilon)
            inv_ref[at : at + 16, :] = jnp.broadcast_to(inv, (16, 128))

    return call(
        body,
        "v" * z.experts + "a" * len(after),
        [shape((z.rows, 128), f32), shape((16, z.width), f32)],
        [pltpu.VMEM((16, fold), f32)],
        8,
        "act_norms",
    )(*chunks, *after)


def act_gates(z, chunks, last, inv, vectors, after):
    def body(*refs):
        chunks, (last, inv_ref, vectors) = refs[: z.experts], refs[z.experts : z.experts + 3]
        affinity_ref = refs[-1]
        gain, router = vectors[0:1, :], vectors[1:2, :]
        for k in range(z.experts + 1):
            h = last[...] if k == z.experts else chunks[k][16:32, : z.width].astype(f32)
            at = k * z.main
            normed = (h * inv_ref[at : at + 16, 0:1] * gain).astype(bf16).astype(f32)
            logits = jnp.sum(normed * router, axis=-1, keepdims=True)
            affinity_ref[at : at + 16, :] = jnp.broadcast_to(jax.nn.sigmoid(logits), (16, 128))

    return call(
        body,
        "v" * (z.experts + 3) + "a" * len(after),
        shape((z.rows, 128), f32),
        [],
        8,
        "act_gates",
    )(*chunks, last, inv, vectors, *after)


def write_parts(z, values, outs, col):
    values = values.astype(bf16)
    for m in range(z.split):
        outs[m][:, col : col + values.shape[1]] = values[m * z.rows : (m + 1) * z.rows]


def experts_forward(z, rows, w_gate, w_down, after):
    def body(*refs):
        rows, (gate_ref, down_ref), outs = (
            refs[: z.split],
            refs[z.split : z.split + 2],
            refs[z.split + 2 + len(after) :],
        )
        held = jnp.concatenate([part[...] for part in rows], axis=0)
        gate_proj = jnp.dot(held, gate_ref[0], preferred_element_type=f32)
        hidden = jax.nn.silu(gate_proj).astype(bf16)
        step = 512
        for col in range(0, z.width, step):
            part = jnp.dot(hidden, down_ref[0, :, col : col + step], preferred_element_type=f32)
            write_parts(z, part, outs, col)

    return call(
        body,
        "v" * (z.split + 2) + "a" * len(after),
        [shape((z.rows, z.width))] * z.split,
        [],
        16,
        "experts_forward",
    )(*rows, w_gate, w_down, *after)


def saved_rows(z, where, saved, weights, after):
    total, slots, width = z.split * z.rows, saved.shape[2], saved.shape[3]

    def body(where, saved_any, *refs):
        ordered_ref, saved_ref, sem = refs[len(weights) + len(after) :]
        copy = pltpu.make_async_copy(saved_any.at[0, 0], saved_ref, sem)
        copy.start()
        row = lax.broadcasted_iota(jnp.int32, (total, slots), 0)
        slot = lax.broadcasted_iota(jnp.int32, (total, slots), 1)
        m, at = row // z.rows, row % z.rows
        is_main = at < z.tokens
        k = jnp.where(is_main, at // z.main, at - z.tokens)
        p = jnp.where(is_main, at % z.main, z.main)
        source = jnp.bitwise_xor(k, where[0]) * z.split + jnp.bitwise_xor(m, where[1])
        wanted = jnp.where(k < z.experts, source * z.cap + p, -1)
        selector = jnp.where(slot == wanted, 1.0, 0.0).astype(bf16)
        copy.wait()
        ordered_ref[...] = jnp.dot(selector, saved_ref[...], preferred_element_type=f32)

    return call(
        body,
        "sh" + "v" * len(weights) + "a" * len(after),
        shape((total, width), f32),
        [pltpu.VMEM((slots, width), bf16), pltpu.SemaphoreType.DMA],
        8,
        "saved_rows",
    )(where, saved, *weights, *after)


def saved_terms(z, ordered, after):
    def body(ordered_ref, *refs):
        hidden_ref, slope_ref = refs[len(after) :]
        gate_proj = ordered_ref[...]
        sg = jax.nn.sigmoid(gate_proj)
        hidden_ref[...] = (gate_proj * sg).astype(bf16)
        slope_ref[...] = sg * (1.0 + gate_proj * (1.0 - sg))

    return call(
        body,
        "v" + "a" * len(after),
        [shape(ordered.shape), shape(ordered.shape, f32)],
        [],
        8,
        "saved_terms",
    )(ordered, *after)


def experts_backward(z, rows, hidden, slope, w_gate, w_down, after):
    def body(*refs):
        rows = refs[: z.split]
        hidden_ref, slope_ref, gate_ref, down_ref = refs[z.split : z.split + 4]
        outs = refs[z.split + 4 + len(after) :]
        held = jnp.concatenate([part[...] for part in rows], axis=0)
        grad_hidden = lax.dot_general(held, down_ref[0], nt, preferred_element_type=f32)
        dots = jnp.sum(grad_hidden * hidden_ref[...].astype(f32), axis=-1, keepdims=True)
        grad_gate = (grad_hidden * slope_ref[...]).astype(bf16)
        step = 512
        for col in range(0, z.width, step):
            part = lax.dot_general(
                grad_gate, gate_ref[0, col : col + step, :], nt, preferred_element_type=f32
            )
            write_parts(z, part, outs, col)
        write_parts(z, jnp.broadcast_to(dots, (dots.shape[0], 128)), outs, z.width)

    return call(
        body,
        "v" * (z.split + 4) + "a" * len(after),
        [shape((z.rows, z.width + 128))] * z.split,
        [],
        16,
        "experts_backward",
    )(*rows, hidden, slope, w_gate, w_down, *after)


def put_last(z, values, source_chunk, tile, out):
    tile[...] = jnp.zeros_like(tile)
    pack_last(values, tile)
    tokens = source_chunk[:16, z.width :].astype(f32)
    tile[z.pieces : z.pieces + 1, :] = tokens[z.pieces : z.pieces + 1, :]
    out[:, z.width :] = tile[...].astype(bf16)


def finish_forward(z, ks, chunks, last, parts, gates, after):
    count = len(ks)

    def body(*refs):
        chunks, last, parts = refs[:count], refs[count], refs[count + 1 : count + 1 + z.split]
        gates, out, tile = refs[count + 1 + z.split], refs[-2], refs[-1]

        def mixed(at):
            y = parts[0][at : at + 16, :].astype(f32)
            for part in parts[1:]:
                y = y + part[at : at + 16, :].astype(f32)
            return route_scale * (gates[at : at + 16, 0:1] * y)

        tail = last[...] + mixed(z.tokens)
        for i, (k, chunk) in enumerate(zip(ks, chunks)):
            h = chunk[:, : z.width].astype(f32)
            rows = out.at[pl.ds(i * 16, 16)]
            rows[:, : z.width] = (h + mixed(k * z.main)).astype(bf16)
            put_last(z, tail[k : k + 1, :], chunk, tile, rows)

    return call(
        body,
        "v" * (count + z.split + 2) + "a" * len(after),
        shape((count * z.main, z.wide)),
        [pltpu.VMEM((16, fold), f32)],
        8,
        "finish_forward_" + "".join(map(str, ks)),
    )(*[chunks[k] for k in ks], last, *parts, gates, *after)


def lower_chunk(z, double, after):
    def body(double, *refs):
        refs[-1][...] = double[16:32, :]

    places = "v" + "a" * len(after)
    return call(body, places, shape((16, z.wide)), [], 8, "lower_chunk")(double, *after)


def finish_backward(z, order, chunks, lasts, terms, parts, vectors, after):
    def body(*refs):
        e = z.experts
        chunks, (last_grad, last_act, inv_ref, affinity_ref) = refs[:e], refs[e : e + 4]
        parts, vectors = refs[e + 4 : e + 4 + z.split], refs[e + 4 + z.split]
        outs, (tile,) = refs[-1 - e : -1], refs[-1:]
        outs = [outs[order.index(k)] for k in range(e)]
        gain, router = vectors[0:1, :], vectors[1:2, :]

        def finished(h, g, at):
            inv, affinity = inv_ref[at : at + 16, 0:1], affinity_ref[at : at + 16, 0:1]
            rows = parts[0][at : at + 16, : z.width].astype(f32)
            dot = parts[0][at : at + 16, z.width :].astype(f32)
            for part in parts[1:]:
                rows = rows + part[at : at + 16, : z.width].astype(f32)
                dot = dot + part[at : at + 16, z.width :].astype(f32)
            dot = dot[:, 0:1]
            grad_logits = (route_scale * dot * affinity * (1.0 - affinity)).astype(bf16).astype(f32)
            grad_pre = (route_scale * affinity * rows + grad_logits * router) * gain
            centre = jnp.mean(grad_pre * h, axis=-1, keepdims=True)
            return g + inv * (grad_pre - h * (inv * inv * centre))

        tail = finished(last_act[...], last_grad[...], z.tokens)
        for k in range(e):
            g = chunks[k][:16, : z.width].astype(f32)
            h = chunks[k][16:32, : z.width].astype(f32)
            outs[k][:, : z.width] = finished(h, g, k * z.main).astype(bf16)
            put_last(z, tail[k : k + 1, :], chunks[k], tile, outs[k])

    return call(
        body,
        "v" * (z.experts + z.split + 5) + "a" * len(after),
        [shape((z.main, z.wide))] * z.experts,
        [pltpu.VMEM((16, fold), f32)],
        8,
        "finish_backward",
    )(*chunks, *lasts, *terms, *parts, vectors, *after)


def order_rows(z, arrays, places, after, name):
    count = len(arrays)
    lanes = z.tokens + 16 * z.experts
    steps = 7 if z.pieces % 7 == 0 else z.pieces

    def body(*refs):
        arrays, (out_any, out, sems) = refs[:count], refs[count + len(after) :]
        chunks = [arrays[i].at[pl.ds(at, 16)] for i, at in places]
        tiles = [chunk[:, z.width :] for chunk in chunks]
        token_row = tiles[0].astype(f32)[z.pieces : z.pieces + 1, :lanes]
        token = lax.broadcasted_iota(jnp.int32, (z.tokens, lanes), 0).astype(f32)
        lane = lax.broadcasted_iota(jnp.int32, (z.tokens, lanes), 1)
        piece = jnp.where(lane < z.tokens, -1, lane % 16)
        ours = token == token_row
        copies = []
        for i in range(z.pieces):
            cols = pl.ds(i * fold, fold)
            mine = ours & ((piece < 0) | (piece == i))
            selector = jnp.where(mine, 1.0, 0.0).astype(bf16)
            rows = jnp.concatenate([chunk[:, cols] for chunk in chunks] + tiles, axis=0)
            out[:, cols] = jnp.dot(selector, rows, preferred_element_type=f32).astype(bf16)
            if (i + 1) % (z.pieces // steps) == 0:
                done = pl.ds((i + 1) * fold - z.width // steps, z.width // steps)
                copy = pltpu.make_async_copy(out.at[:, done], out_any.at[:, done], sems.at[len(copies)])
                copy.start()
                copies.append(copy)
        for copy in copies:
            copy.wait()

    return call(
        body,
        "v" * count + "a" * len(after),
        shape((z.tokens, z.width)),
        [pltpu.VMEM((z.tokens, z.width), bf16), pltpu.SemaphoreType.DMA((steps,))],
        8,
        name,
        spaces["a"],
    )(*arrays, *after)


def permute_blocks(z, arrays, k):
    groups = z.experts * z.split
    pairs = [(i, ((i // z.split) ^ k) * z.split + i % z.split) for i in range(groups)]
    return [lax.ppermute(array, "ep", pairs) for array in arrays]


def dispatch(z, chunks):
    return [chunks[0]] + [permute_blocks(z, [chunks[k]], k)[0] for k in range(1, z.experts)]


def to_core(z, array, m):
    groups = z.experts * z.split
    pairs = [(i, i // z.split * z.split + ((i % z.split) ^ m)) for i in range(groups)]
    return lax.ppermute(array, "ep", pairs)


def to_section(z, chunk, k, by):
    groups = z.experts * z.split
    sections = lax.axis_size("pp")
    pairs = [
        (s * groups + i, (s + by) % sections * groups + ((i // z.split) ^ k) * z.split + i % z.split)
        for s in range(sections)
        for i in range(groups)
    ]
    return lax.ppermute(chunk, ("pp", "ep"), pairs)


def on_device(
    fwd_act, fwd_ids, bwd_act, bwd_ids, bwd_grad, norm_gain, router, w_gate, w_down, saved_gate
):
    groups = lax.axis_size("ep")
    assert fwd_ids.shape[1] == 1
    z = Sizes(groups, router.shape[2], fwd_act.shape[0], fwd_act.shape[1])
    index = lax.axis_index("ep")
    where = jnp.stack([index // z.split, index % z.split]).astype(jnp.int32)
    router = jnp.swapaxes(router, 1, 2)
    others = range(1, z.split)

    fwd_chunks = make_chunks(z, where, fwd_ids, [fwd_act], [], [], "forward_chunks")
    fwd_own = dispatch(z, fwd_chunks)
    *bwd_chunks, vectors = make_chunks(
        z,
        where,
        bwd_ids,
        [bwd_grad, bwd_act],
        [norm_gain, router],
        [fwd_chunks[0]],
        "backward_chunks",
    )
    bwd_own = dispatch(z, bwd_chunks)

    normed, gates, fwd_last = normed_rows(z, fwd_own, vectors)
    fwd_all = [normed] + [to_core(z, normed, m) for m in others]
    ordered = saved_rows(z, where, saved_gate, [w_gate, w_down], [gates])
    fwd_parts = experts_forward(z, fwd_all, w_gate, w_down, [ordered])
    hidden, slope = saved_terms(z, ordered, [fwd_parts[0]])
    fwd_parts = [fwd_parts[0]] + [to_core(z, fwd_parts[m], m) for m in others]

    assert z.experts == 4
    def finish(ks, after):
        return finish_forward(z, ks, fwd_own, fwd_last, fwd_parts, gates, after)

    double = finish([0, 1], [hidden])
    got = to_section(z, double, 0, 1)
    out2 = finish([2], [hidden, double])
    got2 = to_section(z, out2, 2, 1)
    grads, grad_last = grad_rows_of(z, bwd_own, [out2])
    grad_all = [grads] + [to_core(z, grads, m) for m in others]
    inv, act_last = act_norms(z, bwd_own, [grads])
    out3 = finish([3], [inv])
    got3 = to_section(z, out3, 3, 1)
    bwd_parts = experts_backward(z, grad_all, hidden, slope, w_gate, w_down, [inv])
    affinity = act_gates(z, bwd_own, act_last, inv, vectors, [bwd_parts[0], got])
    (relayed,) = permute_blocks(z, [lower_chunk(z, got, [affinity])], 1)
    fwd_done = [got2, got3]
    bwd_parts = [bwd_parts[0]] + [to_core(z, bwd_parts[m], m) for m in others]
    bwd_out = finish_backward(
        z, z.order, bwd_own, [grad_last, act_last], [inv, affinity], bwd_parts, vectors, []
    )
    bwd_done = {k: to_section(z, out, k, -1) for k, out in zip(z.order, bwd_out)}

    places = [(k, 0) for k in range(z.experts)]
    fwd_next = order_rows(z, [got, relayed, *fwd_done], places, [], "forward_rows")
    places = [(z.order.index(k), 0) for k in range(z.experts)]
    bwd_next = order_rows(z, [bwd_done[k] for k in z.order], places, [], "backward_rows")
    return (fwd_next, bwd_next)


def solution(mesh):
    return jax.shard_map(
        on_device,
        mesh=mesh,
        in_specs=(
            P(("pp", "ep"), None),
            P(("pp", "ep"), None),
            P(("pp", "ep"), None),
            P(("pp", "ep"), None),
            P(("pp", "ep"), None),
            P("pp", None),
            P("pp", None, None),
            P(("pp", "ep"), None, None),
            P(("pp", "ep"), None, None),
            P("pp", "ep", None, None),
        ),
        out_specs=(P(("pp", "ep"), None), P(("pp", "ep"), None)),
        check_vma=False,
    )
```

```python
import jax
import jax.numpy as jnp
from jax import lax
from jax.experimental import pallas as pl
from jax.experimental.pallas import tpu as pltpu
from jax.sharding import PartitionSpec as P

epsilon = 1e-06
route_scale = 2.5
fold = 256
none = 255.0
f32 = jnp.float32
bf16 = jnp.bfloat16
nt = (((1,), (1,)), ((), ()))
spaces = {
    "s": pl.BlockSpec(memory_space=pltpu.SMEM),
    "v": pl.BlockSpec(memory_space=pltpu.VMEM),
    "a": pl.BlockSpec(memory_space=pl.ANY),
    "h": pl.BlockSpec(memory_space=pltpu.HBM),
}


cost = {
    "backward_chunks": 10,
    "saved_rows": 15,
    "saved_terms": 15,
    "act_norms": 15,
    "act_gates": 15,
}


def call(body, places, outs, scratch, megabytes, name, out_specs=None):
    def run(*arrays):
        arrays = [
            pltpu.with_memory_space_constraint(array, pltpu.HBM) if place == "h" else array
            for array, place in zip(arrays, places, strict=True)
        ]
        return kernel(*arrays)

    where_to = {} if out_specs is None else {"out_specs": out_specs}
    kernel = pl.pallas_call(
        body,
        out_shape=outs,
        in_specs=[spaces[place] for place in places],
        **where_to,
        scratch_shapes=scratch,
        compiler_params=pltpu.CompilerParams(vmem_limit_bytes=megabytes * 1024 * 1024),
        cost_estimate=pl.CostEstimate(
            flops=int(cost.get(name, 0.1) * 1e9), bytes_accessed=1000, transcendentals=0
        ),
        name=name,
    )
    return run


def shape(dims, kind=bf16):
    return jax.ShapeDtypeStruct(dims, kind)


class Sizes:
    def __init__(self, groups, experts, tokens, width):
        self.experts = experts
        self.split = groups // experts
        self.tokens = tokens
        self.width = width
        self.main = tokens // experts
        self.cap = self.main + 1
        self.pieces = width // fold
        self.wide = width + fold
        self.rows = tokens + 16
        self.order = [experts - 1, *range(1, experts - 1), 0]
        assert self.main == 16 and self.pieces <= 14 and width % fold == 0
        assert experts <= 8 and experts & (experts - 1) == 0 and self.split & (self.split - 1) == 0


def pack_last(row, tile, first=0):
    for i in range(row.shape[1] // fold):
        tile[first + i : first + i + 1, :] = row[:, i * fold : (i + 1) * fold]


def unpack_last(chunk, z, tile, target, at, base=0):
    tile[...] = chunk[base : base + 16, z.width :].astype(f32)
    for i in range(z.pieces):
        target[at : at + 1, i * fold : (i + 1) * fold] = tile[i : i + 1, :]


def slot_matrices(ids_row, block, z):
    tokens = z.tokens
    sub = lax.broadcasted_iota(jnp.int32, (tokens, tokens), 0)
    lane = lax.broadcasted_iota(jnp.int32, (tokens, tokens), 1)
    row = jnp.bitwise_xor(ids_row, block)
    column = jnp.sum(jnp.where(sub == lane, row, 0), axis=1, keepdims=True)
    same = column == row
    place_row = jnp.sum(jnp.where(same & (sub < lane), 1, 0), axis=0, keepdims=True)
    place_column = jnp.sum(jnp.where(same & (lane < sub), 1, 0), axis=1, keepdims=True)

    def slot(expert, place):
        return jnp.where(place < z.main, expert * z.main + place, tokens + expert)

    slot_row = slot(row, place_row)
    slot_column = slot(column, place_column)
    by_slot = lax.broadcasted_iota(jnp.int32, (z.rows, tokens), 0) == slot_row
    lane = lax.broadcasted_iota(jnp.int32, (tokens, fold), 1)
    by_token = jnp.where(lane < tokens, lane, tokens + (lane - tokens) // 16) == slot_column
    token = lax.broadcasted_iota(jnp.int32, (tokens, fold), 0).astype(f32)
    token_row = jnp.sum(jnp.where(by_token, token - none, 0.0), axis=0, keepdims=True) + none
    return jnp.where(by_slot, 1.0, 0.0).astype(bf16), token_row


def write_chunks(z, selector, token_row, rows_ref, ready, tiles, chunks, base):
    step = z.width // 2
    tiles[...] = jnp.zeros_like(tiles)
    for half in range(2):
        if ready:
            ready[half].wait()
        col = half * step
        got = jnp.dot(selector, rows_ref[:, col : col + step], preferred_element_type=f32)
        packed = got[: z.tokens].astype(bf16)
        for k in range(z.experts):
            chunks[k][base : base + 16, col : col + step] = packed[k * z.main : (k + 1) * z.main]
            pack_last(got[z.tokens + k : z.tokens + k + 1], tiles.at[k], half * z.pieces // 2)
    for k in range(z.experts):
        tiles[k, z.pieces : z.pieces + 1, :] = token_row
        chunks[k][base : base + 16, z.width :] = tiles[k].astype(bf16)


def forward_chunks(z, where, ids, act, later_ids, later):
    count = len(later)

    def body(where, ids_any, later_ids_any, act_any, *refs):
        later_any, chunks = refs[:count], refs[count : count + z.experts]
        later_refs = refs[count + z.experts : 2 * count + z.experts]
        selector_ref, token_ref, ids, rows, tiles, sems = refs[2 * count + z.experts :]
        step = z.width // 2
        first = [
            pltpu.make_async_copy(source, ids.at[i : i + 1], sems.at[i])
            for i, source in enumerate((ids_any, later_ids_any))
        ]
        ready = [
            pltpu.make_async_copy(
                act_any.at[:, pl.ds(i * step, step)], rows.at[:, pl.ds(i * step, step)], sems.at[2 + i]
            )
            for i in range(2)
        ]
        rest = [
            pltpu.make_async_copy(source, target, sems.at[4 + i])
            for i, (source, target) in enumerate(zip(later_any, later_refs))
        ]
        for copy in first + ready + rest:
            copy.start()
        for copy in first:
            copy.wait()
        selector, token_row = slot_matrices(ids[0:1, :], where[0], z)
        later_selector, later_row = slot_matrices(ids[1:2, :], where[0], z)
        selector_ref[...] = later_selector
        token_ref[...] = jnp.broadcast_to(later_row, token_ref.shape)
        write_chunks(z, selector, token_row, rows, ready, tiles, chunks, 0)
        for copy in rest:
            copy.wait()

    outs = call(
        body,
        "shhh" + "h" * count,
        [shape((z.main, z.wide))] * z.experts
        + [shape(array.shape, array.dtype) for array in later]
        + [shape((z.rows, z.tokens)), shape((8, fold), f32)],
        [
            pltpu.VMEM((2, z.tokens), jnp.int32),
            pltpu.VMEM((z.tokens, z.width), bf16),
            pltpu.VMEM((z.experts, 16, fold), f32),
            pltpu.SemaphoreType.DMA((4 + count,)),
        ],
        8,
        "forward_chunks",
    )(where, ids.reshape(1, z.tokens), later_ids.reshape(1, z.tokens), act, *later)
    return outs[: z.experts], outs[z.experts : z.experts + count], outs[z.experts + count :]


def backward_chunks(z, where, slots, sources, gain, router):
    count = len(sources)

    def body(where, selector, token_ref, *refs):
        sources, (gain_ref, router_ref) = refs[:count], refs[count : count + 2]
        *chunks, vectors, tiles = refs[count + 2 :]
        for j in range(count):
            write_chunks(
                z, selector[...], token_ref[0:1, :], sources[j], None, tiles, chunks, 16 * j
            )
        vectors[...] = jnp.zeros_like(vectors)
        vectors[0:1, :] = gain_ref[...].astype(f32)
        mine = lax.broadcasted_iota(jnp.int32, (z.experts, 1), 0) == where[0]
        table = jnp.where(mine, router_ref[0].astype(f32), 0.0)
        vectors[1:2, :] = jnp.sum(table, axis=0, keepdims=True)

    *chunks, vectors = call(
        body,
        "svv" + "v" * (count + 2),
        [shape((z.main * count, z.wide))] * z.experts + [shape((8, z.width), f32)],
        [pltpu.VMEM((z.experts, 16, fold), f32)],
        8,
        "backward_chunks",
    )(where, *slots, *sources, gain, router)
    return chunks, vectors


def collect_rows(z, chunks, last, tile, base=0):
    last[...] = jnp.zeros_like(last)
    for k in range(z.experts):
        unpack_last(chunks[k], z, tile, last, k, base)


def norm_rows(h, gain):
    inv = lax.rsqrt(jnp.mean(h * h, axis=-1, keepdims=True) + epsilon)
    return (h * inv * gain).astype(bf16), inv


def normed_rows(z, chunks, vectors):
    def body(*refs):
        chunks, (vectors, normed_ref, gates_ref, last, tile) = refs[: z.experts], refs[z.experts :]
        gain, router = vectors[0:1, :], vectors[1:2, :]
        collect_rows(z, chunks, last, tile)
        for k in range(z.experts + 1):
            h = last[...] if k == z.experts else chunks[k][:, : z.width].astype(f32)
            at = k * z.main
            normed, _ = norm_rows(h, gain)
            normed_ref[at : at + 16, :] = normed
            logits = jnp.sum(normed.astype(f32) * router, axis=-1, keepdims=True)
            gates_ref[at : at + 16, :] = jnp.broadcast_to(jax.nn.sigmoid(logits), (16, 128))

    return call(
        body,
        "v" * (z.experts + 1),
        [shape((z.rows, z.width)), shape((z.rows, 128), f32), shape((16, z.width), f32)],
        [pltpu.VMEM((16, fold), f32)],
        8,
        "normed_rows",
    )(*chunks, vectors)


def grad_rows_of(z, chunks, after):
    def body(*refs):
        chunks, (rows, last, tile) = refs[: z.experts], refs[z.experts + len(after) :]
        for k in range(z.experts):
            rows[k * z.main : (k + 1) * z.main, :] = chunks[k][:16, : z.width]
        collect_rows(z, chunks, last, tile)
        rows[z.tokens :, :] = last[...].astype(bf16)

    return call(
        body,
        "v" * z.experts + "a" * len(after),
        [shape((z.rows, z.width)), shape((16, z.width), f32)],
        [pltpu.VMEM((16, fold), f32)],
        8,
        "grad_rows",
    )(*chunks, *after)


def act_norms(z, chunks, after):
    def body(*refs):
        chunks, (inv_ref, last, tile) = refs[: z.experts], refs[z.experts + len(after) :]
        collect_rows(z, chunks, last, tile, 16)
        for k in range(z.experts + 1):
            h = last[...] if k == z.experts else chunks[k][16:32, : z.width].astype(f32)
            at = k * z.main
            inv = lax.rsqrt(jnp.mean(h * h, axis=-1, keepdims=True) + epsilon)
            inv_ref[at : at + 16, :] = jnp.broadcast_to(inv, (16, 128))

    return call(
        body,
        "v" * z.experts + "a" * len(after),
        [shape((z.rows, 128), f32), shape((16, z.width), f32)],
        [pltpu.VMEM((16, fold), f32)],
        8,
        "act_norms",
    )(*chunks, *after)


def act_gates(z, chunks, last, inv, vectors, after):
    def body(*refs):
        chunks, (last, inv_ref, vectors) = refs[: z.experts], refs[z.experts : z.experts + 3]
        affinity_ref = refs[-1]
        gain, router = vectors[0:1, :], vectors[1:2, :]
        for k in range(z.experts + 1):
            h = last[...] if k == z.experts else chunks[k][16:32, : z.width].astype(f32)
            at = k * z.main
            normed = (h * inv_ref[at : at + 16, 0:1] * gain).astype(bf16).astype(f32)
            logits = jnp.sum(normed * router, axis=-1, keepdims=True)
            affinity_ref[at : at + 16, :] = jnp.broadcast_to(jax.nn.sigmoid(logits), (16, 128))

    return call(
        body,
        "v" * (z.experts + 3) + "a" * len(after),
        shape((z.rows, 128), f32),
        [],
        8,
        "act_gates",
    )(*chunks, last, inv, vectors, *after)


def write_parts(z, values, outs, col):
    values = values.astype(bf16)
    for m in range(z.split):
        outs[m][:, col : col + values.shape[1]] = values[m * z.rows : (m + 1) * z.rows]


def experts_forward(z, rows, w_gate, w_down, after):
    def body(*refs):
        rows, (gate_ref, down_ref), outs = (
            refs[: z.split],
            refs[z.split : z.split + 2],
            refs[z.split + 2 + len(after) :],
        )
        held = jnp.concatenate([part[...] for part in rows], axis=0)
        gate_proj = jnp.dot(held, gate_ref[0], preferred_element_type=f32)
        hidden = jax.nn.silu(gate_proj).astype(bf16)
        step = 512
        for col in range(0, z.width, step):
            part = jnp.dot(hidden, down_ref[0, :, col : col + step], preferred_element_type=f32)
            write_parts(z, part, outs, col)

    return call(
        body,
        "v" * (z.split + 2) + "a" * len(after),
        [shape((z.rows, z.width))] * z.split,
        [],
        16,
        "experts_forward",
    )(*rows, w_gate, w_down, *after)


def saved_rows(z, where, saved, weights, after):
    total, slots, width = z.split * z.rows, saved.shape[2], saved.shape[3]

    def body(where, saved_any, *refs):
        ordered_ref, saved_ref, sem = refs[len(weights) + len(after) :]
        copy = pltpu.make_async_copy(saved_any.at[0, 0], saved_ref, sem)
        copy.start()
        row = lax.broadcasted_iota(jnp.int32, (total, slots), 0)
        slot = lax.broadcasted_iota(jnp.int32, (total, slots), 1)
        m, at = row // z.rows, row % z.rows
        is_main = at < z.tokens
        k = jnp.where(is_main, at // z.main, at - z.tokens)
        p = jnp.where(is_main, at % z.main, z.main)
        source = jnp.bitwise_xor(k, where[0]) * z.split + jnp.bitwise_xor(m, where[1])
        wanted = jnp.where(k < z.experts, source * z.cap + p, -1)
        selector = jnp.where(slot == wanted, 1.0, 0.0).astype(bf16)
        copy.wait()
        ordered_ref[...] = jnp.dot(selector, saved_ref[...], preferred_element_type=f32)

    return call(
        body,
        "sh" + "v" * len(weights) + "a" * len(after),
        shape((total, width), f32),
        [pltpu.VMEM((slots, width), bf16), pltpu.SemaphoreType.DMA],
        8,
        "saved_rows",
    )(where, saved, *weights, *after)


def saved_terms(z, ordered, after):
    def body(ordered_ref, *refs):
        hidden_ref, slope_ref = refs[len(after) :]
        gate_proj = ordered_ref[...]
        sg = jax.nn.sigmoid(gate_proj)
        hidden_ref[...] = (gate_proj * sg).astype(bf16)
        slope_ref[...] = sg * (1.0 + gate_proj * (1.0 - sg))

    return call(
        body,
        "v" + "a" * len(after),
        [shape(ordered.shape), shape(ordered.shape, f32)],
        [],
        8,
        "saved_terms",
    )(ordered, *after)


def experts_backward(z, rows, hidden, slope, w_gate, w_down, after):
    def body(*refs):
        rows = refs[: z.split]
        hidden_ref, slope_ref, gate_ref, down_ref = refs[z.split : z.split + 4]
        outs = refs[z.split + 4 + len(after) :]
        held = jnp.concatenate([part[...] for part in rows], axis=0)
        grad_hidden = lax.dot_general(held, down_ref[0], nt, preferred_element_type=f32)
        dots = jnp.sum(grad_hidden * hidden_ref[...].astype(f32), axis=-1, keepdims=True)
        grad_gate = (grad_hidden * slope_ref[...]).astype(bf16)
        step = 512
        for col in range(0, z.width, step):
            part = lax.dot_general(
                grad_gate, gate_ref[0, col : col + step, :], nt, preferred_element_type=f32
            )
            write_parts(z, part, outs, col)
        write_parts(z, jnp.broadcast_to(dots, (dots.shape[0], 128)), outs, z.width)

    return call(
        body,
        "v" * (z.split + 4) + "a" * len(after),
        [shape((z.rows, z.width + 128))] * z.split,
        [],
        16,
        "experts_backward",
    )(*rows, hidden, slope, w_gate, w_down, *after)


def put_last(z, values, source_chunk, tile, out):
    tile[...] = jnp.zeros_like(tile)
    pack_last(values, tile)
    tokens = source_chunk[:16, z.width :].astype(f32)
    tile[z.pieces : z.pieces + 1, :] = tokens[z.pieces : z.pieces + 1, :]
    out[:, z.width :] = tile[...].astype(bf16)


def finish_forward(z, ks, chunks, last, parts, gates, after):
    count = len(ks)

    def body(*refs):
        chunks, last, parts = refs[:count], refs[count], refs[count + 1 : count + 1 + z.split]
        gates, out, tile = refs[count + 1 + z.split], refs[-2], refs[-1]

        def mixed(at):
            y = parts[0][at : at + 16, :].astype(f32)
            for part in parts[1:]:
                y = y + part[at : at + 16, :].astype(f32)
            return route_scale * (gates[at : at + 16, 0:1] * y)

        tail = last[...] + mixed(z.tokens)
        for i, (k, chunk) in enumerate(zip(ks, chunks)):
            h = chunk[:, : z.width].astype(f32)
            rows = out.at[pl.ds(i * 16, 16)]
            rows[:, : z.width] = (h + mixed(k * z.main)).astype(bf16)
            put_last(z, tail[k : k + 1, :], chunk, tile, rows)

    return call(
        body,
        "v" * (count + z.split + 2) + "a" * len(after),
        shape((count * z.main, z.wide)),
        [pltpu.VMEM((16, fold), f32)],
        8,
        "finish_forward_" + "".join(map(str, ks)),
    )(*[chunks[k] for k in ks], last, *parts, gates, *after)


def lower_chunk(z, double, after):
    def body(double, *refs):
        refs[-1][...] = double[16:32, :]

    places = "v" + "a" * len(after)
    return call(body, places, shape((16, z.wide)), [], 8, "lower_chunk")(double, *after)


def finish_backward(z, order, chunks, lasts, terms, parts, vectors, after):
    def body(*refs):
        e = z.experts
        chunks, (last_grad, last_act, inv_ref, affinity_ref) = refs[:e], refs[e : e + 4]
        parts, vectors = refs[e + 4 : e + 4 + z.split], refs[e + 4 + z.split]
        outs, (tile,) = refs[-1 - e : -1], refs[-1:]
        outs = [outs[order.index(k)] for k in range(e)]
        gain, router = vectors[0:1, :], vectors[1:2, :]

        def finished(h, g, at):
            inv, affinity = inv_ref[at : at + 16, 0:1], affinity_ref[at : at + 16, 0:1]
            rows = parts[0][at : at + 16, : z.width].astype(f32)
            dot = parts[0][at : at + 16, z.width :].astype(f32)
            for part in parts[1:]:
                rows = rows + part[at : at + 16, : z.width].astype(f32)
                dot = dot + part[at : at + 16, z.width :].astype(f32)
            dot = dot[:, 0:1]
            grad_logits = (route_scale * dot * affinity * (1.0 - affinity)).astype(bf16).astype(f32)
            grad_pre = (route_scale * affinity * rows + grad_logits * router) * gain
            centre = jnp.mean(grad_pre * h, axis=-1, keepdims=True)
            return g + inv * (grad_pre - h * (inv * inv * centre))

        tail = finished(last_act[...], last_grad[...], z.tokens)
        for k in range(e):
            g = chunks[k][:16, : z.width].astype(f32)
            h = chunks[k][16:32, : z.width].astype(f32)
            outs[k][:, : z.width] = finished(h, g, k * z.main).astype(bf16)
            put_last(z, tail[k : k + 1, :], chunks[k], tile, outs[k])

    return call(
        body,
        "v" * (z.experts + z.split + 5) + "a" * len(after),
        [shape((z.main, z.wide))] * z.experts,
        [pltpu.VMEM((16, fold), f32)],
        8,
        "finish_backward",
    )(*chunks, *lasts, *terms, *parts, vectors, *after)


def order_rows(z, arrays, places, after, name):
    count = len(arrays)
    lanes = z.tokens + 16 * z.experts
    steps = 7 if z.pieces % 7 == 0 else z.pieces

    def body(*refs):
        arrays, (out_any, out, sems) = refs[:count], refs[count + len(after) :]
        chunks = [arrays[i].at[pl.ds(at, 16)] for i, at in places]
        tiles = [chunk[:, z.width :] for chunk in chunks]
        token_row = tiles[0].astype(f32)[z.pieces : z.pieces + 1, :lanes]
        token = lax.broadcasted_iota(jnp.int32, (z.tokens, lanes), 0).astype(f32)
        lane = lax.broadcasted_iota(jnp.int32, (z.tokens, lanes), 1)
        piece = jnp.where(lane < z.tokens, -1, lane % 16)
        ours = token == token_row
        copies = []
        for i in range(z.pieces):
            cols = pl.ds(i * fold, fold)
            mine = ours & ((piece < 0) | (piece == i))
            selector = jnp.where(mine, 1.0, 0.0).astype(bf16)
            rows = jnp.concatenate([chunk[:, cols] for chunk in chunks] + tiles, axis=0)
            out[:, cols] = jnp.dot(selector, rows, preferred_element_type=f32).astype(bf16)
            if (i + 1) % (z.pieces // steps) == 0:
                done = pl.ds((i + 1) * fold - z.width // steps, z.width // steps)
                copy = pltpu.make_async_copy(out.at[:, done], out_any.at[:, done], sems.at[len(copies)])
                copy.start()
                copies.append(copy)
        for copy in copies:
            copy.wait()

    return call(
        body,
        "v" * count + "a" * len(after),
        shape((z.tokens, z.width)),
        [pltpu.VMEM((z.tokens, z.width), bf16), pltpu.SemaphoreType.DMA((steps,))],
        8,
        name,
        spaces["a"],
    )(*arrays, *after)


def permute_blocks(z, arrays, k):
    groups = z.experts * z.split
    pairs = [(i, ((i // z.split) ^ k) * z.split + i % z.split) for i in range(groups)]
    return [lax.ppermute(array, "ep", pairs) for array in arrays]


def dispatch(z, chunks):
    return [chunks[0]] + [permute_blocks(z, [chunks[k]], k)[0] for k in range(1, z.experts)]


def to_core(z, array, m):
    groups = z.experts * z.split
    pairs = [(i, i // z.split * z.split + ((i % z.split) ^ m)) for i in range(groups)]
    return lax.ppermute(array, "ep", pairs)


def to_section(z, chunk, k, by):
    groups = z.experts * z.split
    sections = lax.axis_size("pp")
    pairs = [
        (s * groups + i, (s + by) % sections * groups + ((i // z.split) ^ k) * z.split + i % z.split)
        for s in range(sections)
        for i in range(groups)
    ]
    return lax.ppermute(chunk, ("pp", "ep"), pairs)


def on_device(
    fwd_act, fwd_ids, bwd_act, bwd_ids, bwd_grad, norm_gain, router, w_gate, w_down, saved_gate
):
    groups = lax.axis_size("ep")
    assert fwd_ids.shape[1] == 1
    z = Sizes(groups, router.shape[2], fwd_act.shape[0], fwd_act.shape[1])
    index = lax.axis_index("ep")
    where = jnp.stack([index // z.split, index % z.split]).astype(jnp.int32)
    router = jnp.swapaxes(router, 1, 2)
    others = range(1, z.split)

    fwd_chunks, (grad, act, gain_row, table), slots = forward_chunks(
        z, where, fwd_ids, fwd_act, bwd_ids, [bwd_grad, bwd_act, norm_gain, router]
    )
    fwd_own = dispatch(z, fwd_chunks)
    bwd_chunks, vectors = backward_chunks(z, where, slots, [grad, act], gain_row, table)
    bwd_own = dispatch(z, bwd_chunks)

    normed, gates, fwd_last = normed_rows(z, fwd_own, vectors)
    fwd_all = [normed] + [to_core(z, normed, m) for m in others]
    ordered = saved_rows(z, where, saved_gate, [w_gate, w_down], [gates])
    fwd_parts = experts_forward(z, fwd_all, w_gate, w_down, [ordered])
    hidden, slope = saved_terms(z, ordered, [fwd_parts[0]])
    fwd_parts = [fwd_parts[0]] + [to_core(z, fwd_parts[m], m) for m in others]

    assert z.experts == 4

    def finish(ks, after):
        return finish_forward(z, ks, fwd_own, fwd_last, fwd_parts, gates, after)

    double = finish([0, 1], [hidden])
    got = to_section(z, double, 0, 1)
    out2 = finish([2], [hidden, double])
    got2 = to_section(z, out2, 2, 1)
    grads, grad_last = grad_rows_of(z, bwd_own, [out2])
    grad_all = [grads] + [to_core(z, grads, m) for m in others]
    inv, act_last = act_norms(z, bwd_own, [grads])
    out3 = finish([3], [inv])
    got3 = to_section(z, out3, 3, 1)
    bwd_parts = experts_backward(z, grad_all, hidden, slope, w_gate, w_down, [inv])
    affinity = act_gates(z, bwd_own, act_last, inv, vectors, [bwd_parts[0], got])
    (relayed,) = permute_blocks(z, [lower_chunk(z, got, [affinity])], 1)
    fwd_done = [got2, got3]
    bwd_parts = [bwd_parts[0]] + [to_core(z, bwd_parts[m], m) for m in others]
    bwd_out = finish_backward(
        z, z.order, bwd_own, [grad_last, act_last], [inv, affinity], bwd_parts, vectors, []
    )
    bwd_done = {k: to_section(z, out, k, -1) for k, out in zip(z.order, bwd_out)}

    places = [(k, 0) for k in range(z.experts)]
    fwd_next = order_rows(z, [got, relayed, *fwd_done], places, [], "forward_rows")
    places = [(z.order.index(k), 0) for k in range(z.experts)]
    bwd_next = order_rows(z, [bwd_done[k] for k in z.order], places, [], "backward_rows")
    return (fwd_next, bwd_next)


def solution(mesh):
    return jax.shard_map(
        on_device,
        mesh=mesh,
        in_specs=(
            P(("pp", "ep"), None),
            P(("pp", "ep"), None),
            P(("pp", "ep"), None),
            P(("pp", "ep"), None),
            P(("pp", "ep"), None),
            P("pp", None),
            P("pp", None, None),
            P(("pp", "ep"), None, None),
            P(("pp", "ep"), None, None),
            P("pp", "ep", None, None),
        ),
        out_specs=(P(("pp", "ep"), None), P(("pp", "ep"), None)),
        check_vma=False,
    )
```

```python
import jax
import jax.numpy as jnp
from jax import lax
from jax.experimental import pallas as pl
from jax.experimental.pallas import tpu as pltpu
from jax.sharding import PartitionSpec as P

epsilon = 1e-06
route_scale = 2.5
fold = 256
none = 255.0
f32 = jnp.float32
bf16 = jnp.bfloat16
nn = (((1,), (0,)), ((), ()))
spaces = {
    "s": pl.BlockSpec(memory_space=pltpu.SMEM),
    "v": pl.BlockSpec(memory_space=pltpu.VMEM),
    "a": pl.BlockSpec(memory_space=pl.ANY),
    "h": pl.BlockSpec(memory_space=pltpu.HBM),
}


cost = {
    "backward_chunks": 10,
    "saved_rows": 15,
    "saved_terms": 15,
    "act_norms": 15,
    "act_gates": 15,
}


def call(body, places, outs, scratch, megabytes, name, out_specs=None):
    def run(*arrays):
        arrays = [
            pltpu.with_memory_space_constraint(array, pltpu.HBM) if place == "h" else array
            for array, place in zip(arrays, places, strict=True)
        ]
        return kernel(*arrays)

    where_to = {} if out_specs is None else {"out_specs": out_specs}
    kernel = pl.pallas_call(
        body,
        out_shape=outs,
        in_specs=[spaces[place] for place in places],
        **where_to,
        scratch_shapes=scratch,
        compiler_params=pltpu.CompilerParams(vmem_limit_bytes=megabytes * 1024 * 1024),
        cost_estimate=pl.CostEstimate(
            flops=int(cost.get(name, 0.1) * 1e9), bytes_accessed=1000, transcendentals=0
        ),
        name=name,
    )
    return run


def shape(dims, kind=bf16):
    return jax.ShapeDtypeStruct(dims, kind)


class Sizes:
    def __init__(self, groups, experts, tokens, width):
        self.experts = experts
        self.split = groups // experts
        self.tokens = tokens
        self.width = width
        self.main = tokens // experts
        self.cap = self.main + 1
        self.pieces = width // fold
        self.wide = width + fold
        self.rows = tokens + 16
        self.order = [experts - 1, *range(1, experts - 1), 0]
        assert self.main == 16 and self.pieces <= 14 and width % fold == 0
        assert experts <= 8 and experts & (experts - 1) == 0 and self.split & (self.split - 1) == 0


def pack_last(row, tile, first=0):
    for i in range(row.shape[1] // fold):
        tile[first + i : first + i + 1, :] = row[:, i * fold : (i + 1) * fold]


def unpack_last(chunk, z, tile, target, at, base=0):
    tile[...] = chunk[base : base + 16, z.width :].astype(f32)
    for i in range(z.pieces):
        target[at : at + 1, i * fold : (i + 1) * fold] = tile[i : i + 1, :]


def slot_matrices(ids_row, block, z):
    tokens = z.tokens
    sub = lax.broadcasted_iota(jnp.int32, (tokens, tokens), 0)
    lane = lax.broadcasted_iota(jnp.int32, (tokens, tokens), 1)
    row = jnp.bitwise_xor(ids_row, block)
    column = jnp.sum(jnp.where(sub == lane, row, 0), axis=1, keepdims=True)
    same = column == row
    place_row = jnp.sum(jnp.where(same & (sub < lane), 1, 0), axis=0, keepdims=True)
    place_column = jnp.sum(jnp.where(same & (lane < sub), 1, 0), axis=1, keepdims=True)

    def slot(expert, place):
        return jnp.where(place < z.main, expert * z.main + place, tokens + expert)

    slot_row = slot(row, place_row)
    slot_column = slot(column, place_column)
    by_slot = lax.broadcasted_iota(jnp.int32, (z.rows, tokens), 0) == slot_row
    lane = lax.broadcasted_iota(jnp.int32, (tokens, fold), 1)
    by_token = jnp.where(lane < tokens, lane, tokens + (lane - tokens) // 16) == slot_column
    token = lax.broadcasted_iota(jnp.int32, (tokens, fold), 0).astype(f32)
    token_row = jnp.sum(jnp.where(by_token, token - none, 0.0), axis=0, keepdims=True) + none
    return jnp.where(by_slot, 1.0, 0.0).astype(bf16), token_row


def write_chunks(z, selector, token_row, rows_ref, ready, tiles, chunks, base):
    step = z.width // 2
    tiles[...] = jnp.zeros_like(tiles)
    for half in range(2):
        if ready:
            ready[half].wait()
        col = half * step
        got = jnp.dot(selector, rows_ref[:, col : col + step], preferred_element_type=f32)
        packed = got[: z.tokens].astype(bf16)
        for k in range(z.experts):
            chunks[k][base : base + 16, col : col + step] = packed[k * z.main : (k + 1) * z.main]
            pack_last(got[z.tokens + k : z.tokens + k + 1], tiles.at[k], half * z.pieces // 2)
    for k in range(z.experts):
        tiles[k, z.pieces : z.pieces + 1, :] = token_row
        chunks[k][base : base + 16, z.width :] = tiles[k].astype(bf16)


def forward_chunks(z, where, ids, act, later_ids, later):
    count = len(later)

    def body(where, ids_any, later_ids_any, act_any, *refs):
        later_any, chunks = refs[:count], refs[count : count + z.experts]
        later_refs = refs[count + z.experts : 2 * count + z.experts]
        selector_ref, token_ref, ids, rows, tiles, sems = refs[2 * count + z.experts :]
        step = z.width // 2
        first = [
            pltpu.make_async_copy(source, ids.at[i : i + 1], sems.at[i])
            for i, source in enumerate((ids_any, later_ids_any))
        ]
        ready = [
            pltpu.make_async_copy(
                act_any.at[:, pl.ds(i * step, step)], rows.at[:, pl.ds(i * step, step)], sems.at[2 + i]
            )
            for i in range(2)
        ]
        rest = [
            pltpu.make_async_copy(source, target, sems.at[4 + i])
            for i, (source, target) in enumerate(zip(later_any, later_refs))
        ]
        for copy in first + ready + rest:
            copy.start()
        for copy in first:
            copy.wait()
        selector, token_row = slot_matrices(ids[0:1, :], where[0], z)
        later_selector, later_row = slot_matrices(ids[1:2, :], where[0], z)
        selector_ref[...] = later_selector
        token_ref[...] = jnp.broadcast_to(later_row, token_ref.shape)
        write_chunks(z, selector, token_row, rows, ready, tiles, chunks, 0)
        for copy in rest:
            copy.wait()

    outs = call(
        body,
        "shhh" + "h" * count,
        [shape((z.main, z.wide))] * z.experts
        + [shape(array.shape, array.dtype) for array in later]
        + [shape((z.rows, z.tokens)), shape((8, fold), f32)],
        [
            pltpu.VMEM((2, z.tokens), jnp.int32),
            pltpu.VMEM((z.tokens, z.width), bf16),
            pltpu.VMEM((z.experts, 16, fold), f32),
            pltpu.SemaphoreType.DMA((4 + count,)),
        ],
        8,
        "forward_chunks",
    )(where, ids.reshape(1, z.tokens), later_ids.reshape(1, z.tokens), act, *later)
    return outs[: z.experts], outs[z.experts : z.experts + count], outs[z.experts + count :]


def backward_chunks(z, where, slots, sources, gain, router):
    count = len(sources)

    def body(where, selector, token_ref, *refs):
        sources, (gain_ref, router_ref) = refs[:count], refs[count : count + 2]
        *chunks, vectors, tiles = refs[count + 2 :]
        for j in range(count):
            write_chunks(
                z, selector[...], token_ref[0:1, :], sources[j], None, tiles, chunks, 16 * j
            )
        vectors[...] = jnp.zeros_like(vectors)
        vectors[0:1, :] = gain_ref[...].astype(f32)
        mine = lax.broadcasted_iota(jnp.int32, (z.experts, 1), 0) == where[0]
        table = jnp.where(mine, router_ref[0].astype(f32), 0.0)
        vectors[1:2, :] = jnp.sum(table, axis=0, keepdims=True)

    *chunks, vectors = call(
        body,
        "svv" + "v" * (count + 2),
        [shape((z.main * count, z.wide))] * z.experts + [shape((8, z.width), f32)],
        [pltpu.VMEM((z.experts, 16, fold), f32)],
        8,
        "backward_chunks",
    )(where, *slots, *sources, gain, router)
    return chunks, vectors


def collect_rows(z, chunks, last, tile, base=0):
    last[...] = jnp.zeros_like(last)
    for k in range(z.experts):
        unpack_last(chunks[k], z, tile, last, k, base)


def norm_rows(h, gain):
    inv = lax.rsqrt(jnp.mean(h * h, axis=-1, keepdims=True) + epsilon)
    return (h * inv * gain).astype(bf16), inv


def normed_rows(z, chunks, vectors, after):
    def body(*refs):
        chunks, vectors = refs[: z.experts], refs[z.experts]
        normed_ref, gates_ref, last, tile = refs[z.experts + 1 + len(after) :]
        gain, router = vectors[0:1, :], vectors[1:2, :]
        collect_rows(z, chunks, last, tile)
        for k in range(z.experts + 1):
            h = last[...] if k == z.experts else chunks[k][:, : z.width].astype(f32)
            at = k * z.main
            normed, _ = norm_rows(h, gain)
            normed_ref[at : at + 16, :] = normed
            logits = jnp.sum(normed.astype(f32) * router, axis=-1, keepdims=True)
            gates_ref[at : at + 16, :] = jnp.broadcast_to(jax.nn.sigmoid(logits), (16, 128))

    return call(
        body,
        "v" * (z.experts + 1) + "a" * len(after),
        [shape((z.rows, z.width)), shape((z.rows, 128), f32), shape((16, z.width), f32)],
        [pltpu.VMEM((16, fold), f32)],
        8,
        "normed_rows",
    )(*chunks, vectors, *after)


def grad_rows_of(z, chunks, after):
    def body(*refs):
        chunks, (rows, last, tile) = refs[: z.experts], refs[z.experts + len(after) :]
        for k in range(z.experts):
            rows[k * z.main : (k + 1) * z.main, :] = chunks[k][:16, : z.width]
        collect_rows(z, chunks, last, tile)
        rows[z.tokens :, :] = last[...].astype(bf16)

    return call(
        body,
        "v" * z.experts + "a" * len(after),
        [shape((z.rows, z.width)), shape((16, z.width), f32)],
        [pltpu.VMEM((16, fold), f32)],
        8,
        "grad_rows",
    )(*chunks, *after)


def act_norms(z, chunks, after):
    def body(*refs):
        chunks, (inv_ref, last, tile) = refs[: z.experts], refs[z.experts + len(after) :]
        collect_rows(z, chunks, last, tile, 16)
        for k in range(z.experts + 1):
            h = last[...] if k == z.experts else chunks[k][16:32, : z.width].astype(f32)
            at = k * z.main
            inv = lax.rsqrt(jnp.mean(h * h, axis=-1, keepdims=True) + epsilon)
            inv_ref[at : at + 16, :] = jnp.broadcast_to(inv, (16, 128))

    return call(
        body,
        "v" * z.experts + "a" * len(after),
        [shape((z.rows, 128), f32), shape((16, z.width), f32)],
        [pltpu.VMEM((16, fold), f32)],
        8,
        "act_norms",
    )(*chunks, *after)


def act_gates(z, chunks, last, inv, vectors, after):
    def body(*refs):
        chunks, (last, inv_ref, vectors) = refs[: z.experts], refs[z.experts : z.experts + 3]
        affinity_ref = refs[-1]
        gain, router = vectors[0:1, :], vectors[1:2, :]
        for k in range(z.experts + 1):
            h = last[...] if k == z.experts else chunks[k][16:32, : z.width].astype(f32)
            at = k * z.main
            normed = (h * inv_ref[at : at + 16, 0:1] * gain).astype(bf16).astype(f32)
            logits = jnp.sum(normed * router, axis=-1, keepdims=True)
            affinity_ref[at : at + 16, :] = jnp.broadcast_to(jax.nn.sigmoid(logits), (16, 128))

    return call(
        body,
        "v" * (z.experts + 3) + "a" * len(after),
        shape((z.rows, 128), f32),
        [],
        8,
        "act_gates",
    )(*chunks, last, inv, vectors, *after)


def write_parts(z, values, outs, col):
    values = values.astype(bf16)
    for m in range(z.split):
        outs[m][:, col : col + values.shape[1]] = values[m * z.rows : (m + 1) * z.rows]


def experts_forward(z, rows, w_gate, w_down, after):
    def body(*refs):
        rows, (gate_ref, down_ref), outs = (
            refs[: z.split],
            refs[z.split : z.split + 2],
            refs[z.split + 2 + len(after) :],
        )
        held = jnp.concatenate([part[...] for part in rows], axis=0)
        gate_proj = jnp.dot(held, gate_ref[0], preferred_element_type=f32)
        hidden = jax.nn.silu(gate_proj).astype(bf16)
        step = 512
        for col in range(0, z.width, step):
            part = jnp.dot(hidden, down_ref[0, :, col : col + step], preferred_element_type=f32)
            write_parts(z, part, outs, col)

    return call(
        body,
        "v" * (z.split + 2) + "a" * len(after),
        [shape((z.rows, z.width))] * z.split,
        [],
        16,
        "experts_forward",
    )(*rows, w_gate, w_down, *after)


def saved_rows(z, where, saved, weights, after):
    total, slots, width = z.split * z.rows, saved.shape[2], saved.shape[3]

    def body(where, saved_any, *refs):
        ordered_ref, saved_ref, sem = refs[len(weights) + len(after) :]
        copy = pltpu.make_async_copy(saved_any.at[0, 0], saved_ref, sem)
        copy.start()
        row = lax.broadcasted_iota(jnp.int32, (total, slots), 0)
        slot = lax.broadcasted_iota(jnp.int32, (total, slots), 1)
        m, at = row // z.rows, row % z.rows
        is_main = at < z.tokens
        k = jnp.where(is_main, at // z.main, at - z.tokens)
        p = jnp.where(is_main, at % z.main, z.main)
        source = jnp.bitwise_xor(k, where[0]) * z.split + jnp.bitwise_xor(m, where[1])
        wanted = jnp.where(k < z.experts, source * z.cap + p, -1)
        selector = jnp.where(slot == wanted, 1.0, 0.0).astype(bf16)
        copy.wait()
        ordered_ref[...] = jnp.dot(selector, saved_ref[...], preferred_element_type=f32)

    return call(
        body,
        "sh" + "v" * len(weights) + "a" * len(after),
        shape((total, width), f32),
        [pltpu.VMEM((slots, width), bf16), pltpu.SemaphoreType.DMA],
        8,
        "saved_rows",
    )(where, saved, *weights, *after)


def saved_terms(z, ordered, after):
    def body(ordered_ref, *refs):
        hidden_ref, slope_ref = refs[len(after) :]
        gate_proj = ordered_ref[...]
        sg = jax.nn.sigmoid(gate_proj)
        hidden_ref[...] = (gate_proj * sg).astype(bf16)
        slope_ref[...] = sg * (1.0 + gate_proj * (1.0 - sg))

    return call(
        body,
        "v" + "a" * len(after),
        [shape(ordered.shape), shape(ordered.shape, f32)],
        [],
        8,
        "saved_terms",
    )(ordered, *after)


def turned(z, weights, held, after, name):
    rows, columns = weights.shape[1:]
    step = min(512, rows, columns)

    def body(weights_ref, *refs):
        for at in range(0, rows, step):
            for col in range(0, columns, step):
                block = weights_ref[0, at : at + step, col : col + step]
                refs[-1][col : col + step, at : at + step] = block.T

    return call(
        body, "v" + "v" * len(held) + "a" * len(after), shape((columns, rows)), [], 12, name
    )(weights, *held, *after)


def experts_backward(z, rows, hidden, slope, w_gate, w_down, after):
    def body(*refs):
        rows = refs[: z.split]
        hidden_ref, slope_ref, gate_ref, down_ref = refs[z.split : z.split + 4]
        outs = refs[z.split + 4 + len(after) :]
        held = jnp.concatenate([part[...] for part in rows], axis=0)
        grad_hidden = lax.dot_general(held, down_ref[...], nn, preferred_element_type=f32)
        dots = jnp.sum(grad_hidden * hidden_ref[...].astype(f32), axis=-1, keepdims=True)
        grad_gate = (grad_hidden * slope_ref[...]).astype(bf16)
        step = 512
        for col in range(0, z.width, step):
            part = lax.dot_general(
                grad_gate, gate_ref[:, col : col + step], nn, preferred_element_type=f32
            )
            write_parts(z, part, outs, col)
        write_parts(z, jnp.broadcast_to(dots, (dots.shape[0], 128)), outs, z.width)

    return call(
        body,
        "v" * (z.split + 4) + "a" * len(after),
        [shape((z.rows, z.width + 128))] * z.split,
        [],
        16,
        "experts_backward",
    )(*rows, hidden, slope, w_gate, w_down, *after)


def put_last(z, values, source_chunk, tile, out):
    tile[...] = jnp.zeros_like(tile)
    pack_last(values, tile)
    tokens = source_chunk[:16, z.width :].astype(f32)
    tile[z.pieces : z.pieces + 1, :] = tokens[z.pieces : z.pieces + 1, :]
    out[:, z.width :] = tile[...].astype(bf16)


def finish_forward(z, ks, chunks, last, parts, gates, after):
    count = len(ks)

    def body(*refs):
        chunks, last, parts = refs[:count], refs[count], refs[count + 1 : count + 1 + z.split]
        gates, out, tile = refs[count + 1 + z.split], refs[-2], refs[-1]

        def mixed(at):
            y = parts[0][at : at + 16, :].astype(f32)
            for part in parts[1:]:
                y = y + part[at : at + 16, :].astype(f32)
            return route_scale * (gates[at : at + 16, 0:1] * y)

        tail = last[...] + mixed(z.tokens)
        for i, (k, chunk) in enumerate(zip(ks, chunks)):
            h = chunk[:, : z.width].astype(f32)
            rows = out.at[pl.ds(i * 16, 16)]
            rows[:, : z.width] = (h + mixed(k * z.main)).astype(bf16)
            put_last(z, tail[k : k + 1, :], chunk, tile, rows)

    return call(
        body,
        "v" * (count + z.split + 2) + "a" * len(after),
        shape((count * z.main, z.wide)),
        [pltpu.VMEM((16, fold), f32)],
        8,
        "finish_forward_" + "".join(map(str, ks)),
    )(*[chunks[k] for k in ks], last, *parts, gates, *after)


def lower_chunk(z, double, after):
    def body(double, *refs):
        refs[-1][...] = double[16:32, :]

    places = "v" + "a" * len(after)
    return call(body, places, shape((16, z.wide)), [], 8, "lower_chunk")(double, *after)


def finish_backward(z, order, chunks, lasts, terms, parts, vectors, after):
    def body(*refs):
        e = z.experts
        chunks, (last_grad, last_act, inv_ref, affinity_ref) = refs[:e], refs[e : e + 4]
        parts, vectors = refs[e + 4 : e + 4 + z.split], refs[e + 4 + z.split]
        outs, (tile,) = refs[-1 - e : -1], refs[-1:]
        outs = [outs[order.index(k)] for k in range(e)]
        gain, router = vectors[0:1, :], vectors[1:2, :]

        def finished(h, g, at):
            inv, affinity = inv_ref[at : at + 16, 0:1], affinity_ref[at : at + 16, 0:1]
            rows = parts[0][at : at + 16, : z.width].astype(f32)
            dot = parts[0][at : at + 16, z.width :].astype(f32)
            for part in parts[1:]:
                rows = rows + part[at : at + 16, : z.width].astype(f32)
                dot = dot + part[at : at + 16, z.width :].astype(f32)
            dot = dot[:, 0:1]
            grad_logits = (route_scale * dot * affinity * (1.0 - affinity)).astype(bf16).astype(f32)
            grad_pre = (route_scale * affinity * rows + grad_logits * router) * gain
            centre = jnp.mean(grad_pre * h, axis=-1, keepdims=True)
            return g + inv * (grad_pre - h * (inv * inv * centre))

        tail = finished(last_act[...], last_grad[...], z.tokens)
        for k in range(e):
            g = chunks[k][:16, : z.width].astype(f32)
            h = chunks[k][16:32, : z.width].astype(f32)
            outs[k][:, : z.width] = finished(h, g, k * z.main).astype(bf16)
            put_last(z, tail[k : k + 1, :], chunks[k], tile, outs[k])

    return call(
        body,
        "v" * (z.experts + z.split + 5) + "a" * len(after),
        [shape((z.main, z.wide))] * z.experts,
        [pltpu.VMEM((16, fold), f32)],
        8,
        "finish_backward",
    )(*chunks, *lasts, *terms, *parts, vectors, *after)


def order_rows(z, arrays, places, after, name):
    count = len(arrays)
    lanes = z.tokens + 16 * z.experts
    steps = 7 if z.pieces % 7 == 0 else z.pieces

    def body(*refs):
        arrays, (out_any, out, sems) = refs[:count], refs[count + len(after) :]
        chunks = [arrays[i].at[pl.ds(at, 16)] for i, at in places]
        tiles = [chunk[:, z.width :] for chunk in chunks]
        token_row = tiles[0].astype(f32)[z.pieces : z.pieces + 1, :lanes]
        token = lax.broadcasted_iota(jnp.int32, (z.tokens, lanes), 0).astype(f32)
        lane = lax.broadcasted_iota(jnp.int32, (z.tokens, lanes), 1)
        piece = jnp.where(lane < z.tokens, -1, lane % 16)
        ours = token == token_row
        copies = []
        for i in range(z.pieces):
            cols = pl.ds(i * fold, fold)
            mine = ours & ((piece < 0) | (piece == i))
            selector = jnp.where(mine, 1.0, 0.0).astype(bf16)
            rows = jnp.concatenate([chunk[:, cols] for chunk in chunks] + tiles, axis=0)
            out[:, cols] = jnp.dot(selector, rows, preferred_element_type=f32).astype(bf16)
            if (i + 1) % (z.pieces // steps) == 0:
                done = pl.ds((i + 1) * fold - z.width // steps, z.width // steps)
                copy = pltpu.make_async_copy(out.at[:, done], out_any.at[:, done], sems.at[len(copies)])
                copy.start()
                copies.append(copy)
        for copy in copies:
            copy.wait()

    return call(
        body,
        "v" * count + "a" * len(after),
        shape((z.tokens, z.width)),
        [pltpu.VMEM((z.tokens, z.width), bf16), pltpu.SemaphoreType.DMA((steps,))],
        8,
        name,
        spaces["a"],
    )(*arrays, *after)


def permute_blocks(z, arrays, k):
    groups = z.experts * z.split
    pairs = [(i, ((i // z.split) ^ k) * z.split + i % z.split) for i in range(groups)]
    return [lax.ppermute(array, "ep", pairs) for array in arrays]


def dispatch(z, chunks):
    return [chunks[0]] + [permute_blocks(z, [chunks[k]], k)[0] for k in range(1, z.experts)]


def to_core(z, array, m):
    groups = z.experts * z.split
    pairs = [(i, i // z.split * z.split + ((i % z.split) ^ m)) for i in range(groups)]
    return lax.ppermute(array, "ep", pairs)


def to_section(z, chunk, k, by):
    groups = z.experts * z.split
    sections = lax.axis_size("pp")
    pairs = [
        (s * groups + i, (s + by) % sections * groups + ((i // z.split) ^ k) * z.split + i % z.split)
        for s in range(sections)
        for i in range(groups)
    ]
    return lax.ppermute(chunk, ("pp", "ep"), pairs)


def on_device(
    fwd_act, fwd_ids, bwd_act, bwd_ids, bwd_grad, norm_gain, router, w_gate, w_down, saved_gate
):
    groups = lax.axis_size("ep")
    assert fwd_ids.shape[1] == 1
    z = Sizes(groups, router.shape[2], fwd_act.shape[0], fwd_act.shape[1])
    index = lax.axis_index("ep")
    where = jnp.stack([index // z.split, index % z.split]).astype(jnp.int32)
    router = jnp.swapaxes(router, 1, 2)
    others = range(1, z.split)

    fwd_chunks, (grad, act, gain_row, table), slots = forward_chunks(
        z, where, fwd_ids, fwd_act, bwd_ids, [bwd_grad, bwd_act, norm_gain, router]
    )
    fwd_own = dispatch(z, fwd_chunks)
    bwd_chunks, vectors = backward_chunks(z, where, slots, [grad, act], gain_row, table)
    bwd_own = dispatch(z, bwd_chunks)

    down_turned = turned(z, w_down, [w_gate], [bwd_chunks[0], fwd_own[1]], "turned_down")
    normed, gates, fwd_last = normed_rows(z, fwd_own, vectors, [down_turned])
    fwd_all = [normed] + [to_core(z, normed, m) for m in others]
    ordered = saved_rows(z, where, saved_gate, [], [gates])
    fwd_parts = experts_forward(z, fwd_all, w_gate, w_down, [ordered])
    hidden, slope = saved_terms(z, ordered, [fwd_parts[0]])
    gate_turned = turned(z, w_gate, [], [hidden], "turned_gate")
    fwd_parts = [fwd_parts[0]] + [to_core(z, fwd_parts[m], m) for m in others]

    assert z.experts == 4

    def finish(ks, after):
        return finish_forward(z, ks, fwd_own, fwd_last, fwd_parts, gates, after)

    double = finish([0, 1], [gate_turned])
    got = to_section(z, double, 0, 1)
    out2 = finish([2], [hidden, double])
    got2 = to_section(z, out2, 2, 1)
    grads, grad_last = grad_rows_of(z, bwd_own, [out2])
    grad_all = [grads] + [to_core(z, grads, m) for m in others]
    inv, act_last = act_norms(z, bwd_own, [grads])
    out3 = finish([3], [inv])
    got3 = to_section(z, out3, 3, 1)
    bwd_parts = experts_backward(z, grad_all, hidden, slope, gate_turned, down_turned, [inv])
    affinity = act_gates(z, bwd_own, act_last, inv, vectors, [bwd_parts[0], got])
    (relayed,) = permute_blocks(z, [lower_chunk(z, got, [affinity])], 1)
    fwd_done = [got2, got3]
    bwd_parts = [bwd_parts[0]] + [to_core(z, bwd_parts[m], m) for m in others]
    bwd_out = finish_backward(
        z, z.order, bwd_own, [grad_last, act_last], [inv, affinity], bwd_parts, vectors, []
    )
    bwd_done = {k: to_section(z, out, k, -1) for k, out in zip(z.order, bwd_out)}

    places = [(k, 0) for k in range(z.experts)]
    fwd_next = order_rows(z, [got, relayed, *fwd_done], places, [], "forward_rows")
    places = [(z.order.index(k), 0) for k in range(z.experts)]
    bwd_next = order_rows(z, [bwd_done[k] for k in z.order], places, [], "backward_rows")
    return (fwd_next, bwd_next)


def solution(mesh):
    return jax.shard_map(
        on_device,
        mesh=mesh,
        in_specs=(
            P(("pp", "ep"), None),
            P(("pp", "ep"), None),
            P(("pp", "ep"), None),
            P(("pp", "ep"), None),
            P(("pp", "ep"), None),
            P("pp", None),
            P("pp", None, None),
            P(("pp", "ep"), None, None),
            P(("pp", "ep"), None, None),
            P("pp", "ep", None, None),
        ),
        out_specs=(P(("pp", "ep"), None), P(("pp", "ep"), None)),
        check_vma=False,
    )
```

```python
import jax
import jax.numpy as jnp
from jax import lax
from jax.experimental import pallas as pl
from jax.experimental.pallas import tpu as pltpu
from jax.sharding import PartitionSpec as P

epsilon = 1e-06
route_scale = 2.5
fold = 256
none = 255.0
f32 = jnp.float32
bf16 = jnp.bfloat16
nn = (((1,), (0,)), ((), ()))
spaces = {
    "s": pl.BlockSpec(memory_space=pltpu.SMEM),
    "v": pl.BlockSpec(memory_space=pltpu.VMEM),
    "a": pl.BlockSpec(memory_space=pl.ANY),
    "h": pl.BlockSpec(memory_space=pltpu.HBM),
}


cost = {
    "backward_chunks": 10,
    "saved_rows": 15,
    "saved_terms": 15,
    "act_norms": 15,
    "act_gates": 15,
}


def call(body, places, outs, scratch, megabytes, name, out_specs=None):
    def run(*arrays):
        arrays = [
            pltpu.with_memory_space_constraint(array, pltpu.HBM) if place == "h" else array
            for array, place in zip(arrays, places, strict=True)
        ]
        return kernel(*arrays)

    where_to = {} if out_specs is None else {"out_specs": out_specs}
    kernel = pl.pallas_call(
        body,
        out_shape=outs,
        in_specs=[spaces[place] for place in places],
        **where_to,
        scratch_shapes=scratch,
        compiler_params=pltpu.CompilerParams(vmem_limit_bytes=megabytes * 1024 * 1024),
        cost_estimate=pl.CostEstimate(
            flops=int(cost.get(name, 0.1) * 1e9), bytes_accessed=1000, transcendentals=0
        ),
        name=name,
    )
    return run


def shape(dims, kind=bf16):
    return jax.ShapeDtypeStruct(dims, kind)


class Sizes:
    def __init__(self, groups, experts, tokens, width):
        self.experts = experts
        self.split = groups // experts
        self.tokens = tokens
        self.width = width
        self.main = tokens // experts
        self.cap = self.main + 1
        self.pieces = width // fold
        self.wide = width + fold
        self.rows = tokens + 16
        self.order = [experts - 1, *range(1, experts - 1), 0]
        assert self.main == 16 and self.pieces <= 14 and width % fold == 0
        assert experts <= 8 and experts & (experts - 1) == 0 and self.split & (self.split - 1) == 0


def pack_last(row, tile, first=0):
    for i in range(row.shape[1] // fold):
        tile[first + i : first + i + 1, :] = row[:, i * fold : (i + 1) * fold]


def unpack_last(chunk, z, tile, target, at, base=0):
    tile[...] = chunk[base : base + 16, z.width :].astype(f32)
    for i in range(z.pieces):
        target[at : at + 1, i * fold : (i + 1) * fold] = tile[i : i + 1, :]


def slot_matrices(ids_row, block, z):
    tokens = z.tokens
    sub = lax.broadcasted_iota(jnp.int32, (tokens, tokens), 0)
    lane = lax.broadcasted_iota(jnp.int32, (tokens, tokens), 1)
    row = jnp.bitwise_xor(ids_row, block)
    column = jnp.sum(jnp.where(sub == lane, row, 0), axis=1, keepdims=True)
    same = column == row
    place_row = jnp.sum(jnp.where(same & (sub < lane), 1, 0), axis=0, keepdims=True)
    place_column = jnp.sum(jnp.where(same & (lane < sub), 1, 0), axis=1, keepdims=True)

    def slot(expert, place):
        return jnp.where(place < z.main, expert * z.main + place, tokens + expert)

    slot_row = slot(row, place_row)
    slot_column = slot(column, place_column)
    by_slot = lax.broadcasted_iota(jnp.int32, (z.rows, tokens), 0) == slot_row
    lane = lax.broadcasted_iota(jnp.int32, (tokens, fold), 1)
    by_token = jnp.where(lane < tokens, lane, tokens + (lane - tokens) // 16) == slot_column
    token = lax.broadcasted_iota(jnp.int32, (tokens, fold), 0).astype(f32)
    token_row = jnp.sum(jnp.where(by_token, token - none, 0.0), axis=0, keepdims=True) + none
    return jnp.where(by_slot, 1.0, 0.0).astype(bf16), token_row


def write_chunks(z, selector, token_row, rows_ref, ready, tiles, chunks, base):
    step = z.width // 2
    tiles[...] = jnp.zeros_like(tiles)
    for half in range(2):
        if ready:
            ready[half].wait()
        col = half * step
        got = jnp.dot(selector, rows_ref[:, col : col + step], preferred_element_type=f32)
        packed = got[: z.tokens].astype(bf16)
        for k in range(z.experts):
            chunks[k][base : base + 16, col : col + step] = packed[k * z.main : (k + 1) * z.main]
            pack_last(got[z.tokens + k : z.tokens + k + 1], tiles.at[k], half * z.pieces // 2)
    for k in range(z.experts):
        tiles[k, z.pieces : z.pieces + 1, :] = token_row
        chunks[k][base : base + 16, z.width :] = tiles[k].astype(bf16)


def forward_chunks(z, where, ids, act, later_ids, later):
    count = len(later)

    def body(where, ids_any, later_ids_any, act_any, *refs):
        later_any, chunks = refs[:count], refs[count : count + z.experts]
        later_refs = refs[count + z.experts : 2 * count + z.experts]
        selector_ref, token_ref, ids, rows, tiles, sems = refs[2 * count + z.experts :]
        step = z.width // 2
        first = [
            pltpu.make_async_copy(source, ids.at[i : i + 1], sems.at[i])
            for i, source in enumerate((ids_any, later_ids_any))
        ]
        ready = [
            pltpu.make_async_copy(
                act_any.at[:, pl.ds(i * step, step)], rows.at[:, pl.ds(i * step, step)], sems.at[2 + i]
            )
            for i in range(2)
        ]
        rest = [
            pltpu.make_async_copy(source, target, sems.at[4 + i])
            for i, (source, target) in enumerate(zip(later_any, later_refs))
        ]
        for copy in first + ready + rest:
            copy.start()
        for copy in first:
            copy.wait()
        selector, token_row = slot_matrices(ids[0:1, :], where[0], z)
        later_selector, later_row = slot_matrices(ids[1:2, :], where[0], z)
        selector_ref[...] = later_selector
        token_ref[...] = jnp.broadcast_to(later_row, token_ref.shape)
        write_chunks(z, selector, token_row, rows, ready, tiles, chunks, 0)
        for copy in rest:
            copy.wait()

    outs = call(
        body,
        "shhh" + "h" * count,
        [shape((z.main, z.wide))] * z.experts
        + [shape(array.shape, array.dtype) for array in later]
        + [shape((z.rows, z.tokens)), shape((8, fold), f32)],
        [
            pltpu.VMEM((2, z.tokens), jnp.int32),
            pltpu.VMEM((z.tokens, z.width), bf16),
            pltpu.VMEM((z.experts, 16, fold), f32),
            pltpu.SemaphoreType.DMA((4 + count,)),
        ],
        8,
        "forward_chunks",
    )(where, ids.reshape(1, z.tokens), later_ids.reshape(1, z.tokens), act, *later)
    return outs[: z.experts], outs[z.experts : z.experts + count], outs[z.experts + count :]


def backward_chunks(z, where, slots, sources, gain, router):
    count = len(sources)

    def body(where, selector, token_ref, *refs):
        sources, (gain_ref, router_ref) = refs[:count], refs[count : count + 2]
        *chunks, vectors, tiles = refs[count + 2 :]
        for j in range(count):
            write_chunks(
                z, selector[...], token_ref[0:1, :], sources[j], None, tiles, chunks, 16 * j
            )
        vectors[...] = jnp.zeros_like(vectors)
        vectors[0:1, :] = gain_ref[...].astype(f32)
        mine = lax.broadcasted_iota(jnp.int32, (z.experts, 1), 0) == where[0]
        table = jnp.where(mine, router_ref[0].astype(f32), 0.0)
        vectors[1:2, :] = jnp.sum(table, axis=0, keepdims=True)

    *chunks, vectors = call(
        body,
        "svv" + "v" * (count + 2),
        [shape((z.main * count, z.wide))] * z.experts + [shape((8, z.width), f32)],
        [pltpu.VMEM((z.experts, 16, fold), f32)],
        8,
        "backward_chunks",
    )(where, *slots, *sources, gain, router)
    return chunks, vectors


def collect_rows(z, chunks, last, tile, base=0):
    last[...] = jnp.zeros_like(last)
    for k in range(z.experts):
        unpack_last(chunks[k], z, tile, last, k, base)


def norm_rows(h, gain):
    inv = lax.rsqrt(jnp.mean(h * h, axis=-1, keepdims=True) + epsilon)
    return (h * inv * gain).astype(bf16), inv


def normed_rows(z, chunks, vectors, after):
    def body(*refs):
        chunks, vectors = refs[: z.experts], refs[z.experts]
        normed_ref, gates_ref, last, tile = refs[z.experts + 1 + len(after) :]
        gain, router = vectors[0:1, :], vectors[1:2, :]
        collect_rows(z, chunks, last, tile)
        for k in range(z.experts + 1):
            h = last[...] if k == z.experts else chunks[k][:, : z.width].astype(f32)
            at = k * z.main
            normed, _ = norm_rows(h, gain)
            normed_ref[at : at + 16, :] = normed
            logits = jnp.sum(normed.astype(f32) * router, axis=-1, keepdims=True)
            gates_ref[at : at + 16, :] = jnp.broadcast_to(jax.nn.sigmoid(logits), (16, 128))

    return call(
        body,
        "v" * (z.experts + 1) + "a" * len(after),
        [shape((z.rows, z.width)), shape((z.rows, 128), f32), shape((16, z.width), f32)],
        [pltpu.VMEM((16, fold), f32)],
        8,
        "normed_rows",
    )(*chunks, vectors, *after)


def grad_rows_of(z, chunks, after):
    def body(*refs):
        chunks, (rows, last, tile) = refs[: z.experts], refs[z.experts + len(after) :]
        for k in range(z.experts):
            rows[k * z.main : (k + 1) * z.main, :] = chunks[k][:16, : z.width]
        collect_rows(z, chunks, last, tile)
        rows[z.tokens :, :] = last[...].astype(bf16)

    return call(
        body,
        "v" * z.experts + "a" * len(after),
        [shape((z.rows, z.width)), shape((16, z.width), f32)],
        [pltpu.VMEM((16, fold), f32)],
        8,
        "grad_rows",
    )(*chunks, *after)


def act_norms(z, chunks, after):
    def body(*refs):
        chunks, (inv_ref, last, tile) = refs[: z.experts], refs[z.experts + len(after) :]
        collect_rows(z, chunks, last, tile, 16)
        for k in range(z.experts + 1):
            h = last[...] if k == z.experts else chunks[k][16:32, : z.width].astype(f32)
            at = k * z.main
            inv = lax.rsqrt(jnp.mean(h * h, axis=-1, keepdims=True) + epsilon)
            inv_ref[at : at + 16, :] = jnp.broadcast_to(inv, (16, 128))

    return call(
        body,
        "v" * z.experts + "a" * len(after),
        [shape((z.rows, 128), f32), shape((16, z.width), f32)],
        [pltpu.VMEM((16, fold), f32)],
        8,
        "act_norms",
    )(*chunks, *after)


def act_gates(z, chunks, last, inv, vectors, after):
    def body(*refs):
        chunks, (last, inv_ref, vectors) = refs[: z.experts], refs[z.experts : z.experts + 3]
        affinity_ref = refs[-1]
        gain, router = vectors[0:1, :], vectors[1:2, :]
        for k in range(z.experts + 1):
            h = last[...] if k == z.experts else chunks[k][16:32, : z.width].astype(f32)
            at = k * z.main
            normed = (h * inv_ref[at : at + 16, 0:1] * gain).astype(bf16).astype(f32)
            logits = jnp.sum(normed * router, axis=-1, keepdims=True)
            affinity_ref[at : at + 16, :] = jnp.broadcast_to(jax.nn.sigmoid(logits), (16, 128))

    return call(
        body,
        "v" * (z.experts + 3) + "a" * len(after),
        shape((z.rows, 128), f32),
        [],
        8,
        "act_gates",
    )(*chunks, last, inv, vectors, *after)


def write_parts(z, values, outs, col):
    values = values.astype(bf16)
    for m in range(z.split):
        outs[m][:, col : col + values.shape[1]] = values[m * z.rows : (m + 1) * z.rows]


def experts_forward(z, rows, w_gate, w_down, after):
    def body(*refs):
        rows, (gate_ref, down_ref), outs = (
            refs[: z.split],
            refs[z.split : z.split + 2],
            refs[z.split + 2 + len(after) :],
        )
        held = jnp.concatenate([part[...] for part in rows], axis=0)
        gate_proj = jnp.dot(held, gate_ref[0], preferred_element_type=f32)
        hidden = jax.nn.silu(gate_proj).astype(bf16)
        step = 512
        for col in range(0, z.width, step):
            part = jnp.dot(hidden, down_ref[0, :, col : col + step], preferred_element_type=f32)
            write_parts(z, part, outs, col)

    return call(
        body,
        "v" * (z.split + 2) + "a" * len(after),
        [shape((z.rows, z.width))] * z.split,
        [],
        16,
        "experts_forward",
    )(*rows, w_gate, w_down, *after)


def saved_rows(z, where, saved, weights, after):
    total, slots, width = z.split * z.rows, saved.shape[2], saved.shape[3]

    def body(where, saved_any, *refs):
        ordered_ref, saved_ref, sem = refs[len(weights) + len(after) :]
        copy = pltpu.make_async_copy(saved_any.at[0, 0], saved_ref, sem)
        copy.start()
        row = lax.broadcasted_iota(jnp.int32, (total, slots), 0)
        slot = lax.broadcasted_iota(jnp.int32, (total, slots), 1)
        m, at = row // z.rows, row % z.rows
        is_main = at < z.tokens
        k = jnp.where(is_main, at // z.main, at - z.tokens)
        p = jnp.where(is_main, at % z.main, z.main)
        source = jnp.bitwise_xor(k, where[0]) * z.split + jnp.bitwise_xor(m, where[1])
        wanted = jnp.where(k < z.experts, source * z.cap + p, -1)
        selector = jnp.where(slot == wanted, 1.0, 0.0).astype(bf16)
        copy.wait()
        ordered_ref[...] = jnp.dot(selector, saved_ref[...], preferred_element_type=f32)

    return call(
        body,
        "sh" + "v" * len(weights) + "a" * len(after),
        shape((total, width), f32),
        [pltpu.VMEM((slots, width), bf16), pltpu.SemaphoreType.DMA],
        8,
        "saved_rows",
    )(where, saved, *weights, *after)


def saved_terms(z, ordered, after):
    def body(ordered_ref, *refs):
        hidden_ref, slope_ref = refs[len(after) :]
        gate_proj = ordered_ref[...]
        sg = jax.nn.sigmoid(gate_proj)
        hidden_ref[...] = (gate_proj * sg).astype(bf16)
        slope_ref[...] = sg * (1.0 + gate_proj * (1.0 - sg))

    return call(
        body,
        "v" + "a" * len(after),
        [shape(ordered.shape), shape(ordered.shape, f32)],
        [],
        8,
        "saved_terms",
    )(ordered, *after)


def turned(z, weights, held, after, name):
    rows, columns = weights.shape[1:]
    step = min(512, rows, columns)

    def body(weights_ref, *refs):
        for at in range(0, rows, step):
            for col in range(0, columns, step):
                block = weights_ref[0, at : at + step, col : col + step]
                refs[-1][col : col + step, at : at + step] = block.T

    return call(
        body, "v" + "v" * len(held) + "a" * len(after), shape((columns, rows)), [], 12, name
    )(weights, *held, *after)


def experts_backward(z, rows, hidden, slope, w_gate, w_down, after):
    def body(*refs):
        rows = refs[: z.split]
        hidden_ref, slope_ref, gate_ref, down_ref = refs[z.split : z.split + 4]
        outs = refs[z.split + 4 + len(after) :]
        held = jnp.concatenate([part[...] for part in rows], axis=0)
        grad_hidden = lax.dot_general(held, down_ref[...], nn, preferred_element_type=f32)
        dots = jnp.sum(grad_hidden * hidden_ref[...].astype(f32), axis=-1, keepdims=True)
        grad_gate = (grad_hidden * slope_ref[...]).astype(bf16)
        step = 512
        for col in range(0, z.width, step):
            part = lax.dot_general(
                grad_gate, gate_ref[:, col : col + step], nn, preferred_element_type=f32
            )
            write_parts(z, part, outs, col)
        write_parts(z, jnp.broadcast_to(dots, (dots.shape[0], 128)), outs, z.width)

    return call(
        body,
        "v" * (z.split + 4) + "a" * len(after),
        [shape((z.rows, z.width + 128))] * z.split,
        [],
        16,
        "experts_backward",
    )(*rows, hidden, slope, w_gate, w_down, *after)


def put_last(z, values, source_chunk, tile, out):
    tile[...] = jnp.zeros_like(tile)
    pack_last(values, tile)
    tokens = source_chunk[:16, z.width :].astype(f32)
    tile[z.pieces : z.pieces + 1, :] = tokens[z.pieces : z.pieces + 1, :]
    out[:, z.width :] = tile[...].astype(bf16)


def finish_forward(z, ks, chunks, last, parts, gates, after):
    count = len(ks)

    def body(*refs):
        chunks, last, parts = refs[:count], refs[count], refs[count + 1 : count + 1 + z.split]
        gates, outs, tile = refs[count + 1 + z.split], refs[-1 - count : -1], refs[-1]

        def mixed(at):
            y = parts[0][at : at + 16, :].astype(f32)
            for part in parts[1:]:
                y = y + part[at : at + 16, :].astype(f32)
            return route_scale * (gates[at : at + 16, 0:1] * y)

        tail = last[...] + mixed(z.tokens)
        for k, chunk, out in zip(ks, chunks, outs):
            h = chunk[:, : z.width].astype(f32)
            out[:, : z.width] = (h + mixed(k * z.main)).astype(bf16)
            put_last(z, tail[k : k + 1, :], chunk, tile, out)

    return call(
        body,
        "v" * (count + z.split + 2) + "a" * len(after),
        [shape((z.main, z.wide))] * count,
        [pltpu.VMEM((16, fold), f32)],
        8,
        "finish_forward_" + "".join(map(str, ks)),
    )(*[chunks[k] for k in ks], last, *parts, gates, *after)


def finish_backward(z, order, chunks, lasts, terms, parts, vectors, after):
    def body(*refs):
        e = z.experts
        chunks, (last_grad, last_act, inv_ref, affinity_ref) = refs[:e], refs[e : e + 4]
        parts, vectors = refs[e + 4 : e + 4 + z.split], refs[e + 4 + z.split]
        outs, (tile,) = refs[-1 - e : -1], refs[-1:]
        outs = [outs[order.index(k)] for k in range(e)]
        gain, router = vectors[0:1, :], vectors[1:2, :]

        def finished(h, g, at):
            inv, affinity = inv_ref[at : at + 16, 0:1], affinity_ref[at : at + 16, 0:1]
            rows = parts[0][at : at + 16, : z.width].astype(f32)
            dot = parts[0][at : at + 16, z.width :].astype(f32)
            for part in parts[1:]:
                rows = rows + part[at : at + 16, : z.width].astype(f32)
                dot = dot + part[at : at + 16, z.width :].astype(f32)
            dot = dot[:, 0:1]
            grad_logits = (route_scale * dot * affinity * (1.0 - affinity)).astype(bf16).astype(f32)
            grad_pre = (route_scale * affinity * rows + grad_logits * router) * gain
            centre = jnp.mean(grad_pre * h, axis=-1, keepdims=True)
            return g + inv * (grad_pre - h * (inv * inv * centre))

        tail = finished(last_act[...], last_grad[...], z.tokens)
        for k in range(e):
            g = chunks[k][:16, : z.width].astype(f32)
            h = chunks[k][16:32, : z.width].astype(f32)
            outs[k][:, : z.width] = finished(h, g, k * z.main).astype(bf16)
            put_last(z, tail[k : k + 1, :], chunks[k], tile, outs[k])

    return call(
        body,
        "v" * (z.experts + z.split + 5) + "a" * len(after),
        [shape((z.main, z.wide))] * z.experts,
        [pltpu.VMEM((16, fold), f32)],
        8,
        "finish_backward",
    )(*chunks, *lasts, *terms, *parts, vectors, *after)


def order_rows(z, arrays, places, after, name):
    count = len(arrays)
    lanes = z.tokens + 16 * z.experts
    steps = 7 if z.pieces % 7 == 0 else z.pieces

    def body(*refs):
        arrays, (out_any, out, sems) = refs[:count], refs[count + len(after) :]
        chunks = [arrays[i].at[pl.ds(at, 16)] for i, at in places]
        tiles = [chunk[:, z.width :] for chunk in chunks]
        token_row = tiles[0].astype(f32)[z.pieces : z.pieces + 1, :lanes]
        token = lax.broadcasted_iota(jnp.int32, (z.tokens, lanes), 0).astype(f32)
        lane = lax.broadcasted_iota(jnp.int32, (z.tokens, lanes), 1)
        piece = jnp.where(lane < z.tokens, -1, lane % 16)
        ours = token == token_row
        copies = []
        for i in range(z.pieces):
            cols = pl.ds(i * fold, fold)
            mine = ours & ((piece < 0) | (piece == i))
            selector = jnp.where(mine, 1.0, 0.0).astype(bf16)
            rows = jnp.concatenate([chunk[:, cols] for chunk in chunks] + tiles, axis=0)
            out[:, cols] = jnp.dot(selector, rows, preferred_element_type=f32).astype(bf16)
            if (i + 1) % (z.pieces // steps) == 0:
                done = pl.ds((i + 1) * fold - z.width // steps, z.width // steps)
                copy = pltpu.make_async_copy(out.at[:, done], out_any.at[:, done], sems.at[len(copies)])
                copy.start()
                copies.append(copy)
        for copy in copies:
            copy.wait()

    return call(
        body,
        "v" * count + "a" * len(after),
        shape((z.tokens, z.width)),
        [pltpu.VMEM((z.tokens, z.width), bf16), pltpu.SemaphoreType.DMA((steps,))],
        8,
        name,
        spaces["a"],
    )(*arrays, *after)


def permute_blocks(z, arrays, k):
    groups = z.experts * z.split
    pairs = [(i, ((i // z.split) ^ k) * z.split + i % z.split) for i in range(groups)]
    return [lax.ppermute(array, "ep", pairs) for array in arrays]


def dispatch(z, chunks):
    return [chunks[0]] + [permute_blocks(z, [chunks[k]], k)[0] for k in range(1, z.experts)]


def to_core(z, array, m):
    groups = z.experts * z.split
    pairs = [(i, i // z.split * z.split + ((i % z.split) ^ m)) for i in range(groups)]
    return lax.ppermute(array, "ep", pairs)


def to_section(z, chunk, k, by):
    groups = z.experts * z.split
    sections = lax.axis_size("pp")
    pairs = [
        (s * groups + i, (s + by) % sections * groups + ((i // z.split) ^ k) * z.split + i % z.split)
        for s in range(sections)
        for i in range(groups)
    ]
    return lax.ppermute(chunk, ("pp", "ep"), pairs)


def on_device(
    fwd_act, fwd_ids, bwd_act, bwd_ids, bwd_grad, norm_gain, router, w_gate, w_down, saved_gate
):
    groups = lax.axis_size("ep")
    assert fwd_ids.shape[1] == 1
    z = Sizes(groups, router.shape[2], fwd_act.shape[0], fwd_act.shape[1])
    index = lax.axis_index("ep")
    where = jnp.stack([index // z.split, index % z.split]).astype(jnp.int32)
    router = jnp.swapaxes(router, 1, 2)
    others = range(1, z.split)

    fwd_chunks, (grad, act, gain_row, table), slots = forward_chunks(
        z, where, fwd_ids, fwd_act, bwd_ids, [bwd_grad, bwd_act, norm_gain, router]
    )
    fwd_own = dispatch(z, fwd_chunks)
    bwd_chunks, vectors = backward_chunks(z, where, slots, [grad, act], gain_row, table)
    bwd_own = dispatch(z, bwd_chunks)

    down_turned = turned(z, w_down, [w_gate], [bwd_chunks[0], fwd_own[1]], "turned_down")
    normed, gates, fwd_last = normed_rows(z, fwd_own, vectors, [down_turned])
    fwd_all = [normed] + [to_core(z, normed, m) for m in others]
    ordered = saved_rows(z, where, saved_gate, [], [gates])
    fwd_parts = experts_forward(z, fwd_all, w_gate, w_down, [ordered])
    hidden, slope = saved_terms(z, ordered, [fwd_parts[0]])
    gate_turned = turned(z, w_gate, [], [hidden], "turned_gate")
    fwd_parts = [fwd_parts[0]] + [to_core(z, fwd_parts[m], m) for m in others]

    done = {}

    def finish(ks, after):
        outs = finish_forward(z, ks, fwd_own, fwd_last, fwd_parts, gates, after)
        for k, out in zip(ks, outs):
            done[k] = to_section(z, out, k, 1)
        return outs[0]

    first, second, third = ([0], [3, 1], [2])
    out = finish(first, [gate_turned])
    grads, grad_last = grad_rows_of(z, bwd_own, [out])
    grad_all = [grads] + [to_core(z, grads, m) for m in others]
    inv, act_last = act_norms(z, bwd_own, [grads])
    out = finish(second, [inv])
    bwd_parts = experts_backward(z, grad_all, hidden, slope, gate_turned, down_turned, [out])
    affinity = act_gates(z, bwd_own, act_last, inv, vectors, [bwd_parts[0], done[0]])
    out = finish(third, [affinity])
    bwd_parts = [bwd_parts[0]] + [to_core(z, bwd_parts[m], m) for m in others]
    bwd_out = finish_backward(
        z, z.order, bwd_own, [grad_last, act_last], [inv, affinity], bwd_parts, vectors, [out]
    )
    fwd_done = [done[k] for k in range(z.experts)]
    bwd_done = {k: to_section(z, out, k, -1) for k, out in zip(z.order, bwd_out)}

    places = [(k, 0) for k in range(z.experts)]
    fwd_next = order_rows(z, fwd_done, places, [], "forward_rows")
    places = [(z.order.index(k), 0) for k in range(z.experts)]
    bwd_next = order_rows(z, [bwd_done[k] for k in z.order], places, [], "backward_rows")
    return (fwd_next, bwd_next)


def solution(mesh):
    return jax.shard_map(
        on_device,
        mesh=mesh,
        in_specs=(
            P(("pp", "ep"), None),
            P(("pp", "ep"), None),
            P(("pp", "ep"), None),
            P(("pp", "ep"), None),
            P(("pp", "ep"), None),
            P("pp", None),
            P("pp", None, None),
            P(("pp", "ep"), None, None),
            P(("pp", "ep"), None, None),
            P("pp", "ep", None, None),
        ),
        out_specs=(P(("pp", "ep"), None), P(("pp", "ep"), None)),
        check_vma=False,
    )
```

```python
import jax
import jax.numpy as jnp
from jax import lax
from jax.experimental import pallas as pl
from jax.experimental.pallas import tpu as pltpu
from jax.sharding import PartitionSpec as P

epsilon = 1e-06
route_scale = 2.5
fold = 256
none = 255.0
f32 = jnp.float32
bf16 = jnp.bfloat16
nn = (((1,), (0,)), ((), ()))
spaces = {
    "s": pl.BlockSpec(memory_space=pltpu.SMEM),
    "v": pl.BlockSpec(memory_space=pltpu.VMEM),
    "a": pl.BlockSpec(memory_space=pl.ANY),
    "h": pl.BlockSpec(memory_space=pltpu.HBM),
}


cost = {
    "backward_chunks": 10,
    "saved_rows": 15,
    "saved_terms": 15,
    "act_norms": 15,
    "act_gates": 15,
}


def call(body, places, outs, scratch, megabytes, name, out_specs=None):
    def run(*arrays):
        arrays = [
            pltpu.with_memory_space_constraint(array, pltpu.HBM) if place == "h" else array
            for array, place in zip(arrays, places, strict=True)
        ]
        return kernel(*arrays)

    where_to = {} if out_specs is None else {"out_specs": out_specs}
    kernel = pl.pallas_call(
        body,
        out_shape=outs,
        in_specs=[spaces[place] for place in places],
        **where_to,
        scratch_shapes=scratch,
        compiler_params=pltpu.CompilerParams(vmem_limit_bytes=megabytes * 1024 * 1024),
        cost_estimate=pl.CostEstimate(
            flops=int(cost.get(name, 0.1) * 1e9), bytes_accessed=1000, transcendentals=0
        ),
        name=name,
    )
    return run


def shape(dims, kind=bf16):
    return jax.ShapeDtypeStruct(dims, kind)


class Sizes:
    def __init__(self, groups, experts, tokens, width):
        self.experts = experts
        self.split = groups // experts
        self.tokens = tokens
        self.width = width
        self.main = tokens // experts
        self.cap = self.main + 1
        self.pieces = width // fold
        self.wide = width + fold
        self.rows = tokens + 16
        self.order = [experts - 1, *range(1, experts - 1), 0]
        assert self.main == 16 and self.pieces <= 14 and width % fold == 0
        assert experts <= 8 and experts & (experts - 1) == 0 and self.split & (self.split - 1) == 0


def pack_last(row, tile, first=0):
    for i in range(row.shape[1] // fold):
        tile[first + i : first + i + 1, :] = row[:, i * fold : (i + 1) * fold]


def unpack_last(chunk, z, tile, target, at, base=0):
    tile[...] = chunk[base : base + 16, z.width :].astype(f32)
    for i in range(z.pieces):
        target[at : at + 1, i * fold : (i + 1) * fold] = tile[i : i + 1, :]


def slot_matrices(ids_row, block, z):
    tokens = z.tokens
    sub = lax.broadcasted_iota(jnp.int32, (tokens, tokens), 0)
    lane = lax.broadcasted_iota(jnp.int32, (tokens, tokens), 1)
    row = jnp.bitwise_xor(ids_row, block)
    column = jnp.sum(jnp.where(sub == lane, row, 0), axis=1, keepdims=True)
    same = column == row
    place_row = jnp.sum(jnp.where(same & (sub < lane), 1, 0), axis=0, keepdims=True)
    place_column = jnp.sum(jnp.where(same & (lane < sub), 1, 0), axis=1, keepdims=True)

    def slot(expert, place):
        return jnp.where(place < z.main, expert * z.main + place, tokens + expert)

    slot_row = slot(row, place_row)
    slot_column = slot(column, place_column)
    by_slot = lax.broadcasted_iota(jnp.int32, (z.rows, tokens), 0) == slot_row
    lane = lax.broadcasted_iota(jnp.int32, (tokens, fold), 1)
    by_token = jnp.where(lane < tokens, lane, tokens + (lane - tokens) // 16) == slot_column
    token = lax.broadcasted_iota(jnp.int32, (tokens, fold), 0).astype(f32)
    token_row = jnp.sum(jnp.where(by_token, token - none, 0.0), axis=0, keepdims=True) + none
    return jnp.where(by_slot, 1.0, 0.0).astype(bf16), token_row


def write_chunks(z, selector, token_row, rows_ref, ready, tiles, chunks, base):
    step = z.width // 2
    tiles[...] = jnp.zeros_like(tiles)
    for half in range(2):
        if ready:
            ready[half].wait()
        col = half * step
        got = jnp.dot(selector, rows_ref[:, col : col + step], preferred_element_type=f32)
        packed = got[: z.tokens].astype(bf16)
        for k in range(z.experts):
            chunks[k][base : base + 16, col : col + step] = packed[k * z.main : (k + 1) * z.main]
            pack_last(got[z.tokens + k : z.tokens + k + 1], tiles.at[k], half * z.pieces // 2)
    for k in range(z.experts):
        tiles[k, z.pieces : z.pieces + 1, :] = token_row
        chunks[k][base : base + 16, z.width :] = tiles[k].astype(bf16)


def forward_chunks(z, where, ids, act, later_ids, later):
    count = len(later)

    def body(where, ids_any, later_ids_any, act_any, *refs):
        later_any, chunks = refs[:count], refs[count : count + z.experts]
        later_refs = refs[count + z.experts : 2 * count + z.experts]
        selector_ref, token_ref, ids, rows, tiles, sems = refs[2 * count + z.experts :]
        step = z.width // 2
        first = [
            pltpu.make_async_copy(source, ids.at[i : i + 1], sems.at[i])
            for i, source in enumerate((ids_any, later_ids_any))
        ]
        ready = [
            pltpu.make_async_copy(
                act_any.at[:, pl.ds(i * step, step)], rows.at[:, pl.ds(i * step, step)], sems.at[2 + i]
            )
            for i in range(2)
        ]
        rest = [
            pltpu.make_async_copy(source, target, sems.at[4 + i])
            for i, (source, target) in enumerate(zip(later_any, later_refs))
        ]
        for copy in first + ready + rest:
            copy.start()
        for copy in first:
            copy.wait()
        selector, token_row = slot_matrices(ids[0:1, :], where[0], z)
        later_selector, later_row = slot_matrices(ids[1:2, :], where[0], z)
        selector_ref[...] = later_selector
        token_ref[...] = jnp.broadcast_to(later_row, token_ref.shape)
        write_chunks(z, selector, token_row, rows, ready, tiles, chunks, 0)
        for copy in rest:
            copy.wait()

    outs = call(
        body,
        "shhh" + "h" * count,
        [shape((z.main, z.wide))] * z.experts
        + [shape(array.shape, array.dtype) for array in later]
        + [shape((z.rows, z.tokens)), shape((8, fold), f32)],
        [
            pltpu.VMEM((2, z.tokens), jnp.int32),
            pltpu.VMEM((z.tokens, z.width), bf16),
            pltpu.VMEM((z.experts, 16, fold), f32),
            pltpu.SemaphoreType.DMA((4 + count,)),
        ],
        8,
        "forward_chunks",
    )(where, ids.reshape(1, z.tokens), later_ids.reshape(1, z.tokens), act, *later)
    return outs[: z.experts], outs[z.experts : z.experts + count], outs[z.experts + count :]


def backward_chunks(z, where, slots, sources, gain, router):
    count = len(sources)

    def body(where, selector, token_ref, *refs):
        sources, (gain_ref, router_ref) = refs[:count], refs[count : count + 2]
        *chunks, vectors, tiles = refs[count + 2 :]
        for j in range(count):
            write_chunks(
                z, selector[...], token_ref[0:1, :], sources[j], None, tiles, chunks, 16 * j
            )
        vectors[...] = jnp.zeros_like(vectors)
        vectors[0:1, :] = gain_ref[...].astype(f32)
        mine = lax.broadcasted_iota(jnp.int32, (z.experts, 1), 0) == where[0]
        table = jnp.where(mine, router_ref[0].astype(f32), 0.0)
        vectors[1:2, :] = jnp.sum(table, axis=0, keepdims=True)

    *chunks, vectors = call(
        body,
        "svv" + "v" * (count + 2),
        [shape((z.main * count, z.wide))] * z.experts + [shape((8, z.width), f32)],
        [pltpu.VMEM((z.experts, 16, fold), f32)],
        8,
        "backward_chunks",
    )(where, *slots, *sources, gain, router)
    return chunks, vectors


def collect_rows(z, chunks, last, tile, base=0):
    last[...] = jnp.zeros_like(last)
    for k in range(z.experts):
        unpack_last(chunks[k], z, tile, last, k, base)


def norm_rows(h, gain):
    inv = lax.rsqrt(jnp.mean(h * h, axis=-1, keepdims=True) + epsilon)
    return (h * inv * gain).astype(bf16), inv


def normed_rows(z, chunks, vectors, after):
    def body(*refs):
        chunks, vectors = refs[: z.experts], refs[z.experts]
        normed_ref, gates_ref, last, tile = refs[z.experts + 1 + len(after) :]
        gain, router = vectors[0:1, :], vectors[1:2, :]
        collect_rows(z, chunks, last, tile)
        for k in range(z.experts + 1):
            h = last[...] if k == z.experts else chunks[k][:, : z.width].astype(f32)
            at = k * z.main
            normed, _ = norm_rows(h, gain)
            normed_ref[at : at + 16, :] = normed
            logits = jnp.sum(normed.astype(f32) * router, axis=-1, keepdims=True)
            gates_ref[at : at + 16, :] = jnp.broadcast_to(jax.nn.sigmoid(logits), (16, 128))

    return call(
        body,
        "v" * (z.experts + 1) + "a" * len(after),
        [shape((z.rows, z.width)), shape((z.rows, 128), f32), shape((16, z.width), f32)],
        [pltpu.VMEM((16, fold), f32)],
        8,
        "normed_rows",
    )(*chunks, vectors, *after)


def grad_rows_of(z, chunks, after):
    def body(*refs):
        chunks, (rows, last, tile) = refs[: z.experts], refs[z.experts + len(after) :]
        for k in range(z.experts):
            rows[k * z.main : (k + 1) * z.main, :] = chunks[k][:16, : z.width]
        collect_rows(z, chunks, last, tile)
        rows[z.tokens :, :] = last[...].astype(bf16)

    return call(
        body,
        "v" * z.experts + "a" * len(after),
        [shape((z.rows, z.width)), shape((16, z.width), f32)],
        [pltpu.VMEM((16, fold), f32)],
        8,
        "grad_rows",
    )(*chunks, *after)


def act_norms(z, chunks, after):
    def body(*refs):
        chunks, (inv_ref, last, tile) = refs[: z.experts], refs[z.experts + len(after) :]
        collect_rows(z, chunks, last, tile, 16)
        for k in range(z.experts + 1):
            h = last[...] if k == z.experts else chunks[k][16:32, : z.width].astype(f32)
            at = k * z.main
            inv = lax.rsqrt(jnp.mean(h * h, axis=-1, keepdims=True) + epsilon)
            inv_ref[at : at + 16, :] = jnp.broadcast_to(inv, (16, 128))

    return call(
        body,
        "v" * z.experts + "a" * len(after),
        [shape((z.rows, 128), f32), shape((16, z.width), f32)],
        [pltpu.VMEM((16, fold), f32)],
        8,
        "act_norms",
    )(*chunks, *after)


def act_gates(z, chunks, last, inv, vectors, after):
    def body(*refs):
        chunks, (last, inv_ref, vectors) = refs[: z.experts], refs[z.experts : z.experts + 3]
        affinity_ref = refs[-1]
        gain, router = vectors[0:1, :], vectors[1:2, :]
        for k in range(z.experts + 1):
            h = last[...] if k == z.experts else chunks[k][16:32, : z.width].astype(f32)
            at = k * z.main
            normed = (h * inv_ref[at : at + 16, 0:1] * gain).astype(bf16).astype(f32)
            logits = jnp.sum(normed * router, axis=-1, keepdims=True)
            affinity_ref[at : at + 16, :] = jnp.broadcast_to(jax.nn.sigmoid(logits), (16, 128))

    return call(
        body,
        "v" * (z.experts + 3) + "a" * len(after),
        shape((z.rows, 128), f32),
        [],
        8,
        "act_gates",
    )(*chunks, last, inv, vectors, *after)


def write_parts(z, values, outs, col):
    values = values.astype(bf16)
    for m in range(z.split):
        outs[m][:, col : col + values.shape[1]] = values[m * z.rows : (m + 1) * z.rows]


def experts_forward(z, rows, w_gate, w_down, after):
    def body(*refs):
        rows, (gate_ref, down_ref), outs = (
            refs[: z.split],
            refs[z.split : z.split + 2],
            refs[z.split + 2 + len(after) :],
        )
        held = jnp.concatenate([part[...] for part in rows], axis=0)
        gate_proj = jnp.dot(held, gate_ref[0], preferred_element_type=f32)
        hidden = jax.nn.silu(gate_proj).astype(bf16)
        step = 512
        for col in range(0, z.width, step):
            part = jnp.dot(hidden, down_ref[0, :, col : col + step], preferred_element_type=f32)
            write_parts(z, part, outs, col)

    return call(
        body,
        "v" * (z.split + 2) + "a" * len(after),
        [shape((z.rows, z.width))] * z.split,
        [],
        16,
        "experts_forward",
    )(*rows, w_gate, w_down, *after)


def saved_rows(z, where, saved, weights, after):
    total, slots, width = z.split * z.rows, saved.shape[2], saved.shape[3]

    def body(where, saved_any, *refs):
        ordered_ref, saved_ref, sem = refs[len(weights) + len(after) :]
        copy = pltpu.make_async_copy(saved_any.at[0, 0], saved_ref, sem)
        copy.start()
        row = lax.broadcasted_iota(jnp.int32, (total, slots), 0)
        slot = lax.broadcasted_iota(jnp.int32, (total, slots), 1)
        m, at = row // z.rows, row % z.rows
        is_main = at < z.tokens
        k = jnp.where(is_main, at // z.main, at - z.tokens)
        p = jnp.where(is_main, at % z.main, z.main)
        source = jnp.bitwise_xor(k, where[0]) * z.split + jnp.bitwise_xor(m, where[1])
        wanted = jnp.where(k < z.experts, source * z.cap + p, -1)
        selector = jnp.where(slot == wanted, 1.0, 0.0).astype(bf16)
        copy.wait()
        ordered_ref[...] = jnp.dot(selector, saved_ref[...], preferred_element_type=f32)

    return call(
        body,
        "sh" + "v" * len(weights) + "a" * len(after),
        shape((total, width), f32),
        [pltpu.VMEM((slots, width), bf16), pltpu.SemaphoreType.DMA],
        8,
        "saved_rows",
    )(where, saved, *weights, *after)


def saved_terms(z, ordered, after):
    def body(ordered_ref, *refs):
        hidden_ref, slope_ref = refs[len(after) :]
        gate_proj = ordered_ref[...]
        sg = jax.nn.sigmoid(gate_proj)
        hidden_ref[...] = (gate_proj * sg).astype(bf16)
        slope_ref[...] = sg * (1.0 + gate_proj * (1.0 - sg))

    return call(
        body,
        "v" + "a" * len(after),
        [shape(ordered.shape), shape(ordered.shape, f32)],
        [],
        8,
        "saved_terms",
    )(ordered, *after)


def turned(z, weights, held, after, name):
    rows, columns = weights.shape[1:]
    step = min(512, rows, columns)

    def body(weights_ref, *refs):
        for at in range(0, rows, step):
            for col in range(0, columns, step):
                block = weights_ref[0, at : at + step, col : col + step]
                refs[-1][col : col + step, at : at + step] = block.T

    return call(
        body, "v" + "v" * len(held) + "a" * len(after), shape((columns, rows)), [], 12, name
    )(weights, *held, *after)


def experts_backward(z, rows, hidden, slope, w_gate, w_down, after):
    def body(*refs):
        rows = refs[: z.split]
        hidden_ref, slope_ref, gate_ref, down_ref = refs[z.split : z.split + 4]
        outs = refs[z.split + 4 + len(after) :]
        held = jnp.concatenate([part[...] for part in rows], axis=0)
        grad_hidden = lax.dot_general(held, down_ref[...], nn, preferred_element_type=f32)
        dots = jnp.sum(grad_hidden * hidden_ref[...].astype(f32), axis=-1, keepdims=True)
        grad_gate = (grad_hidden * slope_ref[...]).astype(bf16)
        step = 512
        for col in range(0, z.width, step):
            part = lax.dot_general(
                grad_gate, gate_ref[:, col : col + step], nn, preferred_element_type=f32
            )
            write_parts(z, part, outs, col)
        write_parts(z, jnp.broadcast_to(dots, (dots.shape[0], 128)), outs, z.width)

    return call(
        body,
        "v" * (z.split + 4) + "a" * len(after),
        [shape((z.rows, z.width + 128))] * z.split,
        [],
        16,
        "experts_backward",
    )(*rows, hidden, slope, w_gate, w_down, *after)


def put_last(z, values, source_chunk, tile, out):
    tile[...] = jnp.zeros_like(tile)
    pack_last(values, tile)
    tokens = source_chunk[:16, z.width :].astype(f32)
    tile[z.pieces : z.pieces + 1, :] = tokens[z.pieces : z.pieces + 1, :]
    out[:, z.width :] = tile[...].astype(bf16)


def finish_forward(z, ks, chunks, last, parts, gates, after):
    count = len(ks)

    def body(*refs):
        chunks, last, parts = refs[:count], refs[count], refs[count + 1 : count + 1 + z.split]
        gates, outs, tile = refs[count + 1 + z.split], refs[-1 - count : -1], refs[-1]

        def mixed(at):
            y = parts[0][at : at + 16, :].astype(f32)
            for part in parts[1:]:
                y = y + part[at : at + 16, :].astype(f32)
            return route_scale * (gates[at : at + 16, 0:1] * y)

        tail = last[...] + mixed(z.tokens)
        for k, chunk, out in zip(ks, chunks, outs):
            h = chunk[:, : z.width].astype(f32)
            out[:, : z.width] = (h + mixed(k * z.main)).astype(bf16)
            put_last(z, tail[k : k + 1, :], chunk, tile, out)

    return call(
        body,
        "v" * (count + z.split + 2) + "a" * len(after),
        [shape((z.main, z.wide))] * count,
        [pltpu.VMEM((16, fold), f32)],
        8,
        "finish_forward_" + "".join(map(str, ks)),
    )(*[chunks[k] for k in ks], last, *parts, gates, *after)


def finish_backward(z, order, chunks, lasts, terms, parts, vectors, after):
    def body(*refs):
        e = z.experts
        chunks, (last_grad, last_act, inv_ref, affinity_ref) = refs[:e], refs[e : e + 4]
        parts, vectors = refs[e + 4 : e + 4 + z.split], refs[e + 4 + z.split]
        outs, (tile,) = refs[-1 - e : -1], refs[-1:]
        outs = [outs[order.index(k)] for k in range(e)]
        gain, router = vectors[0:1, :], vectors[1:2, :]

        def finished(h, g, at):
            inv, affinity = inv_ref[at : at + 16, 0:1], affinity_ref[at : at + 16, 0:1]
            rows = parts[0][at : at + 16, : z.width].astype(f32)
            dot = parts[0][at : at + 16, z.width :].astype(f32)
            for part in parts[1:]:
                rows = rows + part[at : at + 16, : z.width].astype(f32)
                dot = dot + part[at : at + 16, z.width :].astype(f32)
            dot = dot[:, 0:1]
            grad_logits = (route_scale * dot * affinity * (1.0 - affinity)).astype(bf16).astype(f32)
            grad_pre = (route_scale * affinity * rows + grad_logits * router) * gain
            centre = jnp.mean(grad_pre * h, axis=-1, keepdims=True)
            return g + inv * (grad_pre - h * (inv * inv * centre))

        tail = finished(last_act[...], last_grad[...], z.tokens)
        for k in range(e):
            g = chunks[k][:16, : z.width].astype(f32)
            h = chunks[k][16:32, : z.width].astype(f32)
            outs[k][:, : z.width] = finished(h, g, k * z.main).astype(bf16)
            put_last(z, tail[k : k + 1, :], chunks[k], tile, outs[k])

    return call(
        body,
        "v" * (z.experts + z.split + 5) + "a" * len(after),
        [shape((z.main, z.wide))] * z.experts,
        [pltpu.VMEM((16, fold), f32)],
        8,
        "finish_backward",
    )(*chunks, *lasts, *terms, *parts, vectors, *after)


def order_rows(z, arrays, places, after, name):
    count = len(arrays)
    lanes = z.tokens + 16 * z.experts
    steps = 7 if z.pieces % 7 == 0 else z.pieces

    def body(*refs):
        arrays, (out_any, out, sems) = refs[:count], refs[count + len(after) :]
        chunks = [arrays[i].at[pl.ds(at, 16)] for i, at in places]
        tiles = [chunk[:, z.width :] for chunk in chunks]
        token_row = tiles[0].astype(f32)[z.pieces : z.pieces + 1, :lanes]
        token = lax.broadcasted_iota(jnp.int32, (z.tokens, lanes), 0).astype(f32)
        lane = lax.broadcasted_iota(jnp.int32, (z.tokens, lanes), 1)
        piece = jnp.where(lane < z.tokens, -1, lane % 16)
        ours = token == token_row
        copies = []
        for i in range(z.pieces):
            cols = pl.ds(i * fold, fold)
            mine = ours & ((piece < 0) | (piece == i))
            selector = jnp.where(mine, 1.0, 0.0).astype(bf16)
            rows = jnp.concatenate([chunk[:, cols] for chunk in chunks] + tiles, axis=0)
            out[:, cols] = jnp.dot(selector, rows, preferred_element_type=f32).astype(bf16)
            if (i + 1) % (z.pieces // steps) == 0:
                done = pl.ds((i + 1) * fold - z.width // steps, z.width // steps)
                copy = pltpu.make_async_copy(out.at[:, done], out_any.at[:, done], sems.at[len(copies)])
                copy.start()
                copies.append(copy)
        for copy in copies:
            copy.wait()

    return call(
        body,
        "v" * count + "a" * len(after),
        shape((z.tokens, z.width)),
        [pltpu.VMEM((z.tokens, z.width), bf16), pltpu.SemaphoreType.DMA((steps,))],
        8,
        name,
        spaces["a"],
    )(*arrays, *after)


def to_block(z, array, k):
    groups = z.experts * z.split
    pairs = [(i, ((i // z.split) ^ k) * z.split + i % z.split) for i in range(groups)]
    return lax.ppermute(array, "ep", pairs)


def dispatch(z, chunks):
    return [chunks[0]] + [to_block(z, chunks[k], k) for k in range(1, z.experts)]


def to_core(z, array, m):
    groups = z.experts * z.split
    pairs = [(i, i // z.split * z.split + ((i % z.split) ^ m)) for i in range(groups)]
    return lax.ppermute(array, "ep", pairs)


def to_section(z, chunk, k, by):
    groups = z.experts * z.split
    sections = lax.axis_size("pp")
    pairs = [
        (s * groups + i, (s + by) % sections * groups + ((i // z.split) ^ k) * z.split + i % z.split)
        for s in range(sections)
        for i in range(groups)
    ]
    return lax.ppermute(chunk, ("pp", "ep"), pairs)


def on_device(
    fwd_act, fwd_ids, bwd_act, bwd_ids, bwd_grad, norm_gain, router, w_gate, w_down, saved_gate
):
    groups = lax.axis_size("ep")
    assert fwd_ids.shape[1] == 1
    z = Sizes(groups, router.shape[2], fwd_act.shape[0], fwd_act.shape[1])
    index = lax.axis_index("ep")
    where = jnp.stack([index // z.split, index % z.split]).astype(jnp.int32)
    router = jnp.swapaxes(router, 1, 2)
    others = range(1, z.split)

    fwd_chunks, (grad, act, gain_row, table), slots = forward_chunks(
        z, where, fwd_ids, fwd_act, bwd_ids, [bwd_grad, bwd_act, norm_gain, router]
    )
    fwd_own = dispatch(z, fwd_chunks)
    bwd_chunks, vectors = backward_chunks(z, where, slots, [grad, act], gain_row, table)
    bwd_own = dispatch(z, bwd_chunks)

    down_turned = turned(z, w_down, [w_gate], [bwd_chunks[0], fwd_own[1]], "turned_down")
    normed, gates, fwd_last = normed_rows(z, fwd_own, vectors, [down_turned])
    fwd_all = [normed] + [to_core(z, normed, m) for m in others]
    ordered = saved_rows(z, where, saved_gate, [], [gates])
    fwd_parts = experts_forward(z, fwd_all, w_gate, w_down, [ordered])
    hidden, slope = saved_terms(z, ordered, [fwd_parts[0]])
    gate_turned = turned(z, w_gate, [], [hidden], "turned_gate")
    fwd_parts = [fwd_parts[0]] + [to_core(z, fwd_parts[m], m) for m in others]

    done = {}

    def finish(ks, after):
        outs = finish_forward(z, ks, fwd_own, fwd_last, fwd_parts, gates, after)
        for k, out in zip(ks, outs):
            done[k] = to_section(z, out, k, 1)
        return outs[0]

    assert z.experts == 4
    out = finish([0], [gate_turned])
    out = finish([2], [gate_turned, out])
    grads, grad_last = grad_rows_of(z, bwd_own, [out])
    grad_all = [grads] + [to_core(z, grads, m) for m in others]
    inv, act_last = act_norms(z, bwd_own, [grads])
    out = finish([3], [inv])
    bwd_parts = experts_backward(z, grad_all, hidden, slope, gate_turned, down_turned, [out])
    affinity = act_gates(z, bwd_own, act_last, inv, vectors, [bwd_parts[0], done[0]])
    out = finish([1], [affinity])
    bwd_parts = [bwd_parts[0]] + [to_core(z, bwd_parts[m], m) for m in others]
    bwd_out = finish_backward(
        z, z.order, bwd_own, [grad_last, act_last], [inv, affinity], bwd_parts, vectors, [out]
    )
    fwd_done = [done[k] for k in range(z.experts)]
    bwd_done = {k: to_section(z, out, k, -1) for k, out in zip(z.order, bwd_out)}

    places = [(k, 0) for k in range(z.experts)]
    fwd_next = order_rows(z, fwd_done, places, [], "forward_rows")
    places = [(z.order.index(k), 0) for k in range(z.experts)]
    bwd_next = order_rows(z, [bwd_done[k] for k in z.order], places, [], "backward_rows")
    return (fwd_next, bwd_next)


def solution(mesh):
    return jax.shard_map(
        on_device,
        mesh=mesh,
        in_specs=(
            P(("pp", "ep"), None),
            P(("pp", "ep"), None),
            P(("pp", "ep"), None),
            P(("pp", "ep"), None),
            P(("pp", "ep"), None),
            P("pp", None),
            P("pp", None, None),
            P(("pp", "ep"), None, None),
            P(("pp", "ep"), None, None),
            P("pp", "ep", None, None),
        ),
        out_specs=(P(("pp", "ep"), None), P(("pp", "ep"), None)),
        check_vma=False,
    )
```

```python
import functools

import jax
import jax.numpy as jnp
from jax import lax
from jax.experimental import pallas as pl
from jax.experimental.pallas import tpu as pltpu
from jax.sharding import PartitionSpec as P

epsilon = 1e-06
route_scale = 2.5
fold = 256
none = 255.0
f32 = jnp.float32
bf16 = jnp.bfloat16
nn = (((1,), (0,)), ((), ()))
spaces = {
    "s": pl.BlockSpec(memory_space=pltpu.SMEM),
    "v": pl.BlockSpec(memory_space=pltpu.VMEM),
    "a": pl.BlockSpec(memory_space=pl.ANY),
    "h": pl.BlockSpec(memory_space=pltpu.HBM),
}


cost = {
    "backward_chunks": 10,
    "saved_rows": 15,
    "saved_terms": 15,
    "act_norms": 15,
    "act_gates": 15,
    "forward_rows_early": 15,
}


def call(body, places, outs, scratch, megabytes, name, out_specs=None):
    def run(*arrays):
        arrays = [
            pltpu.with_memory_space_constraint(array, pltpu.HBM) if place == "h" else array
            for array, place in zip(arrays, places, strict=True)
        ]
        return kernel(*arrays)

    where_to = {} if out_specs is None else {"out_specs": out_specs}
    kernel = pl.pallas_call(
        body,
        out_shape=outs,
        in_specs=[spaces[place] for place in places],
        **where_to,
        scratch_shapes=scratch,
        compiler_params=pltpu.CompilerParams(vmem_limit_bytes=megabytes * 1024 * 1024),
        cost_estimate=pl.CostEstimate(
            flops=int(cost.get(name, 0.1) * 1e9), bytes_accessed=1000, transcendentals=0
        ),
        name=name,
    )
    return run


def shape(dims, kind=bf16):
    return jax.ShapeDtypeStruct(dims, kind)


class Sizes:
    def __init__(self, groups, experts, tokens, width):
        self.experts = experts
        self.split = groups // experts
        self.tokens = tokens
        self.width = width
        self.main = tokens // experts
        self.cap = self.main + 1
        self.pieces = width // fold
        self.wide = width + fold
        self.rows = tokens + 16
        self.order = [experts - 1, *range(1, experts - 1), 0]
        assert self.main == 16 and self.pieces <= 14 and width % fold == 0
        assert experts <= 8 and experts & (experts - 1) == 0 and self.split & (self.split - 1) == 0


def pack_last(row, tile, first=0):
    for i in range(row.shape[1] // fold):
        tile[first + i : first + i + 1, :] = row[:, i * fold : (i + 1) * fold]


def unpack_last(chunk, z, tile, target, at, base=0):
    tile[...] = chunk[base : base + 16, z.width :].astype(f32)
    for i in range(z.pieces):
        target[at : at + 1, i * fold : (i + 1) * fold] = tile[i : i + 1, :]


def slot_matrices(ids_row, block, z):
    tokens = z.tokens
    sub = lax.broadcasted_iota(jnp.int32, (tokens, tokens), 0)
    lane = lax.broadcasted_iota(jnp.int32, (tokens, tokens), 1)
    row = jnp.bitwise_xor(ids_row, block)
    column = jnp.sum(jnp.where(sub == lane, row, 0), axis=1, keepdims=True)
    same = column == row
    place_row = jnp.sum(jnp.where(same & (sub < lane), 1, 0), axis=0, keepdims=True)
    place_column = jnp.sum(jnp.where(same & (lane < sub), 1, 0), axis=1, keepdims=True)

    def slot(expert, place):
        return jnp.where(place < z.main, expert * z.main + place, tokens + expert)

    slot_row = slot(row, place_row)
    slot_column = slot(column, place_column)
    by_slot = lax.broadcasted_iota(jnp.int32, (z.rows, tokens), 0) == slot_row
    lane = lax.broadcasted_iota(jnp.int32, (tokens, fold), 1)
    by_token = jnp.where(lane < tokens, lane, tokens + (lane - tokens) // 16) == slot_column
    token = lax.broadcasted_iota(jnp.int32, (tokens, fold), 0).astype(f32)
    token_row = jnp.sum(jnp.where(by_token, token - none, 0.0), axis=0, keepdims=True) + none
    return jnp.where(by_slot, 1.0, 0.0).astype(bf16), token_row


def write_chunks(z, selector, token_row, rows_ref, ready, tiles, chunks, base):
    step = z.width // 2
    tiles[...] = jnp.zeros_like(tiles)
    for half in range(2):
        if ready:
            ready[half].wait()
        col = half * step
        got = jnp.dot(selector, rows_ref[:, col : col + step], preferred_element_type=f32)
        packed = got[: z.tokens].astype(bf16)
        for k in range(z.experts):
            chunks[k][base : base + 16, col : col + step] = packed[k * z.main : (k + 1) * z.main]
            pack_last(got[z.tokens + k : z.tokens + k + 1], tiles.at[k], half * z.pieces // 2)
    for k in range(z.experts):
        tiles[k, z.pieces : z.pieces + 1, :] = token_row
        chunks[k][base : base + 16, z.width :] = tiles[k].astype(bf16)


def forward_chunks(z, where, ids, act, later_ids, later):
    count = len(later)

    def body(where, ids_any, later_ids_any, act_any, *refs):
        later_any, chunks = refs[:count], refs[count : count + z.experts]
        later_refs = refs[count + z.experts : 2 * count + z.experts]
        selector_ref, token_ref, ids, rows, tiles, sems = refs[2 * count + z.experts :]
        step = z.width // 2
        first = [
            pltpu.make_async_copy(source, ids.at[i : i + 1], sems.at[i])
            for i, source in enumerate((ids_any, later_ids_any))
        ]
        ready = [
            pltpu.make_async_copy(
                act_any.at[:, pl.ds(i * step, step)], rows.at[:, pl.ds(i * step, step)], sems.at[2 + i]
            )
            for i in range(2)
        ]
        rest = [
            pltpu.make_async_copy(source, target, sems.at[4 + i])
            for i, (source, target) in enumerate(zip(later_any, later_refs))
        ]
        for copy in first + ready + rest:
            copy.start()
        for copy in first:
            copy.wait()
        selector, token_row = slot_matrices(ids[0:1, :], where[0], z)
        later_selector, later_row = slot_matrices(ids[1:2, :], where[0], z)
        selector_ref[...] = later_selector
        token_ref[...] = jnp.broadcast_to(later_row, token_ref.shape)
        write_chunks(z, selector, token_row, rows, ready, tiles, chunks, 0)
        for copy in rest:
            copy.wait()

    outs = call(
        body,
        "shhh" + "h" * count,
        [shape((z.main, z.wide))] * z.experts
        + [shape(array.shape, array.dtype) for array in later]
        + [shape((z.rows, z.tokens)), shape((8, fold), f32)],
        [
            pltpu.VMEM((2, z.tokens), jnp.int32),
            pltpu.VMEM((z.tokens, z.width), bf16),
            pltpu.VMEM((z.experts, 16, fold), f32),
            pltpu.SemaphoreType.DMA((4 + count,)),
        ],
        8,
        "forward_chunks",
    )(where, ids.reshape(1, z.tokens), later_ids.reshape(1, z.tokens), act, *later)
    return outs[: z.experts], outs[z.experts : z.experts + count], outs[z.experts + count :]


def backward_chunks(z, where, slots, sources, gain, router):
    count = len(sources)

    def body(where, selector, token_ref, *refs):
        sources, (gain_ref, router_ref) = refs[:count], refs[count : count + 2]
        *chunks, vectors, tiles = refs[count + 2 :]
        for j in range(count):
            write_chunks(
                z, selector[...], token_ref[0:1, :], sources[j], None, tiles, chunks, 16 * j
            )
        vectors[...] = jnp.zeros_like(vectors)
        vectors[0:1, :] = gain_ref[...].astype(f32)
        mine = lax.broadcasted_iota(jnp.int32, (z.experts, 1), 0) == where[0]
        table = jnp.where(mine, router_ref[0].astype(f32), 0.0)
        vectors[1:2, :] = jnp.sum(table, axis=0, keepdims=True)

    *chunks, vectors = call(
        body,
        "svv" + "v" * (count + 2),
        [shape((z.main * count, z.wide))] * z.experts + [shape((8, z.width), f32)],
        [pltpu.VMEM((z.experts, 16, fold), f32)],
        8,
        "backward_chunks",
    )(where, *slots, *sources, gain, router)
    return chunks, vectors


def collect_rows(z, chunks, last, tile, base=0):
    last[...] = jnp.zeros_like(last)
    for k in range(z.experts):
        unpack_last(chunks[k], z, tile, last, k, base)


def norm_rows(h, gain):
    inv = lax.rsqrt(jnp.mean(h * h, axis=-1, keepdims=True) + epsilon)
    return (h * inv * gain).astype(bf16), inv


def normed_rows(z, chunks, vectors, after):
    def body(*refs):
        chunks, vectors = refs[: z.experts], refs[z.experts]
        normed_ref, gates_ref, last, tile = refs[z.experts + 1 + len(after) :]
        gain, router = vectors[0:1, :], vectors[1:2, :]
        collect_rows(z, chunks, last, tile)
        for k in range(z.experts + 1):
            h = last[...] if k == z.experts else chunks[k][:, : z.width].astype(f32)
            at = k * z.main
            normed, _ = norm_rows(h, gain)
            normed_ref[at : at + 16, :] = normed
            logits = jnp.sum(normed.astype(f32) * router, axis=-1, keepdims=True)
            gates_ref[at : at + 16, :] = jnp.broadcast_to(jax.nn.sigmoid(logits), (16, 128))

    return call(
        body,
        "v" * (z.experts + 1) + "a" * len(after),
        [shape((z.rows, z.width)), shape((z.rows, 128), f32), shape((16, z.width), f32)],
        [pltpu.VMEM((16, fold), f32)],
        8,
        "normed_rows",
    )(*chunks, vectors, *after)


def grad_rows_of(z, chunks, after):
    def body(*refs):
        chunks, (rows, last, tile) = refs[: z.experts], refs[z.experts + len(after) :]
        for k in range(z.experts):
            rows[k * z.main : (k + 1) * z.main, :] = chunks[k][:16, : z.width]
        collect_rows(z, chunks, last, tile)
        rows[z.tokens :, :] = last[...].astype(bf16)

    return call(
        body,
        "v" * z.experts + "a" * len(after),
        [shape((z.rows, z.width)), shape((16, z.width), f32)],
        [pltpu.VMEM((16, fold), f32)],
        8,
        "grad_rows",
    )(*chunks, *after)


def act_norms(z, chunks, after):
    def body(*refs):
        chunks, (inv_ref, last, tile) = refs[: z.experts], refs[z.experts + len(after) :]
        collect_rows(z, chunks, last, tile, 16)
        for k in range(z.experts + 1):
            h = last[...] if k == z.experts else chunks[k][16:32, : z.width].astype(f32)
            at = k * z.main
            inv = lax.rsqrt(jnp.mean(h * h, axis=-1, keepdims=True) + epsilon)
            inv_ref[at : at + 16, :] = jnp.broadcast_to(inv, (16, 128))

    return call(
        body,
        "v" * z.experts + "a" * len(after),
        [shape((z.rows, 128), f32), shape((16, z.width), f32)],
        [pltpu.VMEM((16, fold), f32)],
        8,
        "act_norms",
    )(*chunks, *after)


def act_gates(z, chunks, last, inv, vectors, after):
    def body(*refs):
        chunks, (last, inv_ref, vectors) = refs[: z.experts], refs[z.experts : z.experts + 3]
        affinity_ref = refs[-1]
        gain, router = vectors[0:1, :], vectors[1:2, :]
        for k in range(z.experts + 1):
            h = last[...] if k == z.experts else chunks[k][16:32, : z.width].astype(f32)
            at = k * z.main
            normed = (h * inv_ref[at : at + 16, 0:1] * gain).astype(bf16).astype(f32)
            logits = jnp.sum(normed * router, axis=-1, keepdims=True)
            affinity_ref[at : at + 16, :] = jnp.broadcast_to(jax.nn.sigmoid(logits), (16, 128))

    return call(
        body,
        "v" * (z.experts + 3) + "a" * len(after),
        shape((z.rows, 128), f32),
        [],
        8,
        "act_gates",
    )(*chunks, last, inv, vectors, *after)


def write_parts(z, values, outs, col):
    values = values.astype(bf16)
    for m in range(z.split):
        outs[m][:, col : col + values.shape[1]] = values[m * z.rows : (m + 1) * z.rows]


def experts_forward(z, rows, w_gate, w_down, after):
    def body(*refs):
        rows, (gate_ref, down_ref), outs = (
            refs[: z.split],
            refs[z.split : z.split + 2],
            refs[z.split + 2 + len(after) :],
        )
        held = jnp.concatenate([part[...] for part in rows], axis=0)
        gate_proj = jnp.dot(held, gate_ref[0], preferred_element_type=f32)
        hidden = jax.nn.silu(gate_proj).astype(bf16)
        step = 512
        for col in range(0, z.width, step):
            part = jnp.dot(hidden, down_ref[0, :, col : col + step], preferred_element_type=f32)
            write_parts(z, part, outs, col)

    return call(
        body,
        "v" * (z.split + 2) + "a" * len(after),
        [shape((z.rows, z.width))] * z.split,
        [],
        16,
        "experts_forward",
    )(*rows, w_gate, w_down, *after)


def saved_rows(z, where, saved, weights, after):
    total, slots, width = z.split * z.rows, saved.shape[2], saved.shape[3]

    def body(where, saved_any, *refs):
        ordered_ref, saved_ref, sem = refs[len(weights) + len(after) :]
        copy = pltpu.make_async_copy(saved_any.at[0, 0], saved_ref, sem)
        copy.start()
        row = lax.broadcasted_iota(jnp.int32, (total, slots), 0)
        slot = lax.broadcasted_iota(jnp.int32, (total, slots), 1)
        m, at = row // z.rows, row % z.rows
        is_main = at < z.tokens
        k = jnp.where(is_main, at // z.main, at - z.tokens)
        p = jnp.where(is_main, at % z.main, z.main)
        source = jnp.bitwise_xor(k, where[0]) * z.split + jnp.bitwise_xor(m, where[1])
        wanted = jnp.where(k < z.experts, source * z.cap + p, -1)
        selector = jnp.where(slot == wanted, 1.0, 0.0).astype(bf16)
        copy.wait()
        ordered_ref[...] = jnp.dot(selector, saved_ref[...], preferred_element_type=f32)

    return call(
        body,
        "sh" + "v" * len(weights) + "a" * len(after),
        shape((total, width), f32),
        [pltpu.VMEM((slots, width), bf16), pltpu.SemaphoreType.DMA],
        8,
        "saved_rows",
    )(where, saved, *weights, *after)


def saved_terms(z, ordered, after):
    def body(ordered_ref, *refs):
        hidden_ref, slope_ref = refs[len(after) :]
        gate_proj = ordered_ref[...]
        sg = jax.nn.sigmoid(gate_proj)
        hidden_ref[...] = (gate_proj * sg).astype(bf16)
        slope_ref[...] = sg * (1.0 + gate_proj * (1.0 - sg))

    return call(
        body,
        "v" + "a" * len(after),
        [shape(ordered.shape), shape(ordered.shape, f32)],
        [],
        8,
        "saved_terms",
    )(ordered, *after)


def turned(z, weights, held, after, name):
    rows, columns = weights.shape[1:]
    step = min(512, rows, columns)

    def body(weights_ref, *refs):
        for at in range(0, rows, step):
            for col in range(0, columns, step):
                block = weights_ref[0, at : at + step, col : col + step]
                refs[-1][col : col + step, at : at + step] = block.T

    return call(
        body, "v" + "v" * len(held) + "a" * len(after), shape((columns, rows)), [], 12, name
    )(weights, *held, *after)


def experts_backward(z, rows, hidden, slope, w_gate, w_down, after):
    def body(*refs):
        rows = refs[: z.split]
        hidden_ref, slope_ref, gate_ref, down_ref = refs[z.split : z.split + 4]
        outs = refs[z.split + 4 + len(after) :]
        held = jnp.concatenate([part[...] for part in rows], axis=0)
        grad_hidden = lax.dot_general(held, down_ref[...], nn, preferred_element_type=f32)
        dots = jnp.sum(grad_hidden * hidden_ref[...].astype(f32), axis=-1, keepdims=True)
        grad_gate = (grad_hidden * slope_ref[...]).astype(bf16)
        step = 512
        for col in range(0, z.width, step):
            part = lax.dot_general(
                grad_gate, gate_ref[:, col : col + step], nn, preferred_element_type=f32
            )
            write_parts(z, part, outs, col)
        write_parts(z, jnp.broadcast_to(dots, (dots.shape[0], 128)), outs, z.width)

    return call(
        body,
        "v" * (z.split + 4) + "a" * len(after),
        [shape((z.rows, z.width + 128))] * z.split,
        [],
        16,
        "experts_backward",
    )(*rows, hidden, slope, w_gate, w_down, *after)


def put_last(z, values, source_chunk, tile, out):
    tile[...] = jnp.zeros_like(tile)
    pack_last(values, tile)
    tokens = source_chunk[:16, z.width :].astype(f32)
    tile[z.pieces : z.pieces + 1, :] = tokens[z.pieces : z.pieces + 1, :]
    out[:, z.width :] = tile[...].astype(bf16)


def finish_forward(z, ks, chunks, last, parts, gates, after):
    count = len(ks)

    def body(*refs):
        chunks, last, parts = refs[:count], refs[count], refs[count + 1 : count + 1 + z.split]
        gates, out, tile = refs[count + 1 + z.split], refs[-2], refs[-1]

        def mixed(at):
            y = parts[0][at : at + 16, :].astype(f32)
            for part in parts[1:]:
                y = y + part[at : at + 16, :].astype(f32)
            return route_scale * (gates[at : at + 16, 0:1] * y)

        tail = last[...] + mixed(z.tokens)
        for i, (k, chunk) in enumerate(zip(ks, chunks)):
            h = chunk[:, : z.width].astype(f32)
            rows = out.at[pl.ds(i * 16, 16)]
            rows[:, : z.width] = (h + mixed(k * z.main)).astype(bf16)
            put_last(z, tail[k : k + 1, :], chunk, tile, rows)

    return call(
        body,
        "v" * (count + z.split + 2) + "a" * len(after),
        shape((count * z.main, z.wide)),
        [pltpu.VMEM((16, fold), f32)],
        8,
        "finish_forward_" + "".join(map(str, ks)),
    )(*[chunks[k] for k in ks], last, *parts, gates, *after)


def lower_chunk(z, double, after):
    def body(double, *refs):
        refs[-1][...] = double[16:32, :]

    places = "v" + "a" * len(after)
    return call(body, places, shape((16, z.wide)), [], 8, "lower_chunk")(double, *after)


def finish_backward(z, order, chunks, lasts, terms, parts, vectors, after):
    def body(*refs):
        e = z.experts
        chunks, (last_grad, last_act, inv_ref, affinity_ref) = refs[:e], refs[e : e + 4]
        parts, vectors = refs[e + 4 : e + 4 + z.split], refs[e + 4 + z.split]
        outs, (tile,) = refs[-1 - e : -1], refs[-1:]
        outs = [outs[order.index(k)] for k in range(e)]
        gain, router = vectors[0:1, :], vectors[1:2, :]

        def finished(h, g, at):
            inv, affinity = inv_ref[at : at + 16, 0:1], affinity_ref[at : at + 16, 0:1]
            rows = parts[0][at : at + 16, : z.width].astype(f32)
            dot = parts[0][at : at + 16, z.width :].astype(f32)
            for part in parts[1:]:
                rows = rows + part[at : at + 16, : z.width].astype(f32)
                dot = dot + part[at : at + 16, z.width :].astype(f32)
            dot = dot[:, 0:1]
            grad_logits = (route_scale * dot * affinity * (1.0 - affinity)).astype(bf16).astype(f32)
            grad_pre = (route_scale * affinity * rows + grad_logits * router) * gain
            centre = jnp.mean(grad_pre * h, axis=-1, keepdims=True)
            return g + inv * (grad_pre - h * (inv * inv * centre))

        tail = finished(last_act[...], last_grad[...], z.tokens)
        for k in range(e):
            g = chunks[k][:16, : z.width].astype(f32)
            h = chunks[k][16:32, : z.width].astype(f32)
            outs[k][:, : z.width] = finished(h, g, k * z.main).astype(bf16)
            put_last(z, tail[k : k + 1, :], chunks[k], tile, outs[k])

    return call(
        body,
        "v" * (z.experts + z.split + 5) + "a" * len(after),
        [shape((z.main, z.wide))] * z.experts,
        [pltpu.VMEM((16, fold), f32)],
        8,
        "finish_backward",
    )(*chunks, *lasts, *terms, *parts, vectors, *after)


def ordered_columns(z, chunks):
    lanes = z.tokens + 16 * z.experts
    some = next(iter(chunks))
    filled = [chunks.get(k, chunks[some]) for k in range(z.experts)]
    tiles = [chunk[:16, z.width :] for chunk in filled]
    token_row = tiles[some].astype(f32)[z.pieces : z.pieces + 1, :lanes]
    token = lax.broadcasted_iota(jnp.int32, (z.tokens, lanes), 0).astype(f32)
    lane = lax.broadcasted_iota(jnp.int32, (z.tokens, lanes), 1)
    piece = jnp.where(lane < z.tokens, -1, lane % 16)
    ours = token == token_row
    if len(chunks) < z.experts:
        held = [lane // 16 % z.experts == k for k in chunks]
        ours = ours & functools.reduce(jnp.logical_or, held)
    for i in range(z.pieces):
        cols = pl.ds(i * fold, fold)
        selector = jnp.where(ours & ((piece < 0) | (piece == i)), 1.0, 0.0).astype(bf16)
        rows = jnp.concatenate([chunk[:16, cols] for chunk in filled] + tiles, axis=0)
        yield cols, jnp.dot(selector, rows, preferred_element_type=f32)


def some_rows(z, chunks, after, name):
    ks = list(chunks)

    def body(*refs):
        for cols, rows in ordered_columns(z, dict(zip(ks, refs))):
            refs[-1][:, cols] = rows.astype(bf16)

    places = "v" * len(ks) + "a" * len(after)
    return call(body, places, shape((z.tokens, z.width)), [], 8, name)(*chunks.values(), *after)


def order_rows(z, chunks, others, name):
    ks, count = list(chunks), len(chunks)
    steps = 7 if z.pieces % 7 == 0 else z.pieces

    def body(*refs):
        others, (out_any, out, sems) = refs[count:-3], refs[-3:]
        copies = []
        for i, (cols, rows) in enumerate(ordered_columns(z, dict(zip(ks, refs)))):
            for other in others:
                rows = rows + other[:, cols].astype(f32)
            out[:, cols] = rows.astype(bf16)
            if (i + 1) % (z.pieces // steps) == 0:
                done = pl.ds((i + 1) * fold - z.width // steps, z.width // steps)
                copy = pltpu.make_async_copy(out.at[:, done], out_any.at[:, done], sems.at[len(copies)])
                copy.start()
                copies.append(copy)
        for copy in copies:
            copy.wait()

    return call(
        body,
        "v" * (count + len(others)),
        shape((z.tokens, z.width)),
        [pltpu.VMEM((z.tokens, z.width), bf16), pltpu.SemaphoreType.DMA((steps,))],
        8,
        name,
        spaces["a"],
    )(*chunks.values(), *others)


def permute_blocks(z, arrays, k):
    groups = z.experts * z.split
    pairs = [(i, ((i // z.split) ^ k) * z.split + i % z.split) for i in range(groups)]
    return [lax.ppermute(array, "ep", pairs) for array in arrays]


def dispatch(z, chunks):
    return [chunks[0]] + [permute_blocks(z, [chunks[k]], k)[0] for k in range(1, z.experts)]


def to_core(z, array, m):
    groups = z.experts * z.split
    pairs = [(i, i // z.split * z.split + ((i % z.split) ^ m)) for i in range(groups)]
    return lax.ppermute(array, "ep", pairs)


def to_section(z, chunk, k, by):
    groups = z.experts * z.split
    sections = lax.axis_size("pp")
    pairs = [
        (s * groups + i, (s + by) % sections * groups + ((i // z.split) ^ k) * z.split + i % z.split)
        for s in range(sections)
        for i in range(groups)
    ]
    return lax.ppermute(chunk, ("pp", "ep"), pairs)


def on_device(
    fwd_act, fwd_ids, bwd_act, bwd_ids, bwd_grad, norm_gain, router, w_gate, w_down, saved_gate
):
    groups = lax.axis_size("ep")
    assert fwd_ids.shape[1] == 1
    z = Sizes(groups, router.shape[2], fwd_act.shape[0], fwd_act.shape[1])
    index = lax.axis_index("ep")
    where = jnp.stack([index // z.split, index % z.split]).astype(jnp.int32)
    router = jnp.swapaxes(router, 1, 2)
    others = range(1, z.split)

    fwd_chunks, (grad, act, gain_row, table), slots = forward_chunks(
        z, where, fwd_ids, fwd_act, bwd_ids, [bwd_grad, bwd_act, norm_gain, router]
    )
    fwd_own = dispatch(z, fwd_chunks)
    bwd_chunks, vectors = backward_chunks(z, where, slots, [grad, act], gain_row, table)
    bwd_own = dispatch(z, bwd_chunks)

    down_turned = turned(z, w_down, [w_gate], [bwd_chunks[0], fwd_own[1]], "turned_down")
    normed, gates, fwd_last = normed_rows(z, fwd_own, vectors, [down_turned])
    fwd_all = [normed] + [to_core(z, normed, m) for m in others]
    ordered = saved_rows(z, where, saved_gate, [], [gates])
    fwd_parts = experts_forward(z, fwd_all, w_gate, w_down, [ordered])
    hidden, slope = saved_terms(z, ordered, [fwd_parts[0]])
    gate_turned = turned(z, w_gate, [], [hidden], "turned_gate")
    fwd_parts = [fwd_parts[0]] + [to_core(z, fwd_parts[m], m) for m in others]

    assert z.experts == 4

    def finish(ks, after):
        return finish_forward(z, ks, fwd_own, fwd_last, fwd_parts, gates, after)

    double = finish([0, 1], [gate_turned])
    got = to_section(z, double, 0, 1)
    out2 = finish([2], [hidden, double])
    got2 = to_section(z, out2, 2, 1)
    grads, grad_last = grad_rows_of(z, bwd_own, [out2])
    grad_all = [grads] + [to_core(z, grads, m) for m in others]
    inv, act_last = act_norms(z, bwd_own, [grads])
    out3 = finish([3], [inv])
    got3 = to_section(z, out3, 3, 1)
    bwd_parts = experts_backward(z, grad_all, hidden, slope, gate_turned, down_turned, [inv])
    affinity = act_gates(z, bwd_own, act_last, inv, vectors, [bwd_parts[0]])
    fwd_done = [got2, got3]
    bwd_parts = [bwd_parts[0]] + [to_core(z, bwd_parts[m], m) for m in others]
    bwd_out = finish_backward(
        z, z.order, bwd_own, [grad_last, act_last], [inv, affinity], bwd_parts, vectors, []
    )
    (relayed,) = permute_blocks(z, [lower_chunk(z, got, [bwd_out[0]])], 1)
    bwd_done = {k: to_section(z, out, k, -1) for k, out in zip(z.order, bwd_out)}

    early = some_rows(z, {0: got, 2: got2, 3: got3}, [], "forward_rows_early")
    fwd_next = order_rows(z, {1: relayed}, [early], "forward_rows")
    bwd_next = order_rows(z, {k: bwd_done[k] for k in z.order}, [], "backward_rows")
    return (fwd_next, bwd_next)


def solution(mesh):
    return jax.shard_map(
        on_device,
        mesh=mesh,
        in_specs=(
            P(("pp", "ep"), None),
            P(("pp", "ep"), None),
            P(("pp", "ep"), None),
            P(("pp", "ep"), None),
            P(("pp", "ep"), None),
            P("pp", None),
            P("pp", None, None),
            P(("pp", "ep"), None, None),
            P(("pp", "ep"), None, None),
            P("pp", "ep", None, None),
        ),
        out_specs=(P(("pp", "ep"), None), P(("pp", "ep"), None)),
        check_vma=False,
    )
```

```python
import functools

import jax
import jax.numpy as jnp
from jax import lax
from jax.experimental import pallas as pl
from jax.experimental.pallas import tpu as pltpu
from jax.sharding import PartitionSpec as P

epsilon = 1e-06
route_scale = 2.5
fold = 256
none = 255.0
f32 = jnp.float32
bf16 = jnp.bfloat16
nn = (((1,), (0,)), ((), ()))
spaces = {
    "s": pl.BlockSpec(memory_space=pltpu.SMEM),
    "v": pl.BlockSpec(memory_space=pltpu.VMEM),
    "a": pl.BlockSpec(memory_space=pl.ANY),
    "h": pl.BlockSpec(memory_space=pltpu.HBM),
}


cost = {
    "backward_chunks": 10,
    "saved_rows": 15,
    "saved_terms": 15,
    "act_norms": 15,
    "act_gates": 15,
}


def call(body, places, outs, scratch, megabytes, name, out_specs=None):
    def run(*arrays):
        arrays = [
            pltpu.with_memory_space_constraint(array, pltpu.HBM) if place == "h" else array
            for array, place in zip(arrays, places, strict=True)
        ]
        return kernel(*arrays)

    where_to = {} if out_specs is None else {"out_specs": out_specs}
    kernel = pl.pallas_call(
        body,
        out_shape=outs,
        in_specs=[spaces[place] for place in places],
        **where_to,
        scratch_shapes=scratch,
        compiler_params=pltpu.CompilerParams(vmem_limit_bytes=megabytes * 1024 * 1024),
        cost_estimate=pl.CostEstimate(
            flops=int(cost.get(name, 0.1) * 1e9), bytes_accessed=1000, transcendentals=0
        ),
        name=name,
    )
    return run


def shape(dims, kind=bf16):
    return jax.ShapeDtypeStruct(dims, kind)


class Sizes:
    def __init__(self, groups, experts, tokens, width):
        self.experts = experts
        self.split = groups // experts
        self.tokens = tokens
        self.width = width
        self.main = tokens // experts
        self.cap = self.main + 1
        self.pieces = width // fold
        self.wide = width + fold
        self.rows = tokens + 16
        self.order = [*range(experts - 1, 1, -1), 0, 1]
        assert self.main == 16 and self.pieces <= 14 and width % fold == 0
        assert experts <= 8 and experts & (experts - 1) == 0 and self.split & (self.split - 1) == 0


def pack_last(row, tile, first=0):
    for i in range(row.shape[1] // fold):
        tile[first + i : first + i + 1, :] = row[:, i * fold : (i + 1) * fold]


def unpack_last(chunk, z, tile, target, at, base=0):
    tile[...] = chunk[base : base + 16, z.width :].astype(f32)
    for i in range(z.pieces):
        target[at : at + 1, i * fold : (i + 1) * fold] = tile[i : i + 1, :]


def slot_matrices(ids_row, block, z):
    tokens = z.tokens
    sub = lax.broadcasted_iota(jnp.int32, (tokens, tokens), 0)
    lane = lax.broadcasted_iota(jnp.int32, (tokens, tokens), 1)
    row = jnp.bitwise_xor(ids_row, block)
    column = jnp.sum(jnp.where(sub == lane, row, 0), axis=1, keepdims=True)
    same = column == row
    place_row = jnp.sum(jnp.where(same & (sub < lane), 1, 0), axis=0, keepdims=True)
    place_column = jnp.sum(jnp.where(same & (lane < sub), 1, 0), axis=1, keepdims=True)

    def slot(expert, place):
        return jnp.where(place < z.main, expert * z.main + place, tokens + expert)

    slot_row = slot(row, place_row)
    slot_column = slot(column, place_column)
    by_slot = lax.broadcasted_iota(jnp.int32, (z.rows, tokens), 0) == slot_row
    lane = lax.broadcasted_iota(jnp.int32, (tokens, fold), 1)
    by_token = jnp.where(lane < tokens, lane, tokens + (lane - tokens) // 16) == slot_column
    token = lax.broadcasted_iota(jnp.int32, (tokens, fold), 0).astype(f32)
    token_row = jnp.sum(jnp.where(by_token, token - none, 0.0), axis=0, keepdims=True) + none
    return jnp.where(by_slot, 1.0, 0.0).astype(bf16), token_row


def write_chunks(z, selector, token_row, rows_ref, ready, tiles, chunks, base):
    step = z.width // 2
    tiles[...] = jnp.zeros_like(tiles)
    for half in range(2):
        if ready:
            ready[half].wait()
        col = half * step
        got = jnp.dot(selector, rows_ref[:, col : col + step], preferred_element_type=f32)
        packed = got[: z.tokens].astype(bf16)
        for k in range(z.experts):
            chunks[k][base : base + 16, col : col + step] = packed[k * z.main : (k + 1) * z.main]
            pack_last(got[z.tokens + k : z.tokens + k + 1], tiles.at[k], half * z.pieces // 2)
    for k in range(z.experts):
        tiles[k, z.pieces : z.pieces + 1, :] = token_row
        chunks[k][base : base + 16, z.width :] = tiles[k].astype(bf16)


def forward_chunks(z, where, ids, act, later_ids, later):
    count = len(later)

    def body(where, ids_any, later_ids_any, act_any, *refs):
        later_any, chunks = refs[:count], refs[count : count + z.experts]
        later_refs = refs[count + z.experts : 2 * count + z.experts]
        selector_ref, token_ref, ids, rows, tiles, sems = refs[2 * count + z.experts :]
        step = z.width // 2
        first = [
            pltpu.make_async_copy(source, ids.at[i : i + 1], sems.at[i])
            for i, source in enumerate((ids_any, later_ids_any))
        ]
        ready = [
            pltpu.make_async_copy(
                act_any.at[:, pl.ds(i * step, step)], rows.at[:, pl.ds(i * step, step)], sems.at[2 + i]
            )
            for i in range(2)
        ]
        rest = [
            pltpu.make_async_copy(source, target, sems.at[4 + i])
            for i, (source, target) in enumerate(zip(later_any, later_refs))
        ]
        for copy in first + ready + rest:
            copy.start()
        for copy in first:
            copy.wait()
        selector, token_row = slot_matrices(ids[0:1, :], where[0], z)
        later_selector, later_row = slot_matrices(ids[1:2, :], where[0], z)
        selector_ref[...] = later_selector
        token_ref[...] = jnp.broadcast_to(later_row, token_ref.shape)
        write_chunks(z, selector, token_row, rows, ready, tiles, chunks, 0)
        for copy in rest:
            copy.wait()

    outs = call(
        body,
        "shhh" + "h" * count,
        [shape((z.main, z.wide))] * z.experts
        + [shape(array.shape, array.dtype) for array in later]
        + [shape((z.rows, z.tokens)), shape((8, fold), f32)],
        [
            pltpu.VMEM((2, z.tokens), jnp.int32),
            pltpu.VMEM((z.tokens, z.width), bf16),
            pltpu.VMEM((z.experts, 16, fold), f32),
            pltpu.SemaphoreType.DMA((4 + count,)),
        ],
        8,
        "forward_chunks",
    )(where, ids.reshape(1, z.tokens), later_ids.reshape(1, z.tokens), act, *later)
    return outs[: z.experts], outs[z.experts : z.experts + count], outs[z.experts + count :]


def backward_chunks(z, where, slots, sources, gain, router):
    count = len(sources)

    def body(where, selector, token_ref, *refs):
        sources, (gain_ref, router_ref) = refs[:count], refs[count : count + 2]
        *chunks, vectors, tiles = refs[count + 2 :]
        for j in range(count):
            write_chunks(
                z, selector[...], token_ref[0:1, :], sources[j], None, tiles, chunks, 16 * j
            )
        vectors[...] = jnp.zeros_like(vectors)
        vectors[0:1, :] = gain_ref[...].astype(f32)
        mine = lax.broadcasted_iota(jnp.int32, (z.experts, 1), 0) == where[0]
        table = jnp.where(mine, router_ref[0].astype(f32), 0.0)
        vectors[1:2, :] = jnp.sum(table, axis=0, keepdims=True)

    *chunks, vectors = call(
        body,
        "svv" + "v" * (count + 2),
        [shape((z.main * count, z.wide))] * z.experts + [shape((8, z.width), f32)],
        [pltpu.VMEM((z.experts, 16, fold), f32)],
        8,
        "backward_chunks",
    )(where, *slots, *sources, gain, router)
    return chunks, vectors


def collect_rows(z, chunks, last, tile, base=0):
    last[...] = jnp.zeros_like(last)
    for k in range(z.experts):
        unpack_last(chunks[k], z, tile, last, k, base)


def norm_rows(h, gain):
    inv = lax.rsqrt(jnp.mean(h * h, axis=-1, keepdims=True) + epsilon)
    return (h * inv * gain).astype(bf16), inv


def normed_rows(z, chunks, vectors, after):
    def body(*refs):
        chunks, vectors = refs[: z.experts], refs[z.experts]
        normed_ref, gates_ref, last, tile = refs[z.experts + 1 + len(after) :]
        gain, router = vectors[0:1, :], vectors[1:2, :]
        collect_rows(z, chunks, last, tile)
        for k in range(z.experts + 1):
            h = last[...] if k == z.experts else chunks[k][:, : z.width].astype(f32)
            at = k * z.main
            normed, _ = norm_rows(h, gain)
            normed_ref[at : at + 16, :] = normed
            logits = jnp.sum(normed.astype(f32) * router, axis=-1, keepdims=True)
            gates_ref[at : at + 16, :] = jnp.broadcast_to(jax.nn.sigmoid(logits), (16, 128))

    return call(
        body,
        "v" * (z.experts + 1) + "a" * len(after),
        [shape((z.rows, z.width)), shape((z.rows, 128), f32), shape((16, z.width), f32)],
        [pltpu.VMEM((16, fold), f32)],
        8,
        "normed_rows",
    )(*chunks, vectors, *after)


def grad_rows_of(z, chunks, after):
    def body(*refs):
        chunks, (rows, last, tile) = refs[: z.experts], refs[z.experts + len(after) :]
        for k in range(z.experts):
            rows[k * z.main : (k + 1) * z.main, :] = chunks[k][:16, : z.width]
        collect_rows(z, chunks, last, tile)
        rows[z.tokens :, :] = last[...].astype(bf16)

    return call(
        body,
        "v" * z.experts + "a" * len(after),
        [shape((z.rows, z.width)), shape((16, z.width), f32)],
        [pltpu.VMEM((16, fold), f32)],
        8,
        "grad_rows",
    )(*chunks, *after)


def act_norms(z, chunks, after):
    def body(*refs):
        chunks, (inv_ref, last, tile) = refs[: z.experts], refs[z.experts + len(after) :]
        collect_rows(z, chunks, last, tile, 16)
        for k in range(z.experts + 1):
            h = last[...] if k == z.experts else chunks[k][16:32, : z.width].astype(f32)
            at = k * z.main
            inv = lax.rsqrt(jnp.mean(h * h, axis=-1, keepdims=True) + epsilon)
            inv_ref[at : at + 16, :] = jnp.broadcast_to(inv, (16, 128))

    return call(
        body,
        "v" * z.experts + "a" * len(after),
        [shape((z.rows, 128), f32), shape((16, z.width), f32)],
        [pltpu.VMEM((16, fold), f32)],
        8,
        "act_norms",
    )(*chunks, *after)


def act_gates(z, chunks, last, inv, vectors, after):
    def body(*refs):
        chunks, (last, inv_ref, vectors) = refs[: z.experts], refs[z.experts : z.experts + 3]
        affinity_ref = refs[-1]
        gain, router = vectors[0:1, :], vectors[1:2, :]
        for k in range(z.experts + 1):
            h = last[...] if k == z.experts else chunks[k][16:32, : z.width].astype(f32)
            at = k * z.main
            normed = (h * inv_ref[at : at + 16, 0:1] * gain).astype(bf16).astype(f32)
            logits = jnp.sum(normed * router, axis=-1, keepdims=True)
            affinity_ref[at : at + 16, :] = jnp.broadcast_to(jax.nn.sigmoid(logits), (16, 128))

    return call(
        body,
        "v" * (z.experts + 3) + "a" * len(after),
        shape((z.rows, 128), f32),
        [],
        8,
        "act_gates",
    )(*chunks, last, inv, vectors, *after)


def write_parts(z, values, outs, col):
    values = values.astype(bf16)
    for m in range(z.split):
        outs[m][:, col : col + values.shape[1]] = values[m * z.rows : (m + 1) * z.rows]


def experts_forward(z, rows, w_gate, w_down, after):
    def body(*refs):
        rows, (gate_ref, down_ref), outs = (
            refs[: z.split],
            refs[z.split : z.split + 2],
            refs[z.split + 2 + len(after) :],
        )
        held = jnp.concatenate([part[...] for part in rows], axis=0)
        gate_proj = jnp.dot(held, gate_ref[0], preferred_element_type=f32)
        hidden = jax.nn.silu(gate_proj).astype(bf16)
        step = 512
        for col in range(0, z.width, step):
            part = jnp.dot(hidden, down_ref[0, :, col : col + step], preferred_element_type=f32)
            write_parts(z, part, outs, col)

    return call(
        body,
        "v" * (z.split + 2) + "a" * len(after),
        [shape((z.rows, z.width))] * z.split,
        [],
        16,
        "experts_forward",
    )(*rows, w_gate, w_down, *after)


def saved_rows(z, where, saved, weights, after):
    total, slots, width = z.split * z.rows, saved.shape[2], saved.shape[3]

    def body(where, saved_any, *refs):
        ordered_ref, saved_ref, sem = refs[len(weights) + len(after) :]
        copy = pltpu.make_async_copy(saved_any.at[0, 0], saved_ref, sem)
        copy.start()
        row = lax.broadcasted_iota(jnp.int32, (total, slots), 0)
        slot = lax.broadcasted_iota(jnp.int32, (total, slots), 1)
        m, at = row // z.rows, row % z.rows
        is_main = at < z.tokens
        k = jnp.where(is_main, at // z.main, at - z.tokens)
        p = jnp.where(is_main, at % z.main, z.main)
        source = jnp.bitwise_xor(k, where[0]) * z.split + jnp.bitwise_xor(m, where[1])
        wanted = jnp.where(k < z.experts, source * z.cap + p, -1)
        selector = jnp.where(slot == wanted, 1.0, 0.0).astype(bf16)
        copy.wait()
        ordered_ref[...] = jnp.dot(selector, saved_ref[...], preferred_element_type=f32)

    return call(
        body,
        "sh" + "v" * len(weights) + "a" * len(after),
        shape((total, width), f32),
        [pltpu.VMEM((slots, width), bf16), pltpu.SemaphoreType.DMA],
        8,
        "saved_rows",
    )(where, saved, *weights, *after)


def saved_terms(z, ordered, after):
    def body(ordered_ref, *refs):
        hidden_ref, slope_ref = refs[len(after) :]
        gate_proj = ordered_ref[...]
        sg = jax.nn.sigmoid(gate_proj)
        hidden_ref[...] = (gate_proj * sg).astype(bf16)
        slope_ref[...] = sg * (1.0 + gate_proj * (1.0 - sg))

    return call(
        body,
        "v" + "a" * len(after),
        [shape(ordered.shape), shape(ordered.shape, f32)],
        [],
        8,
        "saved_terms",
    )(ordered, *after)


def turned(z, weights, held, after, name):
    rows, columns = weights.shape[1:]
    step = min(512, rows, columns)

    def body(weights_ref, *refs):
        for at in range(0, rows, step):
            for col in range(0, columns, step):
                block = weights_ref[0, at : at + step, col : col + step]
                refs[-1][col : col + step, at : at + step] = block.T

    return call(
        body, "v" + "v" * len(held) + "a" * len(after), shape((columns, rows)), [], 12, name
    )(weights, *held, *after)


def experts_backward(z, rows, hidden, slope, w_gate, w_down, after):
    def body(*refs):
        rows = refs[: z.split]
        hidden_ref, slope_ref, gate_ref, down_ref = refs[z.split : z.split + 4]
        outs = refs[z.split + 4 + len(after) :]
        held = jnp.concatenate([part[...] for part in rows], axis=0)
        grad_hidden = lax.dot_general(held, down_ref[...], nn, preferred_element_type=f32)
        dots = jnp.sum(grad_hidden * hidden_ref[...].astype(f32), axis=-1, keepdims=True)
        grad_gate = (grad_hidden * slope_ref[...]).astype(bf16)
        step = 512
        for col in range(0, z.width, step):
            part = lax.dot_general(
                grad_gate, gate_ref[:, col : col + step], nn, preferred_element_type=f32
            )
            write_parts(z, part, outs, col)
        write_parts(z, jnp.broadcast_to(dots, (dots.shape[0], 128)), outs, z.width)

    return call(
        body,
        "v" * (z.split + 4) + "a" * len(after),
        [shape((z.rows, z.width + 128))] * z.split,
        [],
        16,
        "experts_backward",
    )(*rows, hidden, slope, w_gate, w_down, *after)


def put_last(z, values, source_chunk, tile, out):
    tile[...] = jnp.zeros_like(tile)
    pack_last(values, tile)
    tokens = source_chunk[:16, z.width :].astype(f32)
    tile[z.pieces : z.pieces + 1, :] = tokens[z.pieces : z.pieces + 1, :]
    out[:, z.width :] = tile[...].astype(bf16)


def finish_forward(z, ks, chunks, last, parts, gates, after):
    count = len(ks)

    def body(*refs):
        chunks, last, parts = refs[:count], refs[count], refs[count + 1 : count + 1 + z.split]
        gates, out, tile = refs[count + 1 + z.split], refs[-2], refs[-1]

        def mixed(at):
            y = parts[0][at : at + 16, :].astype(f32)
            for part in parts[1:]:
                y = y + part[at : at + 16, :].astype(f32)
            return route_scale * (gates[at : at + 16, 0:1] * y)

        tail = last[...] + mixed(z.tokens)
        for i, (k, chunk) in enumerate(zip(ks, chunks)):
            h = chunk[:, : z.width].astype(f32)
            rows = out.at[pl.ds(i * 16, 16)]
            rows[:, : z.width] = (h + mixed(k * z.main)).astype(bf16)
            put_last(z, tail[k : k + 1, :], chunk, tile, rows)

    return call(
        body,
        "v" * (count + z.split + 2) + "a" * len(after),
        shape((count * z.main, z.wide)),
        [pltpu.VMEM((16, fold), f32)],
        8,
        "finish_forward_" + "".join(map(str, ks)),
    )(*[chunks[k] for k in ks], last, *parts, gates, *after)


def lower_chunk(z, double, after):
    def body(double, *refs):
        refs[-1][...] = double[16:32, :]

    places = "v" + "a" * len(after)
    return call(body, places, shape((16, z.wide)), [], 8, "lower_chunk")(double, *after)


def finish_backward(z, order, chunks, lasts, terms, parts, vectors, after):
    def body(*refs):
        e = z.experts
        chunks, (last_grad, last_act, inv_ref, affinity_ref) = refs[:e], refs[e : e + 4]
        parts, vectors = refs[e + 4 : e + 4 + z.split], refs[e + 4 + z.split]
        outs, (tile,) = refs[-1 - e : -1], refs[-1:]
        outs = [outs[order.index(k)] for k in range(e)]
        gain, router = vectors[0:1, :], vectors[1:2, :]

        def finished(h, g, at):
            inv, affinity = inv_ref[at : at + 16, 0:1], affinity_ref[at : at + 16, 0:1]
            rows = parts[0][at : at + 16, : z.width].astype(f32)
            dot = parts[0][at : at + 16, z.width :].astype(f32)
            for part in parts[1:]:
                rows = rows + part[at : at + 16, : z.width].astype(f32)
                dot = dot + part[at : at + 16, z.width :].astype(f32)
            dot = dot[:, 0:1]
            grad_logits = (route_scale * dot * affinity * (1.0 - affinity)).astype(bf16).astype(f32)
            grad_pre = (route_scale * affinity * rows + grad_logits * router) * gain
            centre = jnp.mean(grad_pre * h, axis=-1, keepdims=True)
            return g + inv * (grad_pre - h * (inv * inv * centre))

        tail = finished(last_act[...], last_grad[...], z.tokens)
        for k in range(e):
            g = chunks[k][:16, : z.width].astype(f32)
            h = chunks[k][16:32, : z.width].astype(f32)
            outs[k][:, : z.width] = finished(h, g, k * z.main).astype(bf16)
            put_last(z, tail[k : k + 1, :], chunks[k], tile, outs[k])

    return call(
        body,
        "v" * (z.experts + z.split + 5) + "a" * len(after),
        [shape((z.main, z.wide))] * z.experts,
        [pltpu.VMEM((16, fold), f32)],
        8,
        "finish_backward",
    )(*chunks, *lasts, *terms, *parts, vectors, *after)


def ordered_columns(z, chunks):
    lanes = z.tokens + 16 * z.experts
    some = next(iter(chunks))
    filled = [chunks.get(k, chunks[some]) for k in range(z.experts)]
    tiles = [chunk[:16, z.width :] for chunk in filled]
    token_row = tiles[some].astype(f32)[z.pieces : z.pieces + 1, :lanes]
    token = lax.broadcasted_iota(jnp.int32, (z.tokens, lanes), 0).astype(f32)
    lane = lax.broadcasted_iota(jnp.int32, (z.tokens, lanes), 1)
    piece = jnp.where(lane < z.tokens, -1, lane % 16)
    ours = token == token_row
    if len(chunks) < z.experts:
        held = [lane // 16 % z.experts == k for k in chunks]
        ours = ours & functools.reduce(jnp.logical_or, held)
    for i in range(z.pieces):
        cols = pl.ds(i * fold, fold)
        selector = jnp.where(ours & ((piece < 0) | (piece == i)), 1.0, 0.0).astype(bf16)
        rows = jnp.concatenate([chunk[:16, cols] for chunk in filled] + tiles, axis=0)
        yield cols, jnp.dot(selector, rows, preferred_element_type=f32)


def some_rows(z, chunks, after, name):
    ks = list(chunks)

    def body(*refs):
        for cols, rows in ordered_columns(z, dict(zip(ks, refs))):
            refs[-1][:, cols] = rows.astype(bf16)

    places = "v" * len(ks) + "a" * len(after)
    return call(body, places, shape((z.tokens, z.width)), [], 8, name)(*chunks.values(), *after)


def order_rows(z, outputs, name):
    steps = 7 if z.pieces % 7 == 0 else z.pieces
    arrays, layout = [], []
    for chunks, others in outputs:
        layout.append((len(arrays), list(chunks), len(others)))
        arrays += [*chunks.values(), *others]
    number = len(outputs)

    def body(*refs):
        inputs, anys = refs[: len(arrays)], refs[len(arrays) : len(arrays) + number]
        outs, sems = refs[-1 - number : -1], refs[-1]
        copies = []
        for n, (at, ks, more) in enumerate(layout):
            chunks = dict(zip(ks, inputs[at : at + len(ks)]))
            others = inputs[at + len(ks) : at + len(ks) + more]
            for i, (cols, rows) in enumerate(ordered_columns(z, chunks)):
                for other in others:
                    rows = rows + other[:, cols].astype(f32)
                outs[n][:, cols] = rows.astype(bf16)
                if (i + 1) % (z.pieces // steps) == 0:
                    width = z.width // steps
                    done = pl.ds((i + 1) * fold - width, width)
                    copy = pltpu.make_async_copy(
                        outs[n].at[:, done], anys[n].at[:, done], sems.at[len(copies)]
                    )
                    copy.start()
                    copies.append(copy)
        for copy in copies:
            copy.wait()

    return call(
        body,
        "v" * len(arrays),
        [shape((z.tokens, z.width))] * number,
        [pltpu.VMEM((z.tokens, z.width), bf16)] * number
        + [pltpu.SemaphoreType.DMA((number * steps,))],
        8,
        name,
        [spaces["a"]] * number,
    )(*arrays)


def permute_blocks(z, arrays, k):
    groups = z.experts * z.split
    pairs = [(i, ((i // z.split) ^ k) * z.split + i % z.split) for i in range(groups)]
    return [lax.ppermute(array, "ep", pairs) for array in arrays]


def dispatch(z, chunks):
    return [chunks[0]] + [permute_blocks(z, [chunks[k]], k)[0] for k in range(1, z.experts)]


def to_core(z, array, m):
    groups = z.experts * z.split
    pairs = [(i, i // z.split * z.split + ((i % z.split) ^ m)) for i in range(groups)]
    return lax.ppermute(array, "ep", pairs)


def to_section(z, chunk, k, by):
    groups = z.experts * z.split
    sections = lax.axis_size("pp")
    pairs = [
        (s * groups + i, (s + by) % sections * groups + ((i // z.split) ^ k) * z.split + i % z.split)
        for s in range(sections)
        for i in range(groups)
    ]
    return lax.ppermute(chunk, ("pp", "ep"), pairs)


def on_device(
    fwd_act, fwd_ids, bwd_act, bwd_ids, bwd_grad, norm_gain, router, w_gate, w_down, saved_gate
):
    groups = lax.axis_size("ep")
    assert fwd_ids.shape[1] == 1
    z = Sizes(groups, router.shape[2], fwd_act.shape[0], fwd_act.shape[1])
    index = lax.axis_index("ep")
    where = jnp.stack([index // z.split, index % z.split]).astype(jnp.int32)
    router = jnp.swapaxes(router, 1, 2)
    others = range(1, z.split)

    fwd_chunks, (grad, act, gain_row, table), slots = forward_chunks(
        z, where, fwd_ids, fwd_act, bwd_ids, [bwd_grad, bwd_act, norm_gain, router]
    )
    fwd_own = dispatch(z, fwd_chunks)
    bwd_chunks, vectors = backward_chunks(z, where, slots, [grad, act], gain_row, table)
    bwd_own = dispatch(z, bwd_chunks)

    down_turned = turned(z, w_down, [w_gate], [bwd_chunks[0], fwd_own[1]], "turned_down")
    normed, gates, fwd_last = normed_rows(z, fwd_own, vectors, [down_turned])
    fwd_all = [normed] + [to_core(z, normed, m) for m in others]
    ordered = saved_rows(z, where, saved_gate, [], [gates])
    fwd_parts = experts_forward(z, fwd_all, w_gate, w_down, [ordered])
    hidden, slope = saved_terms(z, ordered, [fwd_parts[0]])
    gate_turned = turned(z, w_gate, [], [hidden], "turned_gate")
    fwd_parts = [fwd_parts[0]] + [to_core(z, fwd_parts[m], m) for m in others]

    assert z.experts == 4

    def finish(ks, after):
        return finish_forward(z, ks, fwd_own, fwd_last, fwd_parts, gates, after)

    double = finish([0, 1], [gate_turned])
    got = to_section(z, double, 0, 1)
    out2 = finish([2], [hidden, double])
    got2 = to_section(z, out2, 2, 1)
    grads, grad_last = grad_rows_of(z, bwd_own, [out2])
    grad_all = [grads] + [to_core(z, grads, m) for m in others]
    inv, act_last = act_norms(z, bwd_own, [grads])
    out3 = finish([3], [inv])
    got3 = to_section(z, out3, 3, 1)
    bwd_parts = experts_backward(z, grad_all, hidden, slope, gate_turned, down_turned, [inv])
    affinity = act_gates(z, bwd_own, act_last, inv, vectors, [bwd_parts[0]])
    fwd_done = [got2, got3]
    bwd_parts = [bwd_parts[0]] + [to_core(z, bwd_parts[m], m) for m in others]
    order = [z.order[-1], *z.order[:-1]]
    bwd_out = finish_backward(
        z, order, bwd_own, [grad_last, act_last], [inv, affinity], bwd_parts, vectors, []
    )
    (relayed,) = permute_blocks(z, [lower_chunk(z, got, [bwd_out[0]])], 1)
    bwd_done = {k: to_section(z, out, k, -1) for k, out in zip(order, bwd_out)}

    early = some_rows(z, {0: got, 2: got2, 3: got3}, [], "forward_rows_early")
    outputs = [({1: relayed}, [early]), ({k: bwd_done[k] for k in z.order}, [])]
    fwd_next, bwd_next = order_rows(z, outputs, "all_rows")
    return (fwd_next, bwd_next)


def solution(mesh):
    return jax.shard_map(
        on_device,
        mesh=mesh,
        in_specs=(
            P(("pp", "ep"), None),
            P(("pp", "ep"), None),
            P(("pp", "ep"), None),
            P(("pp", "ep"), None),
            P(("pp", "ep"), None),
            P("pp", None),
            P("pp", None, None),
            P(("pp", "ep"), None, None),
            P(("pp", "ep"), None, None),
            P("pp", "ep", None, None),
        ),
        out_specs=(P(("pp", "ep"), None), P(("pp", "ep"), None)),
        check_vma=False,
    )
```

```python
import functools

import jax
import jax.numpy as jnp
from jax import lax
from jax.experimental import pallas as pl
from jax.experimental.pallas import tpu as pltpu
from jax.sharding import PartitionSpec as P

epsilon = 1e-06
route_scale = 2.5
fold = 256
none = 255.0
f32 = jnp.float32
bf16 = jnp.bfloat16
nn = (((1,), (0,)), ((), ()))
spaces = {
    "s": pl.BlockSpec(memory_space=pltpu.SMEM),
    "v": pl.BlockSpec(memory_space=pltpu.VMEM),
    "a": pl.BlockSpec(memory_space=pl.ANY),
    "h": pl.BlockSpec(memory_space=pltpu.HBM),
}


cost = {
    "backward_chunks": 10,
    "saved_rows": 15,
    "saved_terms": 15,
    "act_norms": 15,
    "act_gates": 15,
    "forward_rows_early": 15,
}


def call(body, places, outs, scratch, megabytes, name, out_specs=None):
    def run(*arrays):
        arrays = [
            pltpu.with_memory_space_constraint(array, pltpu.HBM) if place == "h" else array
            for array, place in zip(arrays, places, strict=True)
        ]
        return kernel(*arrays)

    where_to = {} if out_specs is None else {"out_specs": out_specs}
    kernel = pl.pallas_call(
        body,
        out_shape=outs,
        in_specs=[spaces[place] for place in places],
        **where_to,
        scratch_shapes=scratch,
        compiler_params=pltpu.CompilerParams(vmem_limit_bytes=megabytes * 1024 * 1024),
        cost_estimate=pl.CostEstimate(
            flops=int(cost.get(name, 0.1) * 1e9), bytes_accessed=1000, transcendentals=0
        ),
        name=name,
    )
    return run


def shape(dims, kind=bf16):
    return jax.ShapeDtypeStruct(dims, kind)


class Sizes:
    def __init__(self, groups, experts, tokens, width):
        self.experts = experts
        self.split = groups // experts
        self.tokens = tokens
        self.width = width
        self.main = tokens // experts
        self.cap = self.main + 1
        self.pieces = width // fold
        self.wide = width + fold
        self.rows = tokens + 16
        self.order = [experts - 1, *range(1, experts - 1), 0]
        assert self.main == 16 and self.pieces <= 14 and width % fold == 0
        assert experts <= 8 and experts & (experts - 1) == 0 and self.split & (self.split - 1) == 0


def pack_last(row, tile, first=0):
    for i in range(row.shape[1] // fold):
        tile[first + i : first + i + 1, :] = row[:, i * fold : (i + 1) * fold]


def unpack_last(chunk, z, tile, target, at, base=0):
    tile[...] = chunk[base : base + 16, z.width :].astype(f32)
    for i in range(z.pieces):
        target[at : at + 1, i * fold : (i + 1) * fold] = tile[i : i + 1, :]


def slot_matrices(ids_row, block, z):
    tokens = z.tokens
    sub = lax.broadcasted_iota(jnp.int32, (tokens, tokens), 0)
    lane = lax.broadcasted_iota(jnp.int32, (tokens, tokens), 1)
    row = jnp.bitwise_xor(ids_row, block)
    column = jnp.sum(jnp.where(sub == lane, row, 0), axis=1, keepdims=True)
    same = column == row
    place_row = jnp.sum(jnp.where(same & (sub < lane), 1, 0), axis=0, keepdims=True)
    place_column = jnp.sum(jnp.where(same & (lane < sub), 1, 0), axis=1, keepdims=True)

    def slot(expert, place):
        return jnp.where(place < z.main, expert * z.main + place, tokens + expert)

    slot_row = slot(row, place_row)
    slot_column = slot(column, place_column)
    by_slot = lax.broadcasted_iota(jnp.int32, (z.rows, tokens), 0) == slot_row
    lane = lax.broadcasted_iota(jnp.int32, (tokens, fold), 1)
    by_token = jnp.where(lane < tokens, lane, tokens + (lane - tokens) // 16) == slot_column
    token = lax.broadcasted_iota(jnp.int32, (tokens, fold), 0).astype(f32)
    token_row = jnp.sum(jnp.where(by_token, token - none, 0.0), axis=0, keepdims=True) + none
    return jnp.where(by_slot, 1.0, 0.0).astype(bf16), token_row


def write_chunks(z, selector, token_row, rows_ref, ready, tiles, chunks, base):
    step = z.width // 2
    tiles[...] = jnp.zeros_like(tiles)
    for half in range(2):
        if ready:
            ready[half].wait()
        col = half * step
        got = jnp.dot(selector, rows_ref[:, col : col + step], preferred_element_type=f32)
        packed = got[: z.tokens].astype(bf16)
        for k in range(z.experts):
            chunks[k][base : base + 16, col : col + step] = packed[k * z.main : (k + 1) * z.main]
            pack_last(got[z.tokens + k : z.tokens + k + 1], tiles.at[k], half * z.pieces // 2)
    for k in range(z.experts):
        tiles[k, z.pieces : z.pieces + 1, :] = token_row
        chunks[k][base : base + 16, z.width :] = tiles[k].astype(bf16)


def forward_chunks(z, where, ids, act, later_ids, later):
    count = len(later)

    def body(where, ids_any, later_ids_any, act_any, *refs):
        later_any, chunks = refs[:count], refs[count : count + z.experts]
        later_refs = refs[count + z.experts : 2 * count + z.experts]
        selector_ref, token_ref, ids, rows, tiles, sems = refs[2 * count + z.experts :]
        step = z.width // 2
        first = [
            pltpu.make_async_copy(source, ids.at[i : i + 1], sems.at[i])
            for i, source in enumerate((ids_any, later_ids_any))
        ]
        ready = [
            pltpu.make_async_copy(
                act_any.at[:, pl.ds(i * step, step)], rows.at[:, pl.ds(i * step, step)], sems.at[2 + i]
            )
            for i in range(2)
        ]
        rest = [
            pltpu.make_async_copy(source, target, sems.at[4 + i])
            for i, (source, target) in enumerate(zip(later_any, later_refs))
        ]
        for copy in first + ready + rest:
            copy.start()
        for copy in first:
            copy.wait()
        selector, token_row = slot_matrices(ids[0:1, :], where[0], z)
        later_selector, later_row = slot_matrices(ids[1:2, :], where[0], z)
        selector_ref[...] = later_selector
        token_ref[...] = jnp.broadcast_to(later_row, token_ref.shape)
        write_chunks(z, selector, token_row, rows, ready, tiles, chunks, 0)
        for copy in rest:
            copy.wait()

    outs = call(
        body,
        "shhh" + "h" * count,
        [shape((z.main, z.wide))] * z.experts
        + [shape(array.shape, array.dtype) for array in later]
        + [shape((z.rows, z.tokens)), shape((8, fold), f32)],
        [
            pltpu.VMEM((2, z.tokens), jnp.int32),
            pltpu.VMEM((z.tokens, z.width), bf16),
            pltpu.VMEM((z.experts, 16, fold), f32),
            pltpu.SemaphoreType.DMA((4 + count,)),
        ],
        8,
        "forward_chunks",
    )(where, ids.reshape(1, z.tokens), later_ids.reshape(1, z.tokens), act, *later)
    return outs[: z.experts], outs[z.experts : z.experts + count], outs[z.experts + count :]


def backward_chunks(z, where, slots, sources, gain, router):
    count = len(sources)

    def body(where, selector, token_ref, *refs):
        sources, (gain_ref, router_ref) = refs[:count], refs[count : count + 2]
        *chunks, vectors, tiles = refs[count + 2 :]
        for j in range(count):
            write_chunks(
                z, selector[...], token_ref[0:1, :], sources[j], None, tiles, chunks, 16 * j
            )
        vectors[...] = jnp.zeros_like(vectors)
        vectors[0:1, :] = gain_ref[...].astype(f32)
        mine = lax.broadcasted_iota(jnp.int32, (z.experts, 1), 0) == where[0]
        table = jnp.where(mine, router_ref[0].astype(f32), 0.0)
        vectors[1:2, :] = jnp.sum(table, axis=0, keepdims=True)

    *chunks, vectors = call(
        body,
        "svv" + "v" * (count + 2),
        [shape((z.main * count, z.wide))] * z.experts + [shape((8, z.width), f32)],
        [pltpu.VMEM((z.experts, 16, fold), f32)],
        8,
        "backward_chunks",
    )(where, *slots, *sources, gain, router)
    return chunks, vectors


def collect_rows(z, chunks, last, tile, base=0):
    last[...] = jnp.zeros_like(last)
    for k in range(z.experts):
        unpack_last(chunks[k], z, tile, last, k, base)


def norm_rows(h, gain):
    inv = lax.rsqrt(jnp.mean(h * h, axis=-1, keepdims=True) + epsilon)
    return (h * inv * gain).astype(bf16), inv


def normed_rows(z, chunks, vectors, after):
    def body(*refs):
        chunks, vectors = refs[: z.experts], refs[z.experts]
        normed_ref, gates_ref, last, tile = refs[z.experts + 1 + len(after) :]
        gain, router = vectors[0:1, :], vectors[1:2, :]
        collect_rows(z, chunks, last, tile)
        for k in range(z.experts + 1):
            h = last[...] if k == z.experts else chunks[k][:, : z.width].astype(f32)
            at = k * z.main
            normed, _ = norm_rows(h, gain)
            normed_ref[at : at + 16, :] = normed
            logits = jnp.sum(normed.astype(f32) * router, axis=-1, keepdims=True)
            gates_ref[at : at + 16, :] = jnp.broadcast_to(jax.nn.sigmoid(logits), (16, 128))

    return call(
        body,
        "v" * (z.experts + 1) + "a" * len(after),
        [shape((z.rows, z.width)), shape((z.rows, 128), f32), shape((16, z.width), f32)],
        [pltpu.VMEM((16, fold), f32)],
        8,
        "normed_rows",
    )(*chunks, vectors, *after)


def grad_rows_of(z, chunks, after):
    def body(*refs):
        chunks, (rows, last, tile) = refs[: z.experts], refs[z.experts + len(after) :]
        for k in range(z.experts):
            rows[k * z.main : (k + 1) * z.main, :] = chunks[k][:16, : z.width]
        collect_rows(z, chunks, last, tile)
        rows[z.tokens :, :] = last[...].astype(bf16)

    return call(
        body,
        "v" * z.experts + "a" * len(after),
        [shape((z.rows, z.width)), shape((16, z.width), f32)],
        [pltpu.VMEM((16, fold), f32)],
        8,
        "grad_rows",
    )(*chunks, *after)


def act_norms(z, chunks, after):
    def body(*refs):
        chunks, (inv_ref, last, tile) = refs[: z.experts], refs[z.experts + len(after) :]
        collect_rows(z, chunks, last, tile, 16)
        for k in range(z.experts + 1):
            h = last[...] if k == z.experts else chunks[k][16:32, : z.width].astype(f32)
            at = k * z.main
            inv = lax.rsqrt(jnp.mean(h * h, axis=-1, keepdims=True) + epsilon)
            inv_ref[at : at + 16, :] = jnp.broadcast_to(inv, (16, 128))

    return call(
        body,
        "v" * z.experts + "a" * len(after),
        [shape((z.rows, 128), f32), shape((16, z.width), f32)],
        [pltpu.VMEM((16, fold), f32)],
        8,
        "act_norms",
    )(*chunks, *after)


def act_gates(z, chunks, last, inv, vectors, after):
    def body(*refs):
        chunks, (last, inv_ref, vectors) = refs[: z.experts], refs[z.experts : z.experts + 3]
        affinity_ref = refs[-1]
        gain, router = vectors[0:1, :], vectors[1:2, :]
        for k in range(z.experts + 1):
            h = last[...] if k == z.experts else chunks[k][16:32, : z.width].astype(f32)
            at = k * z.main
            normed = (h * inv_ref[at : at + 16, 0:1] * gain).astype(bf16).astype(f32)
            logits = jnp.sum(normed * router, axis=-1, keepdims=True)
            affinity_ref[at : at + 16, :] = jnp.broadcast_to(jax.nn.sigmoid(logits), (16, 128))

    return call(
        body,
        "v" * (z.experts + 3) + "a" * len(after),
        shape((z.rows, 128), f32),
        [],
        8,
        "act_gates",
    )(*chunks, last, inv, vectors, *after)


def write_parts(z, values, outs, col):
    values = values.astype(bf16)
    for m in range(z.split):
        outs[m][:, col : col + values.shape[1]] = values[m * z.rows : (m + 1) * z.rows]


def experts_forward(z, rows, w_gate, w_down, after):
    def body(*refs):
        rows, (gate_ref, down_ref), outs = (
            refs[: z.split],
            refs[z.split : z.split + 2],
            refs[z.split + 2 + len(after) :],
        )
        held = jnp.concatenate([part[...] for part in rows], axis=0)
        gate_proj = jnp.dot(held, gate_ref[0], preferred_element_type=f32)
        hidden = jax.nn.silu(gate_proj).astype(bf16)
        step = 512
        for col in range(0, z.width, step):
            part = jnp.dot(hidden, down_ref[0, :, col : col + step], preferred_element_type=f32)
            write_parts(z, part, outs, col)

    return call(
        body,
        "v" * (z.split + 2) + "a" * len(after),
        [shape((z.rows, z.width))] * z.split,
        [],
        16,
        "experts_forward",
    )(*rows, w_gate, w_down, *after)


def saved_rows(z, where, saved, weights, after):
    total, slots, width = z.split * z.rows, saved.shape[2], saved.shape[3]

    def body(where, saved_any, *refs):
        ordered_ref, saved_ref, sem = refs[len(weights) + len(after) :]
        copy = pltpu.make_async_copy(saved_any.at[0, 0], saved_ref, sem)
        copy.start()
        row = lax.broadcasted_iota(jnp.int32, (total, slots), 0)
        slot = lax.broadcasted_iota(jnp.int32, (total, slots), 1)
        m, at = row // z.rows, row % z.rows
        is_main = at < z.tokens
        k = jnp.where(is_main, at // z.main, at - z.tokens)
        p = jnp.where(is_main, at % z.main, z.main)
        source = jnp.bitwise_xor(k, where[0]) * z.split + jnp.bitwise_xor(m, where[1])
        wanted = jnp.where(k < z.experts, source * z.cap + p, -1)
        selector = jnp.where(slot == wanted, 1.0, 0.0).astype(bf16)
        copy.wait()
        ordered_ref[...] = jnp.dot(selector, saved_ref[...], preferred_element_type=f32)

    return call(
        body,
        "sh" + "v" * len(weights) + "a" * len(after),
        shape((total, width), f32),
        [pltpu.VMEM((slots, width), bf16), pltpu.SemaphoreType.DMA],
        8,
        "saved_rows",
    )(where, saved, *weights, *after)


def saved_terms(z, ordered, after):
    def body(ordered_ref, *refs):
        hidden_ref, slope_ref = refs[len(after) :]
        gate_proj = ordered_ref[...]
        sg = jax.nn.sigmoid(gate_proj)
        hidden_ref[...] = (gate_proj * sg).astype(bf16)
        slope_ref[...] = sg * (1.0 + gate_proj * (1.0 - sg))

    return call(
        body,
        "v" + "a" * len(after),
        [shape(ordered.shape), shape(ordered.shape, f32)],
        [],
        8,
        "saved_terms",
    )(ordered, *after)


def turned(z, weights, held, after, name):
    rows, columns = weights.shape[1:]
    step = min(512, rows, columns)

    def body(weights_ref, *refs):
        for at in range(0, rows, step):
            for col in range(0, columns, step):
                block = weights_ref[0, at : at + step, col : col + step]
                refs[-1][col : col + step, at : at + step] = block.T

    return call(
        body, "v" + "v" * len(held) + "a" * len(after), shape((columns, rows)), [], 12, name
    )(weights, *held, *after)


def experts_backward(z, rows, hidden, slope, w_gate, w_down, after):
    def body(*refs):
        rows = refs[: z.split]
        hidden_ref, slope_ref, gate_ref, down_ref = refs[z.split : z.split + 4]
        outs = refs[z.split + 4 + len(after) :]
        held = jnp.concatenate([part[...] for part in rows], axis=0)
        grad_hidden = lax.dot_general(held, down_ref[...], nn, preferred_element_type=f32)
        dots = jnp.sum(grad_hidden * hidden_ref[...].astype(f32), axis=-1, keepdims=True)
        grad_gate = (grad_hidden * slope_ref[...]).astype(bf16)
        step = 512
        for col in range(0, z.width, step):
            part = lax.dot_general(
                grad_gate, gate_ref[:, col : col + step], nn, preferred_element_type=f32
            )
            write_parts(z, part, outs, col)
        write_parts(z, jnp.broadcast_to(dots, (dots.shape[0], 128)), outs, z.width)

    return call(
        body,
        "v" * (z.split + 4) + "a" * len(after),
        [shape((z.rows, z.width + 128))] * z.split,
        [],
        16,
        "experts_backward",
    )(*rows, hidden, slope, w_gate, w_down, *after)


def put_last(z, values, source_chunk, tile, out):
    tile[...] = jnp.zeros_like(tile)
    pack_last(values, tile)
    tokens = source_chunk[:16, z.width :].astype(f32)
    tile[z.pieces : z.pieces + 1, :] = tokens[z.pieces : z.pieces + 1, :]
    out[:, z.width :] = tile[...].astype(bf16)


def finish_forward(z, ks, chunks, last, parts, gates, after):
    count = len(ks)

    def body(*refs):
        chunks, last, parts = refs[:count], refs[count], refs[count + 1 : count + 1 + z.split]
        gates, out, tile = refs[count + 1 + z.split], refs[-2], refs[-1]

        def mixed(at):
            y = parts[0][at : at + 16, :].astype(f32)
            for part in parts[1:]:
                y = y + part[at : at + 16, :].astype(f32)
            return route_scale * (gates[at : at + 16, 0:1] * y)

        tail = last[...] + mixed(z.tokens)
        for i, (k, chunk) in enumerate(zip(ks, chunks)):
            h = chunk[:, : z.width].astype(f32)
            rows = out.at[pl.ds(i * 16, 16)]
            rows[:, : z.width] = (h + mixed(k * z.main)).astype(bf16)
            put_last(z, tail[k : k + 1, :], chunk, tile, rows)

    return call(
        body,
        "v" * (count + z.split + 2) + "a" * len(after),
        shape((count * z.main, z.wide)),
        [pltpu.VMEM((16, fold), f32)],
        8,
        "finish_forward_" + "".join(map(str, ks)),
    )(*[chunks[k] for k in ks], last, *parts, gates, *after)


def lower_chunk(z, double, after):
    def body(double, *refs):
        refs[-1][...] = double[16:32, :]

    places = "v" + "a" * len(after)
    return call(body, places, shape((16, z.wide)), [], 8, "lower_chunk")(double, *after)


def finish_backward(z, order, chunks, lasts, terms, parts, vectors, after):
    def body(*refs):
        e = z.experts
        chunks, (last_grad, last_act, inv_ref, affinity_ref) = refs[:e], refs[e : e + 4]
        parts, vectors = refs[e + 4 : e + 4 + z.split], refs[e + 4 + z.split]
        outs, (tile,) = refs[-1 - e : -1], refs[-1:]
        outs = [outs[order.index(k)] for k in range(e)]
        gain, router = vectors[0:1, :], vectors[1:2, :]

        def finished(h, g, at):
            inv, affinity = inv_ref[at : at + 16, 0:1], affinity_ref[at : at + 16, 0:1]
            rows = parts[0][at : at + 16, : z.width].astype(f32)
            dot = parts[0][at : at + 16, z.width :].astype(f32)
            for part in parts[1:]:
                rows = rows + part[at : at + 16, : z.width].astype(f32)
                dot = dot + part[at : at + 16, z.width :].astype(f32)
            dot = dot[:, 0:1]
            grad_logits = (route_scale * dot * affinity * (1.0 - affinity)).astype(bf16).astype(f32)
            grad_pre = (route_scale * affinity * rows + grad_logits * router) * gain
            centre = jnp.mean(grad_pre * h, axis=-1, keepdims=True)
            return g + inv * (grad_pre - h * (inv * inv * centre))

        tail = finished(last_act[...], last_grad[...], z.tokens)
        for k in range(e):
            g = chunks[k][:16, : z.width].astype(f32)
            h = chunks[k][16:32, : z.width].astype(f32)
            outs[k][:, : z.width] = finished(h, g, k * z.main).astype(bf16)
            put_last(z, tail[k : k + 1, :], chunks[k], tile, outs[k])

    return call(
        body,
        "v" * (z.experts + z.split + 5) + "a" * len(after),
        [shape((z.main, z.wide))] * z.experts,
        [pltpu.VMEM((16, fold), f32)],
        8,
        "finish_backward",
    )(*chunks, *lasts, *terms, *parts, vectors, *after)


def ordered_columns(z, chunks):
    lanes = z.tokens + 16 * z.experts
    some = next(iter(chunks))
    filled = [chunks.get(k, chunks[some]) for k in range(z.experts)]
    tiles = [chunk[:16, z.width :] for chunk in filled]
    token_row = tiles[some].astype(f32)[z.pieces : z.pieces + 1, :lanes]
    token = lax.broadcasted_iota(jnp.int32, (z.tokens, lanes), 0).astype(f32)
    lane = lax.broadcasted_iota(jnp.int32, (z.tokens, lanes), 1)
    piece = jnp.where(lane < z.tokens, -1, lane % 16)
    ours = token == token_row
    if len(chunks) < z.experts:
        held = [lane // 16 % z.experts == k for k in chunks]
        ours = ours & functools.reduce(jnp.logical_or, held)
    for i in range(z.pieces):
        cols = pl.ds(i * fold, fold)
        selector = jnp.where(ours & ((piece < 0) | (piece == i)), 1.0, 0.0).astype(bf16)
        rows = jnp.concatenate([chunk[:16, cols] for chunk in filled] + tiles, axis=0)
        yield cols, jnp.dot(selector, rows, preferred_element_type=f32)


def some_rows(z, chunks, after, name):
    ks = list(chunks)

    def body(*refs):
        for cols, rows in ordered_columns(z, dict(zip(ks, refs))):
            refs[-1][:, cols] = rows.astype(bf16)

    places = "v" * len(ks) + "a" * len(after)
    return call(body, places, shape((z.tokens, z.width)), [], 8, name)(*chunks.values(), *after)


def order_rows(z, outputs, name):
    steps = 7 if z.pieces % 7 == 0 else z.pieces
    arrays, layout = [], []
    for chunks, others in outputs:
        layout.append((len(arrays), list(chunks), len(others)))
        arrays += [*chunks.values(), *others]
    number = len(outputs)

    def body(*refs):
        inputs, anys = refs[: len(arrays)], refs[len(arrays) : len(arrays) + number]
        outs, sems = refs[-1 - number : -1], refs[-1]
        copies = []
        for n, (at, ks, more) in enumerate(layout):
            chunks = dict(zip(ks, inputs[at : at + len(ks)]))
            others = inputs[at + len(ks) : at + len(ks) + more]
            for i, (cols, rows) in enumerate(ordered_columns(z, chunks)):
                for other in others:
                    rows = rows + other[:, cols].astype(f32)
                outs[n][:, cols] = rows.astype(bf16)
                if (i + 1) % (z.pieces // steps) == 0:
                    width = z.width // steps
                    done = pl.ds((i + 1) * fold - width, width)
                    copy = pltpu.make_async_copy(
                        outs[n].at[:, done], anys[n].at[:, done], sems.at[len(copies)]
                    )
                    copy.start()
                    copies.append(copy)
        for copy in copies:
            copy.wait()

    return call(
        body,
        "v" * len(arrays),
        [shape((z.tokens, z.width))] * number,
        [pltpu.VMEM((z.tokens, z.width), bf16)] * number
        + [pltpu.SemaphoreType.DMA((number * steps,))],
        8,
        name,
        [spaces["a"]] * number,
    )(*arrays)


def permute_blocks(z, arrays, k):
    groups = z.experts * z.split
    pairs = [(i, ((i // z.split) ^ k) * z.split + i % z.split) for i in range(groups)]
    return [lax.ppermute(array, "ep", pairs) for array in arrays]


def dispatch(z, chunks):
    return [chunks[0]] + [permute_blocks(z, [chunks[k]], k)[0] for k in range(1, z.experts)]


def to_core(z, array, m):
    groups = z.experts * z.split
    pairs = [(i, i // z.split * z.split + ((i % z.split) ^ m)) for i in range(groups)]
    return lax.ppermute(array, "ep", pairs)


def to_section(z, chunk, k, by):
    groups = z.experts * z.split
    sections = lax.axis_size("pp")
    pairs = [
        (s * groups + i, (s + by) % sections * groups + ((i // z.split) ^ k) * z.split + i % z.split)
        for s in range(sections)
        for i in range(groups)
    ]
    return lax.ppermute(chunk, ("pp", "ep"), pairs)


def on_device(
    fwd_act, fwd_ids, bwd_act, bwd_ids, bwd_grad, norm_gain, router, w_gate, w_down, saved_gate
):
    groups = lax.axis_size("ep")
    assert fwd_ids.shape[1] == 1
    z = Sizes(groups, router.shape[2], fwd_act.shape[0], fwd_act.shape[1])
    index = lax.axis_index("ep")
    where = jnp.stack([index // z.split, index % z.split]).astype(jnp.int32)
    router = jnp.swapaxes(router, 1, 2)
    others = range(1, z.split)

    fwd_chunks, (grad, act, gain_row, table), slots = forward_chunks(
        z, where, fwd_ids, fwd_act, bwd_ids, [bwd_grad, bwd_act, norm_gain, router]
    )
    fwd_own = dispatch(z, fwd_chunks)
    bwd_chunks, vectors = backward_chunks(z, where, slots, [grad, act], gain_row, table)
    bwd_own = dispatch(z, bwd_chunks)

    down_turned = turned(z, w_down, [w_gate], [bwd_chunks[0], fwd_own[1]], "turned_down")
    normed, gates, fwd_last = normed_rows(z, fwd_own, vectors, [down_turned])
    fwd_all = [normed] + [to_core(z, normed, m) for m in others]
    ordered = saved_rows(z, where, saved_gate, [], [gates])
    fwd_parts = experts_forward(z, fwd_all, w_gate, w_down, [ordered])
    hidden, slope = saved_terms(z, ordered, [fwd_parts[0]])
    gate_turned = turned(z, w_gate, [], [hidden], "turned_gate")
    fwd_parts = [fwd_parts[0]] + [to_core(z, fwd_parts[m], m) for m in others]

    assert z.experts == 4

    def finish(ks, after):
        return finish_forward(z, ks, fwd_own, fwd_last, fwd_parts, gates, after)

    double = finish([0, 1], [gate_turned])
    got = to_section(z, double, 0, 1)
    out2 = finish([2], [hidden, double])
    got2 = to_section(z, out2, 2, 1)
    grads, grad_last = grad_rows_of(z, bwd_own, [out2])
    grad_all = [grads] + [to_core(z, grads, m) for m in others]
    inv, act_last = act_norms(z, bwd_own, [grads])
    out3 = finish([3], [inv])
    got3 = to_section(z, out3, 3, 1)
    bwd_parts = experts_backward(z, grad_all, hidden, slope, gate_turned, down_turned, [inv])
    affinity = act_gates(z, bwd_own, act_last, inv, vectors, [bwd_parts[0]])
    fwd_done = [got2, got3]
    bwd_parts = [bwd_parts[0]] + [to_core(z, bwd_parts[m], m) for m in others]
    order = z.order
    bwd_out = finish_backward(
        z, order, bwd_own, [grad_last, act_last], [inv, affinity], bwd_parts, vectors, []
    )
    (relayed,) = permute_blocks(z, [lower_chunk(z, got, [bwd_out[0]])], 1)
    bwd_done = {k: to_section(z, out, k, -1) for k, out in zip(order, bwd_out)}

    early = some_rows(z, {0: got, 2: got2, 3: got3}, [], "forward_rows_early")
    outputs = [({1: relayed}, [early]), ({k: bwd_done[k] for k in z.order}, [])]
    fwd_next, bwd_next = order_rows(z, outputs, "all_rows")
    return (fwd_next, bwd_next)


def solution(mesh):
    return jax.shard_map(
        on_device,
        mesh=mesh,
        in_specs=(
            P(("pp", "ep"), None),
            P(("pp", "ep"), None),
            P(("pp", "ep"), None),
            P(("pp", "ep"), None),
            P(("pp", "ep"), None),
            P("pp", None),
            P("pp", None, None),
            P(("pp", "ep"), None, None),
            P(("pp", "ep"), None, None),
            P("pp", "ep", None, None),
        ),
        out_specs=(P(("pp", "ep"), None), P(("pp", "ep"), None)),
        check_vma=False,
    )
```

```python
import functools

import jax
import jax.numpy as jnp
from jax import lax
from jax.experimental import pallas as pl
from jax.experimental.pallas import tpu as pltpu
from jax.sharding import PartitionSpec as P

epsilon = 1e-06
route_scale = 2.5
fold = 256
none = 255.0
f32 = jnp.float32
bf16 = jnp.bfloat16
nn = (((1,), (0,)), ((), ()))
spaces = {
    "s": pl.BlockSpec(memory_space=pltpu.SMEM),
    "v": pl.BlockSpec(memory_space=pltpu.VMEM),
    "a": pl.BlockSpec(memory_space=pl.ANY),
    "h": pl.BlockSpec(memory_space=pltpu.HBM),
}


cost = {
    "backward_chunks": 10,
    "saved_rows": 15,
    "saved_terms": 15,
    "act_norms": 15,
    "act_gates": 15,
    "forward_rows_early": 15,
}


def call(body, places, outs, scratch, megabytes, name, out_specs=None):
    def run(*arrays):
        arrays = [
            pltpu.with_memory_space_constraint(array, pltpu.HBM) if place == "h" else array
            for array, place in zip(arrays, places, strict=True)
        ]
        return kernel(*arrays)

    where_to = {} if out_specs is None else {"out_specs": out_specs}
    kernel = pl.pallas_call(
        body,
        out_shape=outs,
        in_specs=[spaces[place] for place in places],
        **where_to,
        scratch_shapes=scratch,
        compiler_params=pltpu.CompilerParams(vmem_limit_bytes=megabytes * 1024 * 1024),
        cost_estimate=pl.CostEstimate(
            flops=int(cost.get(name, 0.1) * 1e9), bytes_accessed=1000, transcendentals=0
        ),
        name=name,
    )
    return run


def shape(dims, kind=bf16):
    return jax.ShapeDtypeStruct(dims, kind)


class Sizes:
    def __init__(self, groups, experts, tokens, width):
        self.experts = experts
        self.split = groups // experts
        self.tokens = tokens
        self.width = width
        self.main = tokens // experts
        self.cap = self.main + 1
        self.pieces = width // fold
        self.wide = width + fold
        self.rows = tokens + 16
        self.order = [experts - 1, *range(1, experts - 1), 0]
        assert self.main == 16 and self.pieces <= 14 and width % fold == 0
        assert experts <= 8 and experts & (experts - 1) == 0 and self.split & (self.split - 1) == 0


def pack_last(row, tile, first=0):
    for i in range(row.shape[1] // fold):
        tile[first + i : first + i + 1, :] = row[:, i * fold : (i + 1) * fold]


def unpack_last(chunk, z, tile, target, at, base=0):
    tile[...] = chunk[base : base + 16, z.width :].astype(f32)
    for i in range(z.pieces):
        target[at : at + 1, i * fold : (i + 1) * fold] = tile[i : i + 1, :]


def slot_matrices(ids_row, block, z):
    tokens = z.tokens
    sub = lax.broadcasted_iota(jnp.int32, (tokens, tokens), 0)
    lane = lax.broadcasted_iota(jnp.int32, (tokens, tokens), 1)
    row = jnp.bitwise_xor(ids_row, block)
    column = jnp.sum(jnp.where(sub == lane, row, 0), axis=1, keepdims=True)
    same = column == row
    place_row = jnp.sum(jnp.where(same & (sub < lane), 1, 0), axis=0, keepdims=True)
    place_column = jnp.sum(jnp.where(same & (lane < sub), 1, 0), axis=1, keepdims=True)

    def slot(expert, place):
        return jnp.where(place < z.main, expert * z.main + place, tokens + expert)

    slot_row = slot(row, place_row)
    slot_column = slot(column, place_column)
    by_slot = lax.broadcasted_iota(jnp.int32, (z.rows, tokens), 0) == slot_row
    lane = lax.broadcasted_iota(jnp.int32, (tokens, fold), 1)
    by_token = jnp.where(lane < tokens, lane, tokens + (lane - tokens) // 16) == slot_column
    token = lax.broadcasted_iota(jnp.int32, (tokens, fold), 0).astype(f32)
    token_row = jnp.sum(jnp.where(by_token, token - none, 0.0), axis=0, keepdims=True) + none
    return jnp.where(by_slot, 1.0, 0.0).astype(bf16), token_row


def write_chunks(z, selector, token_row, rows_ref, ready, tiles, chunks, base):
    step = z.width // 2
    tiles[...] = jnp.zeros_like(tiles)
    for half in range(2):
        if ready:
            ready[half].wait()
        col = half * step
        got = jnp.dot(selector, rows_ref[:, col : col + step], preferred_element_type=f32)
        packed = got[: z.tokens].astype(bf16)
        for k in range(z.experts):
            chunks[k][base : base + 16, col : col + step] = packed[k * z.main : (k + 1) * z.main]
            pack_last(got[z.tokens + k : z.tokens + k + 1], tiles.at[k], half * z.pieces // 2)
    for k in range(z.experts):
        tiles[k, z.pieces : z.pieces + 1, :] = token_row
        chunks[k][base : base + 16, z.width :] = tiles[k].astype(bf16)


def forward_chunks(z, where, ids, act, later_ids, later):
    count = len(later)

    def body(where, ids_any, later_ids_any, act_any, *refs):
        later_any, chunks = refs[:count], refs[count : count + z.experts]
        later_refs = refs[count + z.experts : 2 * count + z.experts]
        selector_ref, token_ref, ids, rows, tiles, sems = refs[2 * count + z.experts :]
        step = z.width // 2
        first = [
            pltpu.make_async_copy(source, ids.at[i : i + 1], sems.at[i])
            for i, source in enumerate((ids_any, later_ids_any))
        ]
        ready = [
            pltpu.make_async_copy(
                act_any.at[:, pl.ds(i * step, step)], rows.at[:, pl.ds(i * step, step)], sems.at[2 + i]
            )
            for i in range(2)
        ]
        rest = [
            pltpu.make_async_copy(source, target, sems.at[4 + i])
            for i, (source, target) in enumerate(zip(later_any, later_refs))
        ]
        for copy in first + ready + rest:
            copy.start()
        for copy in first:
            copy.wait()
        selector, token_row = slot_matrices(ids[0:1, :], where[0], z)
        later_selector, later_row = slot_matrices(ids[1:2, :], where[0], z)
        selector_ref[...] = later_selector
        token_ref[...] = jnp.broadcast_to(later_row, token_ref.shape)
        write_chunks(z, selector, token_row, rows, ready, tiles, chunks, 0)
        for copy in rest:
            copy.wait()

    outs = call(
        body,
        "shhh" + "h" * count,
        [shape((z.main, z.wide))] * z.experts
        + [shape(array.shape, array.dtype) for array in later]
        + [shape((z.rows, z.tokens)), shape((8, fold), f32)],
        [
            pltpu.VMEM((2, z.tokens), jnp.int32),
            pltpu.VMEM((z.tokens, z.width), bf16),
            pltpu.VMEM((z.experts, 16, fold), f32),
            pltpu.SemaphoreType.DMA((4 + count,)),
        ],
        8,
        "forward_chunks",
    )(where, ids.reshape(1, z.tokens), later_ids.reshape(1, z.tokens), act, *later)
    return outs[: z.experts], outs[z.experts : z.experts + count], outs[z.experts + count :]


def backward_chunks(z, where, slots, sources, gain, router):
    count = len(sources)

    def body(where, selector, token_ref, *refs):
        sources, (gain_ref, router_ref) = refs[:count], refs[count : count + 2]
        *chunks, vectors, tiles = refs[count + 2 :]
        for j in range(count):
            write_chunks(
                z, selector[...], token_ref[0:1, :], sources[j], None, tiles, chunks, 16 * j
            )
        vectors[...] = jnp.zeros_like(vectors)
        vectors[0:1, :] = gain_ref[...].astype(f32)
        mine = lax.broadcasted_iota(jnp.int32, (z.experts, 1), 0) == where[0]
        table = jnp.where(mine, router_ref[0].astype(f32), 0.0)
        vectors[1:2, :] = jnp.sum(table, axis=0, keepdims=True)

    *chunks, vectors = call(
        body,
        "svv" + "v" * (count + 2),
        [shape((z.main * count, z.wide))] * z.experts + [shape((8, z.width), f32)],
        [pltpu.VMEM((z.experts, 16, fold), f32)],
        8,
        "backward_chunks",
    )(where, *slots, *sources, gain, router)
    return chunks, vectors


def collect_rows(z, chunks, last, tile, base=0):
    last[...] = jnp.zeros_like(last)
    for k in range(z.experts):
        unpack_last(chunks[k], z, tile, last, k, base)


def norm_rows(h, gain):
    inv = lax.rsqrt(jnp.mean(h * h, axis=-1, keepdims=True) + epsilon)
    return (h * inv * gain).astype(bf16), inv


def normed_rows(z, chunks, vectors, after):
    def body(*refs):
        chunks, vectors = refs[: z.experts], refs[z.experts]
        normed_ref, gates_ref, last, tile = refs[z.experts + 1 + len(after) :]
        gain, router = vectors[0:1, :], vectors[1:2, :]
        collect_rows(z, chunks, last, tile)
        for k in range(z.experts + 1):
            h = last[...] if k == z.experts else chunks[k][:, : z.width].astype(f32)
            at = k * z.main
            normed, _ = norm_rows(h, gain)
            normed_ref[at : at + 16, :] = normed
            logits = jnp.sum(normed.astype(f32) * router, axis=-1, keepdims=True)
            gates_ref[at : at + 16, :] = jnp.broadcast_to(jax.nn.sigmoid(logits), (16, 128))

    return call(
        body,
        "v" * (z.experts + 1) + "a" * len(after),
        [shape((z.rows, z.width)), shape((z.rows, 128), f32), shape((16, z.width), f32)],
        [pltpu.VMEM((16, fold), f32)],
        8,
        "normed_rows",
    )(*chunks, vectors, *after)


def grad_rows_of(z, chunks, after):
    def body(*refs):
        chunks, (rows, last, tile) = refs[: z.experts], refs[z.experts + len(after) :]
        for k in range(z.experts):
            rows[k * z.main : (k + 1) * z.main, :] = chunks[k][:16, : z.width]
        collect_rows(z, chunks, last, tile)
        rows[z.tokens :, :] = last[...].astype(bf16)

    return call(
        body,
        "v" * z.experts + "a" * len(after),
        [shape((z.rows, z.width)), shape((16, z.width), f32)],
        [pltpu.VMEM((16, fold), f32)],
        8,
        "grad_rows",
    )(*chunks, *after)


def act_norms(z, chunks, after):
    def body(*refs):
        chunks, (inv_ref, last, tile) = refs[: z.experts], refs[z.experts + len(after) :]
        collect_rows(z, chunks, last, tile, 16)
        for k in range(z.experts + 1):
            h = last[...] if k == z.experts else chunks[k][16:32, : z.width].astype(f32)
            at = k * z.main
            inv = lax.rsqrt(jnp.mean(h * h, axis=-1, keepdims=True) + epsilon)
            inv_ref[at : at + 16, :] = jnp.broadcast_to(inv, (16, 128))

    return call(
        body,
        "v" * z.experts + "a" * len(after),
        [shape((z.rows, 128), f32), shape((16, z.width), f32)],
        [pltpu.VMEM((16, fold), f32)],
        8,
        "act_norms",
    )(*chunks, *after)


def act_gates(z, chunks, last, inv, vectors, after):
    def body(*refs):
        chunks, (last, inv_ref, vectors) = refs[: z.experts], refs[z.experts : z.experts + 3]
        affinity_ref = refs[-1]
        gain, router = vectors[0:1, :], vectors[1:2, :]
        for k in range(z.experts + 1):
            h = last[...] if k == z.experts else chunks[k][16:32, : z.width].astype(f32)
            at = k * z.main
            normed = (h * inv_ref[at : at + 16, 0:1] * gain).astype(bf16).astype(f32)
            logits = jnp.sum(normed * router, axis=-1, keepdims=True)
            affinity_ref[at : at + 16, :] = jnp.broadcast_to(jax.nn.sigmoid(logits), (16, 128))

    return call(
        body,
        "v" * (z.experts + 3) + "a" * len(after),
        shape((z.rows, 128), f32),
        [],
        8,
        "act_gates",
    )(*chunks, last, inv, vectors, *after)


def write_parts(z, values, outs, col):
    values = values.astype(bf16)
    for m in range(z.split):
        outs[m][:, col : col + values.shape[1]] = values[m * z.rows : (m + 1) * z.rows]


def experts_forward(z, rows, w_gate, w_down, after):
    def body(*refs):
        rows, (gate_ref, down_ref), outs = (
            refs[: z.split],
            refs[z.split : z.split + 2],
            refs[z.split + 2 + len(after) :],
        )
        held = jnp.concatenate([part[...] for part in rows], axis=0)
        gate_proj = jnp.dot(held, gate_ref[0], preferred_element_type=f32)
        hidden = jax.nn.silu(gate_proj).astype(bf16)
        step = 512
        for col in range(0, z.width, step):
            part = jnp.dot(hidden, down_ref[0, :, col : col + step], preferred_element_type=f32)
            write_parts(z, part, outs, col)

    return call(
        body,
        "v" * (z.split + 2) + "a" * len(after),
        [shape((z.rows, z.width))] * z.split,
        [],
        16,
        "experts_forward",
    )(*rows, w_gate, w_down, *after)


def saved_rows(z, where, saved, weights, after):
    total, slots, width = z.split * z.rows, saved.shape[2], saved.shape[3]

    def body(where, saved_any, *refs):
        ordered_ref, saved_ref, sem = refs[len(weights) + len(after) :]
        copy = pltpu.make_async_copy(saved_any.at[0, 0], saved_ref, sem)
        copy.start()
        row = lax.broadcasted_iota(jnp.int32, (total, slots), 0)
        slot = lax.broadcasted_iota(jnp.int32, (total, slots), 1)
        m, at = row // z.rows, row % z.rows
        is_main = at < z.tokens
        k = jnp.where(is_main, at // z.main, at - z.tokens)
        p = jnp.where(is_main, at % z.main, z.main)
        source = jnp.bitwise_xor(k, where[0]) * z.split + jnp.bitwise_xor(m, where[1])
        wanted = jnp.where(k < z.experts, source * z.cap + p, -1)
        selector = jnp.where(slot == wanted, 1.0, 0.0).astype(bf16)
        copy.wait()
        ordered_ref[...] = jnp.dot(selector, saved_ref[...], preferred_element_type=f32)

    return call(
        body,
        "sh" + "v" * len(weights) + "a" * len(after),
        shape((total, width), f32),
        [pltpu.VMEM((slots, width), bf16), pltpu.SemaphoreType.DMA],
        8,
        "saved_rows",
    )(where, saved, *weights, *after)


def saved_terms(z, ordered, after):
    def body(ordered_ref, *refs):
        hidden_ref, slope_ref = refs[len(after) :]
        gate_proj = ordered_ref[...]
        sg = jax.nn.sigmoid(gate_proj)
        hidden_ref[...] = (gate_proj * sg).astype(bf16)
        slope_ref[...] = sg * (1.0 + gate_proj * (1.0 - sg))

    return call(
        body,
        "v" + "a" * len(after),
        [shape(ordered.shape), shape(ordered.shape, f32)],
        [],
        8,
        "saved_terms",
    )(ordered, *after)


def turned(z, weights, held, after, name):
    rows, columns = weights.shape[1:]
    step = min(512, rows, columns)

    def body(weights_ref, *refs):
        for at in range(0, rows, step):
            for col in range(0, columns, step):
                block = weights_ref[0, at : at + step, col : col + step]
                refs[-1][col : col + step, at : at + step] = block.T

    return call(
        body, "v" + "v" * len(held) + "a" * len(after), shape((columns, rows)), [], 12, name
    )(weights, *held, *after)


def experts_backward(z, rows, hidden, slope, w_gate, w_down, after):
    def body(*refs):
        rows = refs[: z.split]
        hidden_ref, slope_ref, gate_ref, down_ref = refs[z.split : z.split + 4]
        outs = refs[z.split + 4 + len(after) :]
        held = jnp.concatenate([part[...] for part in rows], axis=0)
        grad_hidden = lax.dot_general(held, down_ref[...], nn, preferred_element_type=f32)
        dots = jnp.sum(grad_hidden * hidden_ref[...].astype(f32), axis=-1, keepdims=True)
        grad_gate = (grad_hidden * slope_ref[...]).astype(bf16)
        step = 512
        for col in range(0, z.width, step):
            part = lax.dot_general(
                grad_gate, gate_ref[:, col : col + step], nn, preferred_element_type=f32
            )
            write_parts(z, part, outs, col)
        write_parts(z, jnp.broadcast_to(dots, (dots.shape[0], 128)), outs, z.width)

    return call(
        body,
        "v" * (z.split + 4) + "a" * len(after),
        [shape((z.rows, z.width + 128))] * z.split,
        [],
        16,
        "experts_backward",
    )(*rows, hidden, slope, w_gate, w_down, *after)


def put_last(z, values, source_chunk, tile, out):
    tile[...] = jnp.zeros_like(tile)
    pack_last(values, tile)
    tokens = source_chunk[:16, z.width :].astype(f32)
    tile[z.pieces : z.pieces + 1, :] = tokens[z.pieces : z.pieces + 1, :]
    out[:, z.width :] = tile[...].astype(bf16)


def finish_forward(z, ks, chunks, last, parts, gates, after):
    count = len(ks)

    def body(*refs):
        chunks, last, parts = refs[:count], refs[count], refs[count + 1 : count + 1 + z.split]
        gates, out, tile = refs[count + 1 + z.split], refs[-2], refs[-1]

        def mixed(at):
            y = parts[0][at : at + 16, :].astype(f32)
            for part in parts[1:]:
                y = y + part[at : at + 16, :].astype(f32)
            return route_scale * (gates[at : at + 16, 0:1] * y)

        tail = last[...] + mixed(z.tokens)
        for i, (k, chunk) in enumerate(zip(ks, chunks)):
            h = chunk[:, : z.width].astype(f32)
            rows = out.at[pl.ds(i * 16, 16)]
            rows[:, : z.width] = (h + mixed(k * z.main)).astype(bf16)
            put_last(z, tail[k : k + 1, :], chunk, tile, rows)

    return call(
        body,
        "v" * (count + z.split + 2) + "a" * len(after),
        shape((count * z.main, z.wide)),
        [pltpu.VMEM((16, fold), f32)],
        8,
        "finish_forward_" + "".join(map(str, ks)),
    )(*[chunks[k] for k in ks], last, *parts, gates, *after)


def lower_chunk(z, double, after):
    def body(double, *refs):
        refs[-1][...] = double[16:32, :]

    places = "v" + "a" * len(after)
    return call(body, places, shape((16, z.wide)), [], 8, "lower_chunk")(double, *after)


def finish_backward(z, ks, chunks, lasts, terms, parts, vectors, after):
    count = len(ks)

    def body(*refs):
        chunks = refs[:count]
        last_grad, last_act, inv_ref, affinity_ref = refs[count : count + 4]
        parts, vectors = refs[count + 4 : count + 4 + z.split], refs[count + 4 + z.split]
        outs, tile = refs[-1 - count : -1], refs[-1]
        gain, router = vectors[0:1, :], vectors[1:2, :]

        def finished(h, g, at):
            inv, affinity = inv_ref[at : at + 16, 0:1], affinity_ref[at : at + 16, 0:1]
            rows = parts[0][at : at + 16, : z.width].astype(f32)
            dot = parts[0][at : at + 16, z.width :].astype(f32)
            for part in parts[1:]:
                rows = rows + part[at : at + 16, : z.width].astype(f32)
                dot = dot + part[at : at + 16, z.width :].astype(f32)
            dot = dot[:, 0:1]
            grad_logits = (route_scale * dot * affinity * (1.0 - affinity)).astype(bf16).astype(f32)
            grad_pre = (route_scale * affinity * rows + grad_logits * router) * gain
            centre = jnp.mean(grad_pre * h, axis=-1, keepdims=True)
            return g + inv * (grad_pre - h * (inv * inv * centre))

        tail = finished(last_act[...], last_grad[...], z.tokens)
        for k, chunk, out in zip(ks, chunks, outs):
            g = chunk[:16, : z.width].astype(f32)
            h = chunk[16:32, : z.width].astype(f32)
            out[:, : z.width] = finished(h, g, k * z.main).astype(bf16)
            put_last(z, tail[k : k + 1, :], chunk, tile, out)

    return call(
        body,
        "v" * (count + z.split + 5) + "a" * len(after),
        [shape((z.main, z.wide))] * count,
        [pltpu.VMEM((16, fold), f32)],
        8,
        "finish_backward_" + "".join(map(str, ks)),
    )(*[chunks[k] for k in ks], *lasts, *terms, *parts, vectors, *after)


def ordered_columns(z, chunks):
    lanes = z.tokens + 16 * z.experts
    some = next(iter(chunks))
    filled = [chunks.get(k, chunks[some]) for k in range(z.experts)]
    tiles = [chunk[:16, z.width :] for chunk in filled]
    token_row = tiles[some].astype(f32)[z.pieces : z.pieces + 1, :lanes]
    token = lax.broadcasted_iota(jnp.int32, (z.tokens, lanes), 0).astype(f32)
    lane = lax.broadcasted_iota(jnp.int32, (z.tokens, lanes), 1)
    piece = jnp.where(lane < z.tokens, -1, lane % 16)
    ours = token == token_row
    if len(chunks) < z.experts:
        held = [lane // 16 % z.experts == k for k in chunks]
        ours = ours & functools.reduce(jnp.logical_or, held)
    for i in range(z.pieces):
        cols = pl.ds(i * fold, fold)
        selector = jnp.where(ours & ((piece < 0) | (piece == i)), 1.0, 0.0).astype(bf16)
        rows = jnp.concatenate([chunk[:16, cols] for chunk in filled] + tiles, axis=0)
        yield cols, jnp.dot(selector, rows, preferred_element_type=f32)


def some_rows(z, chunks, after, name):
    ks = list(chunks)

    def body(*refs):
        for cols, rows in ordered_columns(z, dict(zip(ks, refs))):
            refs[-1][:, cols] = rows.astype(bf16)

    places = "v" * len(ks) + "a" * len(after)
    return call(body, places, shape((z.tokens, z.width)), [], 8, name)(*chunks.values(), *after)


def order_rows(z, outputs, name):
    steps = 7 if z.pieces % 7 == 0 else z.pieces
    arrays, layout = [], []
    for chunks, others in outputs:
        layout.append((len(arrays), list(chunks), len(others)))
        arrays += [*chunks.values(), *others]
    number = len(outputs)

    def body(*refs):
        inputs, anys = refs[: len(arrays)], refs[len(arrays) : len(arrays) + number]
        outs, sems = refs[-1 - number : -1], refs[-1]
        copies = []
        for n, (at, ks, more) in enumerate(layout):
            chunks = dict(zip(ks, inputs[at : at + len(ks)]))
            others = inputs[at + len(ks) : at + len(ks) + more]
            for i, (cols, rows) in enumerate(ordered_columns(z, chunks)):
                for other in others:
                    rows = rows + other[:, cols].astype(f32)
                outs[n][:, cols] = rows.astype(bf16)
                if (i + 1) % (z.pieces // steps) == 0:
                    width = z.width // steps
                    done = pl.ds((i + 1) * fold - width, width)
                    copy = pltpu.make_async_copy(
                        outs[n].at[:, done], anys[n].at[:, done], sems.at[len(copies)]
                    )
                    copy.start()
                    copies.append(copy)
        for copy in copies:
            copy.wait()

    return call(
        body,
        "v" * len(arrays),
        [shape((z.tokens, z.width))] * number,
        [pltpu.VMEM((z.tokens, z.width), bf16)] * number
        + [pltpu.SemaphoreType.DMA((number * steps,))],
        8,
        name,
        [spaces["a"]] * number,
    )(*arrays)


def permute_blocks(z, arrays, k):
    groups = z.experts * z.split
    pairs = [(i, ((i // z.split) ^ k) * z.split + i % z.split) for i in range(groups)]
    return [lax.ppermute(array, "ep", pairs) for array in arrays]


def dispatch(z, chunks):
    return [chunks[0]] + [permute_blocks(z, [chunks[k]], k)[0] for k in range(1, z.experts)]


def to_core(z, array, m):
    groups = z.experts * z.split
    pairs = [(i, i // z.split * z.split + ((i % z.split) ^ m)) for i in range(groups)]
    return lax.ppermute(array, "ep", pairs)


def to_section(z, chunk, k, by):
    groups = z.experts * z.split
    sections = lax.axis_size("pp")
    pairs = [
        (s * groups + i, (s + by) % sections * groups + ((i // z.split) ^ k) * z.split + i % z.split)
        for s in range(sections)
        for i in range(groups)
    ]
    return lax.ppermute(chunk, ("pp", "ep"), pairs)


def on_device(
    fwd_act, fwd_ids, bwd_act, bwd_ids, bwd_grad, norm_gain, router, w_gate, w_down, saved_gate
):
    groups = lax.axis_size("ep")
    assert fwd_ids.shape[1] == 1
    z = Sizes(groups, router.shape[2], fwd_act.shape[0], fwd_act.shape[1])
    index = lax.axis_index("ep")
    where = jnp.stack([index // z.split, index % z.split]).astype(jnp.int32)
    router = jnp.swapaxes(router, 1, 2)
    others = range(1, z.split)

    fwd_chunks, (grad, act, gain_row, table), slots = forward_chunks(
        z, where, fwd_ids, fwd_act, bwd_ids, [bwd_grad, bwd_act, norm_gain, router]
    )
    fwd_own = dispatch(z, fwd_chunks)
    bwd_chunks, vectors = backward_chunks(z, where, slots, [grad, act], gain_row, table)
    bwd_own = dispatch(z, bwd_chunks)

    down_turned = turned(z, w_down, [w_gate], [bwd_chunks[0], fwd_own[1]], "turned_down")
    normed, gates, fwd_last = normed_rows(z, fwd_own, vectors, [down_turned])
    fwd_all = [normed] + [to_core(z, normed, m) for m in others]
    ordered = saved_rows(z, where, saved_gate, [], [gates])
    fwd_parts = experts_forward(z, fwd_all, w_gate, w_down, [ordered])
    hidden, slope = saved_terms(z, ordered, [fwd_parts[0]])
    gate_turned = turned(z, w_gate, [], [hidden], "turned_gate")
    fwd_parts = [fwd_parts[0]] + [to_core(z, fwd_parts[m], m) for m in others]

    assert z.experts == 4

    def finish(ks, after):
        return finish_forward(z, ks, fwd_own, fwd_last, fwd_parts, gates, after)

    double = finish([0, 1], [gate_turned])
    got = to_section(z, double, 0, 1)
    out2 = finish([2], [hidden, double])
    got2 = to_section(z, out2, 2, 1)
    grads, grad_last = grad_rows_of(z, bwd_own, [out2])
    grad_all = [grads] + [to_core(z, grads, m) for m in others]
    inv, act_last = act_norms(z, bwd_own, [grads])
    out3 = finish([3], [inv])
    got3 = to_section(z, out3, 3, 1)
    bwd_parts = experts_backward(z, grad_all, hidden, slope, gate_turned, down_turned, [inv])
    affinity = act_gates(z, bwd_own, act_last, inv, vectors, [bwd_parts[0]])
    fwd_done = [got2, got3]
    bwd_parts = [bwd_parts[0]] + [to_core(z, bwd_parts[m], m) for m in others]
    first, order = [z.order[1]], [k for k in z.order if k != z.order[1]]
    arguments = ([grad_last, act_last], [inv, affinity], bwd_parts, vectors)
    bwd_first = finish_backward(z, first, bwd_own, *arguments, [])
    bwd_out = finish_backward(z, order, bwd_own, *arguments, bwd_first)
    (relayed,) = permute_blocks(z, [lower_chunk(z, got, [bwd_out[0]])], 1)
    bwd_done = {k: to_section(z, out, k, -1) for k, out in zip(first + order, bwd_first + bwd_out)}

    early = some_rows(z, {0: got, 2: got2, 3: got3}, [], "forward_rows_early")
    outputs = [({1: relayed}, [early]), ({k: bwd_done[k] for k in z.order}, [])]
    fwd_next, bwd_next = order_rows(z, outputs, "all_rows")
    return (fwd_next, bwd_next)


def solution(mesh):
    return jax.shard_map(
        on_device,
        mesh=mesh,
        in_specs=(
            P(("pp", "ep"), None),
            P(("pp", "ep"), None),
            P(("pp", "ep"), None),
            P(("pp", "ep"), None),
            P(("pp", "ep"), None),
            P("pp", None),
            P("pp", None, None),
            P(("pp", "ep"), None, None),
            P(("pp", "ep"), None, None),
            P("pp", "ep", None, None),
        ),
        out_specs=(P(("pp", "ep"), None), P(("pp", "ep"), None)),
        check_vma=False,
    )
```

```python
import functools

import jax
import jax.numpy as jnp
from jax import lax
from jax.experimental import pallas as pl
from jax.experimental.pallas import tpu as pltpu
from jax.sharding import PartitionSpec as P

epsilon = 1e-06
route_scale = 2.5
fold = 256
none = 255.0
f32 = jnp.float32
bf16 = jnp.bfloat16
nn = (((1,), (0,)), ((), ()))
spaces = {
    "s": pl.BlockSpec(memory_space=pltpu.SMEM),
    "v": pl.BlockSpec(memory_space=pltpu.VMEM),
    "a": pl.BlockSpec(memory_space=pl.ANY),
    "h": pl.BlockSpec(memory_space=pltpu.HBM),
}


cost = {
    "backward_chunks": 10,
    "saved_rows": 15,
    "saved_terms": 15,
    "act_norms": 15,
    "act_gates": 15,
    "forward_rows_early": 15,
}


def call(body, places, outs, scratch, megabytes, name, out_specs=None):
    def run(*arrays):
        arrays = [
            pltpu.with_memory_space_constraint(array, pltpu.HBM) if place == "h" else array
            for array, place in zip(arrays, places, strict=True)
        ]
        return kernel(*arrays)

    where_to = {} if out_specs is None else {"out_specs": out_specs}
    kernel = pl.pallas_call(
        body,
        out_shape=outs,
        in_specs=[spaces[place] for place in places],
        **where_to,
        scratch_shapes=scratch,
        compiler_params=pltpu.CompilerParams(vmem_limit_bytes=megabytes * 1024 * 1024),
        cost_estimate=pl.CostEstimate(
            flops=int(cost.get(name, 0.1) * 1e9), bytes_accessed=1000, transcendentals=0
        ),
        name=name,
    )
    return run


def shape(dims, kind=bf16):
    return jax.ShapeDtypeStruct(dims, kind)


class Sizes:
    def __init__(self, groups, experts, tokens, width):
        self.experts = experts
        self.split = groups // experts
        self.tokens = tokens
        self.width = width
        self.main = tokens // experts
        self.cap = self.main + 1
        self.pieces = width // fold
        self.wide = width + fold
        self.rows = tokens + 16
        self.order = [experts - 1, *range(1, experts - 1), 0]
        assert self.main == 16 and self.pieces <= 14 and width % fold == 0
        assert experts <= 8 and experts & (experts - 1) == 0 and self.split & (self.split - 1) == 0


def pack_last(row, tile, first=0):
    for i in range(row.shape[1] // fold):
        tile[first + i : first + i + 1, :] = row[:, i * fold : (i + 1) * fold]


def unpack_last(chunk, z, tile, target, at, base=0):
    tile[...] = chunk[base : base + 16, z.width :].astype(f32)
    for i in range(z.pieces):
        target[at : at + 1, i * fold : (i + 1) * fold] = tile[i : i + 1, :]


def slot_matrices(ids_row, block, z):
    tokens = z.tokens
    sub = lax.broadcasted_iota(jnp.int32, (tokens, tokens), 0)
    lane = lax.broadcasted_iota(jnp.int32, (tokens, tokens), 1)
    row = jnp.bitwise_xor(ids_row, block)
    column = jnp.sum(jnp.where(sub == lane, row, 0), axis=1, keepdims=True)
    same = column == row
    place_row = jnp.sum(jnp.where(same & (sub < lane), 1, 0), axis=0, keepdims=True)
    place_column = jnp.sum(jnp.where(same & (lane < sub), 1, 0), axis=1, keepdims=True)

    def slot(expert, place):
        return jnp.where(place < z.main, expert * z.main + place, tokens + expert)

    slot_row = slot(row, place_row)
    slot_column = slot(column, place_column)
    by_slot = lax.broadcasted_iota(jnp.int32, (z.rows, tokens), 0) == slot_row
    lane = lax.broadcasted_iota(jnp.int32, (tokens, fold), 1)
    by_token = jnp.where(lane < tokens, lane, tokens + (lane - tokens) // 16) == slot_column
    token = lax.broadcasted_iota(jnp.int32, (tokens, fold), 0).astype(f32)
    token_row = jnp.sum(jnp.where(by_token, token - none, 0.0), axis=0, keepdims=True) + none
    return jnp.where(by_slot, 1.0, 0.0).astype(bf16), token_row


def write_chunks(z, selector, token_row, rows_ref, ready, tiles, chunks, base):
    step = z.width // 2
    tiles[...] = jnp.zeros_like(tiles)
    for half in range(2):
        if ready:
            ready[half].wait()
        col = half * step
        got = jnp.dot(selector, rows_ref[:, col : col + step], preferred_element_type=f32)
        packed = got[: z.tokens].astype(bf16)
        for k in range(z.experts):
            chunks[k][base : base + 16, col : col + step] = packed[k * z.main : (k + 1) * z.main]
            pack_last(got[z.tokens + k : z.tokens + k + 1], tiles.at[k], half * z.pieces // 2)
    for k in range(z.experts):
        tiles[k, z.pieces : z.pieces + 1, :] = token_row
        chunks[k][base : base + 16, z.width :] = tiles[k].astype(bf16)


def forward_chunks(z, where, ids, act, later_ids, later):
    count = len(later)

    def body(where, ids_any, later_ids_any, act_any, *refs):
        later_any, chunks = refs[:count], refs[count : count + z.experts]
        later_refs = refs[count + z.experts : 2 * count + z.experts]
        selector_ref, token_ref, ids, rows, tiles, sems = refs[2 * count + z.experts :]
        step = z.width // 2
        first = [
            pltpu.make_async_copy(source, ids.at[i : i + 1], sems.at[i])
            for i, source in enumerate((ids_any, later_ids_any))
        ]
        ready = [
            pltpu.make_async_copy(
                act_any.at[:, pl.ds(i * step, step)], rows.at[:, pl.ds(i * step, step)], sems.at[2 + i]
            )
            for i in range(2)
        ]
        rest = [
            pltpu.make_async_copy(source, target, sems.at[4 + i])
            for i, (source, target) in enumerate(zip(later_any, later_refs))
        ]
        for copy in first + ready + rest:
            copy.start()
        for copy in first:
            copy.wait()
        selector, token_row = slot_matrices(ids[0:1, :], where[0], z)
        later_selector, later_row = slot_matrices(ids[1:2, :], where[0], z)
        selector_ref[...] = later_selector
        token_ref[...] = jnp.broadcast_to(later_row, token_ref.shape)
        write_chunks(z, selector, token_row, rows, ready, tiles, chunks, 0)
        for copy in rest:
            copy.wait()

    outs = call(
        body,
        "shhh" + "h" * count,
        [shape((z.main, z.wide))] * z.experts
        + [shape(array.shape, array.dtype) for array in later]
        + [shape((z.rows, z.tokens)), shape((8, fold), f32)],
        [
            pltpu.VMEM((2, z.tokens), jnp.int32),
            pltpu.VMEM((z.tokens, z.width), bf16),
            pltpu.VMEM((z.experts, 16, fold), f32),
            pltpu.SemaphoreType.DMA((4 + count,)),
        ],
        8,
        "forward_chunks",
    )(where, ids.reshape(1, z.tokens), later_ids.reshape(1, z.tokens), act, *later)
    return outs[: z.experts], outs[z.experts : z.experts + count], outs[z.experts + count :]


def backward_chunks(z, where, slots, sources, gain, router):
    count = len(sources)

    def body(where, selector, token_ref, *refs):
        sources, (gain_ref, router_ref) = refs[:count], refs[count : count + 2]
        *chunks, vectors, tiles = refs[count + 2 :]
        for j in range(count):
            write_chunks(
                z, selector[...], token_ref[0:1, :], sources[j], None, tiles, chunks, 16 * j
            )
        vectors[...] = jnp.zeros_like(vectors)
        vectors[0:1, :] = gain_ref[...].astype(f32)
        mine = lax.broadcasted_iota(jnp.int32, (z.experts, 1), 0) == where[0]
        table = jnp.where(mine, router_ref[0].astype(f32), 0.0)
        vectors[1:2, :] = jnp.sum(table, axis=0, keepdims=True)

    *chunks, vectors = call(
        body,
        "svv" + "v" * (count + 2),
        [shape((z.main * count, z.wide))] * z.experts + [shape((8, z.width), f32)],
        [pltpu.VMEM((z.experts, 16, fold), f32)],
        8,
        "backward_chunks",
    )(where, *slots, *sources, gain, router)
    return chunks, vectors


def collect_rows(z, chunks, last, tile, base=0):
    last[...] = jnp.zeros_like(last)
    for k in range(z.experts):
        unpack_last(chunks[k], z, tile, last, k, base)


def norm_rows(h, gain):
    inv = lax.rsqrt(jnp.mean(h * h, axis=-1, keepdims=True) + epsilon)
    return (h * inv * gain).astype(bf16), inv


def normed_rows(z, chunks, vectors, after):
    def body(*refs):
        chunks, vectors = refs[: z.experts], refs[z.experts]
        normed_ref, gates_ref, last, tile = refs[z.experts + 1 + len(after) :]
        gain, router = vectors[0:1, :], vectors[1:2, :]
        collect_rows(z, chunks, last, tile)
        for k in range(z.experts + 1):
            h = last[...] if k == z.experts else chunks[k][:, : z.width].astype(f32)
            at = k * z.main
            normed, _ = norm_rows(h, gain)
            normed_ref[at : at + 16, :] = normed
            logits = jnp.sum(normed.astype(f32) * router, axis=-1, keepdims=True)
            gates_ref[at : at + 16, :] = jnp.broadcast_to(jax.nn.sigmoid(logits), (16, 128))

    return call(
        body,
        "v" * (z.experts + 1) + "a" * len(after),
        [shape((z.rows, z.width)), shape((z.rows, 128), f32), shape((16, z.width), f32)],
        [pltpu.VMEM((16, fold), f32)],
        8,
        "normed_rows",
    )(*chunks, vectors, *after)


def grad_rows_of(z, chunks, after):
    def body(*refs):
        chunks, (rows, last, tile) = refs[: z.experts], refs[z.experts + len(after) :]
        for k in range(z.experts):
            rows[k * z.main : (k + 1) * z.main, :] = chunks[k][:16, : z.width]
        collect_rows(z, chunks, last, tile)
        rows[z.tokens :, :] = last[...].astype(bf16)

    return call(
        body,
        "v" * z.experts + "a" * len(after),
        [shape((z.rows, z.width)), shape((16, z.width), f32)],
        [pltpu.VMEM((16, fold), f32)],
        8,
        "grad_rows",
    )(*chunks, *after)


def act_norms(z, chunks, after):
    def body(*refs):
        chunks, (inv_ref, last, tile) = refs[: z.experts], refs[z.experts + len(after) :]
        collect_rows(z, chunks, last, tile, 16)
        for k in range(z.experts + 1):
            h = last[...] if k == z.experts else chunks[k][16:32, : z.width].astype(f32)
            at = k * z.main
            inv = lax.rsqrt(jnp.mean(h * h, axis=-1, keepdims=True) + epsilon)
            inv_ref[at : at + 16, :] = jnp.broadcast_to(inv, (16, 128))

    return call(
        body,
        "v" * z.experts + "a" * len(after),
        [shape((z.rows, 128), f32), shape((16, z.width), f32)],
        [pltpu.VMEM((16, fold), f32)],
        8,
        "act_norms",
    )(*chunks, *after)


def act_gates(z, chunks, last, inv, vectors, after):
    def body(*refs):
        chunks, (last, inv_ref, vectors) = refs[: z.experts], refs[z.experts : z.experts + 3]
        affinity_ref = refs[-1]
        gain, router = vectors[0:1, :], vectors[1:2, :]
        for k in range(z.experts + 1):
            h = last[...] if k == z.experts else chunks[k][16:32, : z.width].astype(f32)
            at = k * z.main
            normed = (h * inv_ref[at : at + 16, 0:1] * gain).astype(bf16).astype(f32)
            logits = jnp.sum(normed * router, axis=-1, keepdims=True)
            affinity_ref[at : at + 16, :] = jnp.broadcast_to(jax.nn.sigmoid(logits), (16, 128))

    return call(
        body,
        "v" * (z.experts + 3) + "a" * len(after),
        shape((z.rows, 128), f32),
        [],
        8,
        "act_gates",
    )(*chunks, last, inv, vectors, *after)


def write_parts(z, values, outs, col):
    values = values.astype(bf16)
    for m in range(z.split):
        outs[m][:, col : col + values.shape[1]] = values[m * z.rows : (m + 1) * z.rows]


def experts_forward(z, rows, w_gate, w_down, after):
    def body(*refs):
        rows, (gate_ref, down_ref), outs = (
            refs[: z.split],
            refs[z.split : z.split + 2],
            refs[z.split + 2 + len(after) :],
        )
        held = jnp.concatenate([part[...] for part in rows], axis=0)
        gate_proj = jnp.dot(held, gate_ref[0], preferred_element_type=f32)
        hidden = jax.nn.silu(gate_proj).astype(bf16)
        step = 512
        for col in range(0, z.width, step):
            part = jnp.dot(hidden, down_ref[0, :, col : col + step], preferred_element_type=f32)
            write_parts(z, part, outs, col)

    return call(
        body,
        "v" * (z.split + 2) + "a" * len(after),
        [shape((z.rows, z.width))] * z.split,
        [],
        16,
        "experts_forward",
    )(*rows, w_gate, w_down, *after)


def saved_rows(z, where, saved, weights, after):
    total, slots, width = z.split * z.rows, saved.shape[2], saved.shape[3]

    def body(where, saved_any, *refs):
        ordered_ref, saved_ref, sem = refs[len(weights) + len(after) :]
        copy = pltpu.make_async_copy(saved_any.at[0, 0], saved_ref, sem)
        copy.start()
        row = lax.broadcasted_iota(jnp.int32, (total, slots), 0)
        slot = lax.broadcasted_iota(jnp.int32, (total, slots), 1)
        m, at = row // z.rows, row % z.rows
        is_main = at < z.tokens
        k = jnp.where(is_main, at // z.main, at - z.tokens)
        p = jnp.where(is_main, at % z.main, z.main)
        source = jnp.bitwise_xor(k, where[0]) * z.split + jnp.bitwise_xor(m, where[1])
        wanted = jnp.where(k < z.experts, source * z.cap + p, -1)
        selector = jnp.where(slot == wanted, 1.0, 0.0).astype(bf16)
        copy.wait()
        ordered_ref[...] = jnp.dot(selector, saved_ref[...], preferred_element_type=f32)

    return call(
        body,
        "sh" + "v" * len(weights) + "a" * len(after),
        shape((total, width), f32),
        [pltpu.VMEM((slots, width), bf16), pltpu.SemaphoreType.DMA],
        8,
        "saved_rows",
    )(where, saved, *weights, *after)


def saved_terms(z, ordered, after):
    def body(ordered_ref, *refs):
        hidden_ref, slope_ref = refs[len(after) :]
        gate_proj = ordered_ref[...]
        sg = jax.nn.sigmoid(gate_proj)
        hidden_ref[...] = (gate_proj * sg).astype(bf16)
        slope_ref[...] = sg * (1.0 + gate_proj * (1.0 - sg))

    return call(
        body,
        "v" + "a" * len(after),
        [shape(ordered.shape), shape(ordered.shape, f32)],
        [],
        8,
        "saved_terms",
    )(ordered, *after)


def turned(z, weights, held, after, name):
    rows, columns = weights.shape[1:]
    step = min(512, rows, columns)

    def body(weights_ref, *refs):
        for at in range(0, rows, step):
            for col in range(0, columns, step):
                block = weights_ref[0, at : at + step, col : col + step]
                refs[-1][col : col + step, at : at + step] = block.T

    return call(
        body, "v" + "v" * len(held) + "a" * len(after), shape((columns, rows)), [], 12, name
    )(weights, *held, *after)


def experts_backward(z, rows, hidden, slope, w_gate, w_down, after):
    def body(*refs):
        rows = refs[: z.split]
        hidden_ref, slope_ref, gate_ref, down_ref = refs[z.split : z.split + 4]
        outs = refs[z.split + 4 + len(after) :]
        held = jnp.concatenate([part[...] for part in rows], axis=0)
        grad_hidden = lax.dot_general(held, down_ref[...], nn, preferred_element_type=f32)
        dots = jnp.sum(grad_hidden * hidden_ref[...].astype(f32), axis=-1, keepdims=True)
        grad_gate = (grad_hidden * slope_ref[...]).astype(bf16)
        step = 512
        for col in range(0, z.width, step):
            part = lax.dot_general(
                grad_gate, gate_ref[:, col : col + step], nn, preferred_element_type=f32
            )
            write_parts(z, part, outs, col)
        write_parts(z, jnp.broadcast_to(dots, (dots.shape[0], 128)), outs, z.width)

    return call(
        body,
        "v" * (z.split + 4) + "a" * len(after),
        [shape((z.rows, z.width + 128))] * z.split,
        [],
        16,
        "experts_backward",
    )(*rows, hidden, slope, w_gate, w_down, *after)


def put_last(z, values, source_chunk, tile, out):
    tile[...] = jnp.zeros_like(tile)
    pack_last(values, tile)
    tokens = source_chunk[:16, z.width :].astype(f32)
    tile[z.pieces : z.pieces + 1, :] = tokens[z.pieces : z.pieces + 1, :]
    out[:, z.width :] = tile[...].astype(bf16)


def finish_forward(z, ks, chunks, last, parts, gates, after):
    count = len(ks)

    def body(*refs):
        chunks, last, parts = refs[:count], refs[count], refs[count + 1 : count + 1 + z.split]
        gates, out, tile = refs[count + 1 + z.split], refs[-2], refs[-1]

        def mixed(at):
            y = parts[0][at : at + 16, :].astype(f32)
            for part in parts[1:]:
                y = y + part[at : at + 16, :].astype(f32)
            return route_scale * (gates[at : at + 16, 0:1] * y)

        tail = last[...] + mixed(z.tokens)
        for i, (k, chunk) in enumerate(zip(ks, chunks)):
            h = chunk[:, : z.width].astype(f32)
            rows = out.at[pl.ds(i * 16, 16)]
            rows[:, : z.width] = (h + mixed(k * z.main)).astype(bf16)
            put_last(z, tail[k : k + 1, :], chunk, tile, rows)

    return call(
        body,
        "v" * (count + z.split + 2) + "a" * len(after),
        shape((count * z.main, z.wide)),
        [pltpu.VMEM((16, fold), f32)],
        8,
        "finish_forward_" + "".join(map(str, ks)),
    )(*[chunks[k] for k in ks], last, *parts, gates, *after)


def lower_chunk(z, double, after):
    def body(double, *refs):
        refs[-1][...] = double[16:32, :]

    places = "v" + "a" * len(after)
    return call(body, places, shape((16, z.wide)), [], 8, "lower_chunk")(double, *after)


def finish_backward(z, ks, chunks, lasts, terms, parts, vectors, after):
    count = len(ks)

    def body(*refs):
        e = z.experts
        chunks = [refs[k] for k in ks]
        last_grad, last_act, inv_ref, affinity_ref = refs[e : e + 4]
        parts, vectors = refs[e + 4 : e + 4 + z.split], refs[e + 4 + z.split]
        outs, tile = refs[-1 - count : -1], refs[-1]
        gain, router = vectors[0:1, :], vectors[1:2, :]

        def finished(h, g, at):
            inv, affinity = inv_ref[at : at + 16, 0:1], affinity_ref[at : at + 16, 0:1]
            rows = parts[0][at : at + 16, : z.width].astype(f32)
            dot = parts[0][at : at + 16, z.width :].astype(f32)
            for part in parts[1:]:
                rows = rows + part[at : at + 16, : z.width].astype(f32)
                dot = dot + part[at : at + 16, z.width :].astype(f32)
            dot = dot[:, 0:1]
            grad_logits = (route_scale * dot * affinity * (1.0 - affinity)).astype(bf16).astype(f32)
            grad_pre = (route_scale * affinity * rows + grad_logits * router) * gain
            centre = jnp.mean(grad_pre * h, axis=-1, keepdims=True)
            return g + inv * (grad_pre - h * (inv * inv * centre))

        tail = finished(last_act[...], last_grad[...], z.tokens)
        for k, chunk, out in zip(ks, chunks, outs):
            g = chunk[:16, : z.width].astype(f32)
            h = chunk[16:32, : z.width].astype(f32)
            out[:, : z.width] = finished(h, g, k * z.main).astype(bf16)
            put_last(z, tail[k : k + 1, :], chunk, tile, out)

    return call(
        body,
        "v" * (z.experts + z.split + 5) + "a" * len(after),
        [shape((z.main, z.wide))] * count,
        [pltpu.VMEM((16, fold), f32)],
        8,
        "finish_backward_" + "".join(map(str, ks)),
    )(*chunks, *lasts, *terms, *parts, vectors, *after)


def ordered_columns(z, chunks):
    lanes = z.tokens + 16 * z.experts
    some = next(iter(chunks))
    filled = [chunks.get(k, chunks[some]) for k in range(z.experts)]
    tiles = [chunk[:16, z.width :] for chunk in filled]
    token_row = tiles[some].astype(f32)[z.pieces : z.pieces + 1, :lanes]
    token = lax.broadcasted_iota(jnp.int32, (z.tokens, lanes), 0).astype(f32)
    lane = lax.broadcasted_iota(jnp.int32, (z.tokens, lanes), 1)
    piece = jnp.where(lane < z.tokens, -1, lane % 16)
    ours = token == token_row
    if len(chunks) < z.experts:
        held = [lane // 16 % z.experts == k for k in chunks]
        ours = ours & functools.reduce(jnp.logical_or, held)
    for i in range(z.pieces):
        cols = pl.ds(i * fold, fold)
        selector = jnp.where(ours & ((piece < 0) | (piece == i)), 1.0, 0.0).astype(bf16)
        rows = jnp.concatenate([chunk[:16, cols] for chunk in filled] + tiles, axis=0)
        yield cols, jnp.dot(selector, rows, preferred_element_type=f32)


def some_rows(z, chunks, after, name):
    ks = list(chunks)

    def body(*refs):
        for cols, rows in ordered_columns(z, dict(zip(ks, refs))):
            refs[-1][:, cols] = rows.astype(bf16)

    places = "v" * len(ks) + "a" * len(after)
    return call(body, places, shape((z.tokens, z.width)), [], 8, name)(*chunks.values(), *after)


def order_rows(z, outputs, name):
    steps = 7 if z.pieces % 7 == 0 else z.pieces
    arrays, layout = [], []
    for chunks, others in outputs:
        layout.append((len(arrays), list(chunks), len(others)))
        arrays += [*chunks.values(), *others]
    number = len(outputs)

    def body(*refs):
        inputs, anys = refs[: len(arrays)], refs[len(arrays) : len(arrays) + number]
        outs, sems = refs[-1 - number : -1], refs[-1]
        copies = []
        for n, (at, ks, more) in enumerate(layout):
            chunks = dict(zip(ks, inputs[at : at + len(ks)]))
            others = inputs[at + len(ks) : at + len(ks) + more]
            for i, (cols, rows) in enumerate(ordered_columns(z, chunks)):
                for other in others:
                    rows = rows + other[:, cols].astype(f32)
                outs[n][:, cols] = rows.astype(bf16)
                if (i + 1) % (z.pieces // steps) == 0:
                    width = z.width // steps
                    done = pl.ds((i + 1) * fold - width, width)
                    copy = pltpu.make_async_copy(
                        outs[n].at[:, done], anys[n].at[:, done], sems.at[len(copies)]
                    )
                    copy.start()
                    copies.append(copy)
        for copy in copies:
            copy.wait()

    return call(
        body,
        "v" * len(arrays),
        [shape((z.tokens, z.width))] * number,
        [pltpu.VMEM((z.tokens, z.width), bf16)] * number
        + [pltpu.SemaphoreType.DMA((number * steps,))],
        8,
        name,
        [spaces["a"]] * number,
    )(*arrays)


def permute_blocks(z, arrays, k):
    groups = z.experts * z.split
    pairs = [(i, ((i // z.split) ^ k) * z.split + i % z.split) for i in range(groups)]
    return [lax.ppermute(array, "ep", pairs) for array in arrays]


def dispatch(z, chunks):
    return [chunks[0]] + [permute_blocks(z, [chunks[k]], k)[0] for k in range(1, z.experts)]


def to_core(z, array, m):
    groups = z.experts * z.split
    pairs = [(i, i // z.split * z.split + ((i % z.split) ^ m)) for i in range(groups)]
    return lax.ppermute(array, "ep", pairs)


def to_section(z, chunk, k, by):
    groups = z.experts * z.split
    sections = lax.axis_size("pp")
    pairs = [
        (s * groups + i, (s + by) % sections * groups + ((i // z.split) ^ k) * z.split + i % z.split)
        for s in range(sections)
        for i in range(groups)
    ]
    return lax.ppermute(chunk, ("pp", "ep"), pairs)


def on_device(
    fwd_act, fwd_ids, bwd_act, bwd_ids, bwd_grad, norm_gain, router, w_gate, w_down, saved_gate
):
    groups = lax.axis_size("ep")
    assert fwd_ids.shape[1] == 1
    z = Sizes(groups, router.shape[2], fwd_act.shape[0], fwd_act.shape[1])
    index = lax.axis_index("ep")
    where = jnp.stack([index // z.split, index % z.split]).astype(jnp.int32)
    router = jnp.swapaxes(router, 1, 2)
    others = range(1, z.split)

    fwd_chunks, (grad, act, gain_row, table), slots = forward_chunks(
        z, where, fwd_ids, fwd_act, bwd_ids, [bwd_grad, bwd_act, norm_gain, router]
    )
    fwd_own = dispatch(z, fwd_chunks)
    bwd_chunks, vectors = backward_chunks(z, where, slots, [grad, act], gain_row, table)
    bwd_own = dispatch(z, bwd_chunks)

    down_turned = turned(z, w_down, [w_gate], [bwd_chunks[0], fwd_own[1]], "turned_down")
    normed, gates, fwd_last = normed_rows(z, fwd_own, vectors, [down_turned])
    fwd_all = [normed] + [to_core(z, normed, m) for m in others]
    ordered = saved_rows(z, where, saved_gate, [], [gates])
    fwd_parts = experts_forward(z, fwd_all, w_gate, w_down, [ordered])
    hidden, slope = saved_terms(z, ordered, [fwd_parts[0]])
    gate_turned = turned(z, w_gate, [], [hidden], "turned_gate")
    fwd_parts = [fwd_parts[0]] + [to_core(z, fwd_parts[m], m) for m in others]

    assert z.experts == 4

    def finish(ks, after):
        return finish_forward(z, ks, fwd_own, fwd_last, fwd_parts, gates, after)

    double = finish([0, 1], [gate_turned])
    got = to_section(z, double, 0, 1)
    out2 = finish([2], [hidden, double])
    got2 = to_section(z, out2, 2, 1)
    grads, grad_last = grad_rows_of(z, bwd_own, [out2])
    grad_all = [grads] + [to_core(z, grads, m) for m in others]
    inv, act_last = act_norms(z, bwd_own, [grads])
    out3 = finish([3], [inv])
    got3 = to_section(z, out3, 3, 1)
    bwd_parts = experts_backward(z, grad_all, hidden, slope, gate_turned, down_turned, [inv])
    affinity = act_gates(z, bwd_own, act_last, inv, vectors, [bwd_parts[0]])
    fwd_done = [got2, got3]
    bwd_parts = [bwd_parts[0]] + [to_core(z, bwd_parts[m], m) for m in others]
    first, order = [z.order[1]], [k for k in z.order if k != z.order[1]]
    arguments = ([grad_last, act_last], [inv, affinity], bwd_parts, vectors)
    bwd_first = finish_backward(z, first, bwd_own, *arguments, [])
    bwd_out = finish_backward(z, order, bwd_own, *arguments, bwd_first)
    (relayed,) = permute_blocks(z, [lower_chunk(z, got, [bwd_out[0]])], 1)
    bwd_done = {k: to_section(z, out, k, -1) for k, out in zip(first + order, bwd_first + bwd_out)}

    early = some_rows(z, {0: got, 2: got2, 3: got3}, [], "forward_rows_early")
    outputs = [({1: relayed}, [early]), ({k: bwd_done[k] for k in z.order}, [])]
    fwd_next, bwd_next = order_rows(z, outputs, "all_rows")
    return (fwd_next, bwd_next)


def solution(mesh):
    return jax.shard_map(
        on_device,
        mesh=mesh,
        in_specs=(
            P(("pp", "ep"), None),
            P(("pp", "ep"), None),
            P(("pp", "ep"), None),
            P(("pp", "ep"), None),
            P(("pp", "ep"), None),
            P("pp", None),
            P("pp", None, None),
            P(("pp", "ep"), None, None),
            P(("pp", "ep"), None, None),
            P("pp", "ep", None, None),
        ),
        out_specs=(P(("pp", "ep"), None), P(("pp", "ep"), None)),
        check_vma=False,
    )
```

```python
import functools

import jax
import jax.numpy as jnp
from jax import lax
from jax.experimental import pallas as pl
from jax.experimental.pallas import tpu as pltpu
from jax.sharding import PartitionSpec as P

epsilon = 1e-06
route_scale = 2.5
fold = 256
none = 255.0
f32 = jnp.float32
bf16 = jnp.bfloat16
nn = (((1,), (0,)), ((), ()))
spaces = {
    "s": pl.BlockSpec(memory_space=pltpu.SMEM),
    "v": pl.BlockSpec(memory_space=pltpu.VMEM),
    "a": pl.BlockSpec(memory_space=pl.ANY),
    "h": pl.BlockSpec(memory_space=pltpu.HBM),
}


cost = {
    "backward_chunks": 10,
    "saved_rows": 15,
    "saved_terms": 15,
    "finish_forward_3": 15,
    "act_gates": 15,
    "forward_rows_early": 15,
}


def call(body, places, outs, scratch, megabytes, name, out_specs=None):
    def run(*arrays):
        arrays = [
            pltpu.with_memory_space_constraint(array, pltpu.HBM) if place == "h" else array
            for array, place in zip(arrays, places, strict=True)
        ]
        return kernel(*arrays)

    where_to = {} if out_specs is None else {"out_specs": out_specs}
    kernel = pl.pallas_call(
        body,
        out_shape=outs,
        in_specs=[spaces[place] for place in places],
        **where_to,
        scratch_shapes=scratch,
        compiler_params=pltpu.CompilerParams(vmem_limit_bytes=megabytes * 1024 * 1024),
        cost_estimate=pl.CostEstimate(
            flops=int(cost.get(name, 0.1) * 1e9), bytes_accessed=1000, transcendentals=0
        ),
        name=name,
    )
    return run


def shape(dims, kind=bf16):
    return jax.ShapeDtypeStruct(dims, kind)


class Sizes:
    def __init__(self, groups, experts, tokens, width):
        self.experts = experts
        self.split = groups // experts
        self.tokens = tokens
        self.width = width
        self.main = tokens // experts
        self.cap = self.main + 1
        self.pieces = width // fold
        self.wide = width + fold
        self.rows = tokens + 16
        self.order = [experts - 1, *range(1, experts - 1), 0]
        assert self.main == 16 and self.pieces <= 14 and width % fold == 0
        assert experts <= 8 and experts & (experts - 1) == 0 and self.split & (self.split - 1) == 0


def pack_last(row, tile, first=0):
    for i in range(row.shape[1] // fold):
        tile[first + i : first + i + 1, :] = row[:, i * fold : (i + 1) * fold]


def unpack_last(chunk, z, tile, target, at, base=0):
    tile[...] = chunk[base : base + 16, z.width :].astype(f32)
    for i in range(z.pieces):
        target[at : at + 1, i * fold : (i + 1) * fold] = tile[i : i + 1, :]


def slot_matrices(ids_row, block, z):
    tokens = z.tokens
    sub = lax.broadcasted_iota(jnp.int32, (tokens, tokens), 0)
    lane = lax.broadcasted_iota(jnp.int32, (tokens, tokens), 1)
    row = jnp.bitwise_xor(ids_row, block)
    column = jnp.sum(jnp.where(sub == lane, row, 0), axis=1, keepdims=True)
    same = column == row
    place_row = jnp.sum(jnp.where(same & (sub < lane), 1, 0), axis=0, keepdims=True)
    place_column = jnp.sum(jnp.where(same & (lane < sub), 1, 0), axis=1, keepdims=True)

    def slot(expert, place):
        return jnp.where(place < z.main, expert * z.main + place, tokens + expert)

    slot_row = slot(row, place_row)
    slot_column = slot(column, place_column)
    by_slot = lax.broadcasted_iota(jnp.int32, (z.rows, tokens), 0) == slot_row
    lane = lax.broadcasted_iota(jnp.int32, (tokens, fold), 1)
    by_token = jnp.where(lane < tokens, lane, tokens + (lane - tokens) // 16) == slot_column
    token = lax.broadcasted_iota(jnp.int32, (tokens, fold), 0).astype(f32)
    token_row = jnp.sum(jnp.where(by_token, token - none, 0.0), axis=0, keepdims=True) + none
    return jnp.where(by_slot, 1.0, 0.0).astype(bf16), token_row


def write_chunks(z, selector, token_row, rows_ref, ready, tiles, chunks, base):
    step = z.width // 2
    tiles[...] = jnp.zeros_like(tiles)
    for half in range(2):
        if ready:
            ready[half].wait()
        col = half * step
        got = jnp.dot(selector, rows_ref[:, col : col + step], preferred_element_type=f32)
        packed = got[: z.tokens].astype(bf16)
        for k in range(z.experts):
            chunks[k][base : base + 16, col : col + step] = packed[k * z.main : (k + 1) * z.main]
            pack_last(got[z.tokens + k : z.tokens + k + 1], tiles.at[k], half * z.pieces // 2)
    for k in range(z.experts):
        tiles[k, z.pieces : z.pieces + 1, :] = token_row
        chunks[k][base : base + 16, z.width :] = tiles[k].astype(bf16)


def forward_chunks(z, where, ids, act, later_ids, later):
    count = len(later)

    def body(where, ids_any, later_ids_any, act_any, *refs):
        later_any, chunks = refs[:count], refs[count : count + z.experts]
        later_refs = refs[count + z.experts : 2 * count + z.experts]
        selector_ref, token_ref, ids, rows, tiles, sems = refs[2 * count + z.experts :]
        step = z.width // 2
        first = [
            pltpu.make_async_copy(source, ids.at[i : i + 1], sems.at[i])
            for i, source in enumerate((ids_any, later_ids_any))
        ]
        ready = [
            pltpu.make_async_copy(
                act_any.at[:, pl.ds(i * step, step)], rows.at[:, pl.ds(i * step, step)], sems.at[2 + i]
            )
            for i in range(2)
        ]
        rest = [
            pltpu.make_async_copy(source, target, sems.at[4 + i])
            for i, (source, target) in enumerate(zip(later_any, later_refs))
        ]
        for copy in first + ready + rest:
            copy.start()
        for copy in first:
            copy.wait()
        selector, token_row = slot_matrices(ids[0:1, :], where[0], z)
        later_selector, later_row = slot_matrices(ids[1:2, :], where[0], z)
        selector_ref[...] = later_selector
        token_ref[...] = jnp.broadcast_to(later_row, token_ref.shape)
        write_chunks(z, selector, token_row, rows, ready, tiles, chunks, 0)
        for copy in rest:
            copy.wait()

    outs = call(
        body,
        "shhh" + "h" * count,
        [shape((z.main, z.wide))] * z.experts
        + [shape(array.shape, array.dtype) for array in later]
        + [shape((z.rows, z.tokens)), shape((8, fold), f32)],
        [
            pltpu.VMEM((2, z.tokens), jnp.int32),
            pltpu.VMEM((z.tokens, z.width), bf16),
            pltpu.VMEM((z.experts, 16, fold), f32),
            pltpu.SemaphoreType.DMA((4 + count,)),
        ],
        8,
        "forward_chunks",
    )(where, ids.reshape(1, z.tokens), later_ids.reshape(1, z.tokens), act, *later)
    return outs[: z.experts], outs[z.experts : z.experts + count], outs[z.experts + count :]


def backward_chunks(z, where, slots, sources, gain, router):
    count = len(sources)

    def body(where, selector, token_ref, *refs):
        sources, (gain_ref, router_ref) = refs[:count], refs[count : count + 2]
        *chunks, vectors, tiles = refs[count + 2 :]
        for j in range(count):
            write_chunks(
                z, selector[...], token_ref[0:1, :], sources[j], None, tiles, chunks, 16 * j
            )
        vectors[...] = jnp.zeros_like(vectors)
        vectors[0:1, :] = gain_ref[...].astype(f32)
        mine = lax.broadcasted_iota(jnp.int32, (z.experts, 1), 0) == where[0]
        table = jnp.where(mine, router_ref[0].astype(f32), 0.0)
        vectors[1:2, :] = jnp.sum(table, axis=0, keepdims=True)

    *chunks, vectors = call(
        body,
        "svv" + "v" * (count + 2),
        [shape((z.main * count, z.wide))] * z.experts + [shape((8, z.width), f32)],
        [pltpu.VMEM((z.experts, 16, fold), f32)],
        8,
        "backward_chunks",
    )(where, *slots, *sources, gain, router)
    return chunks, vectors


def collect_rows(z, chunks, last, tile, base=0):
    last[...] = jnp.zeros_like(last)
    for k in range(z.experts):
        unpack_last(chunks[k], z, tile, last, k, base)


def norm_rows(h, gain):
    inv = lax.rsqrt(jnp.mean(h * h, axis=-1, keepdims=True) + epsilon)
    return (h * inv * gain).astype(bf16), inv


def normed_rows(z, chunks, vectors, after):
    def body(*refs):
        chunks, vectors = refs[: z.experts], refs[z.experts]
        normed_ref, gates_ref, last, tile = refs[z.experts + 1 + len(after) :]
        gain, router = vectors[0:1, :], vectors[1:2, :]
        collect_rows(z, chunks, last, tile)
        for k in range(z.experts + 1):
            h = last[...] if k == z.experts else chunks[k][:, : z.width].astype(f32)
            at = k * z.main
            normed, _ = norm_rows(h, gain)
            normed_ref[at : at + 16, :] = normed
            logits = jnp.sum(normed.astype(f32) * router, axis=-1, keepdims=True)
            gates_ref[at : at + 16, :] = jnp.broadcast_to(jax.nn.sigmoid(logits), (16, 128))

    return call(
        body,
        "v" * (z.experts + 1) + "a" * len(after),
        [shape((z.rows, z.width)), shape((z.rows, 128), f32), shape((16, z.width), f32)],
        [pltpu.VMEM((16, fold), f32)],
        8,
        "normed_rows",
    )(*chunks, vectors, *after)


def grad_rows_of(z, chunks, after):
    def body(*refs):
        chunks, (rows, last, tile) = refs[: z.experts], refs[z.experts + len(after) :]
        for k in range(z.experts):
            rows[k * z.main : (k + 1) * z.main, :] = chunks[k][:16, : z.width]
        collect_rows(z, chunks, last, tile)
        rows[z.tokens :, :] = last[...].astype(bf16)

    return call(
        body,
        "v" * z.experts + "a" * len(after),
        [shape((z.rows, z.width)), shape((16, z.width), f32)],
        [pltpu.VMEM((16, fold), f32)],
        8,
        "grad_rows",
    )(*chunks, *after)


def act_norms(z, chunks, after):
    def body(*refs):
        chunks, (inv_ref, last, tile) = refs[: z.experts], refs[z.experts + len(after) :]
        collect_rows(z, chunks, last, tile, 16)
        for k in range(z.experts + 1):
            h = last[...] if k == z.experts else chunks[k][16:32, : z.width].astype(f32)
            at = k * z.main
            inv = lax.rsqrt(jnp.mean(h * h, axis=-1, keepdims=True) + epsilon)
            inv_ref[at : at + 16, :] = jnp.broadcast_to(inv, (16, 128))

    return call(
        body,
        "v" * z.experts + "a" * len(after),
        [shape((z.rows, 128), f32), shape((16, z.width), f32)],
        [pltpu.VMEM((16, fold), f32)],
        8,
        "act_norms",
    )(*chunks, *after)


def act_gates(z, chunks, last, inv, vectors, after):
    def body(*refs):
        chunks, (last, inv_ref, vectors) = refs[: z.experts], refs[z.experts : z.experts + 3]
        affinity_ref = refs[-1]
        gain, router = vectors[0:1, :], vectors[1:2, :]
        for k in range(z.experts + 1):
            h = last[...] if k == z.experts else chunks[k][16:32, : z.width].astype(f32)
            at = k * z.main
            normed = (h * inv_ref[at : at + 16, 0:1] * gain).astype(bf16).astype(f32)
            logits = jnp.sum(normed * router, axis=-1, keepdims=True)
            affinity_ref[at : at + 16, :] = jnp.broadcast_to(jax.nn.sigmoid(logits), (16, 128))

    return call(
        body,
        "v" * (z.experts + 3) + "a" * len(after),
        shape((z.rows, 128), f32),
        [],
        8,
        "act_gates",
    )(*chunks, last, inv, vectors, *after)


def write_parts(z, values, outs, col):
    values = values.astype(bf16)
    for m in range(z.split):
        outs[m][:, col : col + values.shape[1]] = values[m * z.rows : (m + 1) * z.rows]


def experts_forward(z, rows, w_gate, w_down, after):
    def body(*refs):
        rows, (gate_ref, down_ref), outs = (
            refs[: z.split],
            refs[z.split : z.split + 2],
            refs[z.split + 2 + len(after) :],
        )
        held = jnp.concatenate([part[...] for part in rows], axis=0)
        gate_proj = jnp.dot(held, gate_ref[0], preferred_element_type=f32)
        hidden = jax.nn.silu(gate_proj).astype(bf16)
        step = 512
        for col in range(0, z.width, step):
            part = jnp.dot(hidden, down_ref[0, :, col : col + step], preferred_element_type=f32)
            write_parts(z, part, outs, col)

    return call(
        body,
        "v" * (z.split + 2) + "a" * len(after),
        [shape((z.rows, z.width))] * z.split,
        [],
        16,
        "experts_forward",
    )(*rows, w_gate, w_down, *after)


def saved_rows(z, where, saved, weights, after):
    total, slots, width = z.split * z.rows, saved.shape[2], saved.shape[3]

    def body(where, saved_any, *refs):
        ordered_ref, saved_ref, sem = refs[len(weights) + len(after) :]
        copy = pltpu.make_async_copy(saved_any.at[0, 0], saved_ref, sem)
        copy.start()
        row = lax.broadcasted_iota(jnp.int32, (total, slots), 0)
        slot = lax.broadcasted_iota(jnp.int32, (total, slots), 1)
        m, at = row // z.rows, row % z.rows
        is_main = at < z.tokens
        k = jnp.where(is_main, at // z.main, at - z.tokens)
        p = jnp.where(is_main, at % z.main, z.main)
        source = jnp.bitwise_xor(k, where[0]) * z.split + jnp.bitwise_xor(m, where[1])
        wanted = jnp.where(k < z.experts, source * z.cap + p, -1)
        selector = jnp.where(slot == wanted, 1.0, 0.0).astype(bf16)
        copy.wait()
        ordered_ref[...] = jnp.dot(selector, saved_ref[...], preferred_element_type=f32)

    return call(
        body,
        "sh" + "v" * len(weights) + "a" * len(after),
        shape((total, width), f32),
        [pltpu.VMEM((slots, width), bf16), pltpu.SemaphoreType.DMA],
        8,
        "saved_rows",
    )(where, saved, *weights, *after)


def saved_terms(z, ordered, after):
    def body(ordered_ref, *refs):
        hidden_ref, slope_ref = refs[len(after) :]
        gate_proj = ordered_ref[...]
        sg = jax.nn.sigmoid(gate_proj)
        hidden_ref[...] = (gate_proj * sg).astype(bf16)
        slope_ref[...] = sg * (1.0 + gate_proj * (1.0 - sg))

    return call(
        body,
        "v" + "a" * len(after),
        [shape(ordered.shape), shape(ordered.shape, f32)],
        [],
        8,
        "saved_terms",
    )(ordered, *after)


def turned(z, weights, held, after, name):
    rows, columns = weights.shape[1:]
    step = min(512, rows, columns)

    def body(weights_ref, *refs):
        for at in range(0, rows, step):
            for col in range(0, columns, step):
                block = weights_ref[0, at : at + step, col : col + step]
                refs[-1][col : col + step, at : at + step] = block.T

    return call(
        body, "v" + "v" * len(held) + "a" * len(after), shape((columns, rows)), [], 12, name
    )(weights, *held, *after)


def experts_backward(z, rows, hidden, slope, w_gate, w_down, after):
    def body(*refs):
        rows = refs[: z.split]
        hidden_ref, slope_ref, gate_ref, down_ref = refs[z.split : z.split + 4]
        outs = refs[z.split + 4 + len(after) :]
        held = jnp.concatenate([part[...] for part in rows], axis=0)
        grad_hidden = lax.dot_general(held, down_ref[...], nn, preferred_element_type=f32)
        dots = jnp.sum(grad_hidden * hidden_ref[...].astype(f32), axis=-1, keepdims=True)
        grad_gate = (grad_hidden * slope_ref[...]).astype(bf16)
        step = 512
        for col in range(0, z.width, step):
            part = lax.dot_general(
                grad_gate, gate_ref[:, col : col + step], nn, preferred_element_type=f32
            )
            write_parts(z, part, outs, col)
        write_parts(z, jnp.broadcast_to(dots, (dots.shape[0], 128)), outs, z.width)

    return call(
        body,
        "v" * (z.split + 4) + "a" * len(after),
        [shape((z.rows, z.width + 128))] * z.split,
        [],
        16,
        "experts_backward",
    )(*rows, hidden, slope, w_gate, w_down, *after)


def put_last(z, values, source_chunk, tile, out):
    tile[...] = jnp.zeros_like(tile)
    pack_last(values, tile)
    tokens = source_chunk[:16, z.width :].astype(f32)
    tile[z.pieces : z.pieces + 1, :] = tokens[z.pieces : z.pieces + 1, :]
    out[:, z.width :] = tile[...].astype(bf16)


def finish_forward(z, ks, chunks, last, parts, gates, after):
    count = len(ks)

    def body(*refs):
        chunks, last, parts = refs[:count], refs[count], refs[count + 1 : count + 1 + z.split]
        gates, out, tile = refs[count + 1 + z.split], refs[-2], refs[-1]

        def mixed(at):
            y = parts[0][at : at + 16, :].astype(f32)
            for part in parts[1:]:
                y = y + part[at : at + 16, :].astype(f32)
            return route_scale * (gates[at : at + 16, 0:1] * y)

        tail = last[...] + mixed(z.tokens)
        for i, (k, chunk) in enumerate(zip(ks, chunks)):
            h = chunk[:, : z.width].astype(f32)
            rows = out.at[pl.ds(i * 16, 16)]
            rows[:, : z.width] = (h + mixed(k * z.main)).astype(bf16)
            put_last(z, tail[k : k + 1, :], chunk, tile, rows)

    return call(
        body,
        "v" * (count + z.split + 2) + "a" * len(after),
        shape((count * z.main, z.wide)),
        [pltpu.VMEM((16, fold), f32)],
        8,
        "finish_forward_" + "".join(map(str, ks)),
    )(*[chunks[k] for k in ks], last, *parts, gates, *after)


def lower_chunk(z, double, after):
    def body(double, *refs):
        refs[-1][...] = double[16:32, :]

    places = "v" + "a" * len(after)
    return call(body, places, shape((16, z.wide)), [], 8, "lower_chunk")(double, *after)


def finish_backward(z, order, chunks, lasts, terms, parts, vectors, after):
    def body(*refs):
        e = z.experts
        chunks, (last_grad, last_act, inv_ref, affinity_ref) = refs[:e], refs[e : e + 4]
        parts, vectors = refs[e + 4 : e + 4 + z.split], refs[e + 4 + z.split]
        outs, (tile,) = refs[-1 - e : -1], refs[-1:]
        outs = [outs[order.index(k)] for k in range(e)]
        gain, router = vectors[0:1, :], vectors[1:2, :]

        def finished(h, g, at):
            inv, affinity = inv_ref[at : at + 16, 0:1], affinity_ref[at : at + 16, 0:1]
            rows = parts[0][at : at + 16, : z.width].astype(f32)
            dot = parts[0][at : at + 16, z.width :].astype(f32)
            for part in parts[1:]:
                rows = rows + part[at : at + 16, : z.width].astype(f32)
                dot = dot + part[at : at + 16, z.width :].astype(f32)
            dot = dot[:, 0:1]
            grad_logits = (route_scale * dot * affinity * (1.0 - affinity)).astype(bf16).astype(f32)
            grad_pre = (route_scale * affinity * rows + grad_logits * router) * gain
            centre = jnp.mean(grad_pre * h, axis=-1, keepdims=True)
            return g + inv * (grad_pre - h * (inv * inv * centre))

        tail = finished(last_act[...], last_grad[...], z.tokens)
        for k in range(e):
            g = chunks[k][:16, : z.width].astype(f32)
            h = chunks[k][16:32, : z.width].astype(f32)
            outs[k][:, : z.width] = finished(h, g, k * z.main).astype(bf16)
            put_last(z, tail[k : k + 1, :], chunks[k], tile, outs[k])

    return call(
        body,
        "v" * (z.experts + z.split + 5) + "a" * len(after),
        [shape((z.main, z.wide))] * z.experts,
        [pltpu.VMEM((16, fold), f32)],
        8,
        "finish_backward",
    )(*chunks, *lasts, *terms, *parts, vectors, *after)


def ordered_columns(z, chunks):
    lanes = z.tokens + 16 * z.experts
    some = next(iter(chunks))
    filled = [chunks.get(k, chunks[some]) for k in range(z.experts)]
    tiles = [chunk[:16, z.width :] for chunk in filled]
    token_row = tiles[some].astype(f32)[z.pieces : z.pieces + 1, :lanes]
    token = lax.broadcasted_iota(jnp.int32, (z.tokens, lanes), 0).astype(f32)
    lane = lax.broadcasted_iota(jnp.int32, (z.tokens, lanes), 1)
    piece = jnp.where(lane < z.tokens, -1, lane % 16)
    ours = token == token_row
    if len(chunks) < z.experts:
        held = [lane // 16 % z.experts == k for k in chunks]
        ours = ours & functools.reduce(jnp.logical_or, held)
    for i in range(z.pieces):
        cols = pl.ds(i * fold, fold)
        selector = jnp.where(ours & ((piece < 0) | (piece == i)), 1.0, 0.0).astype(bf16)
        rows = jnp.concatenate([chunk[:16, cols] for chunk in filled] + tiles, axis=0)
        yield cols, jnp.dot(selector, rows, preferred_element_type=f32)


def some_rows(z, chunks, after, name):
    ks = list(chunks)

    def body(*refs):
        for cols, rows in ordered_columns(z, dict(zip(ks, refs))):
            refs[-1][:, cols] = rows.astype(bf16)

    places = "v" * len(ks) + "a" * len(after)
    return call(body, places, shape((z.tokens, z.width)), [], 8, name)(*chunks.values(), *after)


def order_rows(z, outputs, name):
    steps = 7 if z.pieces % 7 == 0 else z.pieces
    arrays, layout = [], []
    for chunks, others in outputs:
        layout.append((len(arrays), list(chunks), len(others)))
        arrays += [*chunks.values(), *others]
    number = len(outputs)

    def body(*refs):
        inputs, anys = refs[: len(arrays)], refs[len(arrays) : len(arrays) + number]
        outs, sems = refs[-1 - number : -1], refs[-1]
        copies = []
        for n, (at, ks, more) in enumerate(layout):
            chunks = dict(zip(ks, inputs[at : at + len(ks)]))
            others = inputs[at + len(ks) : at + len(ks) + more]
            for i, (cols, rows) in enumerate(ordered_columns(z, chunks)):
                for other in others:
                    rows = rows + other[:, cols].astype(f32)
                outs[n][:, cols] = rows.astype(bf16)
                if (i + 1) % (z.pieces // steps) == 0:
                    width = z.width // steps
                    done = pl.ds((i + 1) * fold - width, width)
                    copy = pltpu.make_async_copy(
                        outs[n].at[:, done], anys[n].at[:, done], sems.at[len(copies)]
                    )
                    copy.start()
                    copies.append(copy)
        for copy in copies:
            copy.wait()

    return call(
        body,
        "v" * len(arrays),
        [shape((z.tokens, z.width))] * number,
        [pltpu.VMEM((z.tokens, z.width), bf16)] * number
        + [pltpu.SemaphoreType.DMA((number * steps,))],
        8,
        name,
        [spaces["a"]] * number,
    )(*arrays)


def permute_blocks(z, arrays, k):
    groups = z.experts * z.split
    pairs = [(i, ((i // z.split) ^ k) * z.split + i % z.split) for i in range(groups)]
    return [lax.ppermute(array, "ep", pairs) for array in arrays]


def dispatch(z, chunks):
    return [chunks[0]] + [permute_blocks(z, [chunks[k]], k)[0] for k in range(1, z.experts)]


def to_core(z, array, m):
    groups = z.experts * z.split
    pairs = [(i, i // z.split * z.split + ((i % z.split) ^ m)) for i in range(groups)]
    return lax.ppermute(array, "ep", pairs)


def to_section(z, chunk, k, by):
    groups = z.experts * z.split
    sections = lax.axis_size("pp")
    pairs = [
        (s * groups + i, (s + by) % sections * groups + ((i // z.split) ^ k) * z.split + i % z.split)
        for s in range(sections)
        for i in range(groups)
    ]
    return lax.ppermute(chunk, ("pp", "ep"), pairs)


def on_device(
    fwd_act, fwd_ids, bwd_act, bwd_ids, bwd_grad, norm_gain, router, w_gate, w_down, saved_gate
):
    groups = lax.axis_size("ep")
    assert fwd_ids.shape[1] == 1
    z = Sizes(groups, router.shape[2], fwd_act.shape[0], fwd_act.shape[1])
    index = lax.axis_index("ep")
    where = jnp.stack([index // z.split, index % z.split]).astype(jnp.int32)
    router = jnp.swapaxes(router, 1, 2)
    others = range(1, z.split)

    fwd_chunks, (grad, act, gain_row, table), slots = forward_chunks(
        z, where, fwd_ids, fwd_act, bwd_ids, [bwd_grad, bwd_act, norm_gain, router]
    )
    fwd_own = dispatch(z, fwd_chunks)
    bwd_chunks, vectors = backward_chunks(z, where, slots, [grad, act], gain_row, table)
    bwd_own = dispatch(z, bwd_chunks)

    down_turned = turned(z, w_down, [w_gate], [bwd_chunks[0], fwd_own[1]], "turned_down")
    normed, gates, fwd_last = normed_rows(z, fwd_own, vectors, [down_turned])
    fwd_all = [normed] + [to_core(z, normed, m) for m in others]
    ordered = saved_rows(z, where, saved_gate, [], [gates])
    fwd_parts = experts_forward(z, fwd_all, w_gate, w_down, [ordered])
    hidden, slope = saved_terms(z, ordered, [fwd_parts[0]])
    gate_turned = turned(z, w_gate, [], [hidden], "turned_gate")
    fwd_parts = [fwd_parts[0]] + [to_core(z, fwd_parts[m], m) for m in others]

    assert z.experts == 4

    def finish(ks, after):
        return finish_forward(z, ks, fwd_own, fwd_last, fwd_parts, gates, after)

    double = finish([0, 1], [gate_turned])
    got = to_section(z, double, 0, 1)
    out2 = finish([2], [hidden, double])
    got2 = to_section(z, out2, 2, 1)
    grads, grad_last = grad_rows_of(z, bwd_own, [out2])
    grad_all = [grads] + [to_core(z, grads, m) for m in others]
    out3 = finish([3], [grads])
    got3 = to_section(z, out3, 3, 1)
    bwd_parts = experts_backward(z, grad_all, hidden, slope, gate_turned, down_turned, [out3])
    inv, act_last = act_norms(z, bwd_own, [bwd_parts[0]])
    affinity = act_gates(z, bwd_own, act_last, inv, vectors, [bwd_parts[0]])
    fwd_done = [got2, got3]
    bwd_parts = [bwd_parts[0]] + [to_core(z, bwd_parts[m], m) for m in others]
    order = z.order
    bwd_out = finish_backward(
        z, order, bwd_own, [grad_last, act_last], [inv, affinity], bwd_parts, vectors, []
    )
    (relayed,) = permute_blocks(z, [lower_chunk(z, got, [bwd_out[0]])], 1)
    bwd_done = {k: to_section(z, out, k, -1) for k, out in zip(order, bwd_out)}

    early = some_rows(z, {0: got, 2: got2, 3: got3}, [], "forward_rows_early")
    outputs = [({1: relayed}, [early]), ({k: bwd_done[k] for k in z.order}, [])]
    fwd_next, bwd_next = order_rows(z, outputs, "all_rows")
    return (fwd_next, bwd_next)


def solution(mesh):
    return jax.shard_map(
        on_device,
        mesh=mesh,
        in_specs=(
            P(("pp", "ep"), None),
            P(("pp", "ep"), None),
            P(("pp", "ep"), None),
            P(("pp", "ep"), None),
            P(("pp", "ep"), None),
            P("pp", None),
            P("pp", None, None),
            P(("pp", "ep"), None, None),
            P(("pp", "ep"), None, None),
            P("pp", "ep", None, None),
        ),
        out_specs=(P(("pp", "ep"), None), P(("pp", "ep"), None)),
        check_vma=False,
    )
```

```python
import functools

import jax
import jax.numpy as jnp
from jax import lax
from jax.experimental import pallas as pl
from jax.experimental.pallas import tpu as pltpu
from jax.sharding import PartitionSpec as P

epsilon = 1e-06
route_scale = 2.5
fold = 256
none = 255.0
f32 = jnp.float32
bf16 = jnp.bfloat16
nn = (((1,), (0,)), ((), ()))
spaces = {
    "s": pl.BlockSpec(memory_space=pltpu.SMEM),
    "v": pl.BlockSpec(memory_space=pltpu.VMEM),
    "a": pl.BlockSpec(memory_space=pl.ANY),
    "h": pl.BlockSpec(memory_space=pltpu.HBM),
}


cost = {
    "backward_chunks": 10,
    "saved_rows": 15,
    "saved_terms": 15,
    "finish_forward_3": 15,
    "act_gates": 15,
    "forward_rows_early": 15,
}


def call(body, places, outs, scratch, megabytes, name, out_specs=None):
    def run(*arrays):
        arrays = [
            pltpu.with_memory_space_constraint(array, pltpu.HBM) if place == "h" else array
            for array, place in zip(arrays, places, strict=True)
        ]
        return kernel(*arrays)

    where_to = {} if out_specs is None else {"out_specs": out_specs}
    kernel = pl.pallas_call(
        body,
        out_shape=outs,
        in_specs=[spaces[place] for place in places],
        **where_to,
        scratch_shapes=scratch,
        compiler_params=pltpu.CompilerParams(vmem_limit_bytes=megabytes * 1024 * 1024),
        cost_estimate=pl.CostEstimate(
            flops=int(cost.get(name, 0.1) * 1e9), bytes_accessed=1000, transcendentals=0
        ),
        name=name,
    )
    return run


def shape(dims, kind=bf16):
    return jax.ShapeDtypeStruct(dims, kind)


class Sizes:
    def __init__(self, groups, experts, tokens, width):
        self.experts = experts
        self.split = groups // experts
        self.tokens = tokens
        self.width = width
        self.main = tokens // experts
        self.cap = self.main + 1
        self.pieces = width // fold
        self.wide = width + fold
        self.rows = tokens + 16
        self.order = [experts - 1, *range(1, experts - 1), 0]
        assert self.main == 16 and self.pieces <= 14 and width % fold == 0
        assert experts <= 8 and experts & (experts - 1) == 0 and self.split & (self.split - 1) == 0


def pack_last(row, tile, first=0):
    for i in range(row.shape[1] // fold):
        tile[first + i : first + i + 1, :] = row[:, i * fold : (i + 1) * fold]


def unpack_last(chunk, z, tile, target, at, base=0):
    tile[...] = chunk[base : base + 16, z.width :].astype(f32)
    for i in range(z.pieces):
        target[at : at + 1, i * fold : (i + 1) * fold] = tile[i : i + 1, :]


def slot_matrices(ids_row, block, z):
    tokens = z.tokens
    sub = lax.broadcasted_iota(jnp.int32, (tokens, tokens), 0)
    lane = lax.broadcasted_iota(jnp.int32, (tokens, tokens), 1)
    row = jnp.bitwise_xor(ids_row, block)
    column = jnp.sum(jnp.where(sub == lane, row, 0), axis=1, keepdims=True)
    same = column == row
    place_row = jnp.sum(jnp.where(same & (sub < lane), 1, 0), axis=0, keepdims=True)
    place_column = jnp.sum(jnp.where(same & (lane < sub), 1, 0), axis=1, keepdims=True)

    def slot(expert, place):
        return jnp.where(place < z.main, expert * z.main + place, tokens + expert)

    slot_row = slot(row, place_row)
    slot_column = slot(column, place_column)
    by_slot = lax.broadcasted_iota(jnp.int32, (z.rows, tokens), 0) == slot_row
    lane = lax.broadcasted_iota(jnp.int32, (tokens, fold), 1)
    by_token = jnp.where(lane < tokens, lane, tokens + (lane - tokens) // 16) == slot_column
    token = lax.broadcasted_iota(jnp.int32, (tokens, fold), 0).astype(f32)
    token_row = jnp.sum(jnp.where(by_token, token - none, 0.0), axis=0, keepdims=True) + none
    return jnp.where(by_slot, 1.0, 0.0).astype(bf16), token_row


def write_chunks(z, selector, token_row, rows_ref, ready, tiles, chunks, base):
    step = z.width // 2
    tiles[...] = jnp.zeros_like(tiles)
    for half in range(2):
        if ready:
            ready[half].wait()
        col = half * step
        got = jnp.dot(selector, rows_ref[:, col : col + step], preferred_element_type=f32)
        packed = got[: z.tokens].astype(bf16)
        for k in range(z.experts):
            chunks[k][base : base + 16, col : col + step] = packed[k * z.main : (k + 1) * z.main]
            pack_last(got[z.tokens + k : z.tokens + k + 1], tiles.at[k], half * z.pieces // 2)
    for k in range(z.experts):
        tiles[k, z.pieces : z.pieces + 1, :] = token_row
        chunks[k][base : base + 16, z.width :] = tiles[k].astype(bf16)


def forward_chunks(z, where, ids, act, later_ids, later):
    count = len(later)

    def body(where, ids_any, later_ids_any, act_any, *refs):
        later_any, chunks = refs[:count], refs[count : count + z.experts]
        later_refs = refs[count + z.experts : 2 * count + z.experts]
        selector_ref, token_ref, ids, rows, tiles, sems = refs[2 * count + z.experts :]
        step = z.width // 2
        first = [
            pltpu.make_async_copy(source, ids.at[i : i + 1], sems.at[i])
            for i, source in enumerate((ids_any, later_ids_any))
        ]
        ready = [
            pltpu.make_async_copy(
                act_any.at[:, pl.ds(i * step, step)], rows.at[:, pl.ds(i * step, step)], sems.at[2 + i]
            )
            for i in range(2)
        ]
        rest = [
            pltpu.make_async_copy(source, target, sems.at[4 + i])
            for i, (source, target) in enumerate(zip(later_any, later_refs))
        ]
        for copy in first + ready + rest:
            copy.start()
        for copy in first:
            copy.wait()
        selector, token_row = slot_matrices(ids[0:1, :], where[0], z)
        later_selector, later_row = slot_matrices(ids[1:2, :], where[0], z)
        selector_ref[...] = later_selector
        token_ref[...] = jnp.broadcast_to(later_row, token_ref.shape)
        write_chunks(z, selector, token_row, rows, ready, tiles, chunks, 0)
        for copy in rest:
            copy.wait()

    outs = call(
        body,
        "shhh" + "h" * count,
        [shape((z.main, z.wide))] * z.experts
        + [shape(array.shape, array.dtype) for array in later]
        + [shape((z.rows, z.tokens)), shape((8, fold), f32)],
        [
            pltpu.VMEM((2, z.tokens), jnp.int32),
            pltpu.VMEM((z.tokens, z.width), bf16),
            pltpu.VMEM((z.experts, 16, fold), f32),
            pltpu.SemaphoreType.DMA((4 + count,)),
        ],
        8,
        "forward_chunks",
    )(where, ids.reshape(1, z.tokens), later_ids.reshape(1, z.tokens), act, *later)
    return outs[: z.experts], outs[z.experts : z.experts + count], outs[z.experts + count :]


def backward_chunks(z, where, slots, sources, gain, router):
    count = len(sources)

    def body(where, selector, token_ref, *refs):
        sources, (gain_ref, router_ref) = refs[:count], refs[count : count + 2]
        *chunks, vectors, tiles = refs[count + 2 :]
        for j in range(count):
            write_chunks(
                z, selector[...], token_ref[0:1, :], sources[j], None, tiles, chunks, 16 * j
            )
        vectors[...] = jnp.zeros_like(vectors)
        vectors[0:1, :] = gain_ref[...].astype(f32)
        mine = lax.broadcasted_iota(jnp.int32, (z.experts, 1), 0) == where[0]
        table = jnp.where(mine, router_ref[0].astype(f32), 0.0)
        vectors[1:2, :] = jnp.sum(table, axis=0, keepdims=True)

    *chunks, vectors = call(
        body,
        "svv" + "v" * (count + 2),
        [shape((z.main * count, z.wide))] * z.experts + [shape((8, z.width), f32)],
        [pltpu.VMEM((z.experts, 16, fold), f32)],
        8,
        "backward_chunks",
    )(where, *slots, *sources, gain, router)
    return chunks, vectors


def collect_rows(z, chunks, last, tile, base=0):
    last[...] = jnp.zeros_like(last)
    for k in range(z.experts):
        unpack_last(chunks[k], z, tile, last, k, base)


def norm_rows(h, gain):
    inv = lax.rsqrt(jnp.mean(h * h, axis=-1, keepdims=True) + epsilon)
    return (h * inv * gain).astype(bf16), inv


def normed_rows(z, chunks, vectors, after):
    def body(*refs):
        chunks, vectors = refs[: z.experts], refs[z.experts]
        normed_ref, gates_ref, last, tile = refs[z.experts + 1 + len(after) :]
        gain, router = vectors[0:1, :], vectors[1:2, :]
        collect_rows(z, chunks, last, tile)
        for k in range(z.experts + 1):
            h = last[...] if k == z.experts else chunks[k][:, : z.width].astype(f32)
            at = k * z.main
            normed, _ = norm_rows(h, gain)
            normed_ref[at : at + 16, :] = normed
            logits = jnp.sum(normed.astype(f32) * router, axis=-1, keepdims=True)
            gates_ref[at : at + 16, :] = jnp.broadcast_to(jax.nn.sigmoid(logits), (16, 128))

    return call(
        body,
        "v" * (z.experts + 1) + "a" * len(after),
        [shape((z.rows, z.width)), shape((z.rows, 128), f32), shape((16, z.width), f32)],
        [pltpu.VMEM((16, fold), f32)],
        8,
        "normed_rows",
    )(*chunks, vectors, *after)


def grad_rows_of(z, chunks, after):
    def body(*refs):
        chunks, (rows, last, tile) = refs[: z.experts], refs[z.experts + len(after) :]
        for k in range(z.experts):
            rows[k * z.main : (k + 1) * z.main, :] = chunks[k][:16, : z.width]
        collect_rows(z, chunks, last, tile)
        rows[z.tokens :, :] = last[...].astype(bf16)

    return call(
        body,
        "v" * z.experts + "a" * len(after),
        [shape((z.rows, z.width)), shape((16, z.width), f32)],
        [pltpu.VMEM((16, fold), f32)],
        8,
        "grad_rows",
    )(*chunks, *after)


def act_norms(z, chunks, after):
    def body(*refs):
        chunks, (inv_ref, last, tile) = refs[: z.experts], refs[z.experts + len(after) :]
        collect_rows(z, chunks, last, tile, 16)
        for k in range(z.experts + 1):
            h = last[...] if k == z.experts else chunks[k][16:32, : z.width].astype(f32)
            at = k * z.main
            inv = lax.rsqrt(jnp.mean(h * h, axis=-1, keepdims=True) + epsilon)
            inv_ref[at : at + 16, :] = jnp.broadcast_to(inv, (16, 128))

    return call(
        body,
        "v" * z.experts + "a" * len(after),
        [shape((z.rows, 128), f32), shape((16, z.width), f32)],
        [pltpu.VMEM((16, fold), f32)],
        8,
        "act_norms",
    )(*chunks, *after)


def act_gates(z, chunks, last, inv, vectors, after):
    def body(*refs):
        chunks, (last, inv_ref, vectors) = refs[: z.experts], refs[z.experts : z.experts + 3]
        affinity_ref = refs[-1]
        gain, router = vectors[0:1, :], vectors[1:2, :]
        for k in range(z.experts + 1):
            h = last[...] if k == z.experts else chunks[k][16:32, : z.width].astype(f32)
            at = k * z.main
            normed = (h * inv_ref[at : at + 16, 0:1] * gain).astype(bf16).astype(f32)
            logits = jnp.sum(normed * router, axis=-1, keepdims=True)
            affinity_ref[at : at + 16, :] = jnp.broadcast_to(jax.nn.sigmoid(logits), (16, 128))

    return call(
        body,
        "v" * (z.experts + 3) + "a" * len(after),
        shape((z.rows, 128), f32),
        [],
        8,
        "act_gates",
    )(*chunks, last, inv, vectors, *after)


def write_parts(z, values, outs, col):
    values = values.astype(bf16)
    for m in range(z.split):
        outs[m][:, col : col + values.shape[1]] = values[m * z.rows : (m + 1) * z.rows]


def experts_forward(z, rows, w_gate, w_down, after):
    def body(*refs):
        rows, (gate_ref, down_ref), outs = (
            refs[: z.split],
            refs[z.split : z.split + 2],
            refs[z.split + 2 + len(after) :],
        )
        held = jnp.concatenate([part[...] for part in rows], axis=0)
        gate_proj = jnp.dot(held, gate_ref[0], preferred_element_type=f32)
        hidden = jax.nn.silu(gate_proj).astype(bf16)
        step = 512
        for col in range(0, z.width, step):
            part = jnp.dot(hidden, down_ref[0, :, col : col + step], preferred_element_type=f32)
            write_parts(z, part, outs, col)

    return call(
        body,
        "v" * (z.split + 2) + "a" * len(after),
        [shape((z.rows, z.width))] * z.split,
        [],
        16,
        "experts_forward",
    )(*rows, w_gate, w_down, *after)


def saved_rows(z, where, saved, weights, after):
    total, slots, width = z.split * z.rows, saved.shape[2], saved.shape[3]

    def body(where, saved_any, *refs):
        ordered_ref, saved_ref, sem = refs[len(weights) + len(after) :]
        copy = pltpu.make_async_copy(saved_any.at[0, 0], saved_ref, sem)
        copy.start()
        row = lax.broadcasted_iota(jnp.int32, (total, slots), 0)
        slot = lax.broadcasted_iota(jnp.int32, (total, slots), 1)
        m, at = row // z.rows, row % z.rows
        is_main = at < z.tokens
        k = jnp.where(is_main, at // z.main, at - z.tokens)
        p = jnp.where(is_main, at % z.main, z.main)
        source = jnp.bitwise_xor(k, where[0]) * z.split + jnp.bitwise_xor(m, where[1])
        wanted = jnp.where(k < z.experts, source * z.cap + p, -1)
        selector = jnp.where(slot == wanted, 1.0, 0.0).astype(bf16)
        copy.wait()
        ordered_ref[...] = jnp.dot(selector, saved_ref[...], preferred_element_type=f32)

    return call(
        body,
        "sh" + "v" * len(weights) + "a" * len(after),
        shape((total, width), f32),
        [pltpu.VMEM((slots, width), bf16), pltpu.SemaphoreType.DMA],
        8,
        "saved_rows",
    )(where, saved, *weights, *after)


def saved_terms(z, ordered, after):
    def body(ordered_ref, *refs):
        hidden_ref, slope_ref = refs[len(after) :]
        gate_proj = ordered_ref[...]
        sg = jax.nn.sigmoid(gate_proj)
        hidden_ref[...] = (gate_proj * sg).astype(bf16)
        slope_ref[...] = sg * (1.0 + gate_proj * (1.0 - sg))

    return call(
        body,
        "v" + "a" * len(after),
        [shape(ordered.shape), shape(ordered.shape, f32)],
        [],
        8,
        "saved_terms",
    )(ordered, *after)


def turned(z, weights, held, after, name):
    rows, columns = weights.shape[1:]
    step = min(512, rows, columns)

    def body(weights_ref, *refs):
        for at in range(0, rows, step):
            for col in range(0, columns, step):
                block = weights_ref[0, at : at + step, col : col + step]
                refs[-1][col : col + step, at : at + step] = block.T

    return call(
        body, "v" + "v" * len(held) + "a" * len(after), shape((columns, rows)), [], 12, name
    )(weights, *held, *after)


def experts_backward(z, rows, hidden, slope, w_gate, w_down, after):
    def body(*refs):
        rows = refs[: z.split]
        hidden_ref, slope_ref, gate_ref, down_ref = refs[z.split : z.split + 4]
        outs = refs[z.split + 4 + len(after) :]
        held = jnp.concatenate([part[...] for part in rows], axis=0)
        grad_hidden = lax.dot_general(held, down_ref[...], nn, preferred_element_type=f32)
        dots = jnp.sum(grad_hidden * hidden_ref[...].astype(f32), axis=-1, keepdims=True)
        grad_gate = (grad_hidden * slope_ref[...]).astype(bf16)
        step = 512
        for col in range(0, z.width, step):
            part = lax.dot_general(
                grad_gate, gate_ref[:, col : col + step], nn, preferred_element_type=f32
            )
            write_parts(z, part, outs, col)
        write_parts(z, jnp.broadcast_to(dots, (dots.shape[0], 128)), outs, z.width)

    return call(
        body,
        "v" * (z.split + 4) + "a" * len(after),
        [shape((z.rows, z.width + 128))] * z.split,
        [],
        16,
        "experts_backward",
    )(*rows, hidden, slope, w_gate, w_down, *after)


def put_last(z, values, source_chunk, tile, out):
    tile[...] = jnp.zeros_like(tile)
    pack_last(values, tile)
    tokens = source_chunk[:16, z.width :].astype(f32)
    tile[z.pieces : z.pieces + 1, :] = tokens[z.pieces : z.pieces + 1, :]
    out[:, z.width :] = tile[...].astype(bf16)


def finish_forward(z, ks, chunks, last, parts, gates, after):
    count = len(ks)

    def body(*refs):
        chunks, last, parts = refs[:count], refs[count], refs[count + 1 : count + 1 + z.split]
        gates, out, tile = refs[count + 1 + z.split], refs[-2], refs[-1]

        def mixed(at):
            y = parts[0][at : at + 16, :].astype(f32)
            for part in parts[1:]:
                y = y + part[at : at + 16, :].astype(f32)
            return route_scale * (gates[at : at + 16, 0:1] * y)

        tail = last[...] + mixed(z.tokens)
        for i, (k, chunk) in enumerate(zip(ks, chunks)):
            h = chunk[:, : z.width].astype(f32)
            rows = out.at[pl.ds(i * 16, 16)]
            rows[:, : z.width] = (h + mixed(k * z.main)).astype(bf16)
            put_last(z, tail[k : k + 1, :], chunk, tile, rows)

    return call(
        body,
        "v" * (count + z.split + 2) + "a" * len(after),
        shape((count * z.main, z.wide)),
        [pltpu.VMEM((16, fold), f32)],
        8,
        "finish_forward_" + "".join(map(str, ks)),
    )(*[chunks[k] for k in ks], last, *parts, gates, *after)


def lower_chunk(z, double, after):
    def body(double, *refs):
        refs[-1][...] = double[16:32, :]

    places = "v" + "a" * len(after)
    return call(body, places, shape((16, z.wide)), [], 8, "lower_chunk")(double, *after)


def finish_backward(z, order, chunks, lasts, terms, parts, vectors, after):
    def body(*refs):
        e = z.experts
        chunks, (last_grad, last_act, inv_ref, affinity_ref) = refs[:e], refs[e : e + 4]
        parts, vectors = refs[e + 4 : e + 4 + z.split], refs[e + 4 + z.split]
        outs, (tile,) = refs[-1 - e : -1], refs[-1:]
        outs = [outs[order.index(k)] for k in range(e)]
        gain, router = vectors[0:1, :], vectors[1:2, :]

        def finished(h, g, at):
            inv, affinity = inv_ref[at : at + 16, 0:1], affinity_ref[at : at + 16, 0:1]
            rows = parts[0][at : at + 16, : z.width].astype(f32)
            dot = parts[0][at : at + 16, z.width :].astype(f32)
            for part in parts[1:]:
                rows = rows + part[at : at + 16, : z.width].astype(f32)
                dot = dot + part[at : at + 16, z.width :].astype(f32)
            dot = dot[:, 0:1]
            grad_logits = (route_scale * dot * affinity * (1.0 - affinity)).astype(bf16).astype(f32)
            grad_pre = (route_scale * affinity * rows + grad_logits * router) * gain
            centre = jnp.mean(grad_pre * h, axis=-1, keepdims=True)
            return g + inv * (grad_pre - h * (inv * inv * centre))

        tail = finished(last_act[...], last_grad[...], z.tokens)
        for k in range(e):
            g = chunks[k][:16, : z.width].astype(f32)
            h = chunks[k][16:32, : z.width].astype(f32)
            outs[k][:, : z.width] = finished(h, g, k * z.main).astype(bf16)
            put_last(z, tail[k : k + 1, :], chunks[k], tile, outs[k])

    return call(
        body,
        "v" * (z.experts + z.split + 5) + "a" * len(after),
        [shape((z.main, z.wide))] * z.experts,
        [pltpu.VMEM((16, fold), f32)],
        8,
        "finish_backward",
    )(*chunks, *lasts, *terms, *parts, vectors, *after)


def ordered_columns(z, chunks):
    lanes = z.tokens + 16 * z.experts
    some = next(iter(chunks))
    filled = [chunks.get(k, chunks[some]) for k in range(z.experts)]
    tiles = [chunk[:16, z.width :] for chunk in filled]
    token_row = tiles[some].astype(f32)[z.pieces : z.pieces + 1, :lanes]
    token = lax.broadcasted_iota(jnp.int32, (z.tokens, lanes), 0).astype(f32)
    lane = lax.broadcasted_iota(jnp.int32, (z.tokens, lanes), 1)
    piece = jnp.where(lane < z.tokens, -1, lane % 16)
    ours = token == token_row
    if len(chunks) < z.experts:
        held = [lane // 16 % z.experts == k for k in chunks]
        ours = ours & functools.reduce(jnp.logical_or, held)
    for i in range(z.pieces):
        cols = pl.ds(i * fold, fold)
        selector = jnp.where(ours & ((piece < 0) | (piece == i)), 1.0, 0.0).astype(bf16)
        rows = jnp.concatenate([chunk[:16, cols] for chunk in filled] + tiles, axis=0)
        yield cols, jnp.dot(selector, rows, preferred_element_type=f32)


def some_rows(z, chunks, after, name):
    ks = list(chunks)

    def body(*refs):
        for cols, rows in ordered_columns(z, dict(zip(ks, refs))):
            refs[-1][:, cols] = rows.astype(bf16)

    places = "v" * len(ks) + "a" * len(after)
    return call(body, places, shape((z.tokens, z.width)), [], 8, name)(*chunks.values(), *after)


def order_rows(z, outputs, name):
    steps = 7 if z.pieces % 7 == 0 else z.pieces
    arrays, layout = [], []
    for chunks, others in outputs:
        layout.append((len(arrays), list(chunks), len(others)))
        arrays += [*chunks.values(), *others]
    number = len(outputs)

    def body(*refs):
        inputs, anys = refs[: len(arrays)], refs[len(arrays) : len(arrays) + number]
        outs, sems = refs[-1 - number : -1], refs[-1]
        copies = []
        for n, (at, ks, more) in enumerate(layout):
            chunks = dict(zip(ks, inputs[at : at + len(ks)]))
            others = inputs[at + len(ks) : at + len(ks) + more]
            for i, (cols, rows) in enumerate(ordered_columns(z, chunks)):
                for other in others:
                    rows = rows + other[:, cols].astype(f32)
                outs[n][:, cols] = rows.astype(bf16)
                if (i + 1) % (z.pieces // steps) == 0:
                    width = z.width // steps
                    done = pl.ds((i + 1) * fold - width, width)
                    copy = pltpu.make_async_copy(
                        outs[n].at[:, done], anys[n].at[:, done], sems.at[len(copies)]
                    )
                    copy.start()
                    copies.append(copy)
        for copy in copies:
            copy.wait()

    return call(
        body,
        "v" * len(arrays),
        [shape((z.tokens, z.width))] * number,
        [pltpu.VMEM((z.tokens, z.width), bf16)] * number
        + [pltpu.SemaphoreType.DMA((number * steps,))],
        8,
        name,
        [spaces["a"]] * number,
    )(*arrays)


def permute_blocks(z, arrays, k):
    groups = z.experts * z.split
    pairs = [(i, ((i // z.split) ^ k) * z.split + i % z.split) for i in range(groups)]
    return [lax.ppermute(array, "ep", pairs) for array in arrays]


def dispatch(z, chunks):
    return [chunks[0]] + [permute_blocks(z, [chunks[k]], k)[0] for k in range(1, z.experts)]


def to_core(z, array, m):
    groups = z.experts * z.split
    pairs = [(i, i // z.split * z.split + ((i % z.split) ^ m)) for i in range(groups)]
    return lax.ppermute(array, "ep", pairs)


def to_section(z, chunk, k, by):
    groups = z.experts * z.split
    sections = lax.axis_size("pp")
    pairs = [
        (s * groups + i, (s + by) % sections * groups + ((i // z.split) ^ k) * z.split + i % z.split)
        for s in range(sections)
        for i in range(groups)
    ]
    return lax.ppermute(chunk, ("pp", "ep"), pairs)


def on_device(
    fwd_act, fwd_ids, bwd_act, bwd_ids, bwd_grad, norm_gain, router, w_gate, w_down, saved_gate
):
    groups = lax.axis_size("ep")
    assert fwd_ids.shape[1] == 1
    z = Sizes(groups, router.shape[2], fwd_act.shape[0], fwd_act.shape[1])
    index = lax.axis_index("ep")
    where = jnp.stack([index // z.split, index % z.split]).astype(jnp.int32)
    router = jnp.swapaxes(router, 1, 2)
    others = range(1, z.split)

    fwd_chunks, (grad, act, gain_row, table), slots = forward_chunks(
        z, where, fwd_ids, fwd_act, bwd_ids, [bwd_grad, bwd_act, norm_gain, router]
    )
    fwd_own = dispatch(z, fwd_chunks)
    bwd_chunks, vectors = backward_chunks(z, where, slots, [grad, act], gain_row, table)
    bwd_own = dispatch(z, bwd_chunks)

    down_turned = turned(z, w_down, [w_gate], [bwd_chunks[0]], "turned_down")
    normed, gates, fwd_last = normed_rows(z, fwd_own, vectors, [down_turned])
    fwd_all = [normed] + [to_core(z, normed, m) for m in others]
    ordered = saved_rows(z, where, saved_gate, [], [gates])
    fwd_parts = experts_forward(z, fwd_all, w_gate, w_down, [ordered])
    hidden, slope = saved_terms(z, ordered, [fwd_parts[0]])
    gate_turned = turned(z, w_gate, [], [hidden], "turned_gate")
    fwd_parts = [fwd_parts[0]] + [to_core(z, fwd_parts[m], m) for m in others]

    assert z.experts == 4

    def finish(ks, after):
        return finish_forward(z, ks, fwd_own, fwd_last, fwd_parts, gates, after)

    double = finish([0, 1], [gate_turned])
    got = to_section(z, double, 0, 1)
    out2 = finish([2], [hidden, double])
    got2 = to_section(z, out2, 2, 1)
    grads, grad_last = grad_rows_of(z, bwd_own, [out2])
    grad_all = [grads] + [to_core(z, grads, m) for m in others]
    out3 = finish([3], [grads])
    got3 = to_section(z, out3, 3, 1)
    bwd_parts = experts_backward(z, grad_all, hidden, slope, gate_turned, down_turned, [out3])
    inv, act_last = act_norms(z, bwd_own, [bwd_parts[0]])
    affinity = act_gates(z, bwd_own, act_last, inv, vectors, [bwd_parts[0]])
    fwd_done = [got2, got3]
    bwd_parts = [bwd_parts[0]] + [to_core(z, bwd_parts[m], m) for m in others]
    order = z.order
    bwd_out = finish_backward(
        z, order, bwd_own, [grad_last, act_last], [inv, affinity], bwd_parts, vectors, []
    )
    (relayed,) = permute_blocks(z, [lower_chunk(z, got, [bwd_out[0]])], 1)
    bwd_done = {k: to_section(z, out, k, -1) for k, out in zip(order, bwd_out)}

    early = some_rows(z, {0: got, 2: got2, 3: got3}, [], "forward_rows_early")
    outputs = [({1: relayed}, [early]), ({k: bwd_done[k] for k in z.order}, [])]
    fwd_next, bwd_next = order_rows(z, outputs, "all_rows")
    return (fwd_next, bwd_next)


def solution(mesh):
    return jax.shard_map(
        on_device,
        mesh=mesh,
        in_specs=(
            P(("pp", "ep"), None),
            P(("pp", "ep"), None),
            P(("pp", "ep"), None),
            P(("pp", "ep"), None),
            P(("pp", "ep"), None),
            P("pp", None),
            P("pp", None, None),
            P(("pp", "ep"), None, None),
            P(("pp", "ep"), None, None),
            P("pp", "ep", None, None),
        ),
        out_specs=(P(("pp", "ep"), None), P(("pp", "ep"), None)),
        check_vma=False,
    )
```
